32 devices in a mesh: gx: 4 (over z), gy: 4 (over x, core), gz: 2 (over y).
Axes of the slice: x: 2, y: 2, z: 4, core: 2. Of those that a mesh axis runs over, the one named last changes fastest.
Arguments:
- plume_flow_variables: float32 [6, 32, 64, 256], P(None, 'gx', 'gy', 'gz'), may hold values from -6 to 6
- thermal_field: float32 [128, 64, 128], P(None, ('gx', 'gz'), 'gy'), may hold values from -6 to 6
- matter_condition: int32 [128, 64, 128], P(None, ('gx', 'gz'), 'gy'), may hold values from 0 to 2
- pool_boundary_level: int32 [32, 64], P('gx', 'gy'), may hold values from 0 to 127
- beam_focus_path: int32 [4, 2], replicated, may hold values from 0 to 127, as said below
Outputs:
- gas_out: float32 [6, 32, 64, 256], P(None, 'gx', 'gy', 'gz')
- temperature_out: float32 [128, 64, 128], P(None, ('gx', 'gz'), 'gy')
The draws below stay inside these ranges and needn't reach their ends.
Inputs may be any that keep to these rules, and one draw needn't show every extreme that they name: `beam_focus_path`: column 0 is a position along the part's first lateral dimension, below 64; column 1 along the second, below 128.
All inputs are finite; a program needn't handle non-finite values.
Results may differ from the reference program's by a relative error of at most 0.0001.
Values sent between devices are 32-bit elements; how exact they have to be, the bound alone decides.
No kernel may reach another device: no remote copies, remote signals or barrier semaphores. Data moves between devices by JAX's collectives and lax.ppermute only.
A program may use at most 64 MiB of HBM per device.

```python
import jax
import jax.numpy as jnp

GZC = 128
WORKPIECE_LAYERS = 128
STEPS = 2
SUBSTEPS = 2
NXG = 32
NYG = 64
NZG = 256
WORKPIECE_ROWS = 64
WORKPIECE_COLS = 128
NSUB = 4


def draw_beam_focus_path(key, part):
    key_rows, key_cols = jax.random.split(jax.random.fold_in(key, 17))
    along_first = jax.random.randint(key_rows, (NSUB, 1), 0, WORKPIECE_ROWS)
    along_second = jax.random.randint(key_cols, (NSUB, 1), 0, WORKPIECE_COLS)
    path_rows = jnp.concatenate([along_first, along_second], axis=1).astype(jnp.int32)
    path_rows = path_rows.at[0, 0].set(0)
    path_rows = path_rows.at[NSUB - 1, 0].set(WORKPIECE_ROWS - 1)
    path_rows = path_rows.at[NSUB - 1, 1].set(WORKPIECE_COLS - 1)
    return path_rows.astype(jnp.int32)


def place_ends(drawn, key, least, high):
    shape = drawn.shape
    place = [jax.random.randint(jax.random.fold_in(key, axis), (), 0, shape[axis]) for axis in range(len(shape))]
    drawn = drawn.at[tuple(place)].set(least)
    longest = shape.index(max(shape))
    place[longest] = (place[longest] + 1) % shape[longest]
    return drawn.at[tuple(place)].set(high)


def shard_levels(own_key, extent, cuts, smallest, largest):
    def one(position, blocks):
        steps = jax.random.uniform(jax.random.fold_in(jax.random.fold_in(own_key, 6), position), (blocks,), jnp.float32, smallest / len(cuts), largest / len(cuts))
        return jnp.repeat(jnp.exp(steps), extent[position] // blocks).reshape((-1,) + (1,) * (len(extent) - position - 1))

    factor_of = one(*cuts[0])
    for cut in cuts[1:]:
        factor_of = factor_of * one(*cut)
    return factor_of


def centred(stream_key, extent, deviation, most, cuts=(), kind=jnp.bfloat16):
    drawn = deviation * jax.random.normal(stream_key, extent, jnp.float32)
    if cuts:
        drawn = drawn * shard_levels(stream_key, extent, cuts, -0.22, 0.18)
    return jnp.clip(drawn, -most, most).astype(kind)


def setup_inputs(seed: int = 0) -> dict:
    keys = jax.random.split(jax.random.key(seed), 6)
    return {
        "plume_flow_variables": centred(keys[0], (6, NXG, NYG, NZG), 1.0, 6.0, ((1, 4), (2, 4), (3, 2)), jnp.float32),
        "thermal_field": centred(keys[1], (WORKPIECE_LAYERS, WORKPIECE_ROWS, WORKPIECE_COLS), 1.0, 6.0, ((1, 8), (2, 4)), jnp.float32),
        "matter_condition": place_ends(jax.random.randint(keys[2], (WORKPIECE_LAYERS, WORKPIECE_ROWS, WORKPIECE_COLS), 0, 3), jax.random.fold_in(keys[2], 1), 0, 2).astype(jnp.int32),
        "pool_boundary_level": place_ends(jax.random.randint(keys[3], (NXG, NYG), 0, GZC), jax.random.fold_in(keys[3], 1), 0, GZC - 1).astype(jnp.int32),
        "beam_focus_path": draw_beam_focus_path(jax.random.fold_in(keys[5], 71), 0),
    }


GAS_STEP = 0.3
DRIFT_SPEED = 0.5
VAPOR_LOAD = 0.3
AMBIENT_LOAD = 0.7
STIFFNESS = 1.0
VISCOSITY = (0.2, 0.1, 0.15, 0.15, 0.15, 0.2)
HEAT_STEP = 1.0
POWDER_COND = 0.04
SOLID_COND = 0.15
LIQUID_COND = 0.09
LASER_POWER = 3.0
SPOT_RADIUS = 6.0
ABSORB_DEPTH = 4.0
BOIL_LEVEL = 1.0
BACK_PRESSURE = 0.5
LATENT_HEAT = 0.3
VAPOR_SOURCE = 0.5
RECOIL_PUSH = 0.4
RECOIL_PRESSURE = 0.6


def gas_rate(padded):
    center = padded[:, 1:-1, 1:-1, 1:-1]
    east_side = padded[:, 2:, 1:-1, 1:-1]
    west_side = padded[:, :-2, 1:-1, 1:-1]
    north_side = padded[:, 1:-1, 2:, 1:-1]
    south_side = padded[:, 1:-1, :-2, 1:-1]
    upper_side = padded[:, 1:-1, 1:-1, 2:]
    lower_side = padded[:, 1:-1, 1:-1, :-2]
    slope_x = 0.5 * (east_side - west_side)
    slope_y = 0.5 * (north_side - south_side)
    slope_z = 0.5 * (upper_side - lower_side)
    laplace = east_side + west_side + north_side + south_side + upper_side + lower_side - 6.0 * center
    spread = slope_x[2] + slope_y[3] + slope_z[4]
    viscous = jnp.array(VISCOSITY, jnp.float32).reshape(6, 1, 1, 1)
    coupled = jnp.stack([-VAPOR_LOAD * spread, -AMBIENT_LOAD * spread, -slope_x[5], -slope_y[5], -slope_z[5], -STIFFNESS * spread])
    return coupled - DRIFT_SPEED * slope_z + viscous * laplace


def neighbours(padded):
    return [padded[2:, 1:-1, 1:-1], padded[:-2, 1:-1, 1:-1], padded[1:-1, 2:, 1:-1],
            padded[1:-1, :-2, 1:-1], padded[1:-1, 1:-1, 2:], padded[1:-1, 1:-1, :-2]]


def heat_rate(padded_temp, padded_cond):
    center = padded_temp[1:-1, 1:-1, 1:-1]
    cond_center = padded_cond[1:-1, 1:-1, 1:-1]
    total = jnp.zeros_like(center)
    for temp_side, cond_side in zip(neighbours(padded_temp), neighbours(padded_cond)):
        total = total + 0.5 * (cond_center + cond_side) * (temp_side - center)
    return total


def conductivity(matter_condition):
    return jnp.where(matter_condition == 0, POWDER_COND, jnp.where(matter_condition == 1, SOLID_COND, LIQUID_COND)).astype(jnp.float32)


def laser_heat(x_cells, y_cells, depth_cells, target):
    along_x = jnp.exp(-((x_cells - target[0].astype(jnp.float32)) / SPOT_RADIUS) ** 2)
    along_y = jnp.exp(-((y_cells - target[1].astype(jnp.float32)) / SPOT_RADIUS) ** 2)
    along_depth = jnp.exp(-depth_cells / ABSORB_DEPTH)
    return LASER_POWER * along_depth[:, None, None] * along_x[None, :, None] * along_y[None, None, :]


def evaporation(surface_temp, pressure):
    return jax.nn.softplus(surface_temp - BOIL_LEVEL - BACK_PRESSURE * pressure)


def refine(values):
    return jnp.repeat(jnp.repeat(values, 2, axis=0), 2, axis=1)


def coarsen(values):
    rows, cols = values.shape
    return 0.25 * jnp.sum(values.reshape(rows // 2, 2, cols // 2, 2), axis=(1, 3))


def reference(plume_flow_variables, thermal_field, matter_condition, pool_boundary_level, beam_focus_path):
    vapor_state = plume_flow_variables
    workpiece_thermal_mesh = thermal_field
    padded_cond = jnp.pad(conductivity(matter_condition), 1)
    heights = jnp.arange(NZG, dtype=jnp.int32)
    surface_mask = (heights[None, None, :] == pool_boundary_level[:, :, None]).astype(jnp.float32)
    x_cells = jnp.arange(WORKPIECE_ROWS, dtype=jnp.int32).astype(jnp.float32)
    y_cells = jnp.arange(WORKPIECE_COLS, dtype=jnp.int32).astype(jnp.float32)
    depth_cells = jnp.arange(WORKPIECE_LAYERS, dtype=jnp.int32).astype(jnp.float32)
    rim = ((0, 0), (1, 1), (1, 1), (1, 1))
    for outer_step in range(STEPS):
        first_section = vapor_state + GAS_STEP * gas_rate(jnp.pad(vapor_state, rim))
        vapor_state = 0.5 * (vapor_state + first_section + GAS_STEP * gas_rate(jnp.pad(first_section, rim)))
        pressure = jnp.sum(vapor_state[5] * surface_mask, axis=2)
        fine_pressure = refine(pressure)
        for substep in range(SUBSTEPS):
            target = beam_focus_path[outer_step * SUBSTEPS + substep]
            change = heat_rate(jnp.pad(workpiece_thermal_mesh, 1), padded_cond) + laser_heat(x_cells, y_cells, depth_cells, target)
            cooling = LATENT_HEAT * evaporation(workpiece_thermal_mesh[0], fine_pressure)
            change = change.at[0].add(-cooling)
            workpiece_thermal_mesh = workpiece_thermal_mesh + HEAT_STEP * change
        surface_temp = coarsen(workpiece_thermal_mesh[0])
        vapor_mass = evaporation(surface_temp, pressure)[:, :, None] * surface_mask
        vapor_state = vapor_state.at[0].add(VAPOR_SOURCE * vapor_mass)
        vapor_state = vapor_state.at[4].add(RECOIL_PUSH * vapor_mass)
        vapor_state = vapor_state.at[5].add(RECOIL_PRESSURE * vapor_mass)
    return vapor_state, workpiece_thermal_mesh
```

```python
import functools

import jax
import jax.numpy as jnp
from jax import lax
from jax.experimental import pallas as pl
from jax.experimental.pallas import tpu as pltpu
from jax.sharding import PartitionSpec as P

STEPS = 2
SUBSTEPS = 2
GAS_STEP = 0.3
DRIFT_SPEED = 0.5
VAPOR_LOAD = 0.3
AMBIENT_LOAD = 0.7
STIFFNESS = 1.0
VISCOSITY = (0.2, 0.1, 0.15, 0.15, 0.15, 0.2)
HEAT_STEP = 1.0
POWDER_COND = 0.04
SOLID_COND = 0.15
LIQUID_COND = 0.09
LASER_POWER = 3.0
SPOT_RADIUS = 6.0
ABSORB_DEPTH = 4.0
BOIL_LEVEL = 1.0
BACK_PRESSURE = 0.5
LATENT_HEAT = 0.3
VAPOR_SOURCE = 0.5
RECOIL_PUSH = 0.4
RECOIL_PRESSURE = 0.6

COMPS = 6
LANES = 128
SUBL = 8
F32 = jnp.float32
REACH = 6
REACH_LAST = 3
SKIN = 4
TOP = 8
GROUP = 16
LEVEL = 6
NEXT = 8


def iota(shape, axis):
    return lax.broadcasted_iota(jnp.int32, shape, axis)


def wrapped(index, own, size):
    return jnp.where(index < own + (size - own) // 2, index, index - size)


def turn(value, amount, axis):
    size = value.shape[axis]
    if isinstance(amount, int):
        amount = amount % size
        if amount == 0:
            return value
    return pltpu.roll(value, amount, axis)


def softplus(x):
    return jnp.maximum(x, 0.0) + jnp.log1p(jnp.exp(-jnp.abs(x)))


def edges(gz):
    return jnp.where(gz == 0, LANES - 1, 0), jnp.where(gz == 0, LANES - 2, 1)


def lane_turn(value, amount):
    return pltpu.roll(value, lax.rem(amount + 2 * LANES, LANES), 1)


def pack_heights(rows, base, lane, edge, behind, acc):
    for c, row in enumerate(rows):
        acc = jnp.where(lane == base + c, lane_turn(row, base + c - edge), acc)
        acc = jnp.where(lane == base + NEXT + c, lane_turn(row, base + NEXT + c - behind), acc)
    return acc


def pack_kernel(cells, meta, u, t, m, lev, out_a, out_b, out_z, out_d, out_h, own):
    rows_x, reach = cells
    gx, gz = meta[0], meta[2]
    even = lax.rem(gx, 2) == 0
    low_z = gz == 0
    tiles = u.shape[2] // SUBL
    for c in range(COMPS):
        for i in range(reach):
            for y in range(tiles):
                lo = u[c, i, y * SUBL : (y + 1) * SUBL, :]
                hi = u[c, rows_x - reach + i, y * SUBL : (y + 1) * SUBL, :]
                n = (c * reach + i) * tiles + y
                out_a[n] = jnp.where(even, hi, lo)
                out_b[n] = jnp.where(even, lo, hi)
    depth = t.shape[0]
    cols = t.shape[2]
    groups = LANES // cols
    deep = depth // groups

    def conduct(v):
        return jnp.where(v == 0, POWDER_COND, jnp.where(v == 1, SOLID_COND, LIQUID_COND)).astype(F32)

    packed_t = jnp.concatenate([t[g * deep : (g + 1) * deep] for g in range(groups)], axis=-1)
    packed_k = conduct(jnp.concatenate([m[g * deep : (g + 1) * deep] for g in range(groups)], axis=-1))
    own[:deep] = packed_t
    own[deep : 2 * deep] = packed_k
    sub = iota((1, SUBL, LANES), 1)
    half = SUBL // 2
    turned_k = pltpu.roll(packed_k, half, 1)
    low_rows = jnp.where(sub < half, packed_t, turned_k)
    high_rows = jnp.where(sub < half, turned_k, packed_t)
    out_z[:deep] = jnp.where(low_z, high_rows, low_rows)
    out_d[:deep] = jnp.where(low_z, low_rows, high_rows)
    tops = []
    for j in range(TOP // groups):
        tops.append(jnp.concatenate([t[j * groups + i] for i in range(groups)], axis=-1))
    for j in range(TOP // groups):
        tops.append(conduct(jnp.concatenate([m[j * groups + i] for i in range(groups)], axis=-1)))
    for j, top in enumerate(tops):
        own[2 * deep + j] = top
        out_z[deep + j] = top
        out_d[deep + j] = top
        out_a[COMPS * reach * tiles + j] = top
        out_b[COMPS * reach * tiles + j] = top
    edge, behind = edges(gz)
    size = u.shape[2]
    lane = iota((size, LANES), 1)
    eye = iota((size, size), 0) == iota((size, size), 1)
    levels = lev[...].astype(F32)
    acc = jnp.zeros((size, LANES), F32)
    for x in range(rows_x):
        acc = pack_heights([u[c, x] for c in range(COMPS)], x * GROUP, lane, edge, behind, acc)
        level = jnp.sum(jnp.where(eye, levels[x : x + 1, :], 0.0), axis=1, keepdims=True)
        acc = jnp.where(lane == x * GROUP + LEVEL, level, acc)
    for y in range(tiles):
        part = acc[y * SUBL : (y + 1) * SUBL]
        out_h[y] = part
        out_z[deep + len(tops) + y] = part
        out_d[deep + len(tops) + y] = part


def relay_kernel(cells, meta, u, own, in_a, in_b, in_z, in_d, in_h, out_a, out_b):
    rows_x, reach = cells
    gx, gy, gz = meta[0], meta[1], meta[2]
    even_x = lax.rem(gx, 2) == 0
    even_y = lax.rem(gy, 2) == 0
    low_z = gz == 0
    tiles = u.shape[2] // SUBL
    deep = (own.shape[0] - 4) // 2

    def put(n, hi, lo):
        out_a[n] = jnp.where(even_y, hi, lo)
        out_b[n] = jnp.where(even_y, lo, hi)

    n = 0
    for c in range(COMPS):
        for x in range(1 - reach, rows_x + reach - 1):
            pair = []
            for y in (tiles - 1, 0):
                if x < 0:
                    k = (c * reach + x + reach) * tiles + y
                    pair.append(jnp.where(even_x, in_b[k], in_a[k]))
                elif x < rows_x:
                    pair.append(u[c, x, y * SUBL : (y + 1) * SUBL, :])
                else:
                    k = (c * reach + x - rows_x) * tiles + y
                    pair.append(jnp.where(even_x, in_a[k], in_b[k]))
            put(n, *pair)
            n += 1
    base = deep + 4
    hi_y, lo_y = tiles - 1, 0
    put(
        n,
        jnp.where(low_z, in_d[base + hi_y], in_h[hi_y]),
        jnp.where(low_z, in_d[base + lo_y], in_h[lo_y]),
    )
    put(n + 1, in_z[base + hi_y], in_z[base + lo_y])
    put(
        n + 2,
        jnp.where(low_z, in_h[hi_y], in_d[base + hi_y]),
        jnp.where(low_z, in_h[lo_y], in_d[base + lo_y]),
    )
    n += 3
    half = SUBL // 2
    sub = iota((SUBL, LANES), 0)
    lane = iota((SUBL, LANES), 1)
    cols = LANES // 4
    slot = lax.rem(lane, cols) // SKIN
    per = cols // SKIN
    for j0 in range(deep // per):
        acc = [[jnp.zeros((SUBL, LANES), F32) for _ in range(4)] for _ in range(2)]
        for i in range(per):
            j = j0 * per + i
            hi = jnp.where(low_z, in_z[j], in_d[j])
            lo = jnp.where(low_z, in_d[j], in_z[j])
            four = (
                own[j],
                jnp.where(sub < half, hi, lo),
                own[deep + j],
                pltpu.roll(jnp.where(sub < half, lo, hi), half, 0),
            )
            for a in range(4):
                acc[0][a] = jnp.where(slot == i, turn(four[a], SKIN * i - (cols - SKIN), 1), acc[0][a])
                acc[1][a] = jnp.where(slot == i, turn(four[a], SKIN * i, 1), acc[1][a])
        for a in range(4):
            put(n + a * (deep // per) + j0, acc[0][a], acc[1][a])
    n += 4 * (deep // per)
    slot = lane // SUBL
    tail = in_a.shape[0] - 4
    for r in range(4):
        hi = jnp.zeros((SUBL, LANES), F32)
        lo = hi
        for j in range(4):
            if r == 0:
                src = own[2 * deep + j]
            elif r == 1:
                src = in_z[deep + j]
            elif r == 2:
                src = jnp.where(even_x, in_a[tail + j], in_b[tail + j])
            else:
                src = in_d[deep + j]
            for q in range(4):
                i = j * 4 + q
                hi = jnp.where(slot == i, turn(src, SUBL * i - cols * q - (cols - SUBL), 1), hi)
                lo = jnp.where(slot == i, turn(src, SUBL * i - cols * q, 1), lo)
        put(n + r, hi, lo)


def heat_source(row, col, beam, step):
    a = beam[step, 0].astype(F32)
    b = beam[step, 1].astype(F32)
    along_x = jnp.exp(-(((row - a) / SPOT_RADIUS) ** 2))
    along_y = jnp.exp(-(((col - b) / SPOT_RADIUS) ** 2))
    return LASER_POWER * along_x * along_y


def bulk_kernel(meta, beam, own, in_z, in_d, gy_a, gy_b, out, temp, kx, ky, kz):
    gx, gy, gz = meta[0], meta[1], meta[2]
    even_y = lax.rem(gy, 2) == 0
    low_z = gz == 0
    deep = (own.shape[0] - 4) // 2
    half = SUBL // 2
    size = 2 * SUBL
    cols = out.shape[2]
    groups = LANES // cols
    depth = out.shape[0]
    per = cols // SKIN
    sub = iota((SUBL, LANES), 0)
    lane = iota((SUBL, LANES), 1)
    base = gy_a.shape[0] - 4 - 4 * (deep // per)

    def unpack(j, carry):
        hi = jnp.where(low_z, in_z[j], in_d[j])
        lo = jnp.where(low_z, in_d[j], in_z[j])
        four = (
            own[j],
            jnp.where(sub < half, hi, lo),
            own[deep + j],
            pltpu.roll(jnp.where(sub < half, lo, hi), half, 0),
        )
        j0 = j // per
        i = lax.rem(j, per)
        for a in range(4):
            k = base + a * (deep // per) + j0
            upper = jnp.where(even_y, gy_a[k], gy_b[k])
            lower = jnp.where(even_y, gy_b[k], gy_a[k])
            for g in range(groups):
                value = turn(four[a], -cols * g, 1)
                up = lane_turn(upper, cols - (cols * g + SKIN * i))
                down = lane_turn(lower, (LANES - SKIN) - (cols * g + SKIN * i))
                value = jnp.where(
                    lane < cols,
                    value,
                    jnp.where(lane < cols + SKIN, up, jnp.where(lane >= LANES - SKIN, down, 0.0)),
                )
                rows = slice(0, SUBL) if a % 2 == 0 else slice(SUBL, size)
                if a < 2:
                    temp[0, g * deep + j, rows, :] = value
                else:
                    kz[g * deep + j, rows, :] = value
        return carry

    lax.fori_loop(0, deep, unpack, 0)

    def faces(d, k):
        nxt = jnp.where(d + 1 < depth, kz[jnp.minimum(d + 1, depth - 1)], 0.0)
        kx[d] = 0.5 * (k + turn(k, -1, 0))
        ky[d] = 0.5 * (k + turn(k, -1, 1))
        kz[d] = 0.5 * (k + nxt)
        return nxt

    first_k = kz[0]
    lax.fori_loop(0, depth, faces, first_k)

    row_l = wrapped(iota((size, LANES), 0), SUBL, size)
    col_l = wrapped(iota((size, LANES), 1), cols, LANES)
    row_g = (gx * meta[5] + gz) * SUBL + row_l
    col_g = gy * cols + col_l
    inside = (
        (row_g >= 0)
        & (row_g < meta[3] * meta[5] * SUBL)
        & (col_g >= 0)
        & (col_g < meta[4] * cols)
    )
    inside_f = jnp.where(inside, 1.0, 0.0)
    row_f, col_f = row_g.astype(F32), col_g.astype(F32)

    for s in range(STEPS * SUBSTEPS):
        src, dst = s % 2, 1 - s % 2
        beam_xy = heat_source(row_f, col_f, beam, s)
        last = s == STEPS * SUBSTEPS - 1

        def layer(d, carry):
            before = carry
            t = temp[src, d]
            below = jnp.where(d + 1 < depth, temp[src, jnp.minimum(d + 1, depth - 1)], 0.0)
            fz = kz[d] * (below - t)
            fx = kx[d] * (turn(t, -1, 0) - t)
            fy = ky[d] * (turn(t, -1, 1) - t)
            laser = beam_xy * jnp.exp(jnp.zeros((size, LANES), F32) - d.astype(F32) / ABSORB_DEPTH)
            change = (fx - turn(fx, 1, 0)) + (fy - turn(fy, 1, 1)) + (fz - before) + laser
            new = (t + HEAT_STEP * change) * inside_f
            if last:
                out[d] = new[:SUBL, :cols]
            else:
                temp[dst, d] = new
            return fz

        t0 = temp[src, 0]
        k0 = jnp.where(inside, first_k, 0.0)
        lax.fori_loop(0, depth, layer, 0.5 * k0 * t0, unroll=4)


def rates(west, mid, east, h, lane, edge):
    size = mid[0].shape[0]
    out_lap, sx, sy, sz = [], {}, {}, []
    for c in range(COMPS):
        north = turn(mid[c], -1, 0)
        south = turn(mid[c], 1, 0)
        halo = jnp.where(lane == edge, lane_turn(h, edge - c), 0.0)
        upper = jnp.where(lane == LANES - 1, halo, turn(mid[c], -1, 1))
        lower = jnp.where(lane == 0, halo, turn(mid[c], 1, 1))
        if c in (2, 5):
            sx[c] = 0.5 * (east[c] - west[c])
        if c in (3, 5):
            sy[c] = 0.5 * (north - south)
        sz.append(0.5 * (upper - lower))
        out_lap.append(east[c] + west[c] + north + south + upper + lower - 6.0 * mid[c])
    spread = sx[2] + sy[3] + sz[4]
    coupled = [-VAPOR_LOAD * spread, -AMBIENT_LOAD * spread, -sx[5], -sy[5], -sz[5], -STIFFNESS * spread]
    return [coupled[c] - DRIFT_SPEED * sz[c] + VISCOSITY[c] * out_lap[c] for c in range(COMPS)]


def halo_rates(h_west, h, h_east, mid, lane, edge, low_z):
    touch = jnp.zeros_like(h)
    for c in range(COMPS):
        touch = jnp.where(lane == c, lane_turn(mid[c], c - edge), touch)
    after = turn(h, -NEXT, 1)
    north = turn(h, -1, 0)
    south = turn(h, 1, 0)
    sx = 0.5 * (h_east - h_west)
    sy = 0.5 * (north - south)
    sz = jnp.where(low_z, 0.5, -0.5) * (after - touch)
    lap = h_east + h_west + north + south + after + touch - 6.0 * h
    q = jnp.where(lane == 2, sx, jnp.where(lane == 3, sy, jnp.where(lane == 4, sz, 0.0)))
    s = q + turn(q, -1, 1) + turn(q, -2, 1)
    coupled = jnp.where(
        lane == 0,
        -VAPOR_LOAD * turn(s, -2, 1),
        jnp.where(
            lane == 1,
            -AMBIENT_LOAD * turn(s, -1, 1),
            jnp.where(
                lane == 2,
                -turn(sx, -3, 1),
                jnp.where(
                    lane == 3,
                    -turn(sy, -2, 1),
                    jnp.where(lane == 4, -turn(sz, -1, 1), -STIFFNESS * turn(s, 3, 1)),
                ),
            ),
        ),
    )
    visc = jnp.where(
        lane == 0, VISCOSITY[0], jnp.where(lane == 1, VISCOSITY[1], jnp.where(lane == 5, VISCOSITY[5], VISCOSITY[2]))
    )
    return coupled - DRIFT_SPEED * sz + visc * lap


def advance(meta, g, h, f, fh, u1, own_x, own_y):
    n, size = g.shape[1], g.shape[2]
    gx, gy, gz = meta[0], meta[1], meta[2]
    low_z = gz == 0
    edge, _ = edges(gz)
    lane = iota((size, LANES), 1)
    y_l = wrapped(iota((size, LANES), 0), own_y, size)
    y_g = gy * own_y + y_l
    inside_y = jnp.where((y_g >= 0) & (y_g < meta[4] * own_y), 1.0, 0.0)
    before = (n - own_x) // 2

    def inside(i):
        x_g = gx * own_x + i - before
        ok = (x_g >= 0) & (x_g < meta[3] * own_x)
        return inside_y * jnp.where(ok, 1.0, 0.0)

    def one(i, carry):
        mid = [g[c, i] for c in range(COMPS)]
        rate = rates([g[c, i - 1] for c in range(COMPS)], mid, [g[c, i + 1] for c in range(COMPS)], h[i], lane, edge)
        m = inside(i)
        for c in range(COMPS):
            f[c, i - 1] = (mid[c] + GAS_STEP * rate[c]) * m
        hr = halo_rates(h[i - 1], h[i], h[i + 1], mid, lane, edge, low_z)
        fh[i - 1] = (h[i] + GAS_STEP * hr) * m
        return carry

    lax.fori_loop(1, n - 1, one, 0)

    part_rows = 4 * SUBL
    col_y = lax.div(wrapped(iota((size, LANES), 1), 2 * own_y, LANES) + LANES, 2) - LANES // 2
    spread_y = jnp.where(col_y == y_l, 1.0, 0.0)
    row_x = lax.div(wrapped(iota((part_rows, LANES), 0), 2 * own_x, part_rows) + LANES, 2) - LANES // 2
    height = iota((size, LANES), 1) + gz * LANES
    height = height.astype(F32)

    def two(i, fine):
        mid = [f[c, i - 1] for c in range(COMPS)]
        rate = rates([f[c, i - 2] for c in range(COMPS)], mid, [f[c, i] for c in range(COMPS)], fh[i - 1], lane, edge)
        m = inside(i)
        for c in range(COMPS):
            new = 0.5 * (g[c, i] + mid[c] + GAS_STEP * rate[c]) * m
            u1[c, i - 2] = new
        level = h[i][:, LEVEL : LEVEL + 1]
        at = jnp.sum(jnp.where(height == level, new, 0.0), axis=1, keepdims=True)
        line = jnp.sum(spread_y * at, axis=0, keepdims=True)
        return fine + jnp.where(row_x == i - before, line, 0.0)

    return lax.fori_loop(2, n - 2, two, jnp.zeros((part_rows, LANES), F32))


def top_heat(meta, beam, first, t, k, fine, own_rows, cols):
    gx, gy = meta[0], meta[1]
    shape = fine.shape
    row = gx * own_rows + wrapped(iota(shape, 0), own_rows, shape[0])
    col = gy * cols + wrapped(iota(shape, 1), cols, shape[1])
    row, col = row.astype(F32), col.astype(F32)
    kx = [0.5 * (v + turn(v, -1, 0)) for v in k]
    ky = [0.5 * (v + turn(v, -1, 1)) for v in k]
    kz = [0.5 * (k[d] + k[d + 1]) for d in range(TOP - 1)]
    for s in range(SUBSTEPS):
        beam_xy = heat_source(row, col, beam, first + s)
        before = 0.5 * k[0] * t[0]
        new = []
        for d in range(TOP):
            fx = kx[d] * (turn(t[d], -1, 0) - t[d])
            fy = ky[d] * (turn(t[d], -1, 1) - t[d])
            fz = kz[d] * (t[d + 1] - t[d]) if d + 1 < TOP else jnp.zeros_like(before)
            factor = jnp.exp(jnp.full(shape, -d / ABSORB_DEPTH, F32))
            change = (fx - turn(fx, 1, 0)) + (fy - turn(fy, 1, 1)) + (fz - before) + beam_xy * factor
            if d == 0:
                change = change - LATENT_HEAT * softplus(t[0] - BOIL_LEVEL - BACK_PRESSURE * fine)
            new.append(jnp.where(k[d] > 0, t[d] + HEAT_STEP * change, 0.0))
            before = fz
        t = new
    return t


def vapor_mass(t0, fine):
    four = t0 + turn(t0, -1, 1)
    four = four + turn(four, -1, 0)
    return softplus(0.25 * four - BOIL_LEVEL - BACK_PRESSURE * fine)


def mass_rows(meta, h, mass, size, own_y):
    gz = meta[2]
    y_l = wrapped(iota((size, LANES), 0), own_y, size)
    col = wrapped(iota((size, LANES), 1), 2 * own_y, LANES)
    pick = col == 2 * y_l
    height = (iota((size, LANES), 1) + gz * LANES).astype(F32)

    def row(i, x):
        r = lax.rem(2 * x + mass.shape[0], mass.shape[0])
        line = mass[pl.ds(r, 1), :]
        at = jnp.sum(jnp.where(pick, line, 0.0), axis=1, keepdims=True)
        return jnp.where(height == h[i][:, LEVEL : LEVEL + 1], at, 0.0)

    return row


def first_kernel(
    cells, meta, beam, u, own, in_a, in_b, in_z, in_d, in_h, gy_a, gy_b,
    out_g, out_m, out_t, out_k, g, h, f, fh, u1, mass,
):
    rows_x, reach = cells
    gx, gy, gz = meta[0], meta[1], meta[2]
    even_x = lax.rem(gx, 2) == 0
    even_y = lax.rem(gy, 2) == 0
    low_z = gz == 0
    own_y = u.shape[2]
    tiles = own_y // SUBL
    size = own_y + 2 * SUBL
    deep = (own.shape[0] - 4) // 2
    zero = jnp.zeros((SUBL, LANES), F32)

    def side(k):
        upper = jnp.where(even_y, gy_a[k], gy_b[k])
        lower = jnp.where(even_y, gy_b[k], gy_a[k])
        return upper, lower

    wide = rows_x + 2 * reach - 2
    for c in range(COMPS):
        for x in range(-reach, rows_x + reach):
            i = x + reach
            for y in range(tiles):
                if x < 0:
                    k = (c * reach + x + reach) * tiles + y
                    value = jnp.where(even_x, in_b[k], in_a[k])
                elif x < rows_x:
                    value = u[c, x, y * SUBL : (y + 1) * SUBL, :]
                else:
                    k = (c * reach + x - rows_x) * tiles + y
                    value = jnp.where(even_x, in_a[k], in_b[k])
                g[c, i, y * SUBL : (y + 1) * SUBL, :] = value
            if 0 < i < rows_x + 2 * reach - 1:
                upper, lower = side(c * wide + i - 1)
            else:
                upper = lower = zero
            g[c, i, own_y : own_y + SUBL, :] = upper
            g[c, i, own_y + SUBL : size, :] = lower
    base = deep + 4
    packed = []
    for b in range(3):
        parts = []
        for y in range(tiles):
            if b == 0:
                parts.append(jnp.where(low_z, in_d[base + y], in_h[y]))
            elif b == 1:
                parts.append(in_z[base + y])
            else:
                parts.append(jnp.where(low_z, in_h[y], in_d[base + y]))
        parts.extend(side(COMPS * wide + b))
        packed.append(jnp.concatenate(parts, axis=0))
    for x in range(-reach, rows_x + reach):
        b, q = divmod(x + rows_x, rows_x)
        h[x + reach] = turn(packed[b], -GROUP * q, 1)

    fine = advance(meta, g, h, f, fh, u1, rows_x, own_y)

    cols = LANES // 4
    part_rows = 4 * SUBL
    lane = iota((part_rows, LANES), 1)
    tail = in_a.shape[0] - 4
    top_at = gy_a.shape[0] - 4
    uppers, lowers = zip(*[side(top_at + r) for r in range(4)])
    uppers = jnp.concatenate(uppers, axis=0)
    lowers = jnp.concatenate(lowers, axis=0)
    layers = []
    for j in range(4):
        high = jnp.where(even_x, in_a[tail + j], in_b[tail + j])
        src = jnp.concatenate([own[2 * deep + j], in_z[deep + j], high, in_d[deep + j]], axis=0)
        for q in range(4):
            i = 4 * j + q
            layers.append(
                jnp.where(
                    lane < cols,
                    turn(src, -cols * q, 1),
                    jnp.where(
                        lane < cols + SUBL,
                        turn(uppers, cols - SUBL * i, 1),
                        jnp.where(lane >= LANES - SUBL, turn(lowers, LANES - SUBL - SUBL * i, 1), 0.0),
                    ),
                )
            )
    t, k = layers[:TOP], layers[TOP:]
    t = top_heat(meta, beam, 0, t, k, fine, 2 * rows_x, cols)
    for d in range(TOP):
        out_t[d] = t[d]
        out_k[d] = k[d]
    mass[...] = vapor_mass(t[0], fine)

    edge, behind = edges(gz)
    mass_of = mass_rows(meta, h, mass, size, own_y)
    x_from = -REACH_LAST
    count = rows_x + 2 * REACH_LAST
    half = SUBL // 2
    sub = iota((SUBL, LANES), 0)
    small = own_y + SUBL
    lane_s = iota((small, LANES), 1)
    shift = reach - 2 - REACH_LAST
    y_l = wrapped(iota((size, LANES), 0), own_y, size)
    y_g = gy * own_y + y_l
    inside_y = jnp.where((y_g >= 0) & (y_g < meta[4] * own_y), 1.0, 0.0)

    def finish(i, carry):
        x = i + x_from
        x_g = gx * rows_x + x
        ok = jnp.where((x_g >= 0) & (x_g < meta[3] * rows_x), 1.0, 0.0)
        add = mass_of(x + reach, x) * inside_y * ok
        rows = []
        for c in range(COMPS):
            value = u1[c, i + shift]
            if c == 0:
                value = value + VAPOR_SOURCE * add
            elif c == 4:
                value = value + RECOIL_PUSH * add
            elif c == 5:
                value = value + RECOIL_PRESSURE * add
            ends = jnp.where(sub < half, value[own_y : own_y + SUBL], value[own_y + SUBL : size])
            value = jnp.concatenate([value[:own_y], ends], axis=0)
            out_g[c, i] = value
            rows.append(value)
        acc = jnp.zeros((small, LANES), F32)
        for c in range(COMPS):
            acc = jnp.where(lane_s == c, lane_turn(rows[c], c - edge), acc)
            acc = jnp.where(lane_s == NEXT + c, lane_turn(rows[c], NEXT + c - behind), acc)
        level = h[x + reach][:, LEVEL : LEVEL + 1]
        ends = jnp.where(sub < half, level[own_y : own_y + SUBL], level[own_y + SUBL : size])
        level = jnp.concatenate([jnp.broadcast_to(level[:own_y], (own_y, LANES)), ends], axis=0)
        acc = jnp.where(lane_s == LEVEL, level, acc)
        acc = jnp.where(lane_s < GROUP, acc, 0.0)
        j = i // (LANES // GROUP)
        q = lax.rem(i, LANES // GROUP)
        out_m[j] = jnp.where(q == 0, 0.0, out_m[j]) + lane_turn(acc, GROUP * q)
        return carry

    out_m[...] = jnp.zeros_like(out_m)
    lax.fori_loop(0, count, finish, 0)


def last_kernel(cells, meta, beam, g, in_m, in_t, in_k, out_g, out_t, out_f, h, f, fh, u1, mass):
    rows_x, own_y = cells
    size = g.shape[2]
    n = g.shape[1]
    for i in range(n):
        j, q = divmod(i, LANES // GROUP)
        h[i] = turn(in_m[j], -GROUP * q, 1)
    fine = advance(meta, g, h, f, fh, u1, rows_x, own_y)
    cols = LANES // 4
    t = [in_t[d] for d in range(TOP)]
    k = [in_k[d] for d in range(TOP)]
    t = top_heat(meta, beam, SUBSTEPS, t, k, fine, 2 * rows_x, cols)
    for d in range(SKIN):
        out_t[d] = t[d][:SUBL]
        out_f[d] = t[d][SUBL : 2 * SUBL]
    mass[...] = vapor_mass(t[0], fine)
    mass_of = mass_rows(meta, h, mass, size, own_y)

    def finish(x, carry):
        add = mass_of(x + REACH_LAST, x)
        for c in range(COMPS):
            value = u1[c, x + REACH_LAST - 2]
            if c == 0:
                value = value + VAPOR_SOURCE * add
            elif c == 4:
                value = value + RECOIL_PUSH * add
            elif c == 5:
                value = value + RECOIL_PRESSURE * add
            out_g[c, x] = value[:own_y]
        return carry

    lax.fori_loop(0, rows_x, finish, 0)


def call(body, outs, scratch=(), scalars=1, count=0):
    vmem = pl.BlockSpec(memory_space=pltpu.VMEM)
    smem = pl.BlockSpec(memory_space=pltpu.SMEM)
    return pl.pallas_call(
        body,
        out_shape=[jax.ShapeDtypeStruct(s, F32) for s in outs],
        in_specs=[smem] * scalars + [vmem] * count,
        out_specs=[vmem] * len(outs),
        scratch_shapes=[pltpu.VMEM(s, F32) for s in scratch],
        compiler_params=pltpu.CompilerParams(vmem_limit_bytes=32 * 1024 * 1024),
    )


def pairs(count, odd):
    out = []
    for i in range(odd, count - 1, 2):
        out += [(i, i + 1), (i + 1, i)]
    return out


def cross(nx, nz, upper):
    out = []
    for i in range(nx - 1):
        a, b = i * nz + (nz - 1 if upper else 0), (i + 1) * nz + (0 if upper else nz - 1)
        out += [(a, b), (b, a)]
    return out


def shards(u, t, m, lev, beam):
    nx, ny, nz = (lax.axis_size(a) for a in ("gx", "gy", "gz"))
    gx, gy, gz = (lax.axis_index(a) for a in ("gx", "gy", "gz"))
    meta = jnp.stack([gx, gy, gz, nx, ny, nz]).astype(jnp.int32)
    _, rows_x, own_y, _ = u.shape
    tiles = own_y // SUBL
    deep = t.shape[0] * t.shape[2] // LANES
    block = (SUBL, LANES)
    n_x = COMPS * REACH * tiles + 4
    n_z = deep + 4 + tiles
    msg_a, msg_b, msg_z, msg_d, msg_h, own = call(
        functools.partial(pack_kernel, (rows_x, REACH)),
        [(n_x, *block), (n_x, *block), (n_z, *block), (n_z, *block), (tiles, *block), (2 * deep + 4, *block)],
        count=4,
    )(meta, u, t, m, lev)
    in_a = lax.ppermute(msg_a, "gx", pairs(nx, 0))
    in_b = lax.ppermute(msg_b, "gx", pairs(nx, 1))
    in_z = lax.ppermute(msg_z, "gz", pairs(nz, 0))
    in_d = lax.ppermute(msg_d, ("gx", "gz"), cross(nx, nz, True))
    in_h = lax.ppermute(msg_h, ("gx", "gz"), cross(nx, nz, False))
    n_y = COMPS * (rows_x + 2 * REACH - 2) + 3 + deep // 2 + 4
    msg_a, msg_b = call(
        functools.partial(relay_kernel, (rows_x, REACH)), [(n_y, *block), (n_y, *block)], count=7
    )(meta, u, own, in_a, in_b, in_z, in_d, in_h)
    gy_a = lax.ppermute(msg_a, "gy", pairs(ny, 0))
    gy_b = lax.ppermute(msg_b, "gy", pairs(ny, 1))

    size = own_y + 2 * SUBL
    n = rows_x + 2 * REACH
    n2 = rows_x + 2 * REACH_LAST
    small = own_y + SUBL
    part_rows = 4 * SUBL
    n_m = -(-n2 // (LANES // GROUP))
    g2, msg_m, top_t, top_k = call(
        functools.partial(first_kernel, (rows_x, REACH)),
        [(COMPS, n2, small, LANES), (n_m, small, LANES), (TOP, part_rows, LANES), (TOP, part_rows, LANES)],
        scratch=[
            (COMPS, n, size, LANES),
            (n, size, LANES),
            (COMPS, n - 2, size, LANES),
            (n - 2, size, LANES),
            (COMPS, n - 4, size, LANES),
            (part_rows, LANES),
        ],
        scalars=2,
        count=9,
    )(meta, beam, u, own, in_a, in_b, in_z, in_d, in_h, gy_a, gy_b)
    in_m = lax.ppermute(msg_m, "gz", pairs(nz, 0))
    (bulk,) = call(
        bulk_kernel,
        [t.shape],
        scratch=[
            (2, t.shape[0], 2 * SUBL, LANES),
            (t.shape[0], 2 * SUBL, LANES),
            (t.shape[0], 2 * SUBL, LANES),
            (t.shape[0], 2 * SUBL, LANES),
        ],
        scalars=2,
        count=5,
    )(meta, beam, own, in_z, in_d, gy_a, gy_b)
    gas, mine, other = call(
        functools.partial(last_kernel, (rows_x, own_y)),
        [u.shape, (SKIN, *block), (SKIN, *block)],
        scratch=[
            (n2, small, LANES),
            (COMPS, n2 - 2, small, LANES),
            (n2 - 2, small, LANES),
            (COMPS, n2 - 4, small, LANES),
            (part_rows, LANES),
        ],
        scalars=2,
        count=4,
    )(meta, beam, g2, in_m, top_t, top_k)
    given = lax.ppermute(other, "gz", pairs(nz, 0))
    skin = jnp.where(gz == 0, mine, given)[:, :, : t.shape[2]]
    return gas, lax.dynamic_update_slice(bulk, skin, (0, 0, 0))


def solution(mesh):
    return jax.shard_map(
        shards,
        mesh=mesh,
        in_specs=(
            P(None, "gx", "gy", "gz"),
            P(None, ("gx", "gz"), "gy"),
            P(None, ("gx", "gz"), "gy"),
            P("gx", "gy"),
            P(),
        ),
        out_specs=(P(None, "gx", "gy", "gz"), P(None, ("gx", "gz"), "gy")),
        check_vma=False,
    )
```

```python
import functools

import jax
import jax.numpy as jnp
from jax import lax
from jax.experimental import pallas as pl
from jax.experimental.pallas import tpu as pltpu
from jax.sharding import PartitionSpec as P

STEPS = 2
SUBSTEPS = 2
GAS_STEP = 0.3
DRIFT_SPEED = 0.5
VAPOR_LOAD = 0.3
AMBIENT_LOAD = 0.7
STIFFNESS = 1.0
VISCOSITY = (0.2, 0.1, 0.15, 0.15, 0.15, 0.2)
HEAT_STEP = 1.0
POWDER_COND = 0.04
SOLID_COND = 0.15
LIQUID_COND = 0.09
LASER_POWER = 3.0
SPOT_RADIUS = 6.0
ABSORB_DEPTH = 4.0
BOIL_LEVEL = 1.0
BACK_PRESSURE = 0.5
LATENT_HEAT = 0.3
VAPOR_SOURCE = 0.5
RECOIL_PUSH = 0.4
RECOIL_PRESSURE = 0.6

COMPS = 6
LANES = 128
SUBL = 8
F32 = jnp.float32
REACH = 6
REACH_LAST = 3
SKIN = 4
TOP = 8
GROUP = 16
LEVEL = 6
NEXT = 8


def iota(shape, axis):
    return lax.broadcasted_iota(jnp.int32, shape, axis)


def wrapped(index, own, size):
    return jnp.where(index < own + (size - own) // 2, index, index - size)


def turn(value, amount, axis):
    size = value.shape[axis]
    if isinstance(amount, int):
        amount = amount % size
        if amount == 0:
            return value
    return pltpu.roll(value, amount, axis)


def softplus(x):
    return jnp.maximum(x, 0.0) + jnp.log1p(jnp.exp(-jnp.abs(x)))


def edges(gz):
    return jnp.where(gz == 0, LANES - 1, 0), jnp.where(gz == 0, LANES - 2, 1)


def lane_turn(value, amount):
    return pltpu.roll(value, lax.rem(amount + 2 * LANES, LANES), 1)


def pack_heights(rows, base, lane, edge, behind, acc):
    for c, row in enumerate(rows):
        acc = jnp.where(lane == base + c, lane_turn(row, base + c - edge), acc)
        acc = jnp.where(lane == base + NEXT + c, lane_turn(row, base + NEXT + c - behind), acc)
    return acc


DEEP_5 = (2, 3, 4, 5)
DEEP_6 = (2, 5)
FULL = 4
QUARTERS = (5, 3, 2, 4)


def slab_index(c, layer, tile, tiles):
    if layer <= FULL:
        return (c * FULL + layer - 1) * tiles + tile
    base = COMPS * FULL * tiles
    if layer == FULL + 1:
        return base + DEEP_5.index(c) * tiles + tile if c in DEEP_5 else None
    base += len(DEEP_5) * tiles
    return base + DEEP_6.index(c) * tiles + tile if c in DEEP_6 else None


def slab_size(tiles):
    return (COMPS * FULL + len(DEEP_5) + len(DEEP_6)) * tiles


def row_tile(c, x, tile, u, in_a, in_b, even_x):
    rows_x, tiles = u.shape[1], u.shape[2] // SUBL
    if 0 <= x < rows_x:
        return u[c, x, tile * SUBL : (tile + 1) * SUBL, :]
    k = slab_index(c, -x if x < 0 else x - rows_x + 1, tile, tiles)
    if k is None:
        return None
    low, high = (in_b[k], in_a[k]) if x < 0 else (in_a[k], in_b[k])
    return jnp.where(even_x, low, high)


def conduct(v):
    return jnp.where(v == 0, POWDER_COND, jnp.where(v == 1, SOLID_COND, LIQUID_COND)).astype(F32)


def pack_kernel(cells, meta, u, t, m, lev, out_a, out_b, out_z, out_d, out_h, own):
    rows_x, reach = cells
    gx, gz = meta[0], meta[2]
    even = lax.rem(gx, 2) == 0
    low_z = gz == 0
    tiles = u.shape[2] // SUBL
    for c in range(COMPS):
        for layer in range(1, reach + 1):
            for y in range(tiles):
                n = slab_index(c, layer, y, tiles)
                if n is None:
                    continue
                lo = u[c, layer - 1, y * SUBL : (y + 1) * SUBL, :]
                hi = u[c, rows_x - layer, y * SUBL : (y + 1) * SUBL, :]
                out_a[n] = jnp.where(even, hi, lo)
                out_b[n] = jnp.where(even, lo, hi)
    rows, cols = t.shape[0], t.shape[1]
    col_tiles = cols // SUBL
    n = 0
    for source in (lambda v: v, conduct):
        ref = t if n == 0 else m
        for r in range(SKIN):
            for y in range(col_tiles):
                lo = source(ref[r, y * SUBL : (y + 1) * SUBL, :])
                hi = source(ref[rows - SKIN + r, y * SUBL : (y + 1) * SUBL, :])
                out_z[n] = jnp.where(low_z, hi, lo)
                out_d[n] = jnp.where(low_z, lo, hi)
                n += 1
    per = LANES // cols
    top_a = slab_size(tiles)
    for j in range(2 * rows // per):
        ref, r = (t, j * per) if j < rows // per else (m, j * per - rows)
        block = ref[r : r + per].reshape(LANES, LANES)
        if ref is m:
            block = conduct(block)
        top = jnp.transpose(block)[:TOP]
        own[j] = top
        out_z[n + j] = top
        out_d[n + j] = top
        out_a[top_a + j] = top
        out_b[top_a + j] = top
    n += 2 * rows // per
    edge, behind = edges(gz)
    size = u.shape[2]
    lane = iota((size, LANES), 1)
    eye = iota((size, size), 0) == iota((size, size), 1)
    levels = lev[...].astype(F32)
    acc = jnp.zeros((size, LANES), F32)
    for x in range(rows_x):
        acc = pack_heights([u[c, x] for c in range(COMPS)], x * GROUP, lane, edge, behind, acc)
        level = jnp.sum(jnp.where(eye, levels[x : x + 1, :], 0.0), axis=1, keepdims=True)
        acc = jnp.where(lane == x * GROUP + LEVEL, level, acc)
    for y in range(tiles):
        part = acc[y * SUBL : (y + 1) * SUBL]
        out_h[y] = part
        out_z[n + y] = part
        out_d[n + y] = part


def part_row(r, tile, ref, at, rows, in_z, in_d, low_z, col_tiles, low_part):
    if 0 <= r < rows:
        value = ref[r, tile * SUBL : (tile + 1) * SUBL, :]
        return conduct(value) if at else value
    k = (at * SKIN + (r + SKIN if r < 0 else r - rows)) * col_tiles + tile
    low, high = (in_d[k], in_z[k]) if r < 0 else (in_z[k], in_d[k])
    return jnp.where(low_z, low, high)


def relay_kernel(cells, meta, u, t, m, own, in_a, in_b, in_z, in_d, in_h, out_a, out_b):
    rows_x, reach = cells
    gx, gy, gz = meta[0], meta[1], meta[2]
    even_x = lax.rem(gx, 2) == 0
    even_y = lax.rem(gy, 2) == 0
    low_z = gz == 0
    tiles = u.shape[2] // SUBL
    rows, cols = t.shape[0], t.shape[1]
    col_tiles = cols // SUBL
    half = SUBL // 2
    sub = iota((SUBL, LANES), 0)
    lane = iota((SUBL, LANES), 1)
    zero = jnp.zeros((SUBL, LANES), F32)

    def put(n, hi, lo):
        out_a[n] = jnp.where(even_y, hi, lo)
        out_b[n] = jnp.where(even_y, lo, hi)

    def both(c, x):
        pair = [row_tile(c, x, y, u, in_a, in_b, even_x) for y in (tiles - 1, 0)]
        return [zero if v is None else v for v in pair]

    n = 0
    for x in range(1 - reach, rows_x + reach - 1):
        for c in range(0, COMPS, 2):
            (hi0, lo0), (hi1, lo1) = both(c, x), both(c + 1, x)
            put(n, jnp.where(sub < half, turn(hi1, half, 0), hi0), jnp.where(sub < half, lo0, turn(lo1, half, 0)))
            n += 1
    for x in range(-1, rows_x + 1):
        hi = lo = zero
        for q, c in enumerate(QUARTERS):
            a, b = both(c, x)
            hi = jnp.where(sub // 2 == q, turn(a, 2 * q - 2, 0), hi)
            lo = jnp.where(sub // 2 == q, turn(b, 2 * q - half, 0), lo)
        put(n, hi, lo)
        n += 1
    base = in_z.shape[0] - tiles
    hi_y, lo_y = tiles - 1, 0
    put(
        n,
        jnp.where(low_z, in_d[base + hi_y], in_h[hi_y]),
        jnp.where(low_z, in_d[base + lo_y], in_h[lo_y]),
    )
    put(n + 1, in_z[base + hi_y], in_z[base + lo_y])
    put(
        n + 2,
        jnp.where(low_z, in_h[hi_y], in_d[base + hi_y]),
        jnp.where(low_z, in_h[lo_y], in_d[base + lo_y]),
    )
    n += 3
    for r in range(-SKIN, rows + SKIN):
        hi_t, lo_t = [part_row(r, y, t, 0, rows, in_z, in_d, low_z, col_tiles, None) for y in (col_tiles - 1, 0)]
        hi_k, lo_k = [part_row(r, y, m, 1, rows, in_z, in_d, low_z, col_tiles, None) for y in (col_tiles - 1, 0)]
        put(n, jnp.where(sub < half, turn(hi_k, half, 0), hi_t), jnp.where(sub < half, lo_t, turn(lo_k, half, 0)))
        n += 1
    sources = surface_sources(own, in_a, in_b, in_z, in_d, even_x, tiles)
    per = LANES // cols
    slot = lax.rem(lane, cols) // SUBL
    for v in range(len(sources) // per):
        hi = lo = zero
        for i in range(per):
            src = sources[v * per + i]
            hi = jnp.where(slot == i, turn(src, SUBL * i - (cols - SUBL), 1), hi)
            lo = jnp.where(slot == i, turn(src, SUBL * i, 1), lo)
        put(n + v, hi, lo)


def surface_sources(own, in_a, in_b, in_z, in_d, even_x, tiles):
    count = own.shape[0]
    tail = in_a.shape[0] - count
    at = in_z.shape[0] - tiles - count
    out = []
    for a in range(2):
        span = range(a * count // 2, (a + 1) * count // 2)
        out += [own[j] for j in span]
        out += [in_z[at + j] for j in span]
        out += [jnp.where(even_x, in_a[tail + j], in_b[tail + j]) for j in span]
        out += [in_d[at + j] for j in span]
    return out


def heat_source(row, col, beam, step):
    a = beam[step, 0].astype(F32)
    b = beam[step, 1].astype(F32)
    along_x = jnp.exp(-(((row - a) / SPOT_RADIUS) ** 2))
    along_y = jnp.exp(-(((col - b) / SPOT_RADIUS) ** 2))
    return LASER_POWER * along_x * along_y


def bulk_kernel(meta, beam, t, m, in_z, in_d, gy_a, gy_b, out, temp, cond, kx, ky, kz):
    gx, gy, gz = meta[0], meta[1], meta[2]
    even_y = lax.rem(gy, 2) == 0
    low_z = gz == 0
    rows, cols, depth = t.shape
    col_tiles = cols // SUBL
    half = SUBL // 2
    size = cols + SUBL
    n = rows + 2 * SKIN
    sub = iota((SUBL, LANES), 0)
    base = gy_a.shape[0] - 4 - n
    for i in range(n):
        for y in range(col_tiles):
            span = slice(y * SUBL, (y + 1) * SUBL)
            temp[0, i, span, :] = part_row(i - SKIN, y, t, 0, rows, in_z, in_d, low_z, col_tiles, None)
            cond[i, span, :] = part_row(i - SKIN, y, m, 1, rows, in_z, in_d, low_z, col_tiles, None)
        up = jnp.where(even_y, gy_a[base + i], gy_b[base + i])
        low = jnp.where(even_y, gy_b[base + i], gy_a[base + i])
        temp[0, i, cols:size, :] = jnp.where(sub < half, up, low)
        cond[i, cols:size, :] = turn(jnp.where(sub < half, low, up), half, 0)

    lane = iota((size, LANES), 1)
    for i in range(n):
        k = cond[i]
        if i + 1 < n:
            kx[i] = 0.5 * (k + cond[i + 1])
        ky[i] = 0.5 * (k + turn(k, -1, 0))
        kz[i] = 0.5 * (k + jnp.where(lane == depth - 1, 0.0, turn(k, -1, 1)))

    col_g = gy * cols + wrapped(iota((size, LANES), 0), cols, size)
    inside_y = jnp.where((col_g >= 0) & (col_g < meta[4] * cols), 1.0, 0.0)
    col_f = col_g.astype(F32)
    fall = jnp.exp(-lane.astype(F32) / ABSORB_DEPTH)
    first_row = (gx * meta[5] + gz) * rows - SKIN

    for s in range(STEPS * SUBSTEPS):
        src, dst = s % 2, 1 - s % 2
        last = s == STEPS * SUBSTEPS - 1
        a = beam[s, 0].astype(F32)
        b = beam[s, 1].astype(F32)
        spot = LASER_POWER * fall * jnp.exp(-(((col_f - b) / SPOT_RADIUS) ** 2))
        lo, hi = s + 1, n - 1 - s
        fx0 = kx[lo - 1] * (temp[src, lo] - temp[src, lo - 1])
        for i in range(lo, hi):
            v = temp[src, i]
            fx = kx[i] * (temp[src, i + 1] - v)
            fy = ky[i] * (turn(v, -1, 0) - v)
            fz = kz[i] * (jnp.where(lane == depth - 1, 0.0, turn(v, -1, 1)) - v)
            above = jnp.where(lane == 0, 0.5 * cond[i] * v, turn(fz, 1, 1))
            row = first_row + i
            along_x = jnp.exp(-((jnp.full((1, LANES), row.astype(F32) - a) / SPOT_RADIUS) ** 2))
            change = (fx - fx0) + (fy - turn(fy, 1, 0)) + (fz - above) + spot * along_x
            new = v + HEAT_STEP * change
            if last:
                out[i - SKIN] = new[:cols]
            else:
                ok = (row >= 0) & (row < meta[3] * meta[5] * rows)
                temp[dst, i] = new * (inside_y * jnp.where(ok, 1.0, 0.0))
            fx0 = fx


def seal_kernel(meta, bulk, mine, given, out):
    rows, cols, depth = bulk.shape
    per = LANES // cols
    lane = iota((LANES, LANES), 1)
    for j in range(mine.shape[0]):
        skin = jnp.where(meta[2] == 0, mine[j], given[j])
        skin = jnp.concatenate([skin, jnp.zeros((LANES - SUBL, LANES), F32)], axis=0)
        block = jnp.where(lane < SKIN, jnp.transpose(skin), bulk[j * per : (j + 1) * per].reshape(LANES, LANES))
        out[j * per : (j + 1) * per] = block.reshape(per, cols, LANES)


def pack_skin(t, rows, cols, scratch, out):
    per = LANES // cols
    lane = iota((SUBL, LANES), 1)
    for j in range(SUBL // per):
        acc = jnp.zeros((SUBL, LANES), F32)
        for q in range(per):
            acc = jnp.where(lane // cols == q, turn(scratch[rows + j * per + q], cols * q, 1), acc)
        out[j] = acc


def rates(west, mid, east, h, lane, edge):
    size = mid[0].shape[0]
    out_lap, sx, sy, sz = [], {}, {}, []
    for c in range(COMPS):
        north = turn(mid[c], -1, 0)
        south = turn(mid[c], 1, 0)
        halo = jnp.where(lane == edge, lane_turn(h, edge - c), 0.0)
        upper = jnp.where(lane == LANES - 1, halo, turn(mid[c], -1, 1))
        lower = jnp.where(lane == 0, halo, turn(mid[c], 1, 1))
        if c in (2, 5):
            sx[c] = 0.5 * (east[c] - west[c])
        if c in (3, 5):
            sy[c] = 0.5 * (north - south)
        sz.append(0.5 * (upper - lower))
        out_lap.append(east[c] + west[c] + north + south + upper + lower - 6.0 * mid[c])
    spread = sx[2] + sy[3] + sz[4]
    coupled = [-VAPOR_LOAD * spread, -AMBIENT_LOAD * spread, -sx[5], -sy[5], -sz[5], -STIFFNESS * spread]
    return [coupled[c] - DRIFT_SPEED * sz[c] + VISCOSITY[c] * out_lap[c] for c in range(COMPS)]


def halo_rates(h_west, h, h_east, mid, lane, edge, low_z):
    touch = jnp.zeros_like(h)
    for c in range(COMPS):
        touch = jnp.where(lane == c, lane_turn(mid[c], c - edge), touch)
    after = turn(h, -NEXT, 1)
    north = turn(h, -1, 0)
    south = turn(h, 1, 0)
    sx = 0.5 * (h_east - h_west)
    sy = 0.5 * (north - south)
    sz = jnp.where(low_z, 0.5, -0.5) * (after - touch)
    lap = h_east + h_west + north + south + after + touch - 6.0 * h
    q = jnp.where(lane == 2, sx, jnp.where(lane == 3, sy, jnp.where(lane == 4, sz, 0.0)))
    s = q + turn(q, -1, 1) + turn(q, -2, 1)
    coupled = jnp.where(
        lane == 0,
        -VAPOR_LOAD * turn(s, -2, 1),
        jnp.where(
            lane == 1,
            -AMBIENT_LOAD * turn(s, -1, 1),
            jnp.where(
                lane == 2,
                -turn(sx, -3, 1),
                jnp.where(
                    lane == 3,
                    -turn(sy, -2, 1),
                    jnp.where(lane == 4, -turn(sz, -1, 1), -STIFFNESS * turn(s, 3, 1)),
                ),
            ),
        ),
    )
    visc = jnp.where(
        lane == 0, VISCOSITY[0], jnp.where(lane == 1, VISCOSITY[1], jnp.where(lane == 5, VISCOSITY[5], VISCOSITY[2]))
    )
    return coupled - DRIFT_SPEED * sz + visc * lap


def advance(meta, g, h, f, fh, u1, own_x, own_y):
    n, size = g.shape[1], g.shape[2]
    gx, gy, gz = meta[0], meta[1], meta[2]
    low_z = gz == 0
    edge, _ = edges(gz)
    lane = iota((size, LANES), 1)
    y_l = wrapped(iota((size, LANES), 0), own_y, size)
    y_g = gy * own_y + y_l
    inside_y = jnp.where((y_g >= 0) & (y_g < meta[4] * own_y), 1.0, 0.0)
    before = (n - own_x) // 2

    def inside(i):
        x_g = gx * own_x + i - before
        ok = (x_g >= 0) & (x_g < meta[3] * own_x)
        return inside_y * jnp.where(ok, 1.0, 0.0)

    def one(i, carry):
        mid = [g[c, i] for c in range(COMPS)]
        rate = rates([g[c, i - 1] for c in range(COMPS)], mid, [g[c, i + 1] for c in range(COMPS)], h[i], lane, edge)
        m = inside(i)
        for c in range(COMPS):
            f[c, i - 1] = (mid[c] + GAS_STEP * rate[c]) * m
        hr = halo_rates(h[i - 1], h[i], h[i + 1], mid, lane, edge, low_z)
        fh[i - 1] = (h[i] + GAS_STEP * hr) * m
        return carry

    lax.fori_loop(1, n - 1, one, 0)

    part_rows = 4 * SUBL
    col_y = lax.div(wrapped(iota((size, LANES), 1), 2 * own_y, LANES) + LANES, 2) - LANES // 2
    spread_y = jnp.where(col_y == y_l, 1.0, 0.0)
    row_x = lax.div(wrapped(iota((part_rows, LANES), 0), 2 * own_x, part_rows) + LANES, 2) - LANES // 2
    height = iota((size, LANES), 1) + gz * LANES
    height = height.astype(F32)

    def two(i, fine):
        mid = [f[c, i - 1] for c in range(COMPS)]
        rate = rates([f[c, i - 2] for c in range(COMPS)], mid, [f[c, i] for c in range(COMPS)], fh[i - 1], lane, edge)
        m = inside(i)
        for c in range(COMPS):
            new = 0.5 * (g[c, i] + mid[c] + GAS_STEP * rate[c]) * m
            u1[c, i - 2] = new
        level = h[i][:, LEVEL : LEVEL + 1]
        at = jnp.sum(jnp.where(height == level, new, 0.0), axis=1, keepdims=True)
        line = jnp.sum(spread_y * at, axis=0, keepdims=True)
        return fine + jnp.where(row_x == i - before, line, 0.0)

    return lax.fori_loop(2, n - 2, two, jnp.zeros((part_rows, LANES), F32))


def top_heat(meta, beam, first, t, k, fine, own_rows, cols):
    gx, gy = meta[0], meta[1]
    shape = fine.shape
    row = gx * own_rows + wrapped(iota(shape, 0), own_rows, shape[0])
    col = gy * cols + wrapped(iota(shape, 1), cols, shape[1])
    row, col = row.astype(F32), col.astype(F32)
    kx = [0.5 * (v + turn(v, -1, 0)) for v in k]
    ky = [0.5 * (v + turn(v, -1, 1)) for v in k]
    kz = [0.5 * (k[d] + k[d + 1]) for d in range(TOP - 1)]
    for s in range(SUBSTEPS):
        beam_xy = heat_source(row, col, beam, first + s)
        before = 0.5 * k[0] * t[0]
        new = []
        for d in range(TOP):
            fx = kx[d] * (turn(t[d], -1, 0) - t[d])
            fy = ky[d] * (turn(t[d], -1, 1) - t[d])
            fz = kz[d] * (t[d + 1] - t[d]) if d + 1 < TOP else jnp.zeros_like(before)
            factor = jnp.exp(jnp.full(shape, -d / ABSORB_DEPTH, F32))
            change = (fx - turn(fx, 1, 0)) + (fy - turn(fy, 1, 1)) + (fz - before) + beam_xy * factor
            if d == 0:
                change = change - LATENT_HEAT * softplus(t[0] - BOIL_LEVEL - BACK_PRESSURE * fine)
            new.append(jnp.where(k[d] > 0, t[d] + HEAT_STEP * change, 0.0))
            before = fz
        t = new
    return t


def vapor_mass(t0, fine):
    four = t0 + turn(t0, -1, 1)
    four = four + turn(four, -1, 0)
    return softplus(0.25 * four - BOIL_LEVEL - BACK_PRESSURE * fine)


def mass_rows(meta, h, mass, size, own_y):
    gz = meta[2]
    y_l = wrapped(iota((size, LANES), 0), own_y, size)
    col = wrapped(iota((size, LANES), 1), 2 * own_y, LANES)
    pick = col == 2 * y_l
    height = (iota((size, LANES), 1) + gz * LANES).astype(F32)

    def row(i, x):
        r = lax.rem(2 * x + mass.shape[0], mass.shape[0])
        line = mass[pl.ds(r, 1), :]
        at = jnp.sum(jnp.where(pick, line, 0.0), axis=1, keepdims=True)
        return jnp.where(height == h[i][:, LEVEL : LEVEL + 1], at, 0.0)

    return row


def first_kernel(
    cells, meta, beam, u, own, in_a, in_b, in_z, in_d, in_h, gy_a, gy_b,
    out_g, out_m, out_t, out_k, g, h, f, fh, u1, mass, skin,
):
    rows_x, reach = cells
    gx, gy, gz = meta[0], meta[1], meta[2]
    even_x = lax.rem(gx, 2) == 0
    even_y = lax.rem(gy, 2) == 0
    low_z = gz == 0
    own_y = u.shape[2]
    tiles = own_y // SUBL
    size = own_y + 2 * SUBL
    half = SUBL // 2
    sub = iota((SUBL, LANES), 0)
    zero = jnp.zeros((SUBL, LANES), F32)

    def side(k):
        upper = jnp.where(even_y, gy_a[k], gy_b[k])
        lower = jnp.where(even_y, gy_b[k], gy_a[k])
        return upper, lower

    wide = rows_x + 2 * reach - 2
    outer = wide * COMPS // 2
    for x in range(-reach, rows_x + reach):
        i = x + reach
        for c in range(COMPS):
            for y in range(tiles):
                value = row_tile(c, x, y, u, in_a, in_b, even_x)
                g[c, i, y * SUBL : (y + 1) * SUBL, :] = zero if value is None else value
            upper = lower = zero
            if 0 < i < wide + 1:
                upper, lower = side((i - 1) * COMPS // 2 + c // 2)
                if c % 2:
                    upper, lower = turn(upper, half, 0), turn(lower, half, 0)
            if -1 <= x < rows_x + 1 and c in QUARTERS:
                q = QUARTERS.index(c)
                far_up, far_low = side(outer + x + 1)
                far_up, far_low = turn(far_up, half - 2 * q, 0), turn(far_low, 2 - 2 * q, 0)
            else:
                far_up = far_low = zero
            g[c, i, own_y : own_y + SUBL, :] = jnp.where(sub < half, upper, jnp.where(sub < half + 2, far_up, 0.0))
            g[c, i, own_y + SUBL : size, :] = jnp.where(sub >= half, lower, jnp.where(sub >= half - 2, far_low, 0.0))
    base = in_z.shape[0] - tiles
    packed = []
    for b in range(3):
        parts = []
        for y in range(tiles):
            if b == 0:
                parts.append(jnp.where(low_z, in_d[base + y], in_h[y]))
            elif b == 1:
                parts.append(in_z[base + y])
            else:
                parts.append(jnp.where(low_z, in_h[y], in_d[base + y]))
        parts.extend(side(outer + rows_x + 2 + b))
        packed.append(jnp.concatenate(parts, axis=0))
    for x in range(-reach, rows_x + reach):
        b, q = divmod(x + rows_x, rows_x)
        h[x + reach] = turn(packed[b], -GROUP * q, 1)

    fine = advance(meta, g, h, f, fh, u1, rows_x, own_y)

    cols = LANES // 4
    per = LANES // cols
    lane = iota((SUBL, LANES), 1)
    sources = surface_sources(own, in_a, in_b, in_z, in_d, even_x, tiles)
    count = len(sources) // 2
    top_at = gy_a.shape[0] - len(sources) // per
    layers = []
    for a in range(2):
        for s in range(count):
            src = sources[a * count + s]
            upper, lower = side(top_at + (a * count + s) // per)
            i = s % per
            for q in range(per):
                at = cols * q + SUBL * i
                skin[s * per + q] = jnp.where(
                    lane < cols,
                    turn(src, -cols * q, 1),
                    jnp.where(
                        lane < cols + SUBL,
                        turn(upper, cols - at, 1),
                        jnp.where(lane >= LANES - SUBL, turn(lower, LANES - SUBL - at, 1), 0.0),
                    ),
                )
        for d in range(TOP):
            layers.append(skin[:, d, :])
    t, k = layers[:TOP], layers[TOP:]
    t = top_heat(meta, beam, 0, t, k, fine, 2 * rows_x, cols)
    for d in range(TOP):
        out_t[d] = t[d]
        out_k[d] = k[d]
    mass[...] = vapor_mass(t[0], fine)

    edge, behind = edges(gz)
    mass_of = mass_rows(meta, h, mass, size, own_y)
    x_from = -REACH_LAST
    count = rows_x + 2 * REACH_LAST
    half = SUBL // 2
    sub = iota((SUBL, LANES), 0)
    small = own_y + SUBL
    lane_s = iota((small, LANES), 1)
    shift = reach - 2 - REACH_LAST
    y_l = wrapped(iota((size, LANES), 0), own_y, size)
    y_g = gy * own_y + y_l
    inside_y = jnp.where((y_g >= 0) & (y_g < meta[4] * own_y), 1.0, 0.0)

    def finish(i, carry):
        x = i + x_from
        x_g = gx * rows_x + x
        ok = jnp.where((x_g >= 0) & (x_g < meta[3] * rows_x), 1.0, 0.0)
        add = mass_of(x + reach, x) * inside_y * ok
        rows = []
        for c in range(COMPS):
            value = u1[c, i + shift]
            if c == 0:
                value = value + VAPOR_SOURCE * add
            elif c == 4:
                value = value + RECOIL_PUSH * add
            elif c == 5:
                value = value + RECOIL_PRESSURE * add
            ends = jnp.where(sub < half, value[own_y : own_y + SUBL], value[own_y + SUBL : size])
            value = jnp.concatenate([value[:own_y], ends], axis=0)
            out_g[c, i] = value
            rows.append(value)
        acc = jnp.zeros((small, LANES), F32)
        for c in range(COMPS):
            acc = jnp.where(lane_s == c, lane_turn(rows[c], c - edge), acc)
            acc = jnp.where(lane_s == NEXT + c, lane_turn(rows[c], NEXT + c - behind), acc)
        level = h[x + reach][:, LEVEL : LEVEL + 1]
        ends = jnp.where(sub < half, level[own_y : own_y + SUBL], level[own_y + SUBL : size])
        level = jnp.concatenate([jnp.broadcast_to(level[:own_y], (own_y, LANES)), ends], axis=0)
        acc = jnp.where(lane_s == LEVEL, level, acc)
        acc = jnp.where(lane_s < GROUP, acc, 0.0)
        j = i // (LANES // GROUP)
        q = lax.rem(i, LANES // GROUP)
        out_m[j] = jnp.where(q == 0, 0.0, out_m[j]) + lane_turn(acc, GROUP * q)
        return carry

    out_m[...] = jnp.zeros_like(out_m)
    lax.fori_loop(0, count, finish, 0)


def last_kernel(cells, meta, beam, g, in_m, in_t, in_k, out_g, out_t, out_f, h, f, fh, u1, mass, skin):
    rows_x, own_y = cells
    size = g.shape[2]
    n = g.shape[1]
    for i in range(n):
        j, q = divmod(i, LANES // GROUP)
        h[i] = turn(in_m[j], -GROUP * q, 1)
    fine = advance(meta, g, h, f, fh, u1, rows_x, own_y)
    cols = LANES // 4
    t = [in_t[d] for d in range(TOP)]
    k = [in_k[d] for d in range(TOP)]
    t = top_heat(meta, beam, SUBSTEPS, t, k, fine, 2 * rows_x, cols)
    for d in range(TOP):
        skin[:, d, :] = t[d]
    pack_skin(t, 0, cols, skin, out_t)
    pack_skin(t, SUBL, cols, skin, out_f)
    mass[...] = vapor_mass(t[0], fine)
    mass_of = mass_rows(meta, h, mass, size, own_y)

    def finish(x, carry):
        add = mass_of(x + REACH_LAST, x)
        for c in range(COMPS):
            value = u1[c, x + REACH_LAST - 2]
            if c == 0:
                value = value + VAPOR_SOURCE * add
            elif c == 4:
                value = value + RECOIL_PUSH * add
            elif c == 5:
                value = value + RECOIL_PRESSURE * add
            out_g[c, x] = value[:own_y]
        return carry

    lax.fori_loop(0, rows_x, finish, 0)


def call(body, outs, scratch=(), scalars=1, count=0):
    vmem = pl.BlockSpec(memory_space=pltpu.VMEM)
    smem = pl.BlockSpec(memory_space=pltpu.SMEM)
    return pl.pallas_call(
        body,
        out_shape=[jax.ShapeDtypeStruct(s, F32) for s in outs],
        in_specs=[smem] * scalars + [vmem] * count,
        out_specs=[vmem] * len(outs),
        scratch_shapes=[pltpu.VMEM(s, F32) for s in scratch],
        compiler_params=pltpu.CompilerParams(vmem_limit_bytes=32 * 1024 * 1024),
    )


def pairs(count, odd):
    out = []
    for i in range(odd, count - 1, 2):
        out += [(i, i + 1), (i + 1, i)]
    return out


def cross(nx, nz, upper):
    out = []
    for i in range(nx - 1):
        a, b = i * nz + (nz - 1 if upper else 0), (i + 1) * nz + (0 if upper else nz - 1)
        out += [(a, b), (b, a)]
    return out


def shards(u, t, m, lev, beam):
    nx, ny, nz = (lax.axis_size(a) for a in ("gx", "gy", "gz"))
    gx, gy, gz = (lax.axis_index(a) for a in ("gx", "gy", "gz"))
    meta = jnp.stack([gx, gy, gz, nx, ny, nz]).astype(jnp.int32)
    _, rows_x, own_y, _ = u.shape
    t, m = jnp.transpose(t, (1, 2, 0)), jnp.transpose(m, (1, 2, 0))
    rows, cols, depth = t.shape
    tiles = own_y // SUBL
    block = (SUBL, LANES)
    n_top = 2 * rows * cols // LANES
    n_x = slab_size(tiles) + n_top
    n_z = 2 * SKIN * cols // SUBL + n_top + tiles
    msg_a, msg_b, msg_z, msg_d, msg_h, own = call(
        functools.partial(pack_kernel, (rows_x, REACH)),
        [(n_x, *block), (n_x, *block), (n_z, *block), (n_z, *block), (tiles, *block), (n_top, *block)],
        count=4,
    )(meta, u, t, m, lev)
    in_a = lax.ppermute(msg_a, "gx", pairs(nx, 0))
    in_b = lax.ppermute(msg_b, "gx", pairs(nx, 1))
    in_z = lax.ppermute(msg_z, "gz", pairs(nz, 0))
    in_d = lax.ppermute(msg_d, ("gx", "gz"), cross(nx, nz, True))
    in_h = lax.ppermute(msg_h, ("gx", "gz"), cross(nx, nz, False))
    wide = rows_x + 2 * REACH - 2
    n_y = wide * COMPS // 2 + rows_x + 2 + 3 + rows + 2 * SKIN + n_top
    msg_a, msg_b = call(
        functools.partial(relay_kernel, (rows_x, REACH)), [(n_y, *block), (n_y, *block)], count=9
    )(meta, u, t, m, own, in_a, in_b, in_z, in_d, in_h)
    gy_a = lax.ppermute(msg_a, "gy", pairs(ny, 0))
    gy_b = lax.ppermute(msg_b, "gy", pairs(ny, 1))

    size = own_y + 2 * SUBL
    n = rows_x + 2 * REACH
    n2 = rows_x + 2 * REACH_LAST
    small = own_y + SUBL
    part_rows = 4 * SUBL
    n_m = -(-n2 // (LANES // GROUP))
    g2, msg_m, top_t, top_k = call(
        functools.partial(first_kernel, (rows_x, REACH)),
        [(COMPS, n2, small, LANES), (n_m, small, LANES), (TOP, part_rows, LANES), (TOP, part_rows, LANES)],
        scratch=[
            (COMPS, n, size, LANES),
            (n, size, LANES),
            (COMPS, n - 2, size, LANES),
            (n - 2, size, LANES),
            (COMPS, n - 4, size, LANES),
            (part_rows, LANES),
            (part_rows, *block),
        ],
        scalars=2,
        count=9,
    )(meta, beam, u, own, in_a, in_b, in_z, in_d, in_h, gy_a, gy_b)
    in_m = lax.ppermute(msg_m, "gz", pairs(nz, 0))
    part = (rows + 2 * SKIN, cols + SUBL, depth)
    (bulk,) = call(
        bulk_kernel, [t.shape], scratch=[(2, *part), part, part, part, part], scalars=2, count=6
    )(meta, beam, t, m, in_z, in_d, gy_a, gy_b)
    gas, mine, other = call(
        functools.partial(last_kernel, (rows_x, own_y)),
        [u.shape, (n_top // 2, *block), (n_top // 2, *block)],
        scratch=[
            (n2, small, LANES),
            (COMPS, n2 - 2, small, LANES),
            (n2 - 2, small, LANES),
            (COMPS, n2 - 4, small, LANES),
            (part_rows, LANES),
            (part_rows, *block),
        ],
        scalars=2,
        count=4,
    )(meta, beam, g2, in_m, top_t, top_k)
    given = lax.ppermute(other, "gz", pairs(nz, 0))
    (out,) = call(seal_kernel, [t.shape], count=3)(meta, bulk, mine, given)
    return gas, jnp.transpose(out, (2, 0, 1))


def solution(mesh):
    return jax.shard_map(
        shards,
        mesh=mesh,
        in_specs=(
            P(None, "gx", "gy", "gz"),
            P(None, ("gx", "gz"), "gy"),
            P(None, ("gx", "gz"), "gy"),
            P("gx", "gy"),
            P(),
        ),
        out_specs=(P(None, "gx", "gy", "gz"), P(None, ("gx", "gz"), "gy")),
        check_vma=False,
    )
```

```python
import functools

import jax
import jax.numpy as jnp
from jax import lax
from jax.experimental import pallas as pl
from jax.experimental.pallas import tpu as pltpu
from jax.sharding import PartitionSpec as P

STEPS = 2
SUBSTEPS = 2
GAS_STEP = 0.3
DRIFT_SPEED = 0.5
VAPOR_LOAD = 0.3
AMBIENT_LOAD = 0.7
STIFFNESS = 1.0
VISCOSITY = (0.2, 0.1, 0.15, 0.15, 0.15, 0.2)
HEAT_STEP = 1.0
POWDER_COND = 0.04
SOLID_COND = 0.15
LIQUID_COND = 0.09
LASER_POWER = 3.0
SPOT_RADIUS = 6.0
ABSORB_DEPTH = 4.0
BOIL_LEVEL = 1.0
BACK_PRESSURE = 0.5
LATENT_HEAT = 0.3
VAPOR_SOURCE = 0.5
RECOIL_PUSH = 0.4
RECOIL_PRESSURE = 0.6

COMPS = 6
LANES = 128
SUBL = 8
F32 = jnp.float32
REACH = 6
REACH_LAST = 3
SKIN = 4
TOP = 8
GROUP = 16
LEVEL = 2 * COMPS


def iota(shape, axis):
    return lax.broadcasted_iota(jnp.int32, shape, axis)


def wrapped(index, own, size):
    return jnp.where(index < own + (size - own) // 2, index, index - size)


def turn(value, amount, axis):
    size = value.shape[axis]
    if isinstance(amount, int):
        amount = amount % size
        if amount == 0:
            return value
    return pltpu.roll(value, amount, axis)


def softplus(x):
    return jnp.maximum(x, 0.0) + jnp.log1p(jnp.exp(-jnp.abs(x)))


def pack_heights(rows, base, lane, low_z, acc):
    more = jnp.where(low_z, 2, 0)
    for c, row in enumerate(rows):
        acc = jnp.where((lane & -2) == base + 2 * c, turn(row, base + 2 * c + more, 1), acc)
    return acc


def unpack_heights(packed, base, low_z, h0, h1, i):
    here = turn(packed, -base, 1)
    other = turn(packed, -base - 1, 1)
    h0[i] = jnp.where(low_z, here, other)
    h1[i] = jnp.where(low_z, other, here)


DEEP_5 = (2, 3, 4, 5)
DEEP_6 = (2, 5)
FULL = 4
QUARTERS = (5, 3, 2, 4)


def slab_index(c, layer, tile, tiles):
    if layer <= FULL:
        return (c * FULL + layer - 1) * tiles + tile
    base = COMPS * FULL * tiles
    if layer == FULL + 1:
        return base + DEEP_5.index(c) * tiles + tile if c in DEEP_5 else None
    base += len(DEEP_5) * tiles
    return base + DEEP_6.index(c) * tiles + tile if c in DEEP_6 else None


def slab_size(tiles):
    return (COMPS * FULL + len(DEEP_5) + len(DEEP_6)) * tiles


def row_tile(c, x, tile, u, in_a, in_b, even_x):
    rows_x, tiles = u.shape[1], u.shape[2] // SUBL
    if 0 <= x < rows_x:
        return u[c, x, tile * SUBL : (tile + 1) * SUBL, :]
    k = slab_index(c, -x if x < 0 else x - rows_x + 1, tile, tiles)
    if k is None:
        return None
    low, high = (in_b[k], in_a[k]) if x < 0 else (in_a[k], in_b[k])
    return jnp.where(even_x, low, high)


def conduct(v):
    return jnp.where(v == 0, POWDER_COND, jnp.where(v == 1, SOLID_COND, LIQUID_COND)).astype(F32)


def pack_kernel(cells, meta, u, t, m, lev, out_a, out_b, out_z, out_d, out_h, own):
    rows_x, reach = cells
    gx, gz = meta[0], meta[2]
    even = lax.rem(gx, 2) == 0
    low_z = gz == 0
    tiles = u.shape[2] // SUBL
    for c in range(COMPS):
        for layer in range(1, reach + 1):
            for y in range(tiles):
                n = slab_index(c, layer, y, tiles)
                if n is None:
                    continue
                lo = u[c, layer - 1, y * SUBL : (y + 1) * SUBL, :]
                hi = u[c, rows_x - layer, y * SUBL : (y + 1) * SUBL, :]
                out_a[n] = jnp.where(even, hi, lo)
                out_b[n] = jnp.where(even, lo, hi)
    rows, cols = t.shape[0], t.shape[1]
    col_tiles = cols // SUBL
    n = 0
    for source in (lambda v: v, conduct):
        ref = t if n == 0 else m
        for r in range(SKIN):
            for y in range(col_tiles):
                lo = source(ref[r, y * SUBL : (y + 1) * SUBL, :])
                hi = source(ref[rows - SKIN + r, y * SUBL : (y + 1) * SUBL, :])
                out_z[n] = jnp.where(low_z, hi, lo)
                out_d[n] = jnp.where(low_z, lo, hi)
                n += 1
    per = LANES // cols
    top_a = slab_size(tiles)
    for j in range(2 * rows // per):
        ref, r = (t, j * per) if j < rows // per else (m, j * per - rows)
        block = ref[r : r + per].reshape(LANES, LANES)
        if ref is m:
            block = conduct(block)
        top = jnp.transpose(block)[:TOP]
        own[j] = top
        out_z[n + j] = top
        out_d[n + j] = top
        out_a[top_a + j] = top
        out_b[top_a + j] = top
    n += 2 * rows // per
    size = u.shape[2]
    lane = iota((size, LANES), 1)
    eye = iota((size, size), 0) == iota((size, size), 1)
    levels = lev[...].astype(F32)
    acc = jnp.zeros((size, LANES), F32)
    for x in range(rows_x):
        acc = pack_heights([u[c, x] for c in range(COMPS)], x * GROUP, lane, low_z, acc)
        level = jnp.sum(jnp.where(eye, levels[x : x + 1, :], 0.0), axis=1, keepdims=True)
        acc = jnp.where((lane & -2) == x * GROUP + LEVEL, level, acc)
    for y in range(tiles):
        part = acc[y * SUBL : (y + 1) * SUBL]
        out_h[y] = part
        out_z[n + y] = part
        out_d[n + y] = part


def part_row(r, tile, ref, at, rows, in_z, in_d, low_z, col_tiles, low_part):
    if 0 <= r < rows:
        value = ref[r, tile * SUBL : (tile + 1) * SUBL, :]
        return conduct(value) if at else value
    k = (at * SKIN + (r + SKIN if r < 0 else r - rows)) * col_tiles + tile
    low, high = (in_d[k], in_z[k]) if r < 0 else (in_z[k], in_d[k])
    return jnp.where(low_z, low, high)


def relay_kernel(cells, meta, u, t, m, own, in_a, in_b, in_z, in_d, in_h, out_a, out_b):
    rows_x, reach = cells
    gx, gy, gz = meta[0], meta[1], meta[2]
    even_x = lax.rem(gx, 2) == 0
    even_y = lax.rem(gy, 2) == 0
    low_z = gz == 0
    tiles = u.shape[2] // SUBL
    rows, cols = t.shape[0], t.shape[1]
    col_tiles = cols // SUBL
    half = SUBL // 2
    sub = iota((SUBL, LANES), 0)
    lane = iota((SUBL, LANES), 1)
    zero = jnp.zeros((SUBL, LANES), F32)

    def put(n, hi, lo):
        out_a[n] = jnp.where(even_y, hi, lo)
        out_b[n] = jnp.where(even_y, lo, hi)

    def both(c, x):
        pair = [row_tile(c, x, y, u, in_a, in_b, even_x) for y in (tiles - 1, 0)]
        return [zero if v is None else v for v in pair]

    n = 0
    for x in range(1 - reach, rows_x + reach - 1):
        for c in range(0, COMPS, 2):
            (hi0, lo0), (hi1, lo1) = both(c, x), both(c + 1, x)
            put(n, jnp.where(sub < half, turn(hi1, half, 0), hi0), jnp.where(sub < half, lo0, turn(lo1, half, 0)))
            n += 1
    for x in range(-1, rows_x + 1):
        hi = lo = zero
        for q, c in enumerate(QUARTERS):
            a, b = both(c, x)
            hi = jnp.where((sub & -2) == 2 * q, turn(a, 2 * q - 2, 0), hi)
            lo = jnp.where((sub & -2) == 2 * q, turn(b, 2 * q - half, 0), lo)
        put(n, hi, lo)
        n += 1
    base = in_z.shape[0] - tiles
    hi_y, lo_y = tiles - 1, 0
    put(
        n,
        jnp.where(low_z, in_d[base + hi_y], in_h[hi_y]),
        jnp.where(low_z, in_d[base + lo_y], in_h[lo_y]),
    )
    put(n + 1, in_z[base + hi_y], in_z[base + lo_y])
    put(
        n + 2,
        jnp.where(low_z, in_h[hi_y], in_d[base + hi_y]),
        jnp.where(low_z, in_h[lo_y], in_d[base + lo_y]),
    )
    n += 3
    for r in range(-SKIN, rows + SKIN):
        hi_t, lo_t = [part_row(r, y, t, 0, rows, in_z, in_d, low_z, col_tiles, None) for y in (col_tiles - 1, 0)]
        hi_k, lo_k = [part_row(r, y, m, 1, rows, in_z, in_d, low_z, col_tiles, None) for y in (col_tiles - 1, 0)]
        put(n, jnp.where(sub < half, turn(hi_k, half, 0), hi_t), jnp.where(sub < half, lo_t, turn(lo_k, half, 0)))
        n += 1
    sources = surface_sources(own, in_a, in_b, in_z, in_d, even_x, tiles)
    per = LANES // cols
    slot = lax.rem(lane, cols) // SUBL
    for v in range(len(sources) // per):
        hi = lo = zero
        for i in range(per):
            src = sources[v * per + i]
            hi = jnp.where(slot == i, turn(src, SUBL * i - (cols - SUBL), 1), hi)
            lo = jnp.where(slot == i, turn(src, SUBL * i, 1), lo)
        put(n + v, hi, lo)


def surface_sources(own, in_a, in_b, in_z, in_d, even_x, tiles):
    count = own.shape[0]
    tail = in_a.shape[0] - count
    at = in_z.shape[0] - tiles - count
    out = []
    for a in range(2):
        span = range(a * count // 2, (a + 1) * count // 2)
        out += [own[j] for j in span]
        out += [in_z[at + j] for j in span]
        out += [jnp.where(even_x, in_a[tail + j], in_b[tail + j]) for j in span]
        out += [in_d[at + j] for j in span]
    return out


def heat_source(row, col, beam, step):
    a = beam[step, 0].astype(F32)
    b = beam[step, 1].astype(F32)
    along_x = jnp.exp(-(((row - a) / SPOT_RADIUS) ** 2))
    along_y = jnp.exp(-(((col - b) / SPOT_RADIUS) ** 2))
    return LASER_POWER * along_x * along_y


def bulk_kernel(meta, beam, t, m, in_z, in_d, gy_a, gy_b, out, temp, cond, kx, ky, kz):
    gx, gy, gz = meta[0], meta[1], meta[2]
    even_y = lax.rem(gy, 2) == 0
    low_z = gz == 0
    rows, cols, depth = t.shape
    col_tiles = cols // SUBL
    half = SUBL // 2
    size = cols + SUBL
    n = rows + 2 * SKIN
    sub = iota((SUBL, LANES), 0)
    base = gy_a.shape[0] - 4 - n
    for i in range(n):
        for y in range(col_tiles):
            span = slice(y * SUBL, (y + 1) * SUBL)
            temp[0, i, span, :] = part_row(i - SKIN, y, t, 0, rows, in_z, in_d, low_z, col_tiles, None)
            cond[i, span, :] = part_row(i - SKIN, y, m, 1, rows, in_z, in_d, low_z, col_tiles, None)
        up = jnp.where(even_y, gy_a[base + i], gy_b[base + i])
        low = jnp.where(even_y, gy_b[base + i], gy_a[base + i])
        temp[0, i, cols:size, :] = jnp.where(sub < half, up, low)
        cond[i, cols:size, :] = turn(jnp.where(sub < half, low, up), half, 0)

    lane = iota((size, LANES), 1)
    for i in range(n):
        k = cond[i]
        if i + 1 < n:
            kx[i] = 0.5 * (k + cond[i + 1])
        ky[i] = 0.5 * (k + turn(k, -1, 0))
        kz[i] = 0.5 * (k + jnp.where(lane == depth - 1, 0.0, turn(k, -1, 1)))

    col_g = gy * cols + wrapped(iota((size, LANES), 0), cols, size)
    inside_y = jnp.where((col_g >= 0) & (col_g < meta[4] * cols), 1.0, 0.0)
    col_f = col_g.astype(F32)
    fall = jnp.exp(-lane.astype(F32) / ABSORB_DEPTH)
    first_row = (gx * meta[5] + gz) * rows - SKIN

    for s in range(STEPS * SUBSTEPS):
        src, dst = s % 2, 1 - s % 2
        last = s == STEPS * SUBSTEPS - 1
        a = beam[s, 0].astype(F32)
        b = beam[s, 1].astype(F32)
        spot = LASER_POWER * fall * jnp.exp(-(((col_f - b) / SPOT_RADIUS) ** 2))
        lo, hi = s + 1, n - 1 - s
        fx0 = kx[lo - 1] * (temp[src, lo] - temp[src, lo - 1])
        for i in range(lo, hi):
            v = temp[src, i]
            fx = kx[i] * (temp[src, i + 1] - v)
            fy = ky[i] * (turn(v, -1, 0) - v)
            fz = kz[i] * (jnp.where(lane == depth - 1, 0.0, turn(v, -1, 1)) - v)
            above = jnp.where(lane == 0, 0.5 * cond[i] * v, turn(fz, 1, 1))
            row = first_row + i
            along_x = jnp.exp(-((jnp.full((1, LANES), row.astype(F32) - a) / SPOT_RADIUS) ** 2))
            change = (fx - fx0) + (fy - turn(fy, 1, 0)) + (fz - above) + spot * along_x
            new = v + HEAT_STEP * change
            if last:
                out[i - SKIN] = new[:cols]
            else:
                ok = (row >= 0) & (row < meta[3] * meta[5] * rows)
                temp[dst, i] = new * (inside_y * jnp.where(ok, 1.0, 0.0))
            fx0 = fx


def seal_kernel(meta, bulk, mine, given, out):
    rows, cols, depth = bulk.shape
    per = LANES // cols
    lane = iota((LANES, LANES), 1)
    for j in range(mine.shape[0]):
        skin = jnp.where(meta[2] == 0, mine[j], given[j])
        skin = jnp.concatenate([skin, jnp.zeros((LANES - SUBL, LANES), F32)], axis=0)
        block = jnp.where(lane < SKIN, jnp.transpose(skin), bulk[j * per : (j + 1) * per].reshape(LANES, LANES))
        out[j * per : (j + 1) * per] = block.reshape(per, cols, LANES)


def pack_skin(t, rows, cols, scratch, out):
    per = LANES // cols
    lane = iota((SUBL, LANES), 1)
    for j in range(SUBL // per):
        acc = jnp.zeros((SUBL, LANES), F32)
        for q in range(per):
            acc = jnp.where(lane // cols == q, turn(scratch[rows + j * per + q], cols * q, 1), acc)
        out[j] = acc


def split(value):
    high = value.astype(jnp.bfloat16)
    rest = (value - high.astype(F32)).astype(jnp.bfloat16)
    return jnp.concatenate([high, rest], axis=1)


def height_matrix():
    shape = (2 * LANES, 2 * LANES)
    k = iota(shape, 0) & (LANES - 1)
    j = iota(shape, 1)
    above = jnp.where(k == (j & (LANES - 1)) + 1, 1.0, 0.0)
    below = jnp.where(k == (j & (LANES - 1)) - 1, 1.0, 0.0)
    return (above + jnp.where(j < LANES, -below, below)).astype(jnp.bfloat16)


def height_terms(ref, first, last, matrix, diff, total):
    size = ref.shape[2]
    for c in range(COMPS):
        rows = ref[c, first:last].reshape((last - first) * size, LANES)
        both = jnp.dot(split(rows), matrix, preferred_element_type=F32)
        diff[c, first:last] = both[:, :LANES].reshape(last - first, size, LANES)
        total[c, first:last] = both[:, LANES:].reshape(last - first, size, LANES)


def cut_weights(size, low_z):
    lane = iota((size, LANES), 1)
    up = (lane == LANES - 1) & low_z
    down = (lane == 0) & jnp.logical_not(low_z)
    sign = jnp.where(up, 1.0, jnp.where(down, -1.0, 0.0))
    return sign, jnp.abs(sign)


def stepped(comps, ref, i, diff, total, h, cut, scale, start, size):
    sign, mark = cut
    half = 0.5 * scale * GAS_STEP
    span = pl.ds(start, size)

    def dx(c):
        return ref[c, i + 1, span, :] - ref[c, i - 1, span, :]

    def dy(c):
        return ref[c, i, pl.ds(start + 1, size), :] - ref[c, i, pl.ds(start - 1, size), :]

    def dz(c):
        return diff[c, i, span, :] + sign * h[i, span, 2 * c : 2 * c + 1]

    spread = half * (dx(2) + dy(3) + dz(4))
    out = {}
    for c in comps:
        v = VISCOSITY[c]
        side = scale * GAS_STEP * v
        drift = 0.5 * DRIFT_SPEED * scale * GAS_STEP
        sides = (ref[c, i + 1, span, :] + ref[c, i - 1, span, :]) + (
            ref[c, i, pl.ds(start + 1, size), :] + ref[c, i, pl.ds(start - 1, size), :]
        )
        across = h[i, span, 2 * c : 2 * c + 1]
        new = (
            scale * (1.0 - 6.0 * GAS_STEP * v) * ref[c, i, span, :]
            + side * (sides + total[c, i, span, :])
            - drift * diff[c, i, span, :]
            + (side * mark - drift * sign) * across
        )
        if c == 2:
            new = new - half * dx(5)
        elif c == 3:
            new = new - half * dy(5)
        elif c == 4:
            new = new - half * dz(5)
        else:
            new = new - {0: VAPOR_LOAD, 1: AMBIENT_LOAD, 5: STIFFNESS}[c] * spread
        out[c] = new
    return out


def by_comp(lane, values):
    out = jnp.full(lane.shape, values[-1], F32)
    for c, v in enumerate(values[:-1]):
        out = jnp.where(lane == 2 * c, v, out)
    return out


def couple_matrix():
    shape = (6 * LANES, LANES)
    k = iota(shape, 0)
    j = iota(shape, 1)
    axis = k // (2 * LANES)
    lane = k & (LANES - 1)
    spread = (lane == 4 + 2 * axis) & ((j == 0) | (j == 2) | (j == 10))
    slope = (lane == 10) & (j == 4 + 2 * axis)
    return jnp.where(spread | slope, 1.0, 0.0).astype(jnp.bfloat16)


def halo_stepped(h0, h1, g, low_z, mask_of, out):
    n, size = h0.shape[0], h0.shape[1]
    rows = (n - 2) * size
    lane = iota((1, LANES), 1)
    more = jnp.where(low_z, 1, 0)
    flat_lane = iota((rows, LANES), 1)
    touch = jnp.zeros((rows, LANES), F32)
    for c in range(COMPS):
        own = g[c, 1 : n - 1].reshape(rows, LANES)
        touch = jnp.where(flat_lane == 2 * c, turn(own, 2 * c + more, 1), touch)
    mid = h0[1 : n - 1].reshape(rows, LANES)
    east = h0[2:n].reshape(rows, LANES)
    west = h0[0 : n - 2].reshape(rows, LANES)
    north = turn(mid, -1, 0)
    south = turn(mid, 1, 0)
    behind = h1[1 : n - 1].reshape(rows, LANES)
    slopes = [east - west, north - south, jnp.where(low_z, 1.0, -1.0) * (behind - touch)]
    coupled = jnp.dot(
        jnp.concatenate([split(v) for v in slopes], axis=1), couple_matrix(), preferred_element_type=F32
    )
    up = by_comp(lane, [GAS_STEP * (v - 0.5 * DRIFT_SPEED) for v in VISCOSITY])
    down = by_comp(lane, [GAS_STEP * (v + 0.5 * DRIFT_SPEED) for v in VISCOSITY])
    half = 0.5 * GAS_STEP
    pull = by_comp(lane, [-half * VAPOR_LOAD, -half * AMBIENT_LOAD, -half, -half, -half, -half * STIFFNESS])
    new = (
        by_comp(lane, [1.0 - 6.0 * GAS_STEP * v for v in VISCOSITY]) * mid
        + by_comp(lane, [GAS_STEP * v for v in VISCOSITY]) * ((east + west) + (north + south))
        + jnp.where(low_z, up, down) * behind
        + jnp.where(low_z, down, up) * touch
        + pull * coupled
    )
    for i in range(1, n - 1):
        out[i - 1] = turn(new[(i - 1) * size : i * size] * mask_of(i, 0, size), -1, 0)


def advance(meta, g, h0, h1, f, fh, diff, total, own_x, own_y, store):
    n, size = g.shape[1], g.shape[2]
    gx, gy, gz = meta[0], meta[1], meta[2]
    low_z = gz == 0
    before = (n - own_x) // 2
    before_y = (size - own_y) // 2
    reach = before - 2

    def mask_of(i, start, count):
        x_g = gx * own_x + i - before
        ok = (x_g >= 0) & (x_g < meta[3] * own_x)
        y_g = gy * own_y + iota((count, LANES), 0) + start - before_y
        return jnp.where((y_g >= 0) & (y_g < meta[4] * own_y) & ok, 1.0, 0.0)

    matrix = height_matrix()
    halo_stepped(h0, h1, g, low_z, mask_of, fh)
    height_terms(g, 1, n - 1, matrix, diff, total)
    everything = tuple(range(COMPS))

    def one(comps):
        def body(i, carry):
            count = size - 2
            new = stepped(comps, g, i, diff, total, h0, cut_weights(count, low_z), 1.0, 1, count)
            m = mask_of(i, 1, count)
            for c in comps:
                f[c, i - 1, :count, :] = new[c] * m
            return carry

        return body

    lax.fori_loop(2, n - 2, one(everything), 0, unroll=2)
    for i in (1, n - 2):
        one((2, 5))(i, 0)

    height_terms(f, 1, n - 3, matrix, diff, total)
    start = before_y - 1 - reach
    count = own_y + 2 * reach

    def two(comps):
        def body(i, carry):
            cut = cut_weights(count, low_z)
            new = stepped(comps, f, i - 1, diff, total, fh, cut, 0.5, start, count)
            m = mask_of(i, start + 1, count)
            for c in comps:
                new[c] = (0.5 * g[c, i, pl.ds(start + 1, count), :] + new[c]) * m
            store(i, new)
            return carry

        return body

    lax.fori_loop(3, n - 3, two(everything), 0, unroll=2)
    for i in (2, n - 3):
        two((5,))(i, 0)


def fine_pressure(meta, p, h0, own_x, own_y, part_rows):
    n, count = p.shape[0], p.shape[1]
    skip = (h0.shape[1] - count) // 2
    skip_x = (h0.shape[0] - n) // 2
    before = (n - own_x) // 2
    y_l = iota((count, LANES), 0) - (count - own_y) // 2
    col_y = lax.div(wrapped(iota((count, LANES), 1), 2 * own_y, LANES) + LANES, 2) - LANES // 2
    pick = col_y == y_l
    row_x = lax.div(wrapped(iota((part_rows, LANES), 0), 2 * own_x, part_rows) + LANES, 2) - LANES // 2
    height = (iota((count, LANES), 1) + meta[2] * LANES).astype(F32)
    fine = jnp.zeros((part_rows, LANES), F32)
    for i in range(n):
        level = h0[i + skip_x, skip : skip + count, LEVEL : LEVEL + 1]
        at = jnp.sum(jnp.where(height == level, p[i], 0.0), axis=1, keepdims=True)
        line = jnp.sum(jnp.where(pick, at, 0.0), axis=0, keepdims=True)
        fine = jnp.where(row_x == i - before, line, fine)
    return fine


def top_heat(meta, beam, first, t, k, fine, own_rows, cols):
    gx, gy = meta[0], meta[1]
    shape = fine.shape
    row = gx * own_rows + wrapped(iota(shape, 0), own_rows, shape[0])
    col = gy * cols + wrapped(iota(shape, 1), cols, shape[1])
    row, col = row.astype(F32), col.astype(F32)
    kx = [0.5 * (v + turn(v, -1, 0)) for v in k]
    ky = [0.5 * (v + turn(v, -1, 1)) for v in k]
    kz = [0.5 * (k[d] + k[d + 1]) for d in range(TOP - 1)]
    for s in range(SUBSTEPS):
        beam_xy = heat_source(row, col, beam, first + s)
        before = 0.5 * k[0] * t[0]
        new = []
        for d in range(TOP):
            fx = kx[d] * (turn(t[d], -1, 0) - t[d])
            fy = ky[d] * (turn(t[d], -1, 1) - t[d])
            fz = kz[d] * (t[d + 1] - t[d]) if d + 1 < TOP else jnp.zeros_like(before)
            factor = jnp.exp(jnp.full(shape, -d / ABSORB_DEPTH, F32))
            change = (fx - turn(fx, 1, 0)) + (fy - turn(fy, 1, 1)) + (fz - before) + beam_xy * factor
            if d == 0:
                change = change - LATENT_HEAT * softplus(t[0] - BOIL_LEVEL - BACK_PRESSURE * fine)
            new.append(jnp.where(k[d] > 0, t[d] + HEAT_STEP * change, 0.0))
            before = fz
        t = new
    return t


def vapor_mass(t0, fine):
    four = t0 + turn(t0, -1, 1)
    four = four + turn(four, -1, 0)
    return softplus(0.25 * four - BOIL_LEVEL - BACK_PRESSURE * fine)


def mass_rows(meta, h, mass, count, own_y):
    skip = (h.shape[1] - count) // 2
    y_l = iota((count, LANES), 0) - (count - own_y) // 2
    col = wrapped(iota((count, LANES), 1), 2 * own_y, LANES)
    pick = col == 2 * y_l
    height = (iota((count, LANES), 1) + meta[2] * LANES).astype(F32)

    def row(i, x):
        r = (2 * x) % mass.shape[0]
        at = jnp.sum(jnp.where(pick, mass[r : r + 1, :], 0.0), axis=1, keepdims=True)
        return jnp.where(height == h[i, skip : skip + count, LEVEL : LEVEL + 1], at, 0.0)

    return row


def first_kernel(
    cells, meta, beam, u, own, in_a, in_b, in_z, in_d, in_h, gy_a, gy_b,
    out_g, out_m, out_t, out_k, g, h, h1, f, fh, diff, total, p, mass, skin,
):
    rows_x, reach = cells
    gx, gy, gz = meta[0], meta[1], meta[2]
    even_x = lax.rem(gx, 2) == 0
    even_y = lax.rem(gy, 2) == 0
    low_z = gz == 0
    own_y = u.shape[2]
    tiles = own_y // SUBL
    size = own_y + 2 * SUBL
    half = SUBL // 2
    sub = iota((SUBL, LANES), 0)
    zero = jnp.zeros((SUBL, LANES), F32)

    def side(k):
        upper = jnp.where(even_y, gy_a[k], gy_b[k])
        lower = jnp.where(even_y, gy_b[k], gy_a[k])
        return upper, lower

    wide = rows_x + 2 * reach - 2
    outer = wide * COMPS // 2
    for x in range(-reach, rows_x + reach):
        i = x + reach
        for c in range(COMPS):
            for y in range(tiles):
                value = row_tile(c, x, y, u, in_a, in_b, even_x)
                g[c, i, (y + 1) * SUBL : (y + 2) * SUBL, :] = zero if value is None else value
            upper = lower = zero
            if 0 < i < wide + 1:
                upper, lower = side((i - 1) * COMPS // 2 + c // 2)
                if c % 2:
                    upper, lower = turn(upper, half, 0), turn(lower, half, 0)
            if -1 <= x < rows_x + 1 and c in QUARTERS:
                q = QUARTERS.index(c)
                far_up, far_low = side(outer + x + 1)
                far_up, far_low = turn(far_up, half - 2 * q, 0), turn(far_low, 2 - 2 * q, 0)
            else:
                far_up = far_low = zero
            g[c, i, own_y + SUBL : size, :] = jnp.where(sub < half, upper, jnp.where(sub < half + 2, far_up, 0.0))
            g[c, i, :SUBL, :] = jnp.where(sub >= half, lower, jnp.where(sub >= half - 2, far_low, 0.0))
    base = in_z.shape[0] - tiles
    packed = []
    for b in range(3):
        parts = []
        for y in range(tiles):
            if b == 0:
                parts.append(jnp.where(low_z, in_d[base + y], in_h[y]))
            elif b == 1:
                parts.append(in_z[base + y])
            else:
                parts.append(jnp.where(low_z, in_h[y], in_d[base + y]))
        upper, lower = side(outer + rows_x + 2 + b)
        packed.append(jnp.concatenate([lower, *parts, upper], axis=0))
    for x in range(-reach, rows_x + reach):
        b, q = divmod(x + rows_x, rows_x)
        unpack_heights(packed[b], GROUP * q, low_z, h, h1, x + reach)

    def store(i, new):
        p[i - 2] = new[COMPS - 1]
        if len(new) == COMPS:
            for c in range(COMPS):
                out_g[c, i - 3] = new[c]

    advance(meta, g, h, h1, f, fh, diff, total, rows_x, own_y, store)
    fine = fine_pressure(meta, p, h, rows_x, own_y, mass.shape[0])

    cols = LANES // 4
    per = LANES // cols
    lane = iota((SUBL, LANES), 1)
    sources = surface_sources(own, in_a, in_b, in_z, in_d, even_x, tiles)
    count = len(sources) // 2
    top_at = gy_a.shape[0] - len(sources) // per
    layers = []
    for a in range(2):
        for s in range(count):
            src = sources[a * count + s]
            upper, lower = side(top_at + (a * count + s) // per)
            i = s % per
            for q in range(per):
                at = cols * q + SUBL * i
                skin[s * per + q] = jnp.where(
                    lane < cols,
                    turn(src, -cols * q, 1),
                    jnp.where(
                        lane < cols + SUBL,
                        turn(upper, cols - at, 1),
                        jnp.where(lane >= LANES - SUBL, turn(lower, LANES - SUBL - at, 1), 0.0),
                    ),
                )
        for d in range(TOP):
            layers.append(skin[:, d, :])
    t, k = layers[:TOP], layers[TOP:]
    t = top_heat(meta, beam, 0, t, k, fine, 2 * rows_x, cols)
    for d in range(TOP):
        out_t[d] = t[d]
        out_k[d] = k[d]
    mass[...] = vapor_mass(t[0], fine)

    count, small = out_g.shape[1], out_g.shape[2]
    mass_of = mass_rows(meta, h, mass, small, own_y)
    lane_s = iota((small, LANES), 1)
    y_g = gy * own_y + iota((small, LANES), 0) - (small - own_y) // 2
    inside_y = jnp.where((y_g >= 0) & (y_g < meta[4] * own_y), 1.0, 0.0)
    skip = (size - small) // 2
    per = LANES // GROUP
    acc = jnp.zeros((small, LANES), F32)
    for i in range(count):
        x = i - REACH_LAST
        x_g = gx * rows_x + x
        ok = jnp.where((x_g >= 0) & (x_g < meta[3] * rows_x), 1.0, 0.0)
        add = mass_of(x + reach, x) * (inside_y * ok)
        rows = [out_g[c, i] for c in range(COMPS)]
        for c, load in ((0, VAPOR_SOURCE), (4, RECOIL_PUSH), (5, RECOIL_PRESSURE)):
            rows[c] = rows[c] + load * add
            out_g[c, i] = rows[c]
        j, q = divmod(i, per)
        acc = pack_heights(rows, GROUP * q, lane_s, low_z, acc)
        level = h[x + reach, skip : skip + small, LEVEL : LEVEL + 1]
        acc = jnp.where((lane_s & -2) == GROUP * q + LEVEL, level, acc)
        if q == per - 1 or i == count - 1:
            out_m[j] = acc
            acc = jnp.zeros((small, LANES), F32)


def last_kernel(
    cells, meta, beam, g, in_m, in_t, in_k, out_g, out_t, out_f, h, h1, f, fh, diff, total, p, mass, skin
):
    rows_x, own_y = cells
    for i in range(g.shape[1]):
        j, q = divmod(i, LANES // GROUP)
        unpack_heights(in_m[j], GROUP * q, meta[2] == 0, h, h1, i)

    def store(i, new):
        p[i - 2] = new[COMPS - 1]
        if len(new) == COMPS:
            for c in range(COMPS):
                out_g[c, i - 3] = new[c][1 : own_y + 1]

    advance(meta, g, h, h1, f, fh, diff, total, rows_x, own_y, store)
    fine = fine_pressure(meta, p, h, rows_x, own_y, mass.shape[0])
    cols = LANES // 4
    t = [in_t[d] for d in range(TOP)]
    k = [in_k[d] for d in range(TOP)]
    t = top_heat(meta, beam, SUBSTEPS, t, k, fine, 2 * rows_x, cols)
    for d in range(TOP):
        skin[:, d, :] = t[d]
    pack_skin(t, 0, cols, skin, out_t)
    pack_skin(t, SUBL, cols, skin, out_f)
    mass[...] = vapor_mass(t[0], fine)
    mass_of = mass_rows(meta, h, mass, own_y, own_y)
    for x in range(rows_x):
        add = mass_of(x + REACH_LAST, x)
        for c, load in ((0, VAPOR_SOURCE), (4, RECOIL_PUSH), (5, RECOIL_PRESSURE)):
            out_g[c, x] = out_g[c, x] + load * add


def call(body, outs, scratch=(), scalars=1, count=0):
    vmem = pl.BlockSpec(memory_space=pltpu.VMEM)
    smem = pl.BlockSpec(memory_space=pltpu.SMEM)
    return pl.pallas_call(
        body,
        out_shape=[jax.ShapeDtypeStruct(s, F32) for s in outs],
        in_specs=[smem] * scalars + [vmem] * count,
        out_specs=[vmem] * len(outs),
        scratch_shapes=[pltpu.VMEM(s, F32) for s in scratch],
        compiler_params=pltpu.CompilerParams(vmem_limit_bytes=32 * 1024 * 1024),
    )


def advance_scratch(n, size, count, bricks):
    row = (size, LANES)
    return ([(COMPS, n, *row)] if bricks else []) + [
        (n, *row),
        (n, *row),
        (COMPS, n - 2, *row),
        (n - 2, *row),
        (COMPS, n - 1, *row),
        (COMPS, n - 1, *row),
        (n - 4, count, LANES),
    ]


def pairs(count, odd):
    out = []
    for i in range(odd, count - 1, 2):
        out += [(i, i + 1), (i + 1, i)]
    return out


def cross(nx, nz, upper):
    out = []
    for i in range(nx - 1):
        a, b = i * nz + (nz - 1 if upper else 0), (i + 1) * nz + (0 if upper else nz - 1)
        out += [(a, b), (b, a)]
    return out


def shards(u, t, m, lev, beam):
    nx, ny, nz = (lax.axis_size(a) for a in ("gx", "gy", "gz"))
    gx, gy, gz = (lax.axis_index(a) for a in ("gx", "gy", "gz"))
    meta = jnp.stack([gx, gy, gz, nx, ny, nz]).astype(jnp.int32)
    _, rows_x, own_y, _ = u.shape
    t, m = jnp.transpose(t, (1, 2, 0)), jnp.transpose(m, (1, 2, 0))
    rows, cols, depth = t.shape
    tiles = own_y // SUBL
    block = (SUBL, LANES)
    n_top = 2 * rows * cols // LANES
    n_x = slab_size(tiles) + n_top
    n_z = 2 * SKIN * cols // SUBL + n_top + tiles
    msg_a, msg_b, msg_z, msg_d, msg_h, own = call(
        functools.partial(pack_kernel, (rows_x, REACH)),
        [(n_x, *block), (n_x, *block), (n_z, *block), (n_z, *block), (tiles, *block), (n_top, *block)],
        count=4,
    )(meta, u, t, m, lev)
    in_a = lax.ppermute(msg_a, "gx", pairs(nx, 0))
    in_b = lax.ppermute(msg_b, "gx", pairs(nx, 1))
    in_z = lax.ppermute(msg_z, "gz", pairs(nz, 0))
    in_d = lax.ppermute(msg_d, ("gx", "gz"), cross(nx, nz, True))
    in_h = lax.ppermute(msg_h, ("gx", "gz"), cross(nx, nz, False))
    wide = rows_x + 2 * REACH - 2
    n_y = wide * COMPS // 2 + rows_x + 2 + 3 + rows + 2 * SKIN + n_top
    msg_a, msg_b = call(
        functools.partial(relay_kernel, (rows_x, REACH)), [(n_y, *block), (n_y, *block)], count=9
    )(meta, u, t, m, own, in_a, in_b, in_z, in_d, in_h)
    gy_a = lax.ppermute(msg_a, "gy", pairs(ny, 0))
    gy_b = lax.ppermute(msg_b, "gy", pairs(ny, 1))

    size = own_y + 2 * SUBL
    n = rows_x + 2 * REACH
    n2 = rows_x + 2 * REACH_LAST
    small = own_y + SUBL
    part_rows = 4 * SUBL
    n_m = -(-n2 // (LANES // GROUP))
    g2, msg_m, top_t, top_k = call(
        functools.partial(first_kernel, (rows_x, REACH)),
        [(COMPS, n2, small, LANES), (n_m, small, LANES), (TOP, part_rows, LANES), (TOP, part_rows, LANES)],
        scratch=advance_scratch(n, size, own_y + 2 * (REACH - 2), True) + [(part_rows, LANES), (part_rows, *block)],
        scalars=2,
        count=9,
    )(meta, beam, u, own, in_a, in_b, in_z, in_d, in_h, gy_a, gy_b)
    in_m = lax.ppermute(msg_m, "gz", pairs(nz, 0))
    part = (rows + 2 * SKIN, cols + SUBL, depth)
    (bulk,) = call(
        bulk_kernel, [t.shape], scratch=[(2, *part), part, part, part, part], scalars=2, count=6
    )(meta, beam, t, m, in_z, in_d, gy_a, gy_b)
    gas, mine, other = call(
        functools.partial(last_kernel, (rows_x, own_y)),
        [u.shape, (n_top // 2, *block), (n_top // 2, *block)],
        scratch=advance_scratch(n2, small, own_y + 2 * (REACH_LAST - 2), False)
        + [(part_rows, LANES), (part_rows, *block)],
        scalars=2,
        count=4,
    )(meta, beam, g2, in_m, top_t, top_k)
    given = lax.ppermute(other, "gz", pairs(nz, 0))
    (out,) = call(seal_kernel, [t.shape], count=3)(meta, bulk, mine, given)
    return gas, jnp.transpose(out, (2, 0, 1))


def solution(mesh):
    return jax.shard_map(
        shards,
        mesh=mesh,
        in_specs=(
            P(None, "gx", "gy", "gz"),
            P(None, ("gx", "gz"), "gy"),
            P(None, ("gx", "gz"), "gy"),
            P("gx", "gy"),
            P(),
        ),
        out_specs=(P(None, "gx", "gy", "gz"), P(None, ("gx", "gz"), "gy")),
        check_vma=False,
    )
```

```python
import functools

import jax
import jax.numpy as jnp
from jax import lax
from jax.experimental import pallas as pl
from jax.experimental.pallas import tpu as pltpu
from jax.sharding import PartitionSpec as P

STEPS = 2
SUBSTEPS = 2
GAS_STEP = 0.3
DRIFT_SPEED = 0.5
VAPOR_LOAD = 0.3
AMBIENT_LOAD = 0.7
STIFFNESS = 1.0
VISCOSITY = (0.2, 0.1, 0.15, 0.15, 0.15, 0.2)
HEAT_STEP = 1.0
POWDER_COND = 0.04
SOLID_COND = 0.15
LIQUID_COND = 0.09
LASER_POWER = 3.0
SPOT_RADIUS = 6.0
ABSORB_DEPTH = 4.0
BOIL_LEVEL = 1.0
BACK_PRESSURE = 0.5
LATENT_HEAT = 0.3
VAPOR_SOURCE = 0.5
RECOIL_PUSH = 0.4
RECOIL_PRESSURE = 0.6

COMPS = 6
LANES = 128
VMEM_LIMIT = 32 * 1024 * 1024
SUBL = 8
F32 = jnp.float32
REACH = 6
REACH_LAST = 3
SKIN = 4
TOP = 8
GROUP = 16
LEVEL = 2 * COMPS


def iota(shape, axis):
    return lax.broadcasted_iota(jnp.int32, shape, axis)


def wrapped(index, own, size):
    return jnp.where(index < own + (size - own) // 2, index, index - size)


def turn(value, amount, axis):
    size = value.shape[axis]
    if isinstance(amount, int):
        amount = amount % size
        if amount == 0:
            return value
    return pltpu.roll(value, amount, axis)


def softplus(x):
    return jnp.maximum(x, 0.0) + jnp.log1p(jnp.exp(-jnp.abs(x)))


def pack_heights(rows, base, lane, low_z, acc):
    more = jnp.where(low_z, 2, 0)
    for c, row in enumerate(rows):
        acc = jnp.where((lane & -2) == base + 2 * c, turn(row, base + 2 * c + more, 1), acc)
    return acc


def unpack_heights(packed, base, low_z, h0, h1, i):
    here = turn(packed, -base, 1)
    other = turn(packed, -base - 1, 1)
    h0[i] = jnp.where(low_z, here, other)
    h1[i] = jnp.where(low_z, other, here)


DEEP_5 = (2, 3, 4, 5)
DEEP_6 = (2, 5)
FULL = 4
QUARTERS = (5, 3, 2, 4)


def slab_index(c, layer, tile, tiles):
    if layer <= FULL:
        return (c * FULL + layer - 1) * tiles + tile
    base = COMPS * FULL * tiles
    if layer == FULL + 1:
        return base + DEEP_5.index(c) * tiles + tile if c in DEEP_5 else None
    base += len(DEEP_5) * tiles
    return base + DEEP_6.index(c) * tiles + tile if c in DEEP_6 else None


def slab_size(tiles):
    return (COMPS * FULL + len(DEEP_5) + len(DEEP_6)) * tiles


def row_tile(c, x, tile, u, in_a, in_b, even_x):
    rows_x, tiles = u.shape[1], u.shape[2] // SUBL
    if 0 <= x < rows_x:
        return u[c, x, tile * SUBL : (tile + 1) * SUBL, :]
    k = slab_index(c, -x if x < 0 else x - rows_x + 1, tile, tiles)
    if k is None:
        return None
    low, high = (in_b[k], in_a[k]) if x < 0 else (in_a[k], in_b[k])
    return jnp.where(even_x, low, high)


def conduct(v):
    return jnp.where(v == 0, POWDER_COND, jnp.where(v == 1, SOLID_COND, LIQUID_COND)).astype(F32)


def surface_tops(t, m):
    rows, cols = t.shape[0], t.shape[1]
    per = LANES // cols
    out = []
    for ref in (t, m):
        for j in range(rows // per):
            block = ref[j * per : (j + 1) * per].reshape(LANES, LANES)
            out.append(jnp.transpose(conduct(block) if ref is m else block)[:TOP])
    return out


def gas_kernel(cells, meta, u_in, t_in, m_in, out_a, out_b, u, t, m, sems):
    copies = [
        pltpu.make_async_copy(src, dst, sems.at[i]) for i, (src, dst) in enumerate(((t_in, t), (m_in, m), (u_in, u)))
    ]
    for copy in copies:
        copy.start()
    rows_x, reach = cells
    even = lax.rem(meta[0], 2) == 0
    tiles = u.shape[2] // SUBL
    copies[0].wait()
    copies[1].wait()
    for j, top in enumerate(surface_tops(t, m)):
        out_a[slab_size(tiles) + j] = top
        out_b[slab_size(tiles) + j] = top
    copies[2].wait()
    for c in range(COMPS):
        for layer in range(1, reach + 1):
            for y in range(tiles):
                n = slab_index(c, layer, y, tiles)
                if n is None:
                    continue
                lo = u[c, layer - 1, y * SUBL : (y + 1) * SUBL, :]
                hi = u[c, rows_x - layer, y * SUBL : (y + 1) * SUBL, :]
                out_a[n] = jnp.where(even, hi, lo)
                out_b[n] = jnp.where(even, lo, hi)


def pack_kernel(meta, u, t, m, lev, out_h, out_z, out_d, own):
    low_z = meta[2] == 0
    rows_x = u.shape[1]
    tiles = u.shape[2] // SUBL
    rows, cols = t.shape[0], t.shape[1]
    col_tiles = cols // SUBL
    n = 0
    for source in (lambda v: v, conduct):
        ref = t if n == 0 else m
        for r in range(SKIN):
            for y in range(col_tiles):
                lo = source(ref[r, y * SUBL : (y + 1) * SUBL, :])
                hi = source(ref[rows - SKIN + r, y * SUBL : (y + 1) * SUBL, :])
                out_z[n] = jnp.where(low_z, hi, lo)
                out_d[n] = jnp.where(low_z, lo, hi)
                n += 1
    tops = surface_tops(t, m)
    for j, top in enumerate(tops):
        own[j] = top
        out_z[n + j] = top
        out_d[n + j] = top
    n += len(tops)
    size = u.shape[2]
    lane = iota((size, LANES), 1)
    eye = iota((size, size), 0) == iota((size, size), 1)
    levels = lev[...].astype(F32)
    acc = jnp.zeros((size, LANES), F32)
    for x in range(rows_x):
        acc = pack_heights([u[c, x] for c in range(COMPS)], x * GROUP, lane, low_z, acc)
        level = jnp.sum(jnp.where(eye, levels[x : x + 1, :], 0.0), axis=1, keepdims=True)
        acc = jnp.where((lane & -2) == x * GROUP + LEVEL, level, acc)
    for y in range(tiles):
        part = acc[y * SUBL : (y + 1) * SUBL]
        out_h[y] = part
        out_z[n + y] = part
        out_d[n + y] = part


def part_row(r, tile, ref, at, rows, in_z, in_d, low_z, col_tiles, low_part):
    if 0 <= r < rows:
        value = ref[r, tile * SUBL : (tile + 1) * SUBL, :]
        return conduct(value) if at else value
    k = (at * SKIN + (r + SKIN if r < 0 else r - rows)) * col_tiles + tile
    low, high = (in_d[k], in_z[k]) if r < 0 else (in_z[k], in_d[k])
    return jnp.where(low_z, low, high)


def relay_kernel(cells, meta, u, t, m, own, in_a, in_b, in_z, in_d, in_h, out_a, out_b):
    rows_x, reach = cells
    gx, gy, gz = meta[0], meta[1], meta[2]
    even_x = lax.rem(gx, 2) == 0
    even_y = lax.rem(gy, 2) == 0
    low_z = gz == 0
    tiles = u.shape[2] // SUBL
    rows, cols = t.shape[0], t.shape[1]
    col_tiles = cols // SUBL
    half = SUBL // 2
    sub = iota((SUBL, LANES), 0)
    lane = iota((SUBL, LANES), 1)
    zero = jnp.zeros((SUBL, LANES), F32)

    def put(n, hi, lo):
        out_a[n] = jnp.where(even_y, hi, lo)
        out_b[n] = jnp.where(even_y, lo, hi)

    def both(c, x):
        pair = [row_tile(c, x, y, u, in_a, in_b, even_x) for y in (tiles - 1, 0)]
        return [zero if v is None else v for v in pair]

    n = 0
    for x in range(1 - reach, rows_x + reach - 1):
        for c in range(0, COMPS, 2):
            (hi0, lo0), (hi1, lo1) = both(c, x), both(c + 1, x)
            put(n, jnp.where(sub < half, turn(hi1, half, 0), hi0), jnp.where(sub < half, lo0, turn(lo1, half, 0)))
            n += 1
    for x in range(-1, rows_x + 1):
        hi = lo = zero
        for q, c in enumerate(QUARTERS):
            a, b = both(c, x)
            hi = jnp.where((sub & -2) == 2 * q, turn(a, 2 * q - 2, 0), hi)
            lo = jnp.where((sub & -2) == 2 * q, turn(b, 2 * q - half, 0), lo)
        put(n, hi, lo)
        n += 1
    base = in_z.shape[0] - tiles
    hi_y, lo_y = tiles - 1, 0
    put(
        n,
        jnp.where(low_z, in_d[base + hi_y], in_h[hi_y]),
        jnp.where(low_z, in_d[base + lo_y], in_h[lo_y]),
    )
    put(n + 1, in_z[base + hi_y], in_z[base + lo_y])
    put(
        n + 2,
        jnp.where(low_z, in_h[hi_y], in_d[base + hi_y]),
        jnp.where(low_z, in_h[lo_y], in_d[base + lo_y]),
    )
    n += 3
    for r in range(-SKIN, rows + SKIN):
        hi_t, lo_t = [part_row(r, y, t, 0, rows, in_z, in_d, low_z, col_tiles, None) for y in (col_tiles - 1, 0)]
        hi_k, lo_k = [part_row(r, y, m, 1, rows, in_z, in_d, low_z, col_tiles, None) for y in (col_tiles - 1, 0)]
        put(n, jnp.where(sub < half, turn(hi_k, half, 0), hi_t), jnp.where(sub < half, lo_t, turn(lo_k, half, 0)))
        n += 1
    sources = surface_sources(own, in_a, in_b, in_z, in_d, even_x, tiles)
    per = LANES // cols
    slot = lax.rem(lane, cols) // SUBL
    for v in range(len(sources) // per):
        hi = lo = zero
        for i in range(per):
            src = sources[v * per + i]
            hi = jnp.where(slot == i, turn(src, SUBL * i - (cols - SUBL), 1), hi)
            lo = jnp.where(slot == i, turn(src, SUBL * i, 1), lo)
        put(n + v, hi, lo)


def surface_sources(own, in_a, in_b, in_z, in_d, even_x, tiles):
    count = own.shape[0]
    tail = in_a.shape[0] - count
    at = in_z.shape[0] - tiles - count
    out = []
    for a in range(2):
        span = range(a * count // 2, (a + 1) * count // 2)
        out += [own[j] for j in span]
        out += [in_z[at + j] for j in span]
        out += [jnp.where(even_x, in_a[tail + j], in_b[tail + j]) for j in span]
        out += [in_d[at + j] for j in span]
    return out


def heat_source(row, col, beam, step):
    a = beam[step, 0].astype(F32)
    b = beam[step, 1].astype(F32)
    along_x = jnp.exp(-(((row - a) / SPOT_RADIUS) ** 2))
    along_y = jnp.exp(-(((col - b) / SPOT_RADIUS) ** 2))
    return LASER_POWER * along_x * along_y


def bulk_kernel(meta, beam, t, m, in_z, in_d, gy_a, gy_b, out, temp, cond, kx, ky, kz):
    gx, gy, gz = meta[0], meta[1], meta[2]
    even_y = lax.rem(gy, 2) == 0
    low_z = gz == 0
    rows, cols, depth = t.shape
    col_tiles = cols // SUBL
    half = SUBL // 2
    size = cols + SUBL
    n = rows + 2 * SKIN
    sub = iota((SUBL, LANES), 0)
    base = gy_a.shape[0] - 4 - n
    for i in range(n):
        for y in range(col_tiles):
            span = slice(y * SUBL, (y + 1) * SUBL)
            temp[0, i, span, :] = part_row(i - SKIN, y, t, 0, rows, in_z, in_d, low_z, col_tiles, None)
            cond[i, span, :] = part_row(i - SKIN, y, m, 1, rows, in_z, in_d, low_z, col_tiles, None)
        up = jnp.where(even_y, gy_a[base + i], gy_b[base + i])
        low = jnp.where(even_y, gy_b[base + i], gy_a[base + i])
        temp[0, i, cols:size, :] = jnp.where(sub < half, up, low)
        cond[i, cols:size, :] = turn(jnp.where(sub < half, low, up), half, 0)

    lane = iota((size, LANES), 1)
    for i in range(n):
        k = cond[i]
        if i + 1 < n:
            kx[i] = 0.5 * (k + cond[i + 1])
        ky[i] = 0.5 * (k + turn(k, -1, 0))
        kz[i] = 0.5 * (k + jnp.where(lane == depth - 1, 0.0, turn(k, -1, 1)))

    col_g = gy * cols + wrapped(iota((size, LANES), 0), cols, size)
    inside_y = jnp.where((col_g >= 0) & (col_g < meta[4] * cols), 1.0, 0.0)
    col_f = col_g.astype(F32)
    fall = jnp.exp(-lane.astype(F32) / ABSORB_DEPTH)
    first_row = (gx * meta[5] + gz) * rows - SKIN

    for s in range(STEPS * SUBSTEPS):
        src, dst = s % 2, 1 - s % 2
        last = s == STEPS * SUBSTEPS - 1
        a = beam[s, 0].astype(F32)
        b = beam[s, 1].astype(F32)
        spot = LASER_POWER * fall * jnp.exp(-(((col_f - b) / SPOT_RADIUS) ** 2))
        lo, hi = s + 1, n - 1 - s
        fx0 = kx[lo - 1] * (temp[src, lo] - temp[src, lo - 1])
        for i in range(lo, hi):
            v = temp[src, i]
            fx = kx[i] * (temp[src, i + 1] - v)
            fy = ky[i] * (turn(v, -1, 0) - v)
            fz = kz[i] * (jnp.where(lane == depth - 1, 0.0, turn(v, -1, 1)) - v)
            above = jnp.where(lane == 0, 0.5 * cond[i] * v, turn(fz, 1, 1))
            row = first_row + i
            along_x = jnp.exp(-((jnp.full((1, LANES), row.astype(F32) - a) / SPOT_RADIUS) ** 2))
            change = (fx - fx0) + (fy - turn(fy, 1, 0)) + (fz - above) + spot * along_x
            new = v + HEAT_STEP * change
            if last:
                out[i - SKIN] = new[:cols]
            else:
                ok = (row >= 0) & (row < meta[3] * meta[5] * rows)
                temp[dst, i] = new * (inside_y * jnp.where(ok, 1.0, 0.0))
            fx0 = fx


def seal_kernel(meta, bulk, mine, given, out):
    rows, cols, depth = bulk.shape
    per = LANES // cols
    lane = iota((LANES, LANES), 1)
    for j in range(mine.shape[0]):
        skin = jnp.where(meta[2] == 0, mine[j], given[j])
        skin = jnp.concatenate([skin, jnp.zeros((LANES - SUBL, LANES), F32)], axis=0)
        block = jnp.where(lane < SKIN, jnp.transpose(skin), bulk[j * per : (j + 1) * per].reshape(LANES, LANES))
        out[j * per : (j + 1) * per] = block.reshape(per, cols, LANES)


def pack_skin(t, rows, cols, scratch, out):
    per = LANES // cols
    lane = iota((SUBL, LANES), 1)
    for j in range(SUBL // per):
        acc = jnp.zeros((SUBL, LANES), F32)
        for q in range(per):
            acc = jnp.where(lane // cols == q, turn(scratch[rows + j * per + q], cols * q, 1), acc)
        out[j] = acc


def split(value):
    high = value.astype(jnp.bfloat16)
    rest = (value - high.astype(F32)).astype(jnp.bfloat16)
    return jnp.concatenate([high, rest], axis=1)


def height_matrix():
    shape = (2 * LANES, 2 * LANES)
    k = iota(shape, 0) & (LANES - 1)
    j = iota(shape, 1)
    above = jnp.where(k == (j & (LANES - 1)) + 1, 1.0, 0.0)
    below = jnp.where(k == (j & (LANES - 1)) - 1, 1.0, 0.0)
    return (above + jnp.where(j < LANES, -below, below)).astype(jnp.bfloat16)


def height_terms(ref, first, last, matrix, diff, total):
    size = ref.shape[2]
    for c in range(COMPS):
        rows = ref[c, first:last].reshape((last - first) * size, LANES)
        both = jnp.dot(split(rows), matrix, preferred_element_type=F32)
        diff[c, first:last] = both[:, :LANES].reshape(last - first, size, LANES)
        total[c, first:last] = both[:, LANES:].reshape(last - first, size, LANES)


def cut_weights(size, low_z):
    lane = iota((size, LANES), 1)
    up = (lane == LANES - 1) & low_z
    down = (lane == 0) & jnp.logical_not(low_z)
    sign = jnp.where(up, 1.0, jnp.where(down, -1.0, 0.0))
    return sign, jnp.abs(sign)


def stepped(comps, ref, i, diff, total, h, cut, scale, start, size):
    sign, mark = cut
    half = 0.5 * scale * GAS_STEP
    span = pl.ds(start, size)

    def dx(c):
        return ref[c, i + 1, span, :] - ref[c, i - 1, span, :]

    def dy(c):
        return ref[c, i, pl.ds(start + 1, size), :] - ref[c, i, pl.ds(start - 1, size), :]

    def dz(c):
        return diff[c, i, span, :] + sign * h[i, span, 2 * c : 2 * c + 1]

    spread = half * (dx(2) + dy(3) + dz(4))
    out = {}
    for c in comps:
        v = VISCOSITY[c]
        side = scale * GAS_STEP * v
        drift = 0.5 * DRIFT_SPEED * scale * GAS_STEP
        sides = (ref[c, i + 1, span, :] + ref[c, i - 1, span, :]) + (
            ref[c, i, pl.ds(start + 1, size), :] + ref[c, i, pl.ds(start - 1, size), :]
        )
        across = h[i, span, 2 * c : 2 * c + 1]
        new = (
            scale * (1.0 - 6.0 * GAS_STEP * v) * ref[c, i, span, :]
            + side * (sides + total[c, i, span, :])
            - drift * diff[c, i, span, :]
            + (side * mark - drift * sign) * across
        )
        if c == 2:
            new = new - half * dx(5)
        elif c == 3:
            new = new - half * dy(5)
        elif c == 4:
            new = new - half * dz(5)
        else:
            new = new - {0: VAPOR_LOAD, 1: AMBIENT_LOAD, 5: STIFFNESS}[c] * spread
        out[c] = new
    return out


def by_comp(lane, values):
    out = jnp.full(lane.shape, values[-1], F32)
    for c, v in enumerate(values[:-1]):
        out = jnp.where(lane == 2 * c, v, out)
    return out


def couple_matrix():
    shape = (6 * LANES, LANES)
    k = iota(shape, 0)
    j = iota(shape, 1)
    axis = k // (2 * LANES)
    lane = k & (LANES - 1)
    spread = (lane == 4 + 2 * axis) & ((j == 0) | (j == 2) | (j == 10))
    slope = (lane == 10) & (j == 4 + 2 * axis)
    return jnp.where(spread | slope, 1.0, 0.0).astype(jnp.bfloat16)


def halo_stepped(h0, h1, g, low_z, mask_of, out):
    n, size = h0.shape[0], h0.shape[1]
    rows = (n - 2) * size
    lane = iota((1, LANES), 1)
    more = jnp.where(low_z, 1, 0)
    flat_lane = iota((rows, LANES), 1)
    touch = jnp.zeros((rows, LANES), F32)
    for c in range(COMPS):
        own = g[c, 1 : n - 1].reshape(rows, LANES)
        touch = jnp.where(flat_lane == 2 * c, turn(own, 2 * c + more, 1), touch)
    mid = h0[1 : n - 1].reshape(rows, LANES)
    east = h0[2:n].reshape(rows, LANES)
    west = h0[0 : n - 2].reshape(rows, LANES)
    north = turn(mid, -1, 0)
    south = turn(mid, 1, 0)
    behind = h1[1 : n - 1].reshape(rows, LANES)
    slopes = [east - west, north - south, jnp.where(low_z, 1.0, -1.0) * (behind - touch)]
    coupled = jnp.dot(
        jnp.concatenate([split(v) for v in slopes], axis=1), couple_matrix(), preferred_element_type=F32
    )
    up = by_comp(lane, [GAS_STEP * (v - 0.5 * DRIFT_SPEED) for v in VISCOSITY])
    down = by_comp(lane, [GAS_STEP * (v + 0.5 * DRIFT_SPEED) for v in VISCOSITY])
    half = 0.5 * GAS_STEP
    pull = by_comp(lane, [-half * VAPOR_LOAD, -half * AMBIENT_LOAD, -half, -half, -half, -half * STIFFNESS])
    new = (
        by_comp(lane, [1.0 - 6.0 * GAS_STEP * v for v in VISCOSITY]) * mid
        + by_comp(lane, [GAS_STEP * v for v in VISCOSITY]) * ((east + west) + (north + south))
        + jnp.where(low_z, up, down) * behind
        + jnp.where(low_z, down, up) * touch
        + pull * coupled
    )
    for i in range(1, n - 1):
        out[i - 1] = turn(new[(i - 1) * size : i * size] * mask_of(i, 0, size), -1, 0)


def advance(meta, g, h0, h1, f, fh, diff, total, own_x, own_y, store):
    n, size = g.shape[1], g.shape[2]
    gx, gy, gz = meta[0], meta[1], meta[2]
    low_z = gz == 0
    before = (n - own_x) // 2
    before_y = (size - own_y) // 2
    reach = before - 2

    def mask_of(i, start, count):
        x_g = gx * own_x + i - before
        ok = (x_g >= 0) & (x_g < meta[3] * own_x)
        y_g = gy * own_y + iota((count, LANES), 0) + start - before_y
        return jnp.where((y_g >= 0) & (y_g < meta[4] * own_y) & ok, 1.0, 0.0)

    matrix = height_matrix()
    halo_stepped(h0, h1, g, low_z, mask_of, fh)
    height_terms(g, 1, n - 1, matrix, diff, total)
    everything = tuple(range(COMPS))

    def one(comps):
        def body(i, carry):
            count = size - 2
            new = stepped(comps, g, i, diff, total, h0, cut_weights(count, low_z), 1.0, 1, count)
            m = mask_of(i, 1, count)
            for c in comps:
                f[c, i - 1, :count, :] = new[c] * m
            return carry

        return body

    lax.fori_loop(2, n - 2, one(everything), 0, unroll=2)
    for i in (1, n - 2):
        one((2, 5))(i, 0)

    height_terms(f, 1, n - 3, matrix, diff, total)
    start = before_y - 1 - reach
    count = own_y + 2 * reach

    def two(comps):
        def body(i, carry):
            cut = cut_weights(count, low_z)
            new = stepped(comps, f, i - 1, diff, total, fh, cut, 0.5, start, count)
            m = mask_of(i, start + 1, count)
            for c in comps:
                new[c] = (0.5 * g[c, i, pl.ds(start + 1, count), :] + new[c]) * m
            store(i, new)
            return carry

        return body

    lax.fori_loop(3, n - 3, two(everything), 0, unroll=2)
    for i in (2, n - 3):
        two((5,))(i, 0)


def lane_sums(value):
    high = value.astype(jnp.bfloat16)
    rest = value - high.astype(F32)
    middle = rest.astype(jnp.bfloat16)
    low = (rest - middle.astype(F32)).astype(jnp.bfloat16)
    parts = jnp.concatenate([high, middle, low], axis=1)
    ones = jnp.ones((3 * LANES, LANES), jnp.bfloat16)
    return jnp.dot(parts, ones, preferred_element_type=F32)


def fine_pressure(meta, p, h0, own_x, own_y, part_rows):
    n, count = p.shape[0], p.shape[1]
    skip = (h0.shape[1] - count) // 2
    skip_x = (h0.shape[0] - n) // 2
    before = (n - own_x) // 2
    y_l = iota((count, LANES), 0) - (count - own_y) // 2
    col_y = lax.div(wrapped(iota((count, LANES), 1), 2 * own_y, LANES) + LANES, 2) - LANES // 2
    pick = col_y == y_l
    row_x = lax.div(wrapped(iota((part_rows, LANES), 0), 2 * own_x, part_rows) + LANES, 2) - LANES // 2
    height = (iota((count, LANES), 1) + meta[2] * LANES).astype(F32)
    fine = jnp.zeros((part_rows, LANES), F32)
    full = -(-count // SUBL) * SUBL
    pad = [jnp.zeros((full - count, LANES), F32)] if full > count else []
    found = []
    for i in range(n):
        level = h0[i + skip_x, skip : skip + count, LEVEL : LEVEL + 1]
        found += [jnp.where(height == level, p[i], 0.0)] + pad
    at = lane_sums(jnp.concatenate(found, axis=0))
    for i in range(n):
        line = jnp.sum(jnp.where(pick, at[i * full : i * full + count], 0.0), axis=0, keepdims=True)
        fine = jnp.where(row_x == i - before, line, fine)
    return fine


def top_heat(meta, beam, first, t, k, fine, own_rows, cols):
    gx, gy = meta[0], meta[1]
    shape = fine.shape
    row = gx * own_rows + wrapped(iota(shape, 0), own_rows, shape[0])
    col = gy * cols + wrapped(iota(shape, 1), cols, shape[1])
    row, col = row.astype(F32), col.astype(F32)
    deep = TOP - 1 - first
    kx = [0.5 * (v + turn(v, -1, 0)) for v in k[:deep]]
    ky = [0.5 * (v + turn(v, -1, 1)) for v in k[:deep]]
    kz = [0.5 * (k[d] + k[d + 1]) for d in range(deep)]
    for s in range(SUBSTEPS):
        beam_xy = heat_source(row, col, beam, first + s)
        before = 0.5 * k[0] * t[0]
        new = []
        for d in range(TOP - 1 - first - s):
            fx = kx[d] * (turn(t[d], -1, 0) - t[d])
            fy = ky[d] * (turn(t[d], -1, 1) - t[d])
            fz = kz[d] * (t[d + 1] - t[d])
            factor = jnp.exp(jnp.full(shape, -d / ABSORB_DEPTH, F32))
            change = (fx - turn(fx, 1, 0)) + (fy - turn(fy, 1, 1)) + (fz - before) + beam_xy * factor
            if d == 0:
                change = change - LATENT_HEAT * softplus(t[0] - BOIL_LEVEL - BACK_PRESSURE * fine)
            new.append(jnp.where(k[d] > 0, t[d] + HEAT_STEP * change, 0.0))
            before = fz
        t = new
    return t


def vapor_mass(t0, fine):
    four = t0 + turn(t0, -1, 1)
    four = four + turn(four, -1, 0)
    return softplus(0.25 * four - BOIL_LEVEL - BACK_PRESSURE * fine)


def mass_rows(meta, h, mass, first, rows, count, own_y):
    skip = (h.shape[1] - count) // 2
    skip_x = (h.shape[0] - rows) // 2
    y_l = iota((count, LANES), 0) - (count - own_y) // 2
    col = wrapped(iota((count, LANES), 1), 2 * own_y, LANES)
    pick = col == 2 * y_l
    height = (iota((count, LANES), 1) + meta[2] * LANES).astype(F32)
    found = []
    for i in range(rows):
        r = (2 * (i + first)) % mass.shape[0]
        found.append(jnp.where(pick, mass[r : r + 1, :], 0.0))
    at = lane_sums(jnp.concatenate(found, axis=0))
    out = []
    for i in range(rows):
        level = h[i + skip_x, skip : skip + count, LEVEL : LEVEL + 1]
        out.append(jnp.where(height == level, at[i * count : (i + 1) * count], 0.0))
    return out


def first_kernel(
    cells, meta, beam, u, own, in_a, in_b, in_z, in_d, in_h, gy_a, gy_b,
    out_g, out_m, out_t, out_k, g, h, h1, f, fh, diff, total, p, mass, skin,
):
    rows_x, reach = cells
    gx, gy, gz = meta[0], meta[1], meta[2]
    even_x = lax.rem(gx, 2) == 0
    even_y = lax.rem(gy, 2) == 0
    low_z = gz == 0
    own_y = u.shape[2]
    tiles = own_y // SUBL
    size = own_y + 2 * SUBL
    half = SUBL // 2
    sub = iota((SUBL, LANES), 0)
    zero = jnp.zeros((SUBL, LANES), F32)

    def side(k):
        upper = jnp.where(even_y, gy_a[k], gy_b[k])
        lower = jnp.where(even_y, gy_b[k], gy_a[k])
        return upper, lower

    wide = rows_x + 2 * reach - 2
    outer = wide * COMPS // 2
    for x in range(-reach, rows_x + reach):
        i = x + reach
        for c in range(COMPS):
            for y in range(tiles):
                value = row_tile(c, x, y, u, in_a, in_b, even_x)
                g[c, i, (y + 1) * SUBL : (y + 2) * SUBL, :] = zero if value is None else value
            upper = lower = zero
            if 0 < i < wide + 1:
                upper, lower = side((i - 1) * COMPS // 2 + c // 2)
                if c % 2:
                    upper, lower = turn(upper, half, 0), turn(lower, half, 0)
            if -1 <= x < rows_x + 1 and c in QUARTERS:
                q = QUARTERS.index(c)
                far_up, far_low = side(outer + x + 1)
                far_up, far_low = turn(far_up, half - 2 * q, 0), turn(far_low, 2 - 2 * q, 0)
            else:
                far_up = far_low = zero
            g[c, i, own_y + SUBL : size, :] = jnp.where(sub < half, upper, jnp.where(sub < half + 2, far_up, 0.0))
            g[c, i, :SUBL, :] = jnp.where(sub >= half, lower, jnp.where(sub >= half - 2, far_low, 0.0))
    base = in_z.shape[0] - tiles
    packed = []
    for b in range(3):
        parts = []
        for y in range(tiles):
            if b == 0:
                parts.append(jnp.where(low_z, in_d[base + y], in_h[y]))
            elif b == 1:
                parts.append(in_z[base + y])
            else:
                parts.append(jnp.where(low_z, in_h[y], in_d[base + y]))
        upper, lower = side(outer + rows_x + 2 + b)
        packed.append(jnp.concatenate([lower, *parts, upper], axis=0))
    for x in range(-reach, rows_x + reach):
        b, q = divmod(x + rows_x, rows_x)
        unpack_heights(packed[b], GROUP * q, low_z, h, h1, x + reach)

    def store(i, new):
        p[i - 2] = new[COMPS - 1]
        if len(new) == COMPS:
            for c in range(COMPS):
                out_g[c, i - 3] = new[c]

    advance(meta, g, h, h1, f, fh, diff, total, rows_x, own_y, store)
    fine = fine_pressure(meta, p, h, rows_x, own_y, mass.shape[0])

    cols = LANES // 4
    per = LANES // cols
    lane = iota((SUBL, LANES), 1)
    sources = surface_sources(own, in_a, in_b, in_z, in_d, even_x, tiles)
    count = len(sources) // 2
    top_at = gy_a.shape[0] - len(sources) // per
    layers = []
    for a in range(2):
        for s in range(count):
            src = sources[a * count + s]
            upper, lower = side(top_at + (a * count + s) // per)
            i = s % per
            for q in range(per):
                at = cols * q + SUBL * i
                skin[s * per + q] = jnp.where(
                    lane < cols,
                    turn(src, -cols * q, 1),
                    jnp.where(
                        lane < cols + SUBL,
                        turn(upper, cols - at, 1),
                        jnp.where(lane >= LANES - SUBL, turn(lower, LANES - SUBL - at, 1), 0.0),
                    ),
                )
        for d in range(TOP):
            layers.append(skin[:, d, :])
    t, k = layers[:TOP], layers[TOP:]
    t = top_heat(meta, beam, 0, t, k, fine, 2 * rows_x, cols)
    for d in range(TOP - SUBSTEPS):
        out_t[d] = t[d]
        out_k[d] = k[d]
    mass[...] = vapor_mass(t[0], fine)

    count, small = out_g.shape[1], out_g.shape[2]
    masses = mass_rows(meta, h, mass, -REACH_LAST, count, small, own_y)
    lane_s = iota((small, LANES), 1)
    y_g = gy * own_y + iota((small, LANES), 0) - (small - own_y) // 2
    inside_y = jnp.where((y_g >= 0) & (y_g < meta[4] * own_y), 1.0, 0.0)
    skip = (size - small) // 2
    per = LANES // GROUP
    acc = jnp.zeros((small, LANES), F32)
    for i in range(count):
        x = i - REACH_LAST
        x_g = gx * rows_x + x
        ok = jnp.where((x_g >= 0) & (x_g < meta[3] * rows_x), 1.0, 0.0)
        add = masses[i] * (inside_y * ok)
        rows = [out_g[c, i] for c in range(COMPS)]
        for c, load in ((0, VAPOR_SOURCE), (4, RECOIL_PUSH), (5, RECOIL_PRESSURE)):
            rows[c] = rows[c] + load * add
            out_g[c, i] = rows[c]
        j, q = divmod(i, per)
        acc = pack_heights(rows, GROUP * q, lane_s, low_z, acc)
        level = h[x + reach, skip : skip + small, LEVEL : LEVEL + 1]
        acc = jnp.where((lane_s & -2) == GROUP * q + LEVEL, level, acc)
        if q == per - 1 or i == count - 1:
            out_m[j] = acc
            acc = jnp.zeros((small, LANES), F32)


def last_kernel(
    cells, meta, beam, g, in_m, in_t, in_k, bulk, out_g, out_t, out_f, mass, h, h1, f, fh, diff, total, p, skin
):
    rows_x, own_y = cells
    for i in range(g.shape[1]):
        j, q = divmod(i, LANES // GROUP)
        unpack_heights(in_m[j], GROUP * q, meta[2] == 0, h, h1, i)

    def store(i, new):
        p[i - 2] = new[COMPS - 1]
        if len(new) == COMPS:
            for c in range(COMPS):
                out_g[c, i - 3] = new[c][1 : own_y + 1]

    advance(meta, g, h, h1, f, fh, diff, total, rows_x, own_y, store)
    fine = fine_pressure(meta, p, h, rows_x, own_y, mass.shape[0])
    cols = LANES // 4
    t = [in_t[d] for d in range(TOP - SUBSTEPS)]
    k = [in_k[d] for d in range(TOP - SUBSTEPS)]
    t = top_heat(meta, beam, SUBSTEPS, t, k, fine, 2 * rows_x, cols)
    skin[...] = jnp.zeros_like(skin)
    for d in range(SKIN):
        skin[:, d, :] = t[d]
    pack_skin(t, 0, cols, skin, out_t)
    pack_skin(t, SUBL, cols, skin, out_f)
    mass[...] = vapor_mass(t[0], fine)


def mass_kernel(meta, gas, in_m, mass, out_g, h, h1):
    rows_x, own_y = gas.shape[1], gas.shape[2]
    n = h.shape[0]
    for i in range((n - rows_x) // 2, (n + rows_x) // 2):
        j, q = divmod(i, LANES // GROUP)
        unpack_heights(in_m[j], GROUP * q, meta[2] == 0, h, h1, i)
    masses = mass_rows(meta, h, mass, 0, rows_x, own_y, own_y)
    loads = {0: VAPOR_SOURCE, 4: RECOIL_PUSH, 5: RECOIL_PRESSURE}
    for x in range(rows_x):
        for c in range(COMPS):
            out_g[c, x] = gas[c, x] + loads[c] * masses[x] if c in loads else gas[c, x]


def call(body, outs, scratch=(), scalars=1, count=0):
    vmem = pl.BlockSpec(memory_space=pltpu.VMEM)
    smem = pl.BlockSpec(memory_space=pltpu.SMEM)
    return pl.pallas_call(
        body,
        out_shape=[jax.ShapeDtypeStruct(s, F32) for s in outs],
        in_specs=[smem] * scalars + [vmem] * count,
        out_specs=[vmem] * len(outs),
        scratch_shapes=[pltpu.VMEM(s, F32) for s in scratch],
        compiler_params=pltpu.CompilerParams(vmem_limit_bytes=VMEM_LIMIT),
    )


def advance_scratch(n, size, count, bricks):
    row = (size, LANES)
    return ([(COMPS, n, *row)] if bricks else []) + [
        (n, *row),
        (n, *row),
        (COMPS, n - 2, *row),
        (n - 2, *row),
        (COMPS, n - 1, *row),
        (COMPS, n - 1, *row),
        (n - 4, count, LANES),
    ]


def pairs(count, odd):
    out = []
    for i in range(odd, count - 1, 2):
        out += [(i, i + 1), (i + 1, i)]
    return out


def cross(nx, nz, upper):
    out = []
    for i in range(nx - 1):
        a, b = i * nz + (nz - 1 if upper else 0), (i + 1) * nz + (0 if upper else nz - 1)
        out += [(a, b), (b, a)]
    return out


def shards(u, t, m, lev, beam):
    nx, ny, nz = (lax.axis_size(a) for a in ("gx", "gy", "gz"))
    gx, gy, gz = (lax.axis_index(a) for a in ("gx", "gy", "gz"))
    meta = jnp.stack([gx, gy, gz, nx, ny, nz]).astype(jnp.int32)
    _, rows_x, own_y, _ = u.shape
    t, m = jnp.transpose(t, (1, 2, 0)), jnp.transpose(m, (1, 2, 0))
    rows, cols, depth = t.shape
    tiles = own_y // SUBL
    block = (SUBL, LANES)
    n_top = 2 * rows * cols // LANES
    n_x = slab_size(tiles) + n_top
    n_z = 2 * SKIN * cols // SUBL + n_top + tiles
    vmem = pl.BlockSpec(memory_space=pltpu.VMEM)
    hbm = pl.BlockSpec(memory_space=pltpu.HBM)
    msg_a, msg_b = pl.pallas_call(
        functools.partial(gas_kernel, (rows_x, REACH)),
        out_shape=[jax.ShapeDtypeStruct((n_x, *block), F32)] * 2,
        in_specs=[pl.BlockSpec(memory_space=pltpu.SMEM)] + [hbm] * 3,
        out_specs=[vmem] * 2,
        scratch_shapes=[
            pltpu.VMEM(u.shape, F32),
            pltpu.VMEM(t.shape, F32),
            pltpu.VMEM(m.shape, jnp.int32),
            pltpu.SemaphoreType.DMA((3,)),
        ],
        compiler_params=pltpu.CompilerParams(vmem_limit_bytes=60 * 1024 * 1024),
    )(meta, u, t, m)
    msg_h, msg_z, msg_d, own = call(
        pack_kernel, [(tiles, *block), (n_z, *block), (n_z, *block), (n_top, *block)], count=4
    )(meta, u, t, m, lev)
    in_a = lax.ppermute(msg_a, "gx", pairs(nx, 0))
    in_b = lax.ppermute(msg_b, "gx", pairs(nx, 1))
    in_z = lax.ppermute(msg_z, "gz", pairs(nz, 0))
    in_d = lax.ppermute(msg_d, ("gx", "gz"), cross(nx, nz, True))
    in_h = lax.ppermute(msg_h, ("gx", "gz"), cross(nx, nz, False))
    wide = rows_x + 2 * REACH - 2
    n_y = wide * COMPS // 2 + rows_x + 2 + 3 + rows + 2 * SKIN + n_top
    msg_a, msg_b = call(
        functools.partial(relay_kernel, (rows_x, REACH)), [(n_y, *block), (n_y, *block)], count=9
    )(meta, u, t, m, own, in_a, in_b, in_z, in_d, in_h)
    gy_b = lax.ppermute(msg_b, "gy", pairs(ny, 1))
    gy_a = lax.ppermute(msg_a, "gy", pairs(ny, 0))

    size = own_y + 2 * SUBL
    n = rows_x + 2 * REACH
    n2 = rows_x + 2 * REACH_LAST
    small = own_y + SUBL
    part_rows = 4 * SUBL
    n_m = -(-n2 // (LANES // GROUP))
    g2, msg_m, top_t, top_k = call(
        functools.partial(first_kernel, (rows_x, REACH)),
        [(COMPS, n2, small, LANES), (n_m, small, LANES), (TOP - SUBSTEPS, part_rows, LANES), (TOP - SUBSTEPS, part_rows, LANES)],
        scratch=advance_scratch(n, size, own_y + 2 * (REACH - 2), True) + [(part_rows, LANES), (part_rows, *block)],
        scalars=2,
        count=9,
    )(meta, beam, u, own, in_a, in_b, in_z, in_d, in_h, gy_a, gy_b)
    in_m = lax.ppermute(msg_m, "gz", pairs(nz, 0))
    part = (rows + 2 * SKIN, cols + SUBL, depth)
    (bulk,) = call(
        bulk_kernel, [t.shape], scratch=[(2, *part), part, part, part, part], scalars=2, count=6
    )(meta, beam, t, m, in_z, in_d, gy_a, gy_b)
    gas, mine, other, mass = call(
        functools.partial(last_kernel, (rows_x, own_y)),
        [u.shape, (n_top // 2, *block), (n_top // 2, *block), (part_rows, LANES)],
        scratch=advance_scratch(n2, small, own_y + 2 * (REACH_LAST - 2), False) + [(part_rows, *block)],
        scalars=2,
        count=5,
    )(meta, beam, g2, in_m, top_t, top_k, bulk)
    (gas,) = call(mass_kernel, [u.shape], scratch=[(n2, small, LANES)] * 2, count=3)(meta, gas, in_m, mass)
    given = lax.ppermute(other, "gz", pairs(nz, 0))
    (out,) = call(seal_kernel, [t.shape], count=3)(meta, bulk, mine, given)
    return gas, jnp.transpose(out, (2, 0, 1))


def solution(mesh):
    return jax.shard_map(
        shards,
        mesh=mesh,
        in_specs=(
            P(None, "gx", "gy", "gz"),
            P(None, ("gx", "gz"), "gy"),
            P(None, ("gx", "gz"), "gy"),
            P("gx", "gy"),
            P(),
        ),
        out_specs=(P(None, "gx", "gy", "gz"), P(None, ("gx", "gz"), "gy")),
        check_vma=False,
    )
```

```python
import functools

import jax
import jax.numpy as jnp
from jax import lax
from jax.experimental import pallas as pl
from jax.experimental.pallas import tpu as pltpu
from jax.sharding import PartitionSpec as P

STEPS = 2
SUBSTEPS = 2
GAS_STEP = 0.3
DRIFT_SPEED = 0.5
VAPOR_LOAD = 0.3
AMBIENT_LOAD = 0.7
STIFFNESS = 1.0
VISCOSITY = (0.2, 0.1, 0.15, 0.15, 0.15, 0.2)
HEAT_STEP = 1.0
POWDER_COND = 0.04
SOLID_COND = 0.15
LIQUID_COND = 0.09
LASER_POWER = 3.0
SPOT_RADIUS = 6.0
ABSORB_DEPTH = 4.0
BOIL_LEVEL = 1.0
BACK_PRESSURE = 0.5
LATENT_HEAT = 0.3
VAPOR_SOURCE = 0.5
RECOIL_PUSH = 0.4
RECOIL_PRESSURE = 0.6

COMPS = 6
LANES = 128
VMEM_LIMIT = 32 * 1024 * 1024
SUBL = 8
F32 = jnp.float32
REACH = 6
REACH_LAST = 3
SKIN = 4
TOP = 8
GROUP = 16
LEVEL = 2 * COMPS


def iota(shape, axis):
    return lax.broadcasted_iota(jnp.int32, shape, axis)


def wrapped(index, own, size):
    return jnp.where(index < own + (size - own) // 2, index, index - size)


def turn(value, amount, axis):
    size = value.shape[axis]
    if isinstance(amount, int):
        amount = amount % size
        if amount == 0:
            return value
    return pltpu.roll(value, amount, axis)


def softplus(x):
    return jnp.maximum(x, 0.0) + jnp.log1p(jnp.exp(-jnp.abs(x)))


def pack_heights(rows, base, lane, low_z, acc):
    more = jnp.where(low_z, 2, 0)
    for c, row in enumerate(rows):
        acc = jnp.where((lane & -2) == base + 2 * c, turn(row, base + 2 * c + more, 1), acc)
    return acc


def unpack_heights(packed, base, low_z, h0, h1, i):
    here = turn(packed, -base, 1)
    other = turn(packed, -base - 1, 1)
    h0[i] = jnp.where(low_z, here, other)
    h1[i] = jnp.where(low_z, other, here)


DEEP_5 = (2, 3, 4, 5)
DEEP_6 = (2, 5)
FULL = 4
QUARTERS = (5, 3, 2, 4)


def slab_index(c, layer, below):
    if layer <= FULL:
        return c * FULL + (FULL - layer if below else layer - 1)
    base = COMPS * FULL
    if layer == FULL + 1:
        return base + DEEP_5.index(c) if c in DEEP_5 else None
    return base + len(DEEP_5) + DEEP_6.index(c) if c in DEEP_6 else None


def slab_size():
    return COMPS * FULL + len(DEEP_5) + len(DEEP_6)


def row_tile(c, x, tile, u, in_a, in_b, even_x):
    rows_x = u.shape[1]
    span = slice(tile * SUBL, (tile + 1) * SUBL)
    if 0 <= x < rows_x:
        return u[c, x, span, :]
    k = slab_index(c, -x if x < 0 else x - rows_x + 1, x < 0)
    if k is None:
        return None
    low, high = (in_b, in_a) if x < 0 else (in_a, in_b)
    return jnp.where(even_x, low[k, span, :], high[k, span, :])


def conduct(v):
    return jnp.where(v == 0, POWDER_COND, jnp.where(v == 1, SOLID_COND, LIQUID_COND)).astype(F32)


def surface_tops(t, m):
    rows, cols = t.shape[0], t.shape[1]
    per = LANES // cols
    out = []
    for ref in (t, m):
        for j in range(rows // per):
            block = ref[j * per : (j + 1) * per].reshape(LANES, LANES)
            out.append(jnp.transpose(conduct(block) if ref is m else block)[:TOP])
    return out


def gas_kernel(reach, meta, u_in, t_in, m_in, out_a, out_b, u, t, m, top, sems):
    pairs_in = ((u_in, u), (t_in, t), (m_in, m))
    fetches = [pltpu.make_async_copy(src, dst, sems.at[i]) for i, (src, dst) in enumerate(pairs_in)]
    for copy in fetches:
        copy.start()
    rows_x, own_y = u.shape[1], u.shape[2]
    even = lax.rem(meta[0], 2) == 0
    copies = []

    def send(src, dst):
        copy = pltpu.make_async_copy(src, dst, sems.at[len(fetches) + len(copies)])
        copy.start()
        copies.append(copy)

    fetches[0].wait()
    for out, high in ((out_a, even), (out_b, jnp.logical_not(even))):
        first = jnp.where(high, rows_x - FULL, 0)
        for c in range(COMPS):
            send(u.at[c, pl.ds(first, FULL)], out.at[pl.ds(c * FULL, FULL)])
        base = COMPS * FULL
        row = jnp.where(high, rows_x - FULL - 1, FULL)
        send(u.at[pl.ds(DEEP_5[0], len(DEEP_5)), row], out.at[pl.ds(base, len(DEEP_5))])
        row = jnp.where(high, rows_x - reach, reach - 1)
        for j, c in enumerate(DEEP_6):
            send(u.at[c, row], out.at[base + len(DEEP_5) + j])
    for copy in fetches[1:]:
        copy.wait()
    for j, value in enumerate(surface_tops(t, m)):
        span = j * SUBL
        top[span // own_y, span % own_y : span % own_y + SUBL, :] = value
    for out in (out_a, out_b):
        send(top, out.at[pl.ds(slab_size(), top.shape[0])])
    for copy in copies:
        copy.wait()


def pack_kernel(meta, u, t, m, lev, out_h, out_z, out_d, own):
    low_z = meta[2] == 0
    rows_x = u.shape[1]
    tiles = u.shape[2] // SUBL
    rows, cols = t.shape[0], t.shape[1]
    col_tiles = cols // SUBL
    n = 0
    for source in (lambda v: v, conduct):
        ref = t if n == 0 else m
        for r in range(SKIN):
            for y in range(col_tiles):
                lo = source(ref[r, y * SUBL : (y + 1) * SUBL, :])
                hi = source(ref[rows - SKIN + r, y * SUBL : (y + 1) * SUBL, :])
                out_z[n] = jnp.where(low_z, hi, lo)
                out_d[n] = jnp.where(low_z, lo, hi)
                n += 1
    tops = surface_tops(t, m)
    for j, top in enumerate(tops):
        own[j] = top
        out_z[n + j] = top
        out_d[n + j] = top
    n += len(tops)
    size = u.shape[2]
    lane = iota((size, LANES), 1)
    eye = iota((size, size), 0) == iota((size, size), 1)
    levels = lev[...].astype(F32)
    acc = jnp.zeros((size, LANES), F32)
    for x in range(rows_x):
        acc = pack_heights([u[c, x] for c in range(COMPS)], x * GROUP, lane, low_z, acc)
        level = jnp.sum(jnp.where(eye, levels[x : x + 1, :], 0.0), axis=1, keepdims=True)
        acc = jnp.where((lane & -2) == x * GROUP + LEVEL, level, acc)
    for y in range(tiles):
        part = acc[y * SUBL : (y + 1) * SUBL]
        out_h[y] = part
        out_z[n + y] = part
        out_d[n + y] = part


def part_row(r, tile, ref, at, rows, in_z, in_d, low_z, col_tiles, low_part):
    if 0 <= r < rows:
        value = ref[r, tile * SUBL : (tile + 1) * SUBL, :]
        return conduct(value) if at else value
    k = (at * SKIN + (r + SKIN if r < 0 else r - rows)) * col_tiles + tile
    low, high = (in_d[k], in_z[k]) if r < 0 else (in_z[k], in_d[k])
    return jnp.where(low_z, low, high)


def relay_kernel(cells, meta, u, t, m, own, in_a, in_b, in_z, in_d, in_h, out_a, out_b, part_a, part_b):
    rows_x, reach = cells
    gx, gy, gz = meta[0], meta[1], meta[2]
    even_x = lax.rem(gx, 2) == 0
    even_y = lax.rem(gy, 2) == 0
    low_z = gz == 0
    tiles = u.shape[2] // SUBL
    rows, cols = t.shape[0], t.shape[1]
    col_tiles = cols // SUBL
    half = SUBL // 2
    sub = iota((SUBL, LANES), 0)
    lane = iota((SUBL, LANES), 1)
    zero = jnp.zeros((SUBL, LANES), F32)

    def put(n, hi, lo):
        out_a[n] = jnp.where(even_y, hi, lo)
        out_b[n] = jnp.where(even_y, lo, hi)

    def both(c, x):
        pair = [row_tile(c, x, y, u, in_a, in_b, even_x) for y in (tiles - 1, 0)]
        return [zero if v is None else v for v in pair]

    n = 0
    for x in range(1 - reach, rows_x + reach - 1):
        for c in range(0, COMPS, 2):
            (hi0, lo0), (hi1, lo1) = both(c, x), both(c + 1, x)
            put(n, jnp.where(sub < half, turn(hi1, half, 0), hi0), jnp.where(sub < half, lo0, turn(lo1, half, 0)))
            n += 1
    for x in range(-1, rows_x + 1):
        hi = lo = zero
        for q, c in enumerate(QUARTERS):
            a, b = both(c, x)
            hi = jnp.where((sub & -2) == 2 * q, turn(a, 2 * q - 2, 0), hi)
            lo = jnp.where((sub & -2) == 2 * q, turn(b, 2 * q - half, 0), lo)
        put(n, hi, lo)
        n += 1
    base = in_z.shape[0] - tiles
    hi_y, lo_y = tiles - 1, 0
    put(
        n,
        jnp.where(low_z, in_d[base + hi_y], in_h[hi_y]),
        jnp.where(low_z, in_d[base + lo_y], in_h[lo_y]),
    )
    put(n + 1, in_z[base + hi_y], in_z[base + lo_y])
    put(
        n + 2,
        jnp.where(low_z, in_h[hi_y], in_d[base + hi_y]),
        jnp.where(low_z, in_h[lo_y], in_d[base + lo_y]),
    )
    n += 3
    for r in range(-SKIN, rows + SKIN):
        hi_t, lo_t = [part_row(r, y, t, 0, rows, in_z, in_d, low_z, col_tiles, None) for y in (col_tiles - 1, 0)]
        hi_k, lo_k = [part_row(r, y, m, 1, rows, in_z, in_d, low_z, col_tiles, None) for y in (col_tiles - 1, 0)]
        hi = jnp.where(sub < half, turn(hi_k, half, 0), hi_t)
        lo = jnp.where(sub < half, lo_t, turn(lo_k, half, 0))
        part_a[r + SKIN] = jnp.where(even_y, hi, lo)
        part_b[r + SKIN] = jnp.where(even_y, lo, hi)
    sources = surface_sources(own, in_a, in_b, in_z, in_d, even_x, tiles)
    per = LANES // cols
    slot = lax.rem(lane, cols) // SUBL
    for v in range(len(sources) // per):
        hi = lo = zero
        for i in range(per):
            src = sources[v * per + i]
            hi = jnp.where(slot == i, turn(src, SUBL * i - (cols - SUBL), 1), hi)
            lo = jnp.where(slot == i, turn(src, SUBL * i, 1), lo)
        put(n + v, hi, lo)


def surface_sources(own, in_a, in_b, in_z, in_d, even_x, tiles):
    count = own.shape[0]
    at = in_z.shape[0] - tiles - count

    def high(j):
        k, span = slab_size() + j // tiles, slice(j % tiles * SUBL, (j % tiles + 1) * SUBL)
        return jnp.where(even_x, in_a[k, span, :], in_b[k, span, :])

    out = []
    for a in range(2):
        span = range(a * count // 2, (a + 1) * count // 2)
        out += [own[j] for j in span]
        out += [in_z[at + j] for j in span]
        out += [high(j) for j in span]
        out += [in_d[at + j] for j in span]
    return out


def heat_source(row, col, beam, step):
    a = beam[step, 0].astype(F32)
    b = beam[step, 1].astype(F32)
    along_x = jnp.exp(-(((row - a) / SPOT_RADIUS) ** 2))
    along_y = jnp.exp(-(((col - b) / SPOT_RADIUS) ** 2))
    return LASER_POWER * along_x * along_y


def bulk_kernel(meta, beam, t, m, in_z, in_d, gy_a, gy_b, out, temp, cond, kx, ky, kz):
    gx, gy, gz = meta[0], meta[1], meta[2]
    even_y = lax.rem(gy, 2) == 0
    low_z = gz == 0
    rows, cols, depth = t.shape
    col_tiles = cols // SUBL
    half = SUBL // 2
    size = cols + SUBL
    n = rows + 2 * SKIN
    sub = iota((SUBL, LANES), 0)
    for i in range(n):
        for y in range(col_tiles):
            span = slice(y * SUBL, (y + 1) * SUBL)
            temp[0, i, span, :] = part_row(i - SKIN, y, t, 0, rows, in_z, in_d, low_z, col_tiles, None)
            cond[i, span, :] = part_row(i - SKIN, y, m, 1, rows, in_z, in_d, low_z, col_tiles, None)
        up = jnp.where(even_y, gy_a[i], gy_b[i])
        low = jnp.where(even_y, gy_b[i], gy_a[i])
        temp[0, i, cols:size, :] = jnp.where(sub < half, up, low)
        cond[i, cols:size, :] = turn(jnp.where(sub < half, low, up), half, 0)

    lane = iota((size, LANES), 1)
    for i in range(n):
        k = cond[i]
        if i + 1 < n:
            kx[i] = 0.5 * (k + cond[i + 1])
        ky[i] = 0.5 * (k + turn(k, -1, 0))
        kz[i] = 0.5 * (k + jnp.where(lane == depth - 1, 0.0, turn(k, -1, 1)))

    col_g = gy * cols + wrapped(iota((size, LANES), 0), cols, size)
    inside_y = jnp.where((col_g >= 0) & (col_g < meta[4] * cols), 1.0, 0.0)
    col_f = col_g.astype(F32)
    fall = jnp.exp(-lane.astype(F32) / ABSORB_DEPTH)
    first_row = (gx * meta[5] + gz) * rows - SKIN

    for s in range(STEPS * SUBSTEPS):
        src, dst = s % 2, 1 - s % 2
        last = s == STEPS * SUBSTEPS - 1
        a = beam[s, 0].astype(F32)
        b = beam[s, 1].astype(F32)
        spot = LASER_POWER * fall * jnp.exp(-(((col_f - b) / SPOT_RADIUS) ** 2))
        lo, hi = s + 1, n - 1 - s
        fx0 = kx[lo - 1] * (temp[src, lo] - temp[src, lo - 1])
        for i in range(lo, hi):
            v = temp[src, i]
            fx = kx[i] * (temp[src, i + 1] - v)
            fy = ky[i] * (turn(v, -1, 0) - v)
            fz = kz[i] * (jnp.where(lane == depth - 1, 0.0, turn(v, -1, 1)) - v)
            above = jnp.where(lane == 0, 0.5 * cond[i] * v, turn(fz, 1, 1))
            row = first_row + i
            along_x = jnp.exp(-((jnp.full((1, LANES), row.astype(F32) - a) / SPOT_RADIUS) ** 2))
            change = (fx - fx0) + (fy - turn(fy, 1, 0)) + (fz - above) + spot * along_x
            new = v + HEAT_STEP * change
            if last:
                out[i - SKIN] = new[:cols]
            else:
                ok = (row >= 0) & (row < meta[3] * meta[5] * rows)
                temp[dst, i] = new * (inside_y * jnp.where(ok, 1.0, 0.0))
            fx0 = fx


def seal_kernel(meta, bulk, mine, given, out):
    rows, cols, depth = bulk.shape
    per = LANES // cols
    lane = iota((LANES, LANES), 1)
    for j in range(mine.shape[0]):
        skin = jnp.where(meta[2] == 0, mine[j], given[j])
        skin = jnp.concatenate([skin, jnp.zeros((LANES - SUBL, LANES), F32)], axis=0)
        block = jnp.where(lane < SKIN, jnp.transpose(skin), bulk[j * per : (j + 1) * per].reshape(LANES, LANES))
        out[j * per : (j + 1) * per] = block.reshape(per, cols, LANES)


def pack_skin(t, rows, cols, scratch, out):
    per = LANES // cols
    lane = iota((SUBL, LANES), 1)
    for j in range(SUBL // per):
        acc = jnp.zeros((SUBL, LANES), F32)
        for q in range(per):
            acc = jnp.where(lane // cols == q, turn(scratch[rows + j * per + q], cols * q, 1), acc)
        out[j] = acc


def split(value):
    high = value.astype(jnp.bfloat16)
    rest = (value - high.astype(F32)).astype(jnp.bfloat16)
    return jnp.concatenate([high, rest], axis=1)


def height_matrix():
    shape = (2 * LANES, 2 * LANES)
    k = iota(shape, 0) & (LANES - 1)
    j = iota(shape, 1)
    above = jnp.where(k == (j & (LANES - 1)) + 1, 1.0, 0.0)
    below = jnp.where(k == (j & (LANES - 1)) - 1, 1.0, 0.0)
    return (above + jnp.where(j < LANES, -below, below)).astype(jnp.bfloat16)


def height_terms(ref, first, last, matrix, diff, total):
    size = ref.shape[2]
    for c in range(COMPS):
        rows = ref[c, first:last].reshape((last - first) * size, LANES)
        both = jnp.dot(split(rows), matrix, preferred_element_type=F32)
        diff[c, first:last] = both[:, :LANES].reshape(last - first, size, LANES)
        total[c, first:last] = both[:, LANES:].reshape(last - first, size, LANES)


def cut_weights(low_z, scale):
    lane = iota((1, LANES), 1)
    up = (lane == LANES - 1) & low_z
    down = (lane == 0) & jnp.logical_not(low_z)
    weight = {}
    for v in sorted(set(VISCOSITY)):
        side = scale * GAS_STEP * v
        drift = 0.5 * DRIFT_SPEED * scale * GAS_STEP
        weight[v] = jnp.where(up, side - drift, jnp.where(down, side + drift, 0.0))
    return jnp.where(up, 1.0, jnp.where(down, -1.0, 0.0)), weight


def stepped(comps, ref, i, diff, total, h, cut, scale, start, size):
    sign, weight = cut
    half = 0.5 * scale * GAS_STEP
    span = pl.ds(start, size)

    def dx(c):
        return ref[c, i + 1, span, :] - ref[c, i - 1, span, :]

    def dy(c):
        return ref[c, i, pl.ds(start + 1, size), :] - ref[c, i, pl.ds(start - 1, size), :]

    def dz(c):
        return diff[c, i, span, :] + sign * h[i, span, 2 * c : 2 * c + 1]

    spread = half * (dx(2) + dy(3) + dz(4))
    out = {}
    for c in comps:
        v = VISCOSITY[c]
        side = scale * GAS_STEP * v
        drift = 0.5 * DRIFT_SPEED * scale * GAS_STEP
        sides = (ref[c, i + 1, span, :] + ref[c, i - 1, span, :]) + (
            ref[c, i, pl.ds(start + 1, size), :] + ref[c, i, pl.ds(start - 1, size), :]
        )
        across = h[i, span, 2 * c : 2 * c + 1]
        new = (
            scale * (1.0 - 6.0 * GAS_STEP * v) * ref[c, i, span, :]
            + side * (sides + total[c, i, span, :])
            - drift * diff[c, i, span, :]
            + weight[v] * across
        )
        if c == 2:
            new = new - half * dx(5)
        elif c == 3:
            new = new - half * dy(5)
        elif c == 4:
            new = new - half * dz(5)
        else:
            new = new - {0: VAPOR_LOAD, 1: AMBIENT_LOAD, 5: STIFFNESS}[c] * spread
        out[c] = new
    return out


def by_comp(lane, values):
    out = jnp.full(lane.shape, values[-1], F32)
    for c, v in enumerate(values[:-1]):
        out = jnp.where(lane == 2 * c, v, out)
    return out


def couple_matrix():
    shape = (6 * LANES, LANES)
    k = iota(shape, 0)
    j = iota(shape, 1)
    axis = k // (2 * LANES)
    lane = k & (LANES - 1)
    spread = (lane == 4 + 2 * axis) & ((j == 0) | (j == 2) | (j == 10))
    slope = (lane == 10) & (j == 4 + 2 * axis)
    return jnp.where(spread | slope, 1.0, 0.0).astype(jnp.bfloat16)


def halo_stepped(h0, h1, g, low_z, mask_of, out):
    n, size = h0.shape[0], h0.shape[1]
    rows = (n - 2) * size
    lane = iota((1, LANES), 1)
    more = jnp.where(low_z, 1, 0)
    flat_lane = iota((rows, LANES), 1)
    touch = jnp.zeros((rows, LANES), F32)
    for c in range(COMPS):
        own = g[c, 1 : n - 1].reshape(rows, LANES)
        touch = jnp.where(flat_lane == 2 * c, turn(own, 2 * c + more, 1), touch)
    mid = h0[1 : n - 1].reshape(rows, LANES)
    east = h0[2:n].reshape(rows, LANES)
    west = h0[0 : n - 2].reshape(rows, LANES)
    north = turn(mid, -1, 0)
    south = turn(mid, 1, 0)
    behind = h1[1 : n - 1].reshape(rows, LANES)
    slopes = [east - west, north - south, jnp.where(low_z, 1.0, -1.0) * (behind - touch)]
    coupled = jnp.dot(
        jnp.concatenate([split(v) for v in slopes], axis=1), couple_matrix(), preferred_element_type=F32
    )
    up = by_comp(lane, [GAS_STEP * (v - 0.5 * DRIFT_SPEED) for v in VISCOSITY])
    down = by_comp(lane, [GAS_STEP * (v + 0.5 * DRIFT_SPEED) for v in VISCOSITY])
    half = 0.5 * GAS_STEP
    pull = by_comp(lane, [-half * VAPOR_LOAD, -half * AMBIENT_LOAD, -half, -half, -half, -half * STIFFNESS])
    new = (
        by_comp(lane, [1.0 - 6.0 * GAS_STEP * v for v in VISCOSITY]) * mid
        + by_comp(lane, [GAS_STEP * v for v in VISCOSITY]) * ((east + west) + (north + south))
        + jnp.where(low_z, up, down) * behind
        + jnp.where(low_z, down, up) * touch
        + pull * coupled
    )
    for i in range(1, n - 1):
        out[i - 1] = turn(new[(i - 1) * size : i * size] * mask_of(i, 0, size), -1, 0)


def advance(meta, g, h0, h1, f, fh, diff, total, own_x, own_y, store, unroll):
    n, size = g.shape[1], g.shape[2]
    gx, gy, gz = meta[0], meta[1], meta[2]
    low_z = gz == 0
    before = (n - own_x) // 2
    before_y = (size - own_y) // 2
    reach = before - 2

    def mask_y(start, count):
        y_g = gy * own_y + iota((count, LANES), 0) + start - before_y
        return jnp.where((y_g >= 0) & (y_g < meta[4] * own_y), 1.0, 0.0)

    def mask_of(i, start, count):
        x_g = gx * own_x + i - before
        ok = (x_g >= 0) & (x_g < meta[3] * own_x)
        return mask_y(start, count) * jnp.where(ok, 1.0, 0.0)

    matrix = height_matrix()
    halo_stepped(h0, h1, g, low_z, mask_of, fh)
    height_terms(g, 1, n - 1, matrix, diff, total)
    everything = tuple(range(COMPS))

    cut = cut_weights(low_z, 1.0)

    def one(comps):
        def body(i, carry):
            count = size - 2
            new = stepped(comps, g, i, diff, total, h0, cut, 1.0, 1, count)
            m = mask_of(i, 1, count)
            for c in comps:
                f[c, i - 1, :count, :] = new[c] * m
            return carry

        return body

    lax.fori_loop(2, n - 2, one(everything), 0, unroll=unroll)
    for i in (1, n - 2):
        one((2, 5))(i, 0)

    height_terms(f, 1, n - 3, matrix, diff, total)
    start = before_y - 1 - reach
    count = own_y + 2 * reach

    half_cut = cut_weights(low_z, 0.5)

    def two(comps):
        def body(i, carry):
            new = stepped(comps, f, i - 1, diff, total, fh, half_cut, 0.5, start, count)
            m = mask_of(i, start + 1, count)
            for c in comps:
                new[c] = (0.5 * g[c, i, pl.ds(start + 1, count), :] + new[c]) * m
            store(i, new)
            return carry

        return body

    outer = 1 if reach > 1 else 0
    lax.fori_loop(3 + outer, n - 3 - outer, two(everything), 0, unroll=unroll)
    for i in (2, n - 3):
        two((5,))(i, 0)
    if outer:
        for i in (3, n - 4):
            two((2, 5))(i, 0)


def lane_sums(value):
    high = value.astype(jnp.bfloat16)
    rest = value - high.astype(F32)
    middle = rest.astype(jnp.bfloat16)
    low = (rest - middle.astype(F32)).astype(jnp.bfloat16)
    parts = jnp.concatenate([high, middle, low], axis=1)
    ones = jnp.ones((3 * LANES, LANES), jnp.bfloat16)
    return jnp.dot(parts, ones, preferred_element_type=F32)


def fine_pressure(meta, p, h0, own_x, own_y, part_rows):
    n, count = p.shape[0], p.shape[1]
    skip = (h0.shape[1] - count) // 2
    skip_x = (h0.shape[0] - n) // 2
    before = (n - own_x) // 2
    y_l = iota((count, LANES), 0) - (count - own_y) // 2
    col_y = lax.div(wrapped(iota((count, LANES), 1), 2 * own_y, LANES) + LANES, 2) - LANES // 2
    pick = col_y == y_l
    row_x = lax.div(wrapped(iota((part_rows, LANES), 0), 2 * own_x, part_rows) + LANES, 2) - LANES // 2
    height = (iota((count, LANES), 1) + meta[2] * LANES).astype(F32)
    fine = jnp.zeros((part_rows, LANES), F32)
    full = -(-count // SUBL) * SUBL
    pad = [jnp.zeros((full - count, LANES), F32)] if full > count else []
    found = []
    for i in range(n):
        level = h0[i + skip_x, skip : skip + count, LEVEL : LEVEL + 1]
        found += [jnp.where(height == level, p[i], 0.0)] + pad
    at = lane_sums(jnp.concatenate(found, axis=0))
    for i in range(n):
        line = jnp.sum(jnp.where(pick, at[i * full : i * full + count], 0.0), axis=0, keepdims=True)
        fine = jnp.where(row_x == i - before, line, fine)
    return fine


def top_heat(meta, beam, first, t, k, fine, own_rows, cols):
    gx, gy = meta[0], meta[1]
    shape = fine.shape
    row = gx * own_rows + wrapped(iota(shape, 0), own_rows, shape[0])
    col = gy * cols + wrapped(iota(shape, 1), cols, shape[1])
    row, col = row.astype(F32), col.astype(F32)
    deep = TOP - 1 - first
    kx = [0.5 * (v + turn(v, -1, 0)) for v in k[:deep]]
    ky = [0.5 * (v + turn(v, -1, 1)) for v in k[:deep]]
    kz = [0.5 * (k[d] + k[d + 1]) for d in range(deep)]
    for s in range(SUBSTEPS):
        beam_xy = heat_source(row, col, beam, first + s)
        before = 0.5 * k[0] * t[0]
        new = []
        for d in range(TOP - 1 - first - s):
            fx = kx[d] * (turn(t[d], -1, 0) - t[d])
            fy = ky[d] * (turn(t[d], -1, 1) - t[d])
            fz = kz[d] * (t[d + 1] - t[d])
            factor = jnp.exp(jnp.full(shape, -d / ABSORB_DEPTH, F32))
            change = (fx - turn(fx, 1, 0)) + (fy - turn(fy, 1, 1)) + (fz - before) + beam_xy * factor
            if d == 0:
                change = change - LATENT_HEAT * softplus(t[0] - BOIL_LEVEL - BACK_PRESSURE * fine)
            new.append(jnp.where(k[d] > 0, t[d] + HEAT_STEP * change, 0.0))
            before = fz
        t = new
    return t


def vapor_mass(t0, fine):
    four = t0 + turn(t0, -1, 1)
    four = four + turn(four, -1, 0)
    return softplus(0.25 * four - BOIL_LEVEL - BACK_PRESSURE * fine)


def mass_rows(meta, h, mass, first, rows, count, own_y):
    skip = (h.shape[1] - count) // 2
    skip_x = (h.shape[0] - rows) // 2
    y_l = iota((count, LANES), 0) - (count - own_y) // 2
    col = wrapped(iota((count, LANES), 1), 2 * own_y, LANES)
    pick = col == 2 * y_l
    height = (iota((count, LANES), 1) + meta[2] * LANES).astype(F32)
    found = []
    for i in range(rows):
        r = (2 * (i + first)) % mass.shape[0]
        found.append(jnp.where(pick, mass[r : r + 1, :], 0.0))
    at = lane_sums(jnp.concatenate(found, axis=0))
    out = []
    for i in range(rows):
        level = h[i + skip_x, skip : skip + count, LEVEL : LEVEL + 1]
        out.append(jnp.where(height == level, at[i * count : (i + 1) * count], 0.0))
    return out


def first_kernel(
    cells, meta, beam, u, own, in_a, in_b, in_z, in_d, in_h, gy_a, gy_b,
    out_g, out_m, out_t, out_k, g, h, h1, f, fh, diff, total, p, mass, skin,
):
    rows_x, reach = cells
    gx, gy, gz = meta[0], meta[1], meta[2]
    even_x = lax.rem(gx, 2) == 0
    even_y = lax.rem(gy, 2) == 0
    low_z = gz == 0
    own_y = u.shape[2]
    tiles = own_y // SUBL
    size = own_y + 2 * SUBL
    half = SUBL // 2
    sub = iota((SUBL, LANES), 0)
    zero = jnp.zeros((SUBL, LANES), F32)

    def side(k):
        upper = jnp.where(even_y, gy_a[k], gy_b[k])
        lower = jnp.where(even_y, gy_b[k], gy_a[k])
        return upper, lower

    wide = rows_x + 2 * reach - 2
    outer = wide * COMPS // 2
    for x in range(-reach, rows_x + reach):
        i = x + reach
        for c in range(COMPS):
            for y in range(tiles):
                value = row_tile(c, x, y, u, in_a, in_b, even_x)
                g[c, i, (y + 1) * SUBL : (y + 2) * SUBL, :] = zero if value is None else value
            upper = lower = zero
            if 0 < i < wide + 1:
                upper, lower = side((i - 1) * COMPS // 2 + c // 2)
                if c % 2:
                    upper, lower = turn(upper, half, 0), turn(lower, half, 0)
            if -1 <= x < rows_x + 1 and c in QUARTERS:
                q = QUARTERS.index(c)
                far_up, far_low = side(outer + x + 1)
                far_up, far_low = turn(far_up, half - 2 * q, 0), turn(far_low, 2 - 2 * q, 0)
            else:
                far_up = far_low = zero
            g[c, i, own_y + SUBL : size, :] = jnp.where(sub < half, upper, jnp.where(sub < half + 2, far_up, 0.0))
            g[c, i, :SUBL, :] = jnp.where(sub >= half, lower, jnp.where(sub >= half - 2, far_low, 0.0))
    base = in_z.shape[0] - tiles
    packed = []
    for b in range(3):
        parts = []
        for y in range(tiles):
            if b == 0:
                parts.append(jnp.where(low_z, in_d[base + y], in_h[y]))
            elif b == 1:
                parts.append(in_z[base + y])
            else:
                parts.append(jnp.where(low_z, in_h[y], in_d[base + y]))
        upper, lower = side(outer + rows_x + 2 + b)
        packed.append(jnp.concatenate([lower, *parts, upper], axis=0))
    for x in range(-reach, rows_x + reach):
        b, q = divmod(x + rows_x, rows_x)
        unpack_heights(packed[b], GROUP * q, low_z, h, h1, x + reach)

    def store(i, new):
        p[i - 2] = new[COMPS - 1]
        if len(new) > 1:
            for c in range(COMPS):
                out_g[c, i - 3] = new[c] if c in new else jnp.zeros_like(new[COMPS - 1])

    advance(meta, g, h, h1, f, fh, diff, total, rows_x, own_y, store, 4)
    fine = fine_pressure(meta, p, h, rows_x, own_y, mass.shape[0])

    cols = LANES // 4
    per = LANES // cols
    lane = iota((SUBL, LANES), 1)
    sources = surface_sources(own, in_a, in_b, in_z, in_d, even_x, tiles)
    count = len(sources) // 2
    top_at = gy_a.shape[0] - len(sources) // per
    layers = []
    for a in range(2):
        for s in range(count):
            src = sources[a * count + s]
            upper, lower = side(top_at + (a * count + s) // per)
            i = s % per
            for q in range(per):
                at = cols * q + SUBL * i
                skin[s * per + q] = jnp.where(
                    lane < cols,
                    turn(src, -cols * q, 1),
                    jnp.where(
                        lane < cols + SUBL,
                        turn(upper, cols - at, 1),
                        jnp.where(lane >= LANES - SUBL, turn(lower, LANES - SUBL - at, 1), 0.0),
                    ),
                )
        for d in range(TOP):
            layers.append(skin[:, d, :])
    t, k = layers[:TOP], layers[TOP:]
    t = top_heat(meta, beam, 0, t, k, fine, 2 * rows_x, cols)
    for d in range(TOP - SUBSTEPS):
        out_t[d] = t[d]
        out_k[d] = k[d]
    mass[...] = vapor_mass(t[0], fine)

    count, small = out_g.shape[1], out_g.shape[2]
    masses = mass_rows(meta, h, mass, -REACH_LAST, count, small, own_y)
    lane_s = iota((small, LANES), 1)
    y_g = gy * own_y + iota((small, LANES), 0) - (small - own_y) // 2
    inside_y = jnp.where((y_g >= 0) & (y_g < meta[4] * own_y), 1.0, 0.0)
    skip = (size - small) // 2
    per = LANES // GROUP
    acc = jnp.zeros((small, LANES), F32)
    for i in range(count):
        x = i - REACH_LAST
        x_g = gx * rows_x + x
        ok = jnp.where((x_g >= 0) & (x_g < meta[3] * rows_x), 1.0, 0.0)
        add = masses[i] * (inside_y * ok)
        rows = [out_g[c, i] for c in range(COMPS)]
        for c, load in ((0, VAPOR_SOURCE), (4, RECOIL_PUSH), (5, RECOIL_PRESSURE)):
            rows[c] = rows[c] + load * add
            out_g[c, i] = rows[c]
        j, q = divmod(i, per)
        acc = pack_heights(rows, GROUP * q, lane_s, low_z, acc)
        level = h[x + reach, skip : skip + small, LEVEL : LEVEL + 1]
        acc = jnp.where((lane_s & -2) == GROUP * q + LEVEL, level, acc)
        if q == per - 1 or i == count - 1:
            out_m[j] = acc
            acc = jnp.zeros((small, LANES), F32)


def last_kernel(
    cells, meta, beam, g, in_m, in_t, in_k, bulk, out_g, out_t, out_f, mass, h, h1, f, fh, diff, total, p, skin
):
    rows_x, own_y = cells
    for i in range(g.shape[1]):
        j, q = divmod(i, LANES // GROUP)
        unpack_heights(in_m[j], GROUP * q, meta[2] == 0, h, h1, i)

    def store(i, new):
        p[i - 2] = new[COMPS - 1]
        if len(new) == COMPS:
            for c in range(COMPS):
                out_g[c, i - 3] = new[c][1 : own_y + 1]

    advance(meta, g, h, h1, f, fh, diff, total, rows_x, own_y, store, True)
    fine = fine_pressure(meta, p, h, rows_x, own_y, mass.shape[0])
    cols = LANES // 4
    t = [in_t[d] for d in range(TOP - SUBSTEPS)]
    k = [in_k[d] for d in range(TOP - SUBSTEPS)]
    t = top_heat(meta, beam, SUBSTEPS, t, k, fine, 2 * rows_x, cols)
    skin[...] = jnp.zeros_like(skin)
    for d in range(SKIN):
        skin[:, d, :] = t[d]
    pack_skin(t, 0, cols, skin, out_t)
    pack_skin(t, SUBL, cols, skin, out_f)
    mass[...] = vapor_mass(t[0], fine)


def mass_kernel(meta, gas, in_m, mass, out_g, h, h1):
    rows_x, own_y = gas.shape[1], gas.shape[2]
    n = h.shape[0]
    for i in range((n - rows_x) // 2, (n + rows_x) // 2):
        j, q = divmod(i, LANES // GROUP)
        unpack_heights(in_m[j], GROUP * q, meta[2] == 0, h, h1, i)
    masses = mass_rows(meta, h, mass, 0, rows_x, own_y, own_y)
    loads = {0: VAPOR_SOURCE, 4: RECOIL_PUSH, 5: RECOIL_PRESSURE}
    for x in range(rows_x):
        for c in range(COMPS):
            out_g[c, x] = gas[c, x] + loads[c] * masses[x] if c in loads else gas[c, x]


def places():
    axes = ("gx", "gy", "gz")
    return [lax.axis_index(a) for a in axes] + [lax.axis_size(a) for a in axes]


def call(body, outs, scratch=(), scalars=0, count=0):
    def kernel(*refs):
        body(places(), *refs)

    vmem = pl.BlockSpec(memory_space=pltpu.VMEM)
    smem = pl.BlockSpec(memory_space=pltpu.SMEM)
    return pl.pallas_call(
        kernel,
        out_shape=[jax.ShapeDtypeStruct(s, F32) for s in outs],
        in_specs=[smem] * scalars + [vmem] * count,
        out_specs=[vmem] * len(outs),
        scratch_shapes=[pltpu.VMEM(s, F32) for s in scratch],
        compiler_params=pltpu.CompilerParams(vmem_limit_bytes=VMEM_LIMIT),
    )


def advance_scratch(n, size, count, bricks):
    row = (size, LANES)
    return ([(COMPS, n, *row)] if bricks else []) + [
        (n, *row),
        (n, *row),
        (COMPS, n - 2, *row),
        (n - 2, *row),
        (COMPS, n - 1, *row),
        (COMPS, n - 1, *row),
        (n - 4, count, LANES),
    ]


def pairs(count, odd):
    out = []
    for i in range(odd, count - 1, 2):
        out += [(i, i + 1), (i + 1, i)]
    return out


def cross(nx, nz, upper):
    out = []
    for i in range(nx - 1):
        a, b = i * nz + (nz - 1 if upper else 0), (i + 1) * nz + (0 if upper else nz - 1)
        out += [(a, b), (b, a)]
    return out


def shards(u, t, m, lev, beam):
    nx, ny, nz = (lax.axis_size(a) for a in ("gx", "gy", "gz"))
    _, rows_x, own_y, _ = u.shape
    t, m = jnp.transpose(t, (1, 2, 0)), jnp.transpose(m, (1, 2, 0))
    rows, cols, depth = t.shape
    tiles = own_y // SUBL
    block = (SUBL, LANES)
    n_top = 2 * rows * cols // LANES
    top = (n_top // tiles, own_y, LANES)
    n_x = slab_size() + top[0]
    n_z = 2 * SKIN * cols // SUBL + n_top + tiles
    vmem = pl.BlockSpec(memory_space=pltpu.VMEM)
    hbm = pl.BlockSpec(memory_space=pltpu.HBM)
    hbm = pl.BlockSpec(memory_space=pltpu.HBM)

    def gas_pack(*refs):
        gas_kernel(REACH, places(), *refs)

    copies = 5 + 2 * (COMPS + 1 + len(DEEP_6))
    msg_a, msg_b = pl.pallas_call(
        gas_pack,
        out_shape=[jax.ShapeDtypeStruct((n_x, own_y, LANES), F32)] * 2,
        in_specs=[hbm] * 3,
        out_specs=[hbm] * 2,
        scratch_shapes=[
            pltpu.VMEM(u.shape, F32),
            pltpu.VMEM(t.shape, F32),
            pltpu.VMEM(m.shape, jnp.int32),
            pltpu.VMEM(top, F32),
            pltpu.SemaphoreType.DMA((copies,)),
        ],
        compiler_params=pltpu.CompilerParams(vmem_limit_bytes=60 * 1024 * 1024),
    )(u, t, m)
    msg_h, msg_z, msg_d, own = call(
        pack_kernel, [(tiles, *block), (n_z, *block), (n_z, *block), (n_top, *block)], count=4
    )(u, t, m, lev)
    in_a = lax.ppermute(msg_a, "gx", pairs(nx, 0))
    in_b = lax.ppermute(msg_b, "gx", pairs(nx, 1))
    in_z = lax.ppermute(msg_z, "gz", pairs(nz, 0))
    in_d = lax.ppermute(msg_d, ("gx", "gz"), cross(nx, nz, True))
    in_h = lax.ppermute(msg_h, ("gx", "gz"), cross(nx, nz, False))
    wide = rows_x + 2 * REACH - 2
    n_y = wide * COMPS // 2 + rows_x + 2 + 3 + n_top
    n_part = rows + 2 * SKIN
    msg_a, msg_b, part_a, part_b = call(
        functools.partial(relay_kernel, (rows_x, REACH)), [(n_y, *block)] * 2 + [(n_part, *block)] * 2, count=9
    )(u, t, m, own, in_a, in_b, in_z, in_d, in_h)
    gy_b = lax.ppermute(msg_b, "gy", pairs(ny, 1))
    gy_a = lax.ppermute(msg_a, "gy", pairs(ny, 0))
    part_b = lax.ppermute(part_b, "gy", pairs(ny, 1))
    part_a = lax.ppermute(part_a, "gy", pairs(ny, 0))

    size = own_y + 2 * SUBL
    n = rows_x + 2 * REACH
    n2 = rows_x + 2 * REACH_LAST
    small = own_y + SUBL
    part_rows = 4 * SUBL
    n_m = -(-n2 // (LANES // GROUP))
    g2, msg_m, top_t, top_k = call(
        functools.partial(first_kernel, (rows_x, REACH)),
        [(COMPS, n2, small, LANES), (n_m, small, LANES), (TOP - SUBSTEPS, part_rows, LANES), (TOP - SUBSTEPS, part_rows, LANES)],
        scratch=advance_scratch(n, size, own_y + 2 * (REACH - 2), True) + [(part_rows, LANES), (part_rows, *block)],
        scalars=1,
        count=9,
    )(beam, u, own, in_a, in_b, in_z, in_d, in_h, gy_a, gy_b)
    in_m = lax.ppermute(msg_m, "gz", pairs(nz, 0))
    part = (rows + 2 * SKIN, cols + SUBL, depth)
    (bulk,) = call(
        bulk_kernel, [t.shape], scratch=[(2, *part), part, part, part, part], scalars=1, count=6
    )(beam, t, m, in_z, in_d, part_a, part_b)
    gas, mine, other, mass = call(
        functools.partial(last_kernel, (rows_x, own_y)),
        [u.shape, (n_top // 2, *block), (n_top // 2, *block), (part_rows, LANES)],
        scratch=advance_scratch(n2, small, own_y + 2 * (REACH_LAST - 2), False) + [(part_rows, *block)],
        scalars=1,
        count=5,
    )(beam, g2, in_m, top_t, top_k, bulk)
    (gas,) = call(mass_kernel, [u.shape], scratch=[(n2, small, LANES)] * 2, count=3)(gas, in_m, mass)
    given = lax.ppermute(other, "gz", pairs(nz, 0))
    (out,) = call(seal_kernel, [t.shape], count=3)(bulk, mine, given)
    return gas, jnp.transpose(out, (2, 0, 1))


def solution(mesh):
    return jax.shard_map(
        shards,
        mesh=mesh,
        in_specs=(
            P(None, "gx", "gy", "gz"),
            P(None, ("gx", "gz"), "gy"),
            P(None, ("gx", "gz"), "gy"),
            P("gx", "gy"),
            P(),
        ),
        out_specs=(P(None, "gx", "gy", "gz"), P(None, ("gx", "gz"), "gy")),
        check_vma=False,
    )
```

```python
import functools

import jax
import jax.numpy as jnp
from jax import lax
from jax.experimental import pallas as pl
from jax.experimental.pallas import tpu as pltpu
from jax.sharding import PartitionSpec as P

STEPS = 2
SUBSTEPS = 2
GAS_STEP = 0.3
DRIFT_SPEED = 0.5
VAPOR_LOAD = 0.3
AMBIENT_LOAD = 0.7
STIFFNESS = 1.0
VISCOSITY = (0.2, 0.1, 0.15, 0.15, 0.15, 0.2)
HEAT_STEP = 1.0
POWDER_COND = 0.04
SOLID_COND = 0.15
LIQUID_COND = 0.09
LASER_POWER = 3.0
SPOT_RADIUS = 6.0
ABSORB_DEPTH = 4.0
BOIL_LEVEL = 1.0
BACK_PRESSURE = 0.5
LATENT_HEAT = 0.3
VAPOR_SOURCE = 0.5
RECOIL_PUSH = 0.4
RECOIL_PRESSURE = 0.6

COMPS = 6
LANES = 128
VMEM_LIMIT = 32 * 1024 * 1024
SUBL = 8
F32 = jnp.float32
REACH = 6
REACH_LAST = 3
SKIN = 4
TOP = 8
GROUP = 16
LEVEL = 2 * COMPS


def iota(shape, axis):
    return lax.broadcasted_iota(jnp.int32, shape, axis)


def wrapped(index, own, size):
    return jnp.where(index < own + (size - own) // 2, index, index - size)


def turn(value, amount, axis):
    size = value.shape[axis]
    if isinstance(amount, int):
        amount = amount % size
        if amount == 0:
            return value
    return pltpu.roll(value, amount, axis)


def softplus(x):
    return jnp.maximum(x, 0.0) + jnp.log1p(jnp.exp(-jnp.abs(x)))


def pack_heights(rows, base, lane, low_z, acc):
    more = jnp.where(low_z, 2, 0)
    for c, row in enumerate(rows):
        acc = jnp.where((lane & -2) == base + 2 * c, turn(row, base + 2 * c + more, 1), acc)
    return acc


def unpack_heights(packed, base, low_z, h0, h1, i):
    here = turn(packed, -base, 1)
    other = turn(packed, -base - 1, 1)
    h0[i] = jnp.where(low_z, here, other)
    h1[i] = jnp.where(low_z, other, here)


DEEP_5 = (2, 3, 4, 5)
DEEP_6 = (2, 5)
FULL = 4
QUARTERS = (5, 3, 2, 4)
NEAR = 3


def quarter_rows(rows_x, reach):
    far = [x for d in range(NEAR + 1, reach) for x in (-d, rows_x + d - 1)]
    return [(x, 0) for x in far] + [(x, FULL) for x in range(-1, rows_x + 1)]


def slab_index(c, layer, below):
    if layer <= FULL:
        return c * FULL + (FULL - layer if below else layer - 1)
    base = COMPS * FULL
    if layer == FULL + 1:
        return base + DEEP_5.index(c) if c in DEEP_5 else None
    return base + len(DEEP_5) + DEEP_6.index(c) if c in DEEP_6 else None


def slab_size():
    return COMPS * FULL + len(DEEP_5) + len(DEEP_6)


def row_tile(c, x, tile, u, in_a, in_b, even_x):
    rows_x = u.shape[1]
    span = slice(tile * SUBL, (tile + 1) * SUBL)
    if 0 <= x < rows_x:
        return u[c, x, span, :]
    k = slab_index(c, -x if x < 0 else x - rows_x + 1, x < 0)
    if k is None:
        return None
    low, high = (in_b, in_a) if x < 0 else (in_a, in_b)
    return jnp.where(even_x, low[k, span, :], high[k, span, :])


def conduct(v):
    return jnp.where(v == 0, POWDER_COND, jnp.where(v == 1, SOLID_COND, LIQUID_COND)).astype(F32)


def surface_tops(t, m):
    rows, cols = t.shape[0], t.shape[1]
    per = LANES // cols
    out = []
    for ref in (t, m):
        for j in range(rows // per):
            block = ref[j * per : (j + 1) * per].reshape(LANES, LANES)
            out.append(jnp.transpose(block)[:TOP])
    return out


def pack_kernel(
    reach, meta, u_in, t_in, m_in, lev_in, to_a, to_b, to_z, to_d, to_h, to_part,
    u, m, lev, out_z, out_d, out_h, part, sems,
):
    rows_x, own_y = u.shape[1], u.shape[2]
    rows, cols = m.shape[0], m.shape[1]
    t, k = part.at[0:rows], part.at[rows : 2 * rows]
    pairs_in = ((u_in, u), (t_in, t), (m_in, m), (lev_in, lev))
    fetches = [pltpu.make_async_copy(src, dst, sems.at[i]) for i, (src, dst) in enumerate(pairs_in)]
    for copy in fetches:
        copy.start()
    even = lax.rem(meta[0], 2) == 0
    low_z = meta[2] == 0
    tiles = own_y // SUBL
    copies = []

    def send(src, dst):
        copy = pltpu.make_async_copy(src, dst, sems.at[len(fetches) + len(copies)])
        copy.start()
        copies.append(copy)

    fetches[0].wait()
    for out, high in ((to_a, even), (to_b, jnp.logical_not(even))):
        first = jnp.where(high, rows_x - FULL, 0)
        for c in range(COMPS):
            send(u.at[c, pl.ds(first, FULL)], out.at[pl.ds(c * FULL, FULL)])
        base = COMPS * FULL
        row = jnp.where(high, rows_x - FULL - 1, FULL)
        send(u.at[pl.ds(DEEP_5[0], len(DEEP_5)), row], out.at[pl.ds(base, len(DEEP_5))])
        row = jnp.where(high, rows_x - reach, reach - 1)
        for j, c in enumerate(DEEP_6):
            send(u.at[c, row], out.at[base + len(DEEP_5) + j])
    for copy in fetches[1:]:
        copy.wait()
    k[...] = conduct(m[...])
    tops = surface_tops(t, k)
    for j, value in enumerate(tops):
        part[2 * rows, j * SUBL : (j + 1) * SUBL, :] = value
    for out in (to_a, to_b):
        for j in range(cols // own_y):
            send(part.at[2 * rows, pl.ds(j * own_y, own_y)], out.at[slab_size() + j])
    send(part, to_part)
    col_tiles = cols // SUBL
    n = 0
    for ref in (t, k):
        for r in range(SKIN):
            for y in range(col_tiles):
                lo = ref[r, y * SUBL : (y + 1) * SUBL, :]
                hi = ref[rows - SKIN + r, y * SUBL : (y + 1) * SUBL, :]
                out_z[n] = jnp.where(low_z, hi, lo)
                out_d[n] = jnp.where(low_z, lo, hi)
                n += 1
    for j, value in enumerate(tops):
        out_z[n + j] = value
        out_d[n + j] = value
    n += len(tops)
    size = u.shape[2]
    lane = iota((size, LANES), 1)
    eye = iota((size, size), 0) == iota((size, size), 1)
    levels = lev[...].astype(F32)
    acc = jnp.zeros((size, LANES), F32)
    for x in range(rows_x):
        acc = pack_heights([u[c, x] for c in range(COMPS)], x * GROUP, lane, low_z, acc)
        level = jnp.sum(jnp.where(eye, levels[x : x + 1, :], 0.0), axis=1, keepdims=True)
        acc = jnp.where((lane & -2) == x * GROUP + LEVEL, level, acc)
    for y in range(tiles):
        part = acc[y * SUBL : (y + 1) * SUBL]
        out_h[y] = part
        out_z[n + y] = part
        out_d[n + y] = part
    for src, dst in ((out_z, to_z), (out_d, to_d), (out_h, to_h)):
        send(src, dst)
    for copy in copies:
        copy.wait()


def hold_kernel(meta, u_in, part_in, u, part):
    u[...] = u_in[...]
    part[...] = part_in[...]


def part_row(r, tile, ref, at, rows, in_z, in_d, low_z, col_tiles, low_part):
    if 0 <= r < rows:
        return ref[r, tile * SUBL : (tile + 1) * SUBL, :]
    k = (at * SKIN + (r + SKIN if r < 0 else r - rows)) * col_tiles + tile
    low, high = (in_d[k], in_z[k]) if r < 0 else (in_z[k], in_d[k])
    return jnp.where(low_z, low, high)


def relay_kernel(cells, meta, u, part, in_a, in_b, in_z, in_d, in_h, out_a, out_b, part_a, part_b):
    rows = part.shape[0] // 2
    t, m = part.at[0:rows], part.at[rows : 2 * rows]
    rows_x, reach = cells
    gx, gy, gz = meta[0], meta[1], meta[2]
    even_x = lax.rem(gx, 2) == 0
    even_y = lax.rem(gy, 2) == 0
    low_z = gz == 0
    tiles = u.shape[2] // SUBL
    rows, cols = t.shape[0], t.shape[1]
    col_tiles = cols // SUBL
    half = SUBL // 2
    sub = iota((SUBL, LANES), 0)
    lane = iota((SUBL, LANES), 1)
    zero = jnp.zeros((SUBL, LANES), F32)

    def put(n, hi, lo):
        out_a[n] = jnp.where(even_y, hi, lo)
        out_b[n] = jnp.where(even_y, lo, hi)

    def both(c, x):
        pair = [row_tile(c, x, y, u, in_a, in_b, even_x) for y in (tiles - 1, 0)]
        return [zero if v is None else v for v in pair]

    n = 0
    for x in range(-NEAR, rows_x + NEAR):
        for c in range(0, COMPS, 2):
            (hi0, lo0), (hi1, lo1) = both(c, x), both(c + 1, x)
            put(n, jnp.where(sub < half, turn(hi1, half, 0), hi0), jnp.where(sub < half, lo0, turn(lo1, half, 0)))
            n += 1
    for x, skip in quarter_rows(rows_x, reach):
        hi = lo = zero
        for q, c in enumerate(QUARTERS):
            a, b = both(c, x)
            hi = jnp.where((sub & -2) == 2 * q, turn(a, 2 * q - (SUBL - 2 - skip), 0), hi)
            lo = jnp.where((sub & -2) == 2 * q, turn(b, 2 * q - skip, 0), lo)
        put(n, hi, lo)
        n += 1
    base = in_z.shape[0] - tiles
    hi_y, lo_y = tiles - 1, 0
    put(
        n,
        jnp.where(low_z, in_d[base + hi_y], in_h[hi_y]),
        jnp.where(low_z, in_d[base + lo_y], in_h[lo_y]),
    )
    put(n + 1, in_z[base + hi_y], in_z[base + lo_y])
    put(
        n + 2,
        jnp.where(low_z, in_h[hi_y], in_d[base + hi_y]),
        jnp.where(low_z, in_h[lo_y], in_d[base + lo_y]),
    )
    n += 3
    for r in range(-SKIN, rows + SKIN):
        hi_t, lo_t = [part_row(r, y, t, 0, rows, in_z, in_d, low_z, col_tiles, None) for y in (col_tiles - 1, 0)]
        hi_k, lo_k = [part_row(r, y, m, 1, rows, in_z, in_d, low_z, col_tiles, None) for y in (col_tiles - 1, 0)]
        hi = jnp.where(sub < half, turn(hi_k, half, 0), hi_t)
        lo = jnp.where(sub < half, lo_t, turn(lo_k, half, 0))
        part_a[r + SKIN] = jnp.where(even_y, hi, lo)
        part_b[r + SKIN] = jnp.where(even_y, lo, hi)
    sources = surface_sources(part, in_a, in_b, in_z, in_d, even_x, tiles)
    per = LANES // cols
    slot = lax.rem(lane, cols) // SUBL
    for v in range(len(sources) // per):
        hi = lo = zero
        for i in range(per):
            src = sources[v * per + i]
            hi = jnp.where(slot == i, turn(src, SUBL * i - (cols - SUBL), 1), hi)
            lo = jnp.where(slot == i, turn(src, SUBL * i, 1), lo)
        put(n + v, hi, lo)


def surface_sources(part, in_a, in_b, in_z, in_d, even_x, tiles):
    count = part.shape[1] // SUBL
    at = in_z.shape[0] - tiles - count

    def high(j):
        k, span = slab_size() + j // tiles, slice(j % tiles * SUBL, (j % tiles + 1) * SUBL)
        return jnp.where(even_x, in_a[k, span, :], in_b[k, span, :])

    out = []
    for a in range(2):
        span = range(a * count // 2, (a + 1) * count // 2)
        out += [part[part.shape[0] - 1, j * SUBL : (j + 1) * SUBL, :] for j in span]
        out += [in_z[at + j] for j in span]
        out += [high(j) for j in span]
        out += [in_d[at + j] for j in span]
    return out


def heat_source(row, col, beam, step):
    a = beam[step, 0].astype(F32)
    b = beam[step, 1].astype(F32)
    along_x = jnp.exp(-(((row - a) / SPOT_RADIUS) ** 2))
    along_y = jnp.exp(-(((col - b) / SPOT_RADIUS) ** 2))
    return LASER_POWER * along_x * along_y


def bulk_kernel(meta, beam, part, in_z, in_d, gy_a, gy_b, out, temp, cond, kx, ky, kz):
    rows = part.shape[0] // 2
    t, m = part.at[0:rows], part.at[rows : 2 * rows]
    gx, gy, gz = meta[0], meta[1], meta[2]
    even_y = lax.rem(gy, 2) == 0
    low_z = gz == 0
    rows, cols, depth = t.shape
    col_tiles = cols // SUBL
    half = SUBL // 2
    size = cols + SUBL
    n = rows + 2 * SKIN
    sub = iota((SUBL, LANES), 0)
    for i in range(n):
        for y in range(col_tiles):
            span = slice(y * SUBL, (y + 1) * SUBL)
            temp[0, i, span, :] = part_row(i - SKIN, y, t, 0, rows, in_z, in_d, low_z, col_tiles, None)
            cond[i, span, :] = part_row(i - SKIN, y, m, 1, rows, in_z, in_d, low_z, col_tiles, None)
        up = jnp.where(even_y, gy_a[i], gy_b[i])
        low = jnp.where(even_y, gy_b[i], gy_a[i])
        temp[0, i, cols:size, :] = jnp.where(sub < half, up, low)
        cond[i, cols:size, :] = turn(jnp.where(sub < half, low, up), half, 0)

    lane = iota((size, LANES), 1)
    for i in range(n):
        k = cond[i]
        if i + 1 < n:
            kx[i] = 0.5 * (k + cond[i + 1])
        ky[i] = 0.5 * (k + turn(k, -1, 0))
        kz[i] = 0.5 * (k + jnp.where(lane == depth - 1, 0.0, turn(k, -1, 1)))

    col_g = gy * cols + wrapped(iota((size, LANES), 0), cols, size)
    inside_y = jnp.where((col_g >= 0) & (col_g < meta[4] * cols), 1.0, 0.0)
    col_f = col_g.astype(F32)
    fall = jnp.exp(-lane.astype(F32) / ABSORB_DEPTH)
    first_row = (gx * meta[5] + gz) * rows - SKIN

    for s in range(STEPS * SUBSTEPS):
        src, dst = s % 2, 1 - s % 2
        last = s == STEPS * SUBSTEPS - 1
        a = beam[s, 0].astype(F32)
        b = beam[s, 1].astype(F32)
        spot = LASER_POWER * fall * jnp.exp(-(((col_f - b) / SPOT_RADIUS) ** 2))
        lo, hi = s + 1, n - 1 - s
        fx0 = kx[lo - 1] * (temp[src, lo] - temp[src, lo - 1])
        for i in range(lo, hi):
            v = temp[src, i]
            fx = kx[i] * (temp[src, i + 1] - v)
            fy = ky[i] * (turn(v, -1, 0) - v)
            fz = kz[i] * (jnp.where(lane == depth - 1, 0.0, turn(v, -1, 1)) - v)
            above = jnp.where(lane == 0, 0.5 * cond[i] * v, turn(fz, 1, 1))
            row = first_row + i
            along_x = jnp.exp(-((jnp.full((1, LANES), row.astype(F32) - a) / SPOT_RADIUS) ** 2))
            change = (fx - fx0) + (fy - turn(fy, 1, 0)) + (fz - above) + spot * along_x
            new = v + HEAT_STEP * change
            if last:
                out[i - SKIN] = new[:cols]
            else:
                ok = (row >= 0) & (row < meta[3] * meta[5] * rows)
                temp[dst, i] = new * (inside_y * jnp.where(ok, 1.0, 0.0))
            fx0 = fx


def seal_kernel(meta, bulk, mine, given, out):
    rows, cols, depth = bulk.shape
    per = LANES // cols
    lane = iota((LANES, LANES), 1)
    for j in range(mine.shape[0]):
        skin = jnp.where(meta[2] == 0, mine[j], given[j])
        skin = jnp.concatenate([skin, jnp.zeros((LANES - SUBL, LANES), F32)], axis=0)
        block = jnp.where(lane < SKIN, jnp.transpose(skin), bulk[j * per : (j + 1) * per].reshape(LANES, LANES))
        out[j * per : (j + 1) * per] = block.reshape(per, cols, LANES)


def pack_skin(t, rows, cols, scratch, out):
    per = LANES // cols
    lane = iota((SUBL, LANES), 1)
    for j in range(SUBL // per):
        acc = jnp.zeros((SUBL, LANES), F32)
        for q in range(per):
            acc = jnp.where(lane // cols == q, turn(scratch[rows + j * per + q], cols * q, 1), acc)
        out[j] = acc


def split(value):
    high = value.astype(jnp.bfloat16)
    rest = (value - high.astype(F32)).astype(jnp.bfloat16)
    return jnp.concatenate([high, rest], axis=1)


def height_matrix():
    shape = (2 * LANES, 2 * LANES)
    k = iota(shape, 0) & (LANES - 1)
    j = iota(shape, 1)
    above = jnp.where(k == (j & (LANES - 1)) + 1, 1.0, 0.0)
    below = jnp.where(k == (j & (LANES - 1)) - 1, 1.0, 0.0)
    return (above + jnp.where(j < LANES, -below, below)).astype(jnp.bfloat16)


def height_terms(ref, first, last, matrix, diff, total, start=0):
    size = diff.shape[2]
    for c in range(COMPS):
        rows = ref[c, first:last, start : start + size].reshape((last - first) * size, LANES)
        both = jnp.dot(split(rows), matrix, preferred_element_type=F32)
        diff[c, first:last] = both[:, :LANES].reshape(last - first, size, LANES)
        total[c, first:last] = both[:, LANES:].reshape(last - first, size, LANES)


def cut_weights(low_z, scale):
    lane = iota((1, LANES), 1)
    up = (lane == LANES - 1) & low_z
    down = (lane == 0) & jnp.logical_not(low_z)
    weight = {}
    for v in sorted(set(VISCOSITY)):
        side = scale * GAS_STEP * v
        drift = 0.5 * DRIFT_SPEED * scale * GAS_STEP
        weight[v] = jnp.where(up, side - drift, jnp.where(down, side + drift, 0.0))
    return jnp.where(up, 1.0, jnp.where(down, -1.0, 0.0)), weight


def stepped(comps, ref, i, diff, total, h, cut, scale, start, size, skip=0):
    sign, weight = cut
    half = 0.5 * scale * GAS_STEP
    span = pl.ds(start, size)
    terms = pl.ds(start - skip, size)

    def dx(c):
        return ref[c, i + 1, span, :] - ref[c, i - 1, span, :]

    def dy(c):
        return ref[c, i, pl.ds(start + 1, size), :] - ref[c, i, pl.ds(start - 1, size), :]

    def dz(c):
        return diff[c, i, terms, :] + sign * h[i, span, 2 * c : 2 * c + 1]

    spread = half * (dx(2) + dy(3) + dz(4))
    out = {}
    for c in comps:
        v = VISCOSITY[c]
        side = scale * GAS_STEP * v
        drift = 0.5 * DRIFT_SPEED * scale * GAS_STEP
        sides = (ref[c, i + 1, span, :] + ref[c, i - 1, span, :]) + (
            ref[c, i, pl.ds(start + 1, size), :] + ref[c, i, pl.ds(start - 1, size), :]
        )
        across = h[i, span, 2 * c : 2 * c + 1]
        new = (
            scale * (1.0 - 6.0 * GAS_STEP * v) * ref[c, i, span, :]
            + side * (sides + total[c, i, terms, :])
            - drift * diff[c, i, terms, :]
            + weight[v] * across
        )
        if c == 2:
            new = new - half * dx(5)
        elif c == 3:
            new = new - half * dy(5)
        elif c == 4:
            new = new - half * dz(5)
        else:
            new = new - {0: VAPOR_LOAD, 1: AMBIENT_LOAD, 5: STIFFNESS}[c] * spread
        out[c] = new
    return out


def by_comp(lane, values):
    out = jnp.full(lane.shape, values[-1], F32)
    for c, v in enumerate(values[:-1]):
        out = jnp.where(lane == 2 * c, v, out)
    return out


def couple_matrix():
    shape = (6 * LANES, LANES)
    k = iota(shape, 0)
    j = iota(shape, 1)
    axis = k // (2 * LANES)
    lane = k & (LANES - 1)
    spread = (lane == 4 + 2 * axis) & ((j == 0) | (j == 2) | (j == 10))
    slope = (lane == 10) & (j == 4 + 2 * axis)
    return jnp.where(spread | slope, 1.0, 0.0).astype(jnp.bfloat16)


def halo_stepped(h0, h1, g, low_z, mask_of, start, size, out, at):
    n = h0.shape[0]
    span = slice(start, start + size)
    rows = (n - 2) * size
    lane = iota((1, LANES), 1)
    more = jnp.where(low_z, 1, 0)
    flat_lane = iota((rows, LANES), 1)
    touch = jnp.zeros((rows, LANES), F32)
    for c in range(COMPS):
        own = g[c, 1 : n - 1, span].reshape(rows, LANES)
        touch = jnp.where(flat_lane == 2 * c, turn(own, 2 * c + more, 1), touch)
    mid = h0[1 : n - 1, span].reshape(rows, LANES)
    east = h0[2:n, span].reshape(rows, LANES)
    west = h0[0 : n - 2, span].reshape(rows, LANES)
    if start:
        north = h0[1 : n - 1, start + 1 : start + size + 1].reshape(rows, LANES)
        south = h0[1 : n - 1, start - 1 : start + size - 1].reshape(rows, LANES)
    else:
        north, south = turn(mid, -1, 0), turn(mid, 1, 0)
    behind = h1[1 : n - 1, span].reshape(rows, LANES)
    slopes = [east - west, north - south, jnp.where(low_z, 1.0, -1.0) * (behind - touch)]
    coupled = jnp.dot(
        jnp.concatenate([split(v) for v in slopes], axis=1), couple_matrix(), preferred_element_type=F32
    )
    up = by_comp(lane, [GAS_STEP * (v - 0.5 * DRIFT_SPEED) for v in VISCOSITY])
    down = by_comp(lane, [GAS_STEP * (v + 0.5 * DRIFT_SPEED) for v in VISCOSITY])
    half = 0.5 * GAS_STEP
    pull = by_comp(lane, [-half * VAPOR_LOAD, -half * AMBIENT_LOAD, -half, -half, -half, -half * STIFFNESS])
    new = (
        by_comp(lane, [1.0 - 6.0 * GAS_STEP * v for v in VISCOSITY]) * mid
        + by_comp(lane, [GAS_STEP * v for v in VISCOSITY]) * ((east + west) + (north + south))
        + jnp.where(low_z, up, down) * behind
        + jnp.where(low_z, down, up) * touch
        + pull * coupled
    )
    for i in range(1, n - 1):
        row = new[(i - 1) * size : i * size] * mask_of(i, start, size)
        if at < 0:
            row, at_row = turn(row, at, 0), 0
        else:
            at_row = at
        out[i - 1, at_row : at_row + size] = row


def grid_masks(meta, n, size, own_x, own_y):
    before, before_y = (n - own_x) // 2, (size - own_y) // 2

    def mask_of(i, start, count):
        x_g = meta[0] * own_x + i - before
        ok = (x_g >= 0) & (x_g < meta[3] * own_x)
        y_g = meta[1] * own_y + iota((count, LANES), 0) + start - before_y
        return jnp.where((y_g >= 0) & (y_g < meta[4] * own_y), 1.0, 0.0) * jnp.where(ok, 1.0, 0.0)

    return mask_of


def first_stage(meta, g, h0, windows, f, mask_of, unroll):
    n = g.shape[1]
    cut = cut_weights(meta[2] == 0, 1.0)

    def one(comps):
        def body(i, carry):
            for start, size, diff, total, skip, at in windows:
                new = stepped(comps, g, i, diff, total, h0, cut, 1.0, start, size, skip)
                m = mask_of(i, start, size)
                for c in comps:
                    f[c, i - 1, at : at + size, :] = new[c] * m
            return carry

        return body

    lax.fori_loop(2, n - 2, one(tuple(range(COMPS))), 0, unroll=unroll)
    for i in (1, n - 2):
        one((2, 5))(i, 0)


def second_stage(meta, g, f, fh, diff, total, skip, reach, own_y, mask_of, store, unroll):
    n = g.shape[1]
    height_terms(f, 1, n - 3, height_matrix(), diff, total)
    start = (g.shape[2] - own_y) // 2 - reach
    count = own_y + 2 * reach
    cut = cut_weights(meta[2] == 0, 0.5)

    def two(comps):
        def body(i, carry):
            new = stepped(comps, f, i - 1, diff, total, fh, cut, 0.5, start - skip, count)
            m = mask_of(i, start, count)
            for c in comps:
                new[c] = (0.5 * g[c, i, pl.ds(start, count), :] + new[c]) * m
            store(i, new)
            return carry

        return body

    outer = 1 if reach > 1 else 0
    lax.fori_loop(3 + outer, n - 3 - outer, two(tuple(range(COMPS))), 0, unroll=unroll)
    for i in (2, n - 3):
        two((5,))(i, 0)
    if outer:
        for i in (3, n - 4):
            two((2, 5))(i, 0)


def lane_sums(value):
    high = value.astype(jnp.bfloat16)
    rest = value - high.astype(F32)
    middle = rest.astype(jnp.bfloat16)
    low = (rest - middle.astype(F32)).astype(jnp.bfloat16)
    parts = jnp.concatenate([high, middle, low], axis=1)
    ones = jnp.ones((3 * LANES, LANES), jnp.bfloat16)
    return jnp.dot(parts, ones, preferred_element_type=F32)


def fine_pressure(meta, p, h0, own_x, own_y, part_rows):
    n, count = p.shape[0], p.shape[1]
    skip = (h0.shape[1] - count) // 2
    skip_x = (h0.shape[0] - n) // 2
    before = (n - own_x) // 2
    y_l = iota((count, LANES), 0) - (count - own_y) // 2
    col_y = lax.div(wrapped(iota((count, LANES), 1), 2 * own_y, LANES) + LANES, 2) - LANES // 2
    pick = col_y == y_l
    row_x = lax.div(wrapped(iota((part_rows, LANES), 0), 2 * own_x, part_rows) + LANES, 2) - LANES // 2
    height = (iota((count, LANES), 1) + meta[2] * LANES).astype(F32)
    fine = jnp.zeros((part_rows, LANES), F32)
    full = -(-count // SUBL) * SUBL
    pad = [jnp.zeros((full - count, LANES), F32)] if full > count else []
    found = []
    for i in range(n):
        level = h0[i + skip_x, skip : skip + count, LEVEL : LEVEL + 1]
        found += [jnp.where(height == level, p[i], 0.0)] + pad
    at = lane_sums(jnp.concatenate(found, axis=0))
    for i in range(n):
        line = jnp.sum(jnp.where(pick, at[i * full : i * full + count], 0.0), axis=0, keepdims=True)
        fine = jnp.where(row_x == i - before, line, fine)
    return fine


def top_heat(meta, beam, first, t, k, fine, own_rows, cols):
    gx, gy = meta[0], meta[1]
    shape = fine.shape
    row = gx * own_rows + wrapped(iota(shape, 0), own_rows, shape[0])
    col = gy * cols + wrapped(iota(shape, 1), cols, shape[1])
    row, col = row.astype(F32), col.astype(F32)
    deep = TOP - 1 - first
    kx = [0.5 * (v + turn(v, -1, 0)) for v in k[:deep]]
    ky = [0.5 * (v + turn(v, -1, 1)) for v in k[:deep]]
    kz = [0.5 * (k[d] + k[d + 1]) for d in range(deep)]
    for s in range(SUBSTEPS):
        beam_xy = heat_source(row, col, beam, first + s)
        before = 0.5 * k[0] * t[0]
        new = []
        for d in range(TOP - 1 - first - s):
            fx = kx[d] * (turn(t[d], -1, 0) - t[d])
            fy = ky[d] * (turn(t[d], -1, 1) - t[d])
            fz = kz[d] * (t[d + 1] - t[d])
            factor = jnp.exp(jnp.full(shape, -d / ABSORB_DEPTH, F32))
            change = (fx - turn(fx, 1, 0)) + (fy - turn(fy, 1, 1)) + (fz - before) + beam_xy * factor
            if d == 0:
                change = change - LATENT_HEAT * softplus(t[0] - BOIL_LEVEL - BACK_PRESSURE * fine)
            new.append(jnp.where(k[d] > 0, t[d] + HEAT_STEP * change, 0.0))
            before = fz
        t = new
    return t


def vapor_mass(t0, fine):
    four = t0 + turn(t0, -1, 1)
    four = four + turn(four, -1, 0)
    return softplus(0.25 * four - BOIL_LEVEL - BACK_PRESSURE * fine)


def mass_rows(meta, h, mass, first, rows, count, own_y):
    skip = (h.shape[1] - count) // 2
    skip_x = (h.shape[0] - rows) // 2
    y_l = iota((count, LANES), 0) - (count - own_y) // 2
    col = wrapped(iota((count, LANES), 1), 2 * own_y, LANES)
    pick = col == 2 * y_l
    height = (iota((count, LANES), 1) + meta[2] * LANES).astype(F32)
    found = []
    for i in range(rows):
        r = (2 * (i + first)) % mass.shape[0]
        found.append(jnp.where(pick, mass[r : r + 1, :], 0.0))
    at = lane_sums(jnp.concatenate(found, axis=0))
    out = []
    for i in range(rows):
        level = h[i + skip_x, skip : skip + count, LEVEL : LEVEL + 1]
        out.append(jnp.where(height == level, at[i * count : (i + 1) * count], 0.0))
    return out


def inner_kernel(cells, meta, u, in_a, in_b, in_z, in_d, in_h, g, f, h0, h1, fh, diff, total):
    rows_x, reach = cells
    even_x = lax.rem(meta[0], 2) == 0
    low_z = meta[2] == 0
    own_y = u.shape[2]
    tiles = own_y // SUBL
    size = g.shape[2]
    n = g.shape[1]
    zero = jnp.zeros((SUBL, LANES), F32)
    for x in range(-reach, rows_x + reach):
        for c in range(COMPS):
            for y in range(tiles):
                value = row_tile(c, x, y, u, in_a, in_b, even_x)
                g[c, x + reach, (y + 1) * SUBL : (y + 2) * SUBL, :] = zero if value is None else value
    base = in_z.shape[0] - tiles
    for b in range(3):
        parts = []
        for y in range(tiles):
            if b == 0:
                parts.append(jnp.where(low_z, in_d[base + y], in_h[y]))
            elif b == 1:
                parts.append(in_z[base + y])
            else:
                parts.append(jnp.where(low_z, in_h[y], in_d[base + y]))
        unpack_group(jnp.concatenate(parts, axis=0), b, rows_x, reach, low_z, h0, h1, SUBL, own_y)
    mask_of = grid_masks(meta, n, size, rows_x, own_y)
    halo_stepped(h0, h1, g, low_z, mask_of, SUBL, own_y, fh, 0)
    height_terms(g, 1, n - 1, height_matrix(), diff, total, SUBL)
    first_stage(meta, g, h0, [(SUBL, own_y, diff, total, SUBL, 0)], f, mask_of, 4)


def unpack_group(packed, b, rows_x, reach, low_z, h0, h1, start, size):
    for x in range(-reach, rows_x + reach):
        if (x + rows_x) // rows_x == b:
            base = GROUP * ((x + rows_x) % rows_x)
            here, other = turn(packed, -base, 1), turn(packed, -base - 1, 1)
            h0[x + reach, start : start + size] = jnp.where(low_z, here, other)
            h1[x + reach, start : start + size] = jnp.where(low_z, other, here)


def first_kernel(
    cells, meta, beam, part, in_a, in_b, in_z, in_d, gy_a, gy_b, g_in, f_in, h0_in, h1_in, fh_in,
    out_g, out_m, out_t, out_k, g, h, h1, f, fh, diff_lo, total_lo, diff_hi, total_hi, diff, total, p, mass, skin,
):
    rows_x, reach = cells
    gx, gy, gz = meta[0], meta[1], meta[2]
    even_x = lax.rem(gx, 2) == 0
    even_y = lax.rem(gy, 2) == 0
    low_z = gz == 0
    n, size = g.shape[1], g.shape[2]
    own_y = size - 2 * SUBL
    tiles = own_y // SUBL
    half = SUBL // 2
    sub = iota((SUBL, LANES), 0)
    zero = jnp.zeros((SUBL, LANES), F32)
    inner = slice(SUBL, SUBL + own_y)

    def side(k):
        upper = jnp.where(even_y, gy_a[k], gy_b[k])
        lower = jnp.where(even_y, gy_b[k], gy_a[k])
        return upper, lower

    quarter = (rows_x + 2 * NEAR) * COMPS // 2
    places_of = {}
    for k, (x, skip) in enumerate(quarter_rows(rows_x, reach)):
        places_of[x, skip] = quarter + k
    for x in range(-reach, rows_x + reach):
        i = x + reach
        for c in range(COMPS):
            g[c, i, inner, :] = g_in[c, i, inner, :]
            upper = lower = zero
            if -NEAR <= x < rows_x + NEAR:
                near_up, near_low = side((x + NEAR) * COMPS // 2 + c // 2)
                if c % 2:
                    near_up, near_low = turn(near_up, half, 0), turn(near_low, half, 0)
                upper = jnp.where(sub < half, near_up, 0.0)
                lower = jnp.where(sub >= half, near_low, 0.0)
            for skip in (0, FULL):
                if (x, skip) in places_of and c in QUARTERS:
                    q = 2 * QUARTERS.index(c)
                    up, low = side(places_of[x, skip])
                    upper = jnp.where((sub & -2) == skip, turn(up, skip - q, 0), upper)
                    lower = jnp.where((sub & -2) == SUBL - 2 - skip, turn(low, SUBL - 2 - skip - q, 0), lower)
            g[c, i, own_y + SUBL : size, :] = upper
            g[c, i, :SUBL, :] = lower
    h[:, inner, :] = h0_in[:, inner, :]
    h1[:, inner, :] = h1_in[:, inner, :]
    for b in range(3):
        upper, lower = side(quarter + len(places_of) + b)
        unpack_group(lower, b, rows_x, reach, low_z, h, h1, 0, SUBL)
        unpack_group(upper, b, rows_x, reach, low_z, h, h1, own_y + SUBL, SUBL)

    def store(i, new):
        p[i - 2] = new[COMPS - 1]
        if len(new) > 1:
            for c in range(COMPS):
                out_g[c, i - 3] = new[c] if c in new else jnp.zeros_like(new[COMPS - 1])

    mask_of = grid_masks(meta, n, size, rows_x, own_y)
    f[:, :, inner, :] = f_in[...]
    fh[:, inner, :] = fh_in[...]
    upper_at = size - SUBL - 1
    windows = []
    for start, d, t in ((1, diff_lo, total_lo), (upper_at, diff_hi, total_hi)):
        halo_stepped(h, h1, g, low_z, mask_of, start, SUBL, fh, start)
        height_terms(g, 1, n - 1, height_matrix(), d, t, start)
        windows.append((start, SUBL, d, t, start, start))
    first_stage(meta, g, h, windows, f, mask_of, 4)
    second_stage(meta, g, f, fh, diff, total, 0, reach - 2, own_y, mask_of, store, 4)
    fine = fine_pressure(meta, p, h, rows_x, own_y, mass.shape[0])

    cols = LANES // 4
    per = LANES // cols
    lane = iota((SUBL, LANES), 1)
    sources = surface_sources(part, in_a, in_b, in_z, in_d, even_x, tiles)
    count = len(sources) // 2
    top_at = gy_a.shape[0] - len(sources) // per
    layers = []
    for a in range(2):
        for s in range(count):
            src = sources[a * count + s]
            upper, lower = side(top_at + (a * count + s) // per)
            i = s % per
            for q in range(per):
                at = cols * q + SUBL * i
                skin[s * per + q] = jnp.where(
                    lane < cols,
                    turn(src, -cols * q, 1),
                    jnp.where(
                        lane < cols + SUBL,
                        turn(upper, cols - at, 1),
                        jnp.where(lane >= LANES - SUBL, turn(lower, LANES - SUBL - at, 1), 0.0),
                    ),
                )
        for d in range(TOP):
            layers.append(skin[:, d, :])
    t, k = layers[:TOP], layers[TOP:]
    t = top_heat(meta, beam, 0, t, k, fine, 2 * rows_x, cols)
    for d in range(TOP - SUBSTEPS):
        out_t[d] = t[d]
        out_k[d] = k[d]
    mass[...] = vapor_mass(t[0], fine)

    count, small = out_g.shape[1], out_g.shape[2]
    masses = mass_rows(meta, h, mass, -REACH_LAST, count, small, own_y)
    lane_s = iota((small, LANES), 1)
    y_g = gy * own_y + iota((small, LANES), 0) - (small - own_y) // 2
    inside_y = jnp.where((y_g >= 0) & (y_g < meta[4] * own_y), 1.0, 0.0)
    skip = (size - small) // 2
    per = LANES // GROUP
    acc = jnp.zeros((small, LANES), F32)
    for i in range(count):
        x = i - REACH_LAST
        x_g = gx * rows_x + x
        ok = jnp.where((x_g >= 0) & (x_g < meta[3] * rows_x), 1.0, 0.0)
        add = masses[i] * (inside_y * ok)
        rows = [out_g[c, i] for c in range(COMPS)]
        for c, load in ((0, VAPOR_SOURCE), (4, RECOIL_PUSH), (5, RECOIL_PRESSURE)):
            rows[c] = rows[c] + load * add
            out_g[c, i] = rows[c]
        j, q = divmod(i, per)
        acc = pack_heights(rows, GROUP * q, lane_s, low_z, acc)
        level = h[x + reach, skip : skip + small, LEVEL : LEVEL + 1]
        acc = jnp.where((lane_s & -2) == GROUP * q + LEVEL, level, acc)
        if q == per - 1 or i == count - 1:
            out_m[j] = acc
            acc = jnp.zeros((small, LANES), F32)


def last_kernel(
    cells, meta, beam, g, in_m, in_t, in_k, bulk, out_g, out_t, out_f, mass, h, h1, f, fh, diff, total, p, skin
):
    rows_x, own_y = cells
    for i in range(g.shape[1]):
        j, q = divmod(i, LANES // GROUP)
        unpack_heights(in_m[j], GROUP * q, meta[2] == 0, h, h1, i)

    def store(i, new):
        p[i - 2] = new[COMPS - 1]
        if len(new) == COMPS:
            for c in range(COMPS):
                out_g[c, i - 3] = new[c][1 : own_y + 1]

    n, size = g.shape[1], g.shape[2]
    mask_of = grid_masks(meta, n, size, rows_x, own_y)
    halo_stepped(h, h1, g, meta[2] == 0, mask_of, 0, size, fh, -1)
    height_terms(g, 1, n - 1, height_matrix(), diff, total)
    first_stage(meta, g, h, [(1, size - 2, diff, total, 0, 0)], f, mask_of, True)
    second_stage(meta, g, f, fh, diff, total, 1, REACH_LAST - 2, own_y, mask_of, store, True)
    fine = fine_pressure(meta, p, h, rows_x, own_y, mass.shape[0])
    cols = LANES // 4
    t = [in_t[d] for d in range(TOP - SUBSTEPS)]
    k = [in_k[d] for d in range(TOP - SUBSTEPS)]
    t = top_heat(meta, beam, SUBSTEPS, t, k, fine, 2 * rows_x, cols)
    skin[...] = jnp.zeros_like(skin)
    for d in range(SKIN):
        skin[:, d, :] = t[d]
    pack_skin(t, 0, cols, skin, out_t)
    pack_skin(t, SUBL, cols, skin, out_f)
    mass[...] = vapor_mass(t[0], fine)


def mass_kernel(meta, gas, in_m, mass, out_g, h, h1):
    rows_x, own_y = gas.shape[1], gas.shape[2]
    n = h.shape[0]
    for i in range((n - rows_x) // 2, (n + rows_x) // 2):
        j, q = divmod(i, LANES // GROUP)
        unpack_heights(in_m[j], GROUP * q, meta[2] == 0, h, h1, i)
    masses = mass_rows(meta, h, mass, 0, rows_x, own_y, own_y)
    loads = {0: VAPOR_SOURCE, 4: RECOIL_PUSH, 5: RECOIL_PRESSURE}
    for x in range(rows_x):
        for c in range(COMPS):
            out_g[c, x] = gas[c, x] + loads[c] * masses[x] if c in loads else gas[c, x]


def places():
    axes = ("gx", "gy", "gz")
    return [lax.axis_index(a) for a in axes] + [lax.axis_size(a) for a in axes]


def call(body, outs, scratch=(), scalars=0, count=0):
    def kernel(*refs):
        body(places(), *refs)

    vmem = pl.BlockSpec(memory_space=pltpu.VMEM)
    smem = pl.BlockSpec(memory_space=pltpu.SMEM)
    return pl.pallas_call(
        kernel,
        out_shape=[jax.ShapeDtypeStruct(s, F32) for s in outs],
        in_specs=[smem] * scalars + [vmem] * count,
        out_specs=[vmem] * len(outs),
        scratch_shapes=[pltpu.VMEM(s, F32) for s in scratch],
        compiler_params=pltpu.CompilerParams(vmem_limit_bytes=VMEM_LIMIT),
    )


def pairs(count, odd):
    out = []
    for i in range(odd, count - 1, 2):
        out += [(i, i + 1), (i + 1, i)]
    return out


def cross(nx, nz, upper):
    out = []
    for i in range(nx - 1):
        a, b = i * nz + (nz - 1 if upper else 0), (i + 1) * nz + (0 if upper else nz - 1)
        out += [(a, b), (b, a)]
    return out


def shards(u, t, m, lev, beam):
    nx, ny, nz = (lax.axis_size(a) for a in ("gx", "gy", "gz"))
    _, rows_x, own_y, _ = u.shape
    t, m = jnp.transpose(t, (1, 2, 0)), jnp.transpose(m, (1, 2, 0))
    rows, cols, depth = t.shape
    tiles = own_y // SUBL
    block = (SUBL, LANES)
    n_top = 2 * rows * cols // LANES
    top = (n_top // tiles, own_y, LANES)
    n_x = slab_size() + top[0]
    n_z = 2 * SKIN * cols // SUBL + n_top + tiles
    vmem = pl.BlockSpec(memory_space=pltpu.VMEM)
    hbm = pl.BlockSpec(memory_space=pltpu.HBM)

    def pack(*refs):
        pack_kernel(REACH, places(), *refs)

    whole = (2 * rows + 1, cols, depth)
    copies = 4 + 2 * (COMPS + 1 + len(DEEP_6) + top[0]) + 4
    shapes = [(n_x, own_y, LANES)] * 2 + [(n_z, *block)] * 2 + [(tiles, *block), whole]
    msg_a, msg_b, msg_z, msg_d, msg_h, part = pl.pallas_call(
        pack,
        out_shape=[jax.ShapeDtypeStruct(v, F32) for v in shapes],
        in_specs=[hbm] * 4,
        out_specs=[hbm] * 6,
        scratch_shapes=[pltpu.VMEM(u.shape, F32), pltpu.VMEM(m.shape, jnp.int32), pltpu.VMEM(lev.shape, jnp.int32)]
        + [pltpu.VMEM(v, F32) for v in shapes[2:]]
        + [pltpu.SemaphoreType.DMA((copies,))],
        compiler_params=pltpu.CompilerParams(vmem_limit_bytes=60 * 1024 * 1024),
    )(u, t, m, lev)
    u, part = call(hold_kernel, [u.shape, whole], count=2)(u, part)
    in_a = lax.ppermute(msg_a, "gx", pairs(nx, 0))
    in_b = lax.ppermute(msg_b, "gx", pairs(nx, 1))
    in_z = lax.ppermute(msg_z, "gz", pairs(nz, 0))
    in_d = lax.ppermute(msg_d, ("gx", "gz"), cross(nx, nz, True))
    in_h = lax.ppermute(msg_h, ("gx", "gz"), cross(nx, nz, False))
    n_y = (rows_x + 2 * NEAR) * COMPS // 2 + len(quarter_rows(rows_x, REACH)) + 3 + n_top
    n_part = rows + 2 * SKIN
    msg_a, msg_b, part_a, part_b = call(
        functools.partial(relay_kernel, (rows_x, REACH)), [(n_y, *block)] * 2 + [(n_part, *block)] * 2, count=7
    )(u, part, in_a, in_b, in_z, in_d, in_h)
    gy_b = lax.ppermute(msg_b, "gy", pairs(ny, 1))
    gy_a = lax.ppermute(msg_a, "gy", pairs(ny, 0))
    part_b = lax.ppermute(part_b, "gy", pairs(ny, 1))
    part_a = lax.ppermute(part_a, "gy", pairs(ny, 0))

    size = own_y + 2 * SUBL
    n = rows_x + 2 * REACH
    n2 = rows_x + 2 * REACH_LAST
    small = own_y + SUBL
    part_rows = 4 * SUBL
    n_m = -(-n2 // (LANES // GROUP))
    row = (size, LANES)
    own_row = (own_y, LANES)
    g1, f1, h0, h1, fh1 = call(
        functools.partial(inner_kernel, (rows_x, REACH)),
        [(COMPS, n, *row), (COMPS, n - 2, *own_row), (n, *row), (n, *row), (n - 2, *own_row)],
        scratch=[(COMPS, n - 1, *own_row)] * 2,
        count=6,
    )(u, in_a, in_b, in_z, in_d, in_h)
    g2, msg_m, top_t, top_k = call(
        functools.partial(first_kernel, (rows_x, REACH)),
        [
            (COMPS, n2, small, LANES),
            (n_m, small, LANES),
            (TOP - SUBSTEPS, part_rows, LANES),
            (TOP - SUBSTEPS, part_rows, LANES),
        ],
        scratch=[(COMPS, n, *row), (n, *row), (n, *row), (COMPS, n - 2, *row), (n - 2, *row)]
        + [(COMPS, n - 1, *block)] * 4
        + [(COMPS, n - 3, *row)] * 2
        + [(n - 4, own_y + 2 * (REACH - 2), LANES), (part_rows, LANES), (part_rows, *block)],
        scalars=1,
        count=12,
    )(beam, part, in_a, in_b, in_z, in_d, gy_a, gy_b, g1, f1, h0, h1, fh1)
    in_m = lax.ppermute(msg_m, "gz", pairs(nz, 0))
    field = (rows + 2 * SKIN, cols + SUBL, depth)
    (bulk,) = call(
        bulk_kernel, [t.shape], scratch=[(2, *field), field, field, field, field], scalars=1, count=5
    )(beam, part, in_z, in_d, part_a, part_b)
    gas, mine, other, mass = call(
        functools.partial(last_kernel, (rows_x, own_y)),
        [u.shape, (n_top // 2, *block), (n_top // 2, *block), (part_rows, LANES)],
        scratch=[(n2, small, LANES)] * 2
        + [(COMPS, n2 - 2, small, LANES), (n2 - 2, small, LANES)]
        + [(COMPS, n2 - 1, small, LANES)] * 2
        + [(n2 - 4, own_y + 2 * (REACH_LAST - 2), LANES), (part_rows, *block)],
        scalars=1,
        count=5,
    )(beam, g2, in_m, top_t, top_k, bulk)
    (gas,) = call(mass_kernel, [u.shape], scratch=[(n2, small, LANES)] * 2, count=3)(gas, in_m, mass)
    given = lax.ppermute(other, "gz", pairs(nz, 0))
    (out,) = call(seal_kernel, [t.shape], count=3)(bulk, mine, given)
    return gas, jnp.transpose(out, (2, 0, 1))


def solution(mesh):
    return jax.shard_map(
        shards,
        mesh=mesh,
        in_specs=(
            P(None, "gx", "gy", "gz"),
            P(None, ("gx", "gz"), "gy"),
            P(None, ("gx", "gz"), "gy"),
            P("gx", "gy"),
            P(),
        ),
        out_specs=(P(None, "gx", "gy", "gz"), P(None, ("gx", "gz"), "gy")),
        check_vma=False,
    )
```

```python
import functools

import jax
import jax.numpy as jnp
from jax import lax
from jax.experimental import pallas as pl
from jax.experimental.pallas import tpu as pltpu
from jax.sharding import PartitionSpec as P

STEPS = 2
SUBSTEPS = 2
GAS_STEP = 0.3
DRIFT_SPEED = 0.5
VAPOR_LOAD = 0.3
AMBIENT_LOAD = 0.7
STIFFNESS = 1.0
VISCOSITY = (0.2, 0.1, 0.15, 0.15, 0.15, 0.2)
HEAT_STEP = 1.0
POWDER_COND = 0.04
SOLID_COND = 0.15
LIQUID_COND = 0.09
LASER_POWER = 3.0
SPOT_RADIUS = 6.0
ABSORB_DEPTH = 4.0
BOIL_LEVEL = 1.0
BACK_PRESSURE = 0.5
LATENT_HEAT = 0.3
VAPOR_SOURCE = 0.5
RECOIL_PUSH = 0.4
RECOIL_PRESSURE = 0.6

COMPS = 6
LANES = 128
VMEM_LIMIT = 32 * 1024 * 1024
SUBL = 8
F32 = jnp.float32
REACH = 6
REACH_LAST = 3
SKIN = 4
TOP = 8
GROUP = 16
LEVEL = 2 * COMPS


def iota(shape, axis):
    return lax.broadcasted_iota(jnp.int32, shape, axis)


def wrapped(index, own, size):
    return jnp.where(index < own + (size - own) // 2, index, index - size)


def turn(value, amount, axis):
    size = value.shape[axis]
    if isinstance(amount, int):
        amount = amount % size
        if amount == 0:
            return value
    return pltpu.roll(value, amount, axis)


def softplus(x):
    return jnp.maximum(x, 0.0) + jnp.log1p(jnp.exp(-jnp.abs(x)))


def pack_heights(rows, base, lane, low_z, acc):
    more = jnp.where(low_z, 2, 0)
    for c, row in enumerate(rows):
        acc = jnp.where((lane & -2) == base + 2 * c, turn(row, base + 2 * c + more, 1), acc)
    return acc


def unpack_heights(packed, base, low_z, h0, h1, i):
    here = turn(packed, -base, 1)
    other = turn(packed, -base - 1, 1)
    h0[i] = jnp.where(low_z, here, other)
    h1[i] = jnp.where(low_z, other, here)


DEEP_5 = (2, 3, 4, 5)
DEEP_6 = (2, 5)
FULL = 4
QUARTERS = (5, 3, 2, 4)
NEAR = 3


def quarter_rows(rows_x, reach):
    far = [x for d in range(NEAR + 1, reach) for x in (-d, rows_x + d - 1)]
    return [(x, 0) for x in far] + [(x, FULL) for x in range(-1, rows_x + 1)]


def slab_index(c, layer, below):
    if layer <= FULL:
        return c * FULL + (FULL - layer if below else layer - 1)
    base = COMPS * FULL
    if layer == FULL + 1:
        return base + DEEP_5.index(c) if c in DEEP_5 else None
    return base + len(DEEP_5) + DEEP_6.index(c) if c in DEEP_6 else None


def slab_size():
    return COMPS * FULL + len(DEEP_5) + len(DEEP_6)


def row_tile(c, x, tile, u, in_a, in_b, even_x):
    rows_x = u.shape[1]
    span = slice(tile * SUBL, (tile + 1) * SUBL)
    if 0 <= x < rows_x:
        return u[c, x, span, :]
    k = slab_index(c, -x if x < 0 else x - rows_x + 1, x < 0)
    if k is None:
        return None
    low, high = (in_b, in_a) if x < 0 else (in_a, in_b)
    return jnp.where(even_x, low[k, span, :], high[k, span, :])


def conduct(v):
    return jnp.where(v == 0, POWDER_COND, jnp.where(v == 1, SOLID_COND, LIQUID_COND)).astype(F32)


def surface_tops(t, m):
    rows, cols = t.shape[0], t.shape[1]
    per = LANES // cols
    out = []
    for ref in (t, m):
        for j in range(rows // per):
            block = ref[j * per : (j + 1) * per].reshape(LANES, LANES)
            out.append(jnp.transpose(block)[:TOP])
    return out


def pack_kernel(
    reach, meta, u_in, t_in, m_in, lev_in, to_a, to_b, to_z, to_d, to_h, to_part,
    u, m, lev, out_z, out_d, out_h, part, sems,
):
    rows_x, own_y = u.shape[1], u.shape[2]
    rows, cols = m.shape[0], m.shape[1]
    t, k = part.at[0:rows], part.at[rows : 2 * rows]
    pairs_in = ((u_in, u), (t_in, t), (m_in, m), (lev_in, lev))
    fetches = [pltpu.make_async_copy(src, dst, sems.at[i]) for i, (src, dst) in enumerate(pairs_in)]
    for copy in fetches:
        copy.start()
    even = lax.rem(meta[0], 2) == 0
    low_z = meta[2] == 0
    tiles = own_y // SUBL
    copies = []

    def send(src, dst):
        copy = pltpu.make_async_copy(src, dst, sems.at[len(fetches) + len(copies)])
        copy.start()
        copies.append(copy)

    fetches[0].wait()
    for out, high in ((to_a, even), (to_b, jnp.logical_not(even))):
        first = jnp.where(high, rows_x - FULL, 0)
        for c in range(COMPS):
            send(u.at[c, pl.ds(first, FULL)], out.at[pl.ds(c * FULL, FULL)])
        base = COMPS * FULL
        row = jnp.where(high, rows_x - FULL - 1, FULL)
        send(u.at[pl.ds(DEEP_5[0], len(DEEP_5)), row], out.at[pl.ds(base, len(DEEP_5))])
        row = jnp.where(high, rows_x - reach, reach - 1)
        for j, c in enumerate(DEEP_6):
            send(u.at[c, row], out.at[base + len(DEEP_5) + j])
    for copy in fetches[1:]:
        copy.wait()
    k[...] = conduct(m[...])
    tops = surface_tops(t, k)
    for j, value in enumerate(tops):
        part[2 * rows, j * SUBL : (j + 1) * SUBL, :] = value
    for out in (to_a, to_b):
        for j in range(cols // own_y):
            send(part.at[2 * rows, pl.ds(j * own_y, own_y)], out.at[slab_size() + j])
    send(part, to_part)
    col_tiles = cols // SUBL
    n = 0
    for ref in (t, k):
        for r in range(SKIN):
            for y in range(col_tiles):
                lo = ref[r, y * SUBL : (y + 1) * SUBL, :]
                hi = ref[rows - SKIN + r, y * SUBL : (y + 1) * SUBL, :]
                out_z[n] = jnp.where(low_z, hi, lo)
                out_d[n] = jnp.where(low_z, lo, hi)
                n += 1
    for j, value in enumerate(tops):
        out_z[n + j] = value
        out_d[n + j] = value
    n += len(tops)
    size = u.shape[2]
    lane = iota((size, LANES), 1)
    eye = iota((size, size), 0) == iota((size, size), 1)
    levels = lev[...].astype(F32)
    acc = jnp.zeros((size, LANES), F32)
    for x in range(rows_x):
        acc = pack_heights([u[c, x] for c in range(COMPS)], x * GROUP, lane, low_z, acc)
        level = jnp.sum(jnp.where(eye, levels[x : x + 1, :], 0.0), axis=1, keepdims=True)
        acc = jnp.where((lane & -2) == x * GROUP + LEVEL, level, acc)
    for y in range(tiles):
        part = acc[y * SUBL : (y + 1) * SUBL]
        out_h[y] = part
        out_z[n + y] = part
        out_d[n + y] = part
    for src, dst in ((out_z, to_z), (out_d, to_d), (out_h, to_h)):
        send(src, dst)
    for copy in copies:
        copy.wait()


def hold_kernel(meta, u_in, part_in, u, part):
    u[...] = u_in[...]
    part[...] = part_in[...]


def part_row(r, tile, ref, at, rows, in_z, in_d, low_z, col_tiles, low_part):
    if 0 <= r < rows:
        return ref[r, tile * SUBL : (tile + 1) * SUBL, :]
    k = (at * SKIN + (r + SKIN if r < 0 else r - rows)) * col_tiles + tile
    low, high = (in_d[k], in_z[k]) if r < 0 else (in_z[k], in_d[k])
    return jnp.where(low_z, low, high)


def relay_kernel(cells, meta, u, part, in_a, in_b, in_z, in_d, in_h, out_a, out_b, part_a, part_b):
    rows = part.shape[0] // 2
    t, m = part.at[0:rows], part.at[rows : 2 * rows]
    rows_x, reach = cells
    gx, gy, gz = meta[0], meta[1], meta[2]
    even_x = lax.rem(gx, 2) == 0
    even_y = lax.rem(gy, 2) == 0
    low_z = gz == 0
    tiles = u.shape[2] // SUBL
    rows, cols = t.shape[0], t.shape[1]
    col_tiles = cols // SUBL
    half = SUBL // 2
    sub = iota((SUBL, LANES), 0)
    lane = iota((SUBL, LANES), 1)
    zero = jnp.zeros((SUBL, LANES), F32)

    def put(n, hi, lo):
        out_a[n] = jnp.where(even_y, hi, lo)
        out_b[n] = jnp.where(even_y, lo, hi)

    def both(c, x):
        pair = [row_tile(c, x, y, u, in_a, in_b, even_x) for y in (tiles - 1, 0)]
        return [zero if v is None else v for v in pair]

    n = 0
    for x in range(-NEAR, rows_x + NEAR):
        for c in range(0, COMPS, 2):
            (hi0, lo0), (hi1, lo1) = both(c, x), both(c + 1, x)
            put(n, jnp.where(sub < half, turn(hi1, half, 0), hi0), jnp.where(sub < half, lo0, turn(lo1, half, 0)))
            n += 1
    for x, skip in quarter_rows(rows_x, reach):
        hi = lo = zero
        for q, c in enumerate(QUARTERS):
            a, b = both(c, x)
            hi = jnp.where((sub & -2) == 2 * q, turn(a, 2 * q - (SUBL - 2 - skip), 0), hi)
            lo = jnp.where((sub & -2) == 2 * q, turn(b, 2 * q - skip, 0), lo)
        put(n, hi, lo)
        n += 1
    base = in_z.shape[0] - tiles
    hi_y, lo_y = tiles - 1, 0
    put(
        n,
        jnp.where(low_z, in_d[base + hi_y], in_h[hi_y]),
        jnp.where(low_z, in_d[base + lo_y], in_h[lo_y]),
    )
    put(n + 1, in_z[base + hi_y], in_z[base + lo_y])
    put(
        n + 2,
        jnp.where(low_z, in_h[hi_y], in_d[base + hi_y]),
        jnp.where(low_z, in_h[lo_y], in_d[base + lo_y]),
    )
    n += 3
    for r in range(-SKIN, rows + SKIN):
        hi_t, lo_t = [part_row(r, y, t, 0, rows, in_z, in_d, low_z, col_tiles, None) for y in (col_tiles - 1, 0)]
        hi_k, lo_k = [part_row(r, y, m, 1, rows, in_z, in_d, low_z, col_tiles, None) for y in (col_tiles - 1, 0)]
        hi = jnp.where(sub < half, turn(hi_k, half, 0), hi_t)
        lo = jnp.where(sub < half, lo_t, turn(lo_k, half, 0))
        part_a[r + SKIN] = jnp.where(even_y, hi, lo)
        part_b[r + SKIN] = jnp.where(even_y, lo, hi)
    sources = surface_sources(part, in_a, in_b, in_z, in_d, even_x, tiles)
    per = LANES // cols
    slot = lax.rem(lane, cols) // SUBL
    for v in range(len(sources) // per):
        hi = lo = zero
        for i in range(per):
            src = sources[v * per + i]
            hi = jnp.where(slot == i, turn(src, SUBL * i - (cols - SUBL), 1), hi)
            lo = jnp.where(slot == i, turn(src, SUBL * i, 1), lo)
        put(n + v, hi, lo)


def surface_sources(part, in_a, in_b, in_z, in_d, even_x, tiles):
    count = part.shape[1] // SUBL
    at = in_z.shape[0] - tiles - count

    def high(j):
        k, span = slab_size() + j // tiles, slice(j % tiles * SUBL, (j % tiles + 1) * SUBL)
        return jnp.where(even_x, in_a[k, span, :], in_b[k, span, :])

    out = []
    for a in range(2):
        span = range(a * count // 2, (a + 1) * count // 2)
        out += [part[part.shape[0] - 1, j * SUBL : (j + 1) * SUBL, :] for j in span]
        out += [in_z[at + j] for j in span]
        out += [high(j) for j in span]
        out += [in_d[at + j] for j in span]
    return out


def heat_source(row, col, beam, step):
    a = beam[step, 0].astype(F32)
    b = beam[step, 1].astype(F32)
    along_x = jnp.exp(-(((row - a) / SPOT_RADIUS) ** 2))
    along_y = jnp.exp(-(((col - b) / SPOT_RADIUS) ** 2))
    return LASER_POWER * along_x * along_y


def bulk_kernel(meta, beam, part, in_z, in_d, gy_a, gy_b, out, temp, cond, kx, ky, kz):
    rows = part.shape[0] // 2
    t, m = part.at[0:rows], part.at[rows : 2 * rows]
    gx, gy, gz = meta[0], meta[1], meta[2]
    even_y = lax.rem(gy, 2) == 0
    low_z = gz == 0
    rows, cols, depth = t.shape
    col_tiles = cols // SUBL
    half = SUBL // 2
    size = cols + SUBL
    n = rows + 2 * SKIN
    sub = iota((SUBL, LANES), 0)
    for i in range(n):
        for y in range(col_tiles):
            span = slice(y * SUBL, (y + 1) * SUBL)
            temp[0, i, span, :] = part_row(i - SKIN, y, t, 0, rows, in_z, in_d, low_z, col_tiles, None)
            cond[i, span, :] = part_row(i - SKIN, y, m, 1, rows, in_z, in_d, low_z, col_tiles, None)
        up = jnp.where(even_y, gy_a[i], gy_b[i])
        low = jnp.where(even_y, gy_b[i], gy_a[i])
        temp[0, i, cols:size, :] = jnp.where(sub < half, up, low)
        cond[i, cols:size, :] = turn(jnp.where(sub < half, low, up), half, 0)

    lane = iota((size, LANES), 1)
    for i in range(n):
        k = cond[i]
        if i + 1 < n:
            kx[i] = 0.5 * (k + cond[i + 1])
        ky[i] = 0.5 * (k + turn(k, -1, 0))
        kz[i] = 0.5 * (k + jnp.where(lane == depth - 1, 0.0, turn(k, -1, 1)))

    col_g = gy * cols + wrapped(iota((size, LANES), 0), cols, size)
    inside_y = jnp.where((col_g >= 0) & (col_g < meta[4] * cols), 1.0, 0.0)
    col_f = col_g.astype(F32)
    fall = jnp.exp(-lane.astype(F32) / ABSORB_DEPTH)
    first_row = (gx * meta[5] + gz) * rows - SKIN

    for s in range(STEPS * SUBSTEPS):
        src, dst = s % 2, 1 - s % 2
        last = s == STEPS * SUBSTEPS - 1
        a = beam[s, 0].astype(F32)
        b = beam[s, 1].astype(F32)
        spot = LASER_POWER * fall * jnp.exp(-(((col_f - b) / SPOT_RADIUS) ** 2))
        lo, hi = s + 1, n - 1 - s
        fx0 = kx[lo - 1] * (temp[src, lo] - temp[src, lo - 1])
        for i in range(lo, hi):
            v = temp[src, i]
            fx = kx[i] * (temp[src, i + 1] - v)
            fy = ky[i] * (turn(v, -1, 0) - v)
            fz = kz[i] * (jnp.where(lane == depth - 1, 0.0, turn(v, -1, 1)) - v)
            above = jnp.where(lane == 0, 0.5 * cond[i] * v, turn(fz, 1, 1))
            row = first_row + i
            along_x = jnp.exp(-((jnp.full((1, LANES), row.astype(F32) - a) / SPOT_RADIUS) ** 2))
            change = (fx - fx0) + (fy - turn(fy, 1, 0)) + (fz - above) + spot * along_x
            new = v + HEAT_STEP * change
            if last:
                out[i - SKIN] = new[:cols]
            else:
                ok = (row >= 0) & (row < meta[3] * meta[5] * rows)
                temp[dst, i] = new * (inside_y * jnp.where(ok, 1.0, 0.0))
            fx0 = fx


def seal_kernel(meta, bulk, mine, given, out):
    rows, cols, depth = bulk.shape
    per = LANES // cols
    lane = iota((LANES, LANES), 1)
    for j in range(mine.shape[0]):
        skin = jnp.where(meta[2] == 0, mine[j], given[j])
        skin = jnp.concatenate([skin, jnp.zeros((LANES - SUBL, LANES), F32)], axis=0)
        block = jnp.where(lane < SKIN, jnp.transpose(skin), bulk[j * per : (j + 1) * per].reshape(LANES, LANES))
        out[j * per : (j + 1) * per] = block.reshape(per, cols, LANES)


def pack_skin(t, rows, cols, scratch, out):
    per = LANES // cols
    lane = iota((SUBL, LANES), 1)
    for j in range(SUBL // per):
        acc = jnp.zeros((SUBL, LANES), F32)
        for q in range(per):
            acc = jnp.where(lane // cols == q, turn(scratch[rows + j * per + q], cols * q, 1), acc)
        out[j] = acc


def split(value):
    high = value.astype(jnp.bfloat16)
    rest = (value - high.astype(F32)).astype(jnp.bfloat16)
    return jnp.concatenate([high, rest], axis=1)


def height_matrix():
    shape = (2 * LANES, 2 * LANES)
    k = iota(shape, 0) & (LANES - 1)
    j = iota(shape, 1)
    above = jnp.where(k == (j & (LANES - 1)) + 1, 1.0, 0.0)
    below = jnp.where(k == (j & (LANES - 1)) - 1, 1.0, 0.0)
    return (above + jnp.where(j < LANES, -below, below)).astype(jnp.bfloat16)


def height_terms(ref, first, last, matrix, diff, total, start=0, comps=tuple(range(COMPS))):
    size = diff.shape[2]
    for c in comps:
        rows = ref[c, first:last, start : start + size].reshape((last - first) * size, LANES)
        both = jnp.dot(split(rows), matrix, preferred_element_type=F32)
        diff[c, first:last] = both[:, :LANES].reshape(last - first, size, LANES)
        total[c, first:last] = both[:, LANES:].reshape(last - first, size, LANES)


def cut_weights(low_z, scale):
    lane = iota((1, LANES), 1)
    up = (lane == LANES - 1) & low_z
    down = (lane == 0) & jnp.logical_not(low_z)
    weight = {}
    for v in sorted(set(VISCOSITY)):
        side = scale * GAS_STEP * v
        drift = 0.5 * DRIFT_SPEED * scale * GAS_STEP
        weight[v] = jnp.where(up, side - drift, jnp.where(down, side + drift, 0.0))
    return jnp.where(up, 1.0, jnp.where(down, -1.0, 0.0)), weight


def stepped(comps, ref, i, diff, total, h, cut, scale, start, size, skip=0):
    sign, weight = cut
    half = 0.5 * scale * GAS_STEP
    span = pl.ds(start, size)
    terms = pl.ds(start - skip, size)

    def dx(c):
        return ref[c, i + 1, span, :] - ref[c, i - 1, span, :]

    def dy(c):
        return ref[c, i, pl.ds(start + 1, size), :] - ref[c, i, pl.ds(start - 1, size), :]

    def dz(c):
        return diff[c, i, terms, :] + sign * h[i, span, 2 * c : 2 * c + 1]

    spread = half * (dx(2) + dy(3) + dz(4))
    out = {}
    for c in comps:
        v = VISCOSITY[c]
        side = scale * GAS_STEP * v
        drift = 0.5 * DRIFT_SPEED * scale * GAS_STEP
        sides = (ref[c, i + 1, span, :] + ref[c, i - 1, span, :]) + (
            ref[c, i, pl.ds(start + 1, size), :] + ref[c, i, pl.ds(start - 1, size), :]
        )
        across = h[i, span, 2 * c : 2 * c + 1]
        new = (
            scale * (1.0 - 6.0 * GAS_STEP * v) * ref[c, i, span, :]
            + side * (sides + total[c, i, terms, :])
            - drift * diff[c, i, terms, :]
            + weight[v] * across
        )
        if c == 2:
            new = new - half * dx(5)
        elif c == 3:
            new = new - half * dy(5)
        elif c == 4:
            new = new - half * dz(5)
        else:
            new = new - {0: VAPOR_LOAD, 1: AMBIENT_LOAD, 5: STIFFNESS}[c] * spread
        out[c] = new
    return out


def by_comp(lane, values):
    out = jnp.full(lane.shape, values[-1], F32)
    for c, v in enumerate(values[:-1]):
        out = jnp.where(lane == 2 * c, v, out)
    return out


def couple_matrix():
    shape = (6 * LANES, LANES)
    k = iota(shape, 0)
    j = iota(shape, 1)
    axis = k // (2 * LANES)
    lane = k & (LANES - 1)
    spread = (lane == 4 + 2 * axis) & ((j == 0) | (j == 2) | (j == 10))
    slope = (lane == 10) & (j == 4 + 2 * axis)
    return jnp.where(spread | slope, 1.0, 0.0).astype(jnp.bfloat16)


def halo_stepped(h0, h1, g, low_z, mask_of, start, size, out, at):
    n = h0.shape[0]
    span = slice(start, start + size)
    rows = (n - 2) * size
    lane = iota((1, LANES), 1)
    more = jnp.where(low_z, 1, 0)
    flat_lane = iota((rows, LANES), 1)
    touch = jnp.zeros((rows, LANES), F32)
    for c in range(COMPS):
        own = g[c, 1 : n - 1, span].reshape(rows, LANES)
        touch = jnp.where(flat_lane == 2 * c, turn(own, 2 * c + more, 1), touch)
    mid = h0[1 : n - 1, span].reshape(rows, LANES)
    east = h0[2:n, span].reshape(rows, LANES)
    west = h0[0 : n - 2, span].reshape(rows, LANES)
    if start:
        north = h0[1 : n - 1, start + 1 : start + size + 1].reshape(rows, LANES)
        south = h0[1 : n - 1, start - 1 : start + size - 1].reshape(rows, LANES)
    else:
        north, south = turn(mid, -1, 0), turn(mid, 1, 0)
    behind = h1[1 : n - 1, span].reshape(rows, LANES)
    slopes = [east - west, north - south, jnp.where(low_z, 1.0, -1.0) * (behind - touch)]
    coupled = jnp.dot(
        jnp.concatenate([split(v) for v in slopes], axis=1), couple_matrix(), preferred_element_type=F32
    )
    up = by_comp(lane, [GAS_STEP * (v - 0.5 * DRIFT_SPEED) for v in VISCOSITY])
    down = by_comp(lane, [GAS_STEP * (v + 0.5 * DRIFT_SPEED) for v in VISCOSITY])
    half = 0.5 * GAS_STEP
    pull = by_comp(lane, [-half * VAPOR_LOAD, -half * AMBIENT_LOAD, -half, -half, -half, -half * STIFFNESS])
    new = (
        by_comp(lane, [1.0 - 6.0 * GAS_STEP * v for v in VISCOSITY]) * mid
        + by_comp(lane, [GAS_STEP * v for v in VISCOSITY]) * ((east + west) + (north + south))
        + jnp.where(low_z, up, down) * behind
        + jnp.where(low_z, down, up) * touch
        + pull * coupled
    )
    for i in range(1, n - 1):
        row = new[(i - 1) * size : i * size] * mask_of(i, start, size)
        if at < 0:
            row, at_row = turn(row, at, 0), 0
        else:
            at_row = at
        out[i - 1, at_row : at_row + size] = row


def grid_masks(meta, n, size, own_x, own_y):
    before, before_y = (n - own_x) // 2, (size - own_y) // 2

    def mask_of(i, start, count):
        x_g = meta[0] * own_x + i - before
        ok = (x_g >= 0) & (x_g < meta[3] * own_x)
        y_g = meta[1] * own_y + iota((count, LANES), 0) + start - before_y
        return jnp.where((y_g >= 0) & (y_g < meta[4] * own_y), 1.0, 0.0) * jnp.where(ok, 1.0, 0.0)

    return mask_of


def first_stage(meta, g, h0, windows, f, mask_of, unroll, comps=tuple(range(COMPS)), edge=(2, 5)):
    n = g.shape[1]
    cut = cut_weights(meta[2] == 0, 1.0)

    def one(comps):
        def body(i, carry):
            for start, size, diff, total, skip, at in windows:
                new = stepped(comps, g, i, diff, total, h0, cut, 1.0, start, size, skip)
                m = mask_of(i, start, size)
                for c in comps:
                    f[c, i - 1, at : at + size, :] = new[c] * m
            return carry

        return body

    lax.fori_loop(2, n - 2, one(comps), 0, unroll=unroll)
    for i in (1, n - 2) if edge else ():
        one(edge)(i, 0)


def second_stage(meta, g, f, fh, diff, total, skip, reach, own_y, mask_of, store):
    start = (g.shape[2] - own_y) // 2 - reach
    count = own_y + 2 * reach
    cut = cut_weights(meta[2] == 0, 0.5)

    def two(comps):
        def body(i, carry):
            new = stepped(comps, f, i - 1, diff, total, fh, cut, 0.5, start - skip, count)
            m = mask_of(i, start, count)
            for c in comps:
                new[c] = (0.5 * g[c, i, pl.ds(start, count), :] + new[c]) * m
            store(i, new)
            return carry

        return body

    return two


class Joined:
    def __init__(self, low, high):
        self.low, self.high = low, high

    def __getitem__(self, key):
        return (self.low if key[0] < self.low.shape[0] else self.high)[key]


def lane_sums(value):
    high = value.astype(jnp.bfloat16)
    rest = value - high.astype(F32)
    middle = rest.astype(jnp.bfloat16)
    low = (rest - middle.astype(F32)).astype(jnp.bfloat16)
    parts = jnp.concatenate([high, middle, low], axis=1)
    ones = jnp.ones((3 * LANES, LANES), jnp.bfloat16)
    return jnp.dot(parts, ones, preferred_element_type=F32)


def fine_pressure(meta, p, h0, own_x, own_y, part_rows):
    n, count = p.shape[0], p.shape[1]
    skip = (h0.shape[1] - count) // 2
    skip_x = (h0.shape[0] - n) // 2
    before = (n - own_x) // 2
    y_l = iota((count, LANES), 0) - (count - own_y) // 2
    col_y = lax.div(wrapped(iota((count, LANES), 1), 2 * own_y, LANES) + LANES, 2) - LANES // 2
    pick = col_y == y_l
    row_x = lax.div(wrapped(iota((part_rows, LANES), 0), 2 * own_x, part_rows) + LANES, 2) - LANES // 2
    height = (iota((count, LANES), 1) + meta[2] * LANES).astype(F32)
    fine = jnp.zeros((part_rows, LANES), F32)
    full = -(-count // SUBL) * SUBL
    pad = [jnp.zeros((full - count, LANES), F32)] if full > count else []
    found = []
    for i in range(n):
        level = h0[i + skip_x, skip : skip + count, LEVEL : LEVEL + 1]
        found += [jnp.where(height == level, p[i], 0.0)] + pad
    at = lane_sums(jnp.concatenate(found, axis=0))
    for i in range(n):
        line = jnp.sum(jnp.where(pick, at[i * full : i * full + count], 0.0), axis=0, keepdims=True)
        fine = jnp.where(row_x == i - before, line, fine)
    return fine


def top_heat(meta, beam, first, t, k, fine, own_rows, cols):
    gx, gy = meta[0], meta[1]
    shape = fine.shape
    row = gx * own_rows + wrapped(iota(shape, 0), own_rows, shape[0])
    col = gy * cols + wrapped(iota(shape, 1), cols, shape[1])
    row, col = row.astype(F32), col.astype(F32)
    deep = TOP - 1 - first
    kx = [0.5 * (v + turn(v, -1, 0)) for v in k[:deep]]
    ky = [0.5 * (v + turn(v, -1, 1)) for v in k[:deep]]
    kz = [0.5 * (k[d] + k[d + 1]) for d in range(deep)]
    for s in range(SUBSTEPS):
        beam_xy = heat_source(row, col, beam, first + s)
        before = 0.5 * k[0] * t[0]
        new = []
        for d in range(TOP - 1 - first - s):
            fx = kx[d] * (turn(t[d], -1, 0) - t[d])
            fy = ky[d] * (turn(t[d], -1, 1) - t[d])
            fz = kz[d] * (t[d + 1] - t[d])
            factor = jnp.exp(jnp.full(shape, -d / ABSORB_DEPTH, F32))
            change = (fx - turn(fx, 1, 0)) + (fy - turn(fy, 1, 1)) + (fz - before) + beam_xy * factor
            if d == 0:
                change = change - LATENT_HEAT * softplus(t[0] - BOIL_LEVEL - BACK_PRESSURE * fine)
            new.append(jnp.where(k[d] > 0, t[d] + HEAT_STEP * change, 0.0))
            before = fz
        t = new
    return t


def vapor_mass(t0, fine):
    four = t0 + turn(t0, -1, 1)
    four = four + turn(four, -1, 0)
    return softplus(0.25 * four - BOIL_LEVEL - BACK_PRESSURE * fine)


def mass_rows(meta, h, mass, first, rows, count, own_y):
    skip = (h.shape[1] - count) // 2
    skip_x = (h.shape[0] - rows) // 2
    y_l = iota((count, LANES), 0) - (count - own_y) // 2
    col = wrapped(iota((count, LANES), 1), 2 * own_y, LANES)
    pick = col == 2 * y_l
    height = (iota((count, LANES), 1) + meta[2] * LANES).astype(F32)
    found = []
    for i in range(rows):
        r = (2 * (i + first)) % mass.shape[0]
        found.append(jnp.where(pick, mass[r : r + 1, :], 0.0))
    at = lane_sums(jnp.concatenate(found, axis=0))
    out = []
    for i in range(rows):
        level = h[i + skip_x, skip : skip + count, LEVEL : LEVEL + 1]
        out.append(jnp.where(height == level, at[i * count : (i + 1) * count], 0.0))
    return out


def inner_kernel(cells, meta, u, in_a, in_b, in_z, in_d, in_h, g, f, h0, h1, fh, diff, total):
    rows_x, reach = cells
    even_x = lax.rem(meta[0], 2) == 0
    low_z = meta[2] == 0
    own_y = u.shape[2]
    tiles = own_y // SUBL
    size = g.shape[2]
    n = g.shape[1]
    zero = jnp.zeros((SUBL, LANES), F32)
    for x in range(-reach, rows_x + reach):
        for c in range(COMPS):
            for y in range(tiles):
                value = row_tile(c, x, y, u, in_a, in_b, even_x)
                g[c, x + reach, (y + 1) * SUBL : (y + 2) * SUBL, :] = zero if value is None else value
    base = in_z.shape[0] - tiles
    for b in range(3):
        parts = []
        for y in range(tiles):
            if b == 0:
                parts.append(jnp.where(low_z, in_d[base + y], in_h[y]))
            elif b == 1:
                parts.append(in_z[base + y])
            else:
                parts.append(jnp.where(low_z, in_h[y], in_d[base + y]))
        unpack_group(jnp.concatenate(parts, axis=0), b, rows_x, reach, low_z, h0, h1, SUBL, own_y)
    mask_of = grid_masks(meta, n, size, rows_x, own_y)
    halo_stepped(h0, h1, g, low_z, mask_of, SUBL, own_y, fh, 0)
    height_terms(g, 1, n - 1, height_matrix(), diff, total, SUBL)
    first_stage(meta, g, h0, [(SUBL, own_y, diff, total, SUBL, 0)], f, mask_of, 4)


def unpack_group(packed, b, rows_x, reach, low_z, h0, h1, start, size):
    for x in range(-reach, rows_x + reach):
        if (x + rows_x) // rows_x == b:
            base = GROUP * ((x + rows_x) % rows_x)
            here, other = turn(packed, -base, 1), turn(packed, -base - 1, 1)
            h0[x + reach, start : start + size] = jnp.where(low_z, here, other)
            h1[x + reach, start : start + size] = jnp.where(low_z, other, here)


def first_kernel(
    cells, meta, beam, part, in_a, in_b, in_z, in_d, gy_a, gy_b, g_in, f_in, h0_in, h1_in, fh_in,
    out_g, out_m, out_t, out_k, g, h, h1, f, fh, diff_lo, total_lo, diff_hi, total_hi, diff, total, p, mass, skin,
):
    rows_x, reach = cells
    gx, gy, gz = meta[0], meta[1], meta[2]
    even_x = lax.rem(gx, 2) == 0
    even_y = lax.rem(gy, 2) == 0
    low_z = gz == 0
    n, size = g.shape[1], g.shape[2]
    own_y = size - 2 * SUBL
    tiles = own_y // SUBL
    half = SUBL // 2
    sub = iota((SUBL, LANES), 0)
    zero = jnp.zeros((SUBL, LANES), F32)
    inner = slice(SUBL, SUBL + own_y)

    def side(k):
        upper = jnp.where(even_y, gy_a[k], gy_b[k])
        lower = jnp.where(even_y, gy_b[k], gy_a[k])
        return upper, lower

    quarter = (rows_x + 2 * NEAR) * COMPS // 2
    places_of = {}
    for k, (x, skip) in enumerate(quarter_rows(rows_x, reach)):
        places_of[x, skip] = quarter + k
    for x in range(-reach, rows_x + reach):
        i = x + reach
        for c in range(COMPS):
            g[c, i, inner, :] = g_in[c, i, inner, :]
            upper = lower = zero
            if -NEAR <= x < rows_x + NEAR:
                near_up, near_low = side((x + NEAR) * COMPS // 2 + c // 2)
                if c % 2:
                    near_up, near_low = turn(near_up, half, 0), turn(near_low, half, 0)
                upper = jnp.where(sub < half, near_up, 0.0)
                lower = jnp.where(sub >= half, near_low, 0.0)
            for skip in (0, FULL):
                if (x, skip) in places_of and c in QUARTERS:
                    q = 2 * QUARTERS.index(c)
                    up, low = side(places_of[x, skip])
                    upper = jnp.where((sub & -2) == skip, turn(up, skip - q, 0), upper)
                    lower = jnp.where((sub & -2) == SUBL - 2 - skip, turn(low, SUBL - 2 - skip - q, 0), lower)
            g[c, i, own_y + SUBL : size, :] = upper
            g[c, i, :SUBL, :] = lower
    h[:, inner, :] = h0_in[:, inner, :]
    h1[:, inner, :] = h1_in[:, inner, :]
    for b in range(3):
        upper, lower = side(quarter + len(places_of) + b)
        unpack_group(lower, b, rows_x, reach, low_z, h, h1, 0, SUBL)
        unpack_group(upper, b, rows_x, reach, low_z, h, h1, own_y + SUBL, SUBL)

    def store(i, new):
        p[i - 2] = new[COMPS - 1]
        if len(new) > 1:
            for c in range(COMPS):
                out_g[c, i - 3] = new[c] if c in new else jnp.zeros_like(new[COMPS - 1])

    mask_of = grid_masks(meta, n, size, rows_x, own_y)
    f[:, :, inner, :] = f_in[...]
    fh[:, inner, :] = fh_in[...]
    upper_at = size - SUBL - 1
    windows = []
    for start, d, t in ((1, diff_lo, total_lo), (upper_at, diff_hi, total_hi)):
        halo_stepped(h, h1, g, low_z, mask_of, start, SUBL, fh, start)
        height_terms(g, 1, n - 1, height_matrix(), d, t, start)
        windows.append((start, SUBL, d, t, start, start))
    first_stage(meta, g, h, windows, f, mask_of, 4)
    height_terms(f, 1, n - 3, height_matrix(), diff, total)
    two = second_stage(meta, g, f, fh, diff, total, 0, reach - 2, own_y, mask_of, store)
    lax.fori_loop(4, n - 4, two(tuple(range(COMPS))), 0, unroll=4)
    for i in (2, n - 3):
        two((5,))(i, 0)
    for i in (3, n - 4):
        two((2, 5))(i, 0)
    fine = fine_pressure(meta, p, h, rows_x, own_y, mass.shape[0])

    cols = LANES // 4
    per = LANES // cols
    lane = iota((SUBL, LANES), 1)
    sources = surface_sources(part, in_a, in_b, in_z, in_d, even_x, tiles)
    count = len(sources) // 2
    top_at = gy_a.shape[0] - len(sources) // per
    layers = []
    for a in range(2):
        for s in range(count):
            src = sources[a * count + s]
            upper, lower = side(top_at + (a * count + s) // per)
            i = s % per
            for q in range(per):
                at = cols * q + SUBL * i
                skin[s * per + q] = jnp.where(
                    lane < cols,
                    turn(src, -cols * q, 1),
                    jnp.where(
                        lane < cols + SUBL,
                        turn(upper, cols - at, 1),
                        jnp.where(lane >= LANES - SUBL, turn(lower, LANES - SUBL - at, 1), 0.0),
                    ),
                )
        for d in range(TOP):
            layers.append(skin[:, d, :])
    t, k = layers[:TOP], layers[TOP:]
    t = top_heat(meta, beam, 0, t, k, fine, 2 * rows_x, cols)
    for d in range(TOP - SUBSTEPS):
        out_t[d] = t[d]
        out_k[d] = k[d]
    mass[...] = vapor_mass(t[0], fine)

    count, small = out_g.shape[1], out_g.shape[2]
    masses = mass_rows(meta, h, mass, -REACH_LAST, count, small, own_y)
    lane_s = iota((small, LANES), 1)
    y_g = gy * own_y + iota((small, LANES), 0) - (small - own_y) // 2
    inside_y = jnp.where((y_g >= 0) & (y_g < meta[4] * own_y), 1.0, 0.0)
    skip = (size - small) // 2
    per = LANES // GROUP
    acc = jnp.zeros((small, LANES), F32)
    for i in range(count):
        x = i - REACH_LAST
        x_g = gx * rows_x + x
        ok = jnp.where((x_g >= 0) & (x_g < meta[3] * rows_x), 1.0, 0.0)
        add = masses[i] * (inside_y * ok)
        rows = [out_g[c, i] for c in range(COMPS)]
        for c, load in ((0, VAPOR_SOURCE), (4, RECOIL_PUSH), (5, RECOIL_PRESSURE)):
            rows[c] = rows[c] + load * add
            out_g[c, i] = rows[c]
        j, q = divmod(i, per)
        acc = pack_heights(rows, GROUP * q, lane_s, low_z, acc)
        level = h[x + reach, skip : skip + small, LEVEL : LEVEL + 1]
        acc = jnp.where((lane_s & -2) == GROUP * q + LEVEL, level, acc)
        if q == per - 1 or i == count - 1:
            out_m[j] = acc
            acc = jnp.zeros((small, LANES), F32)


def last_kernel(
    cells, meta, beam, g, in_m, in_t, in_k, bulk, out_t, out_f, mass, p, h, f, fh, h1, diff, total, skin
):
    rows_x, own_y = cells
    n, size = g.shape[1], g.shape[2]
    for i in range(n):
        j, q = divmod(i, LANES // GROUP)
        unpack_heights(in_m[j], GROUP * q, meta[2] == 0, h, h1, i)
    mask_of = grid_masks(meta, n, size, rows_x, own_y)
    matrix = height_matrix()
    halo_stepped(h, h1, g, meta[2] == 0, mask_of, 0, size, fh, -1)
    flow = tuple(range(2, COMPS))
    height_terms(g, 1, n - 1, matrix, diff, total, 0, flow)
    first_stage(meta, g, h, [(1, size - 2, diff, total, 0, 0)], f, mask_of, True, flow)
    height_terms(f, 1, n - 3, matrix, diff, total, 0, (4, 5))

    def store(i, new):
        p[i - 2] = new[COMPS - 1]

    two = second_stage(meta, g, f, fh, diff, total, 1, REACH_LAST - 2, own_y, mask_of, store)
    lax.fori_loop(2, n - 2, two((COMPS - 1,)), 0, unroll=True)
    fine = fine_pressure(meta, p, h, rows_x, own_y, mass.shape[0])
    cols = LANES // 4
    t = [in_t[d] for d in range(TOP - SUBSTEPS)]
    k = [in_k[d] for d in range(TOP - SUBSTEPS)]
    t = top_heat(meta, beam, SUBSTEPS, t, k, fine, 2 * rows_x, cols)
    skin[...] = jnp.zeros_like(skin)
    for d in range(SKIN):
        skin[:, d, :] = t[d]
    pack_skin(t, 0, cols, skin, out_t)
    pack_skin(t, SUBL, cols, skin, out_f)
    mass[...] = vapor_mass(t[0], fine)


def gas_kernel(meta, g, mass, p, h, flow, fh, out_g, f, diff, total):
    rows_x, own_y = out_g.shape[1], out_g.shape[2]
    n, size = g.shape[1], g.shape[2]
    matrix = height_matrix()
    height_terms(g, 1, n - 1, matrix, diff, total, 0, (0, 1, 4))
    mask_of = grid_masks(meta, n, size, rows_x, own_y)
    first_stage(meta, g, h, [(1, size - 2, diff, total, 0, 0)], f, mask_of, True, (0, 1), ())
    both = Joined(f, flow)
    height_terms(both, 2, n - 4, matrix, diff, total, 0, tuple(range(COMPS)))
    masses = mass_rows(meta, h, mass, 0, rows_x, own_y, own_y)
    loads = {0: VAPOR_SOURCE, 4: RECOIL_PUSH, 5: RECOIL_PRESSURE}

    def store(i, new):
        x = i - (n - rows_x) // 2
        for c in new:
            out_g[c, x] = new[c] + loads[c] * masses[x] if c in loads else new[c]

    two = second_stage(meta, g, both, fh, diff, total, 1, 0, own_y, lambda i, start, count: 1.0, store)
    for i in range(REACH_LAST, n - REACH_LAST):
        two(tuple(range(COMPS - 1)))(i, 0)
        x = i - (n - rows_x) // 2
        out_g[COMPS - 1, x] = p[i - 2, 1 : own_y + 1] + RECOIL_PRESSURE * masses[x]


def places():
    axes = ("gx", "gy", "gz")
    return [lax.axis_index(a) for a in axes] + [lax.axis_size(a) for a in axes]


def call(body, outs, scratch=(), scalars=0, count=0):
    def kernel(*refs):
        body(places(), *refs)

    vmem = pl.BlockSpec(memory_space=pltpu.VMEM)
    smem = pl.BlockSpec(memory_space=pltpu.SMEM)
    return pl.pallas_call(
        kernel,
        out_shape=[jax.ShapeDtypeStruct(s, F32) for s in outs],
        in_specs=[smem] * scalars + [vmem] * count,
        out_specs=[vmem] * len(outs),
        scratch_shapes=[pltpu.VMEM(s, F32) for s in scratch],
        compiler_params=pltpu.CompilerParams(vmem_limit_bytes=VMEM_LIMIT),
    )


def pairs(count, odd):
    out = []
    for i in range(odd, count - 1, 2):
        out += [(i, i + 1), (i + 1, i)]
    return out


def cross(nx, nz, upper):
    out = []
    for i in range(nx - 1):
        a, b = i * nz + (nz - 1 if upper else 0), (i + 1) * nz + (0 if upper else nz - 1)
        out += [(a, b), (b, a)]
    return out


def shards(u, t, m, lev, beam):
    nx, ny, nz = (lax.axis_size(a) for a in ("gx", "gy", "gz"))
    _, rows_x, own_y, _ = u.shape
    t, m = jnp.transpose(t, (1, 2, 0)), jnp.transpose(m, (1, 2, 0))
    rows, cols, depth = t.shape
    tiles = own_y // SUBL
    block = (SUBL, LANES)
    n_top = 2 * rows * cols // LANES
    top = (n_top // tiles, own_y, LANES)
    n_x = slab_size() + top[0]
    n_z = 2 * SKIN * cols // SUBL + n_top + tiles
    vmem = pl.BlockSpec(memory_space=pltpu.VMEM)
    hbm = pl.BlockSpec(memory_space=pltpu.HBM)

    def pack(*refs):
        pack_kernel(REACH, places(), *refs)

    whole = (2 * rows + 1, cols, depth)
    copies = 4 + 2 * (COMPS + 1 + len(DEEP_6) + top[0]) + 4
    shapes = [(n_x, own_y, LANES)] * 2 + [(n_z, *block)] * 2 + [(tiles, *block), whole]
    msg_a, msg_b, msg_z, msg_d, msg_h, part = pl.pallas_call(
        pack,
        out_shape=[jax.ShapeDtypeStruct(v, F32) for v in shapes],
        in_specs=[hbm] * 4,
        out_specs=[hbm] * 6,
        scratch_shapes=[pltpu.VMEM(u.shape, F32), pltpu.VMEM(m.shape, jnp.int32), pltpu.VMEM(lev.shape, jnp.int32)]
        + [pltpu.VMEM(v, F32) for v in shapes[2:]]
        + [pltpu.SemaphoreType.DMA((copies,))],
        compiler_params=pltpu.CompilerParams(vmem_limit_bytes=60 * 1024 * 1024),
    )(u, t, m, lev)
    u, part = call(hold_kernel, [u.shape, whole], count=2)(u, part)
    in_a = lax.ppermute(msg_a, "gx", pairs(nx, 0))
    in_b = lax.ppermute(msg_b, "gx", pairs(nx, 1))
    in_z = lax.ppermute(msg_z, "gz", pairs(nz, 0))
    in_d = lax.ppermute(msg_d, ("gx", "gz"), cross(nx, nz, True))
    in_h = lax.ppermute(msg_h, ("gx", "gz"), cross(nx, nz, False))
    n_y = (rows_x + 2 * NEAR) * COMPS // 2 + len(quarter_rows(rows_x, REACH)) + 3 + n_top
    n_part = rows + 2 * SKIN
    msg_a, msg_b, part_a, part_b = call(
        functools.partial(relay_kernel, (rows_x, REACH)), [(n_y, *block)] * 2 + [(n_part, *block)] * 2, count=7
    )(u, part, in_a, in_b, in_z, in_d, in_h)
    gy_b = lax.ppermute(msg_b, "gy", pairs(ny, 1))
    gy_a = lax.ppermute(msg_a, "gy", pairs(ny, 0))
    part_b = lax.ppermute(part_b, "gy", pairs(ny, 1))
    part_a = lax.ppermute(part_a, "gy", pairs(ny, 0))

    size = own_y + 2 * SUBL
    n = rows_x + 2 * REACH
    n2 = rows_x + 2 * REACH_LAST
    small = own_y + SUBL
    part_rows = 4 * SUBL
    n_m = -(-n2 // (LANES // GROUP))
    row = (size, LANES)
    own_row = (own_y, LANES)
    g1, f1, h0, h1, fh1 = call(
        functools.partial(inner_kernel, (rows_x, REACH)),
        [(COMPS, n, *row), (COMPS, n - 2, *own_row), (n, *row), (n, *row), (n - 2, *own_row)],
        scratch=[(COMPS, n - 1, *own_row)] * 2,
        count=6,
    )(u, in_a, in_b, in_z, in_d, in_h)
    g2, msg_m, top_t, top_k = call(
        functools.partial(first_kernel, (rows_x, REACH)),
        [
            (COMPS, n2, small, LANES),
            (n_m, small, LANES),
            (TOP - SUBSTEPS, part_rows, LANES),
            (TOP - SUBSTEPS, part_rows, LANES),
        ],
        scratch=[(COMPS, n, *row), (n, *row), (n, *row), (COMPS, n - 2, *row), (n - 2, *row)]
        + [(COMPS, n - 1, *block)] * 4
        + [(COMPS, n - 3, *row)] * 2
        + [(n - 4, own_y + 2 * (REACH - 2), LANES), (part_rows, LANES), (part_rows, *block)],
        scalars=1,
        count=12,
    )(beam, part, in_a, in_b, in_z, in_d, gy_a, gy_b, g1, f1, h0, h1, fh1)
    in_m = lax.ppermute(msg_m, "gz", pairs(nz, 0))
    field = (rows + 2 * SKIN, cols + SUBL, depth)
    (bulk,) = call(
        bulk_kernel, [t.shape], scratch=[(2, *field), field, field, field, field], scalars=1, count=5
    )(beam, part, in_z, in_d, part_a, part_b)
    low_row = (small, LANES)
    mine, other, mass, p, h, f, fh = call(
        functools.partial(last_kernel, (rows_x, own_y)),
        [
            (n_top // 2, *block),
            (n_top // 2, *block),
            (part_rows, LANES),
            (n2 - 4, own_y + 2 * (REACH_LAST - 2), LANES),
            (n2, *low_row),
            (COMPS, n2 - 2, *low_row),
            (n2 - 2, *low_row),
        ],
        scratch=[(n2, *low_row)] + [(COMPS, n2 - 1, *low_row)] * 2 + [(part_rows, *block)],
        scalars=1,
        count=5,
    )(beam, g2, in_m, top_t, top_k, bulk)
    (gas,) = call(
        gas_kernel,
        [u.shape],
        scratch=[(2, n2 - 2, *low_row)] + [(COMPS, n2 - 1, *low_row)] * 2,
        count=6,
    )(g2, mass, p, h, f, fh)
    given = lax.ppermute(other, "gz", pairs(nz, 0))
    (out,) = call(seal_kernel, [t.shape], count=3)(bulk, mine, given)
    return gas, jnp.transpose(out, (2, 0, 1))


def solution(mesh):
    return jax.shard_map(
        shards,
        mesh=mesh,
        in_specs=(
            P(None, "gx", "gy", "gz"),
            P(None, ("gx", "gz"), "gy"),
            P(None, ("gx", "gz"), "gy"),
            P("gx", "gy"),
            P(),
        ),
        out_specs=(P(None, "gx", "gy", "gz"), P(None, ("gx", "gz"), "gy")),
        check_vma=False,
    )
```

```python
import functools

import jax
import jax.numpy as jnp
from jax import lax
from jax.experimental import pallas as pl
from jax.experimental.pallas import tpu as pltpu
from jax.sharding import PartitionSpec as P

STEPS = 2
SUBSTEPS = 2
GAS_STEP = 0.3
DRIFT_SPEED = 0.5
VAPOR_LOAD = 0.3
AMBIENT_LOAD = 0.7
STIFFNESS = 1.0
VISCOSITY = (0.2, 0.1, 0.15, 0.15, 0.15, 0.2)
HEAT_STEP = 1.0
POWDER_COND = 0.04
SOLID_COND = 0.15
LIQUID_COND = 0.09
LASER_POWER = 3.0
SPOT_RADIUS = 6.0
ABSORB_DEPTH = 4.0
BOIL_LEVEL = 1.0
BACK_PRESSURE = 0.5
LATENT_HEAT = 0.3
VAPOR_SOURCE = 0.5
RECOIL_PUSH = 0.4
RECOIL_PRESSURE = 0.6

COMPS = 6
LANES = 128
VMEM_LIMIT = 32 * 1024 * 1024
SUBL = 8
F32 = jnp.float32
REACH = 6
REACH_LAST = 3
SKIN = 4
TOP = 8
GROUP = 16
LEVEL = 2 * COMPS


def iota(shape, axis):
    return lax.broadcasted_iota(jnp.int32, shape, axis)


def wrapped(index, own, size):
    return jnp.where(index < own + (size - own) // 2, index, index - size)


def turn(value, amount, axis):
    size = value.shape[axis]
    if isinstance(amount, int):
        amount = amount % size
        if amount == 0:
            return value
    return pltpu.roll(value, amount, axis)


def softplus(x):
    return jnp.maximum(x, 0.0) + jnp.log1p(jnp.exp(-jnp.abs(x)))


def pack_heights(rows, base, lane, low_z, acc):
    more = jnp.where(low_z, 2, 0)
    for c, row in enumerate(rows):
        acc = jnp.where((lane & -2) == base + 2 * c, turn(row, base + 2 * c + more, 1), acc)
    return acc


def unpack_heights(packed, base, low_z, h0, h1, i):
    here = turn(packed, -base, 1)
    other = turn(packed, -base - 1, 1)
    h0[i] = jnp.where(low_z, here, other)
    h1[i] = jnp.where(low_z, other, here)


DEEP_5 = (2, 3, 4, 5)
DEEP_6 = (2, 5)
FULL = 4
QUARTERS = (5, 3, 2, 4)
NEAR = 3


def quarter_rows(rows_x, reach):
    far = [x for d in range(NEAR + 1, reach) for x in (-d, rows_x + d - 1)]
    return [(x, 0) for x in far] + [(x, FULL) for x in range(-1, rows_x + 1)]


def slab_index(c, layer, below):
    if layer <= FULL:
        return c * FULL + (FULL - layer if below else layer - 1)
    base = COMPS * FULL
    if layer == FULL + 1:
        return base + DEEP_5.index(c) if c in DEEP_5 else None
    return base + len(DEEP_5) + DEEP_6.index(c) if c in DEEP_6 else None


def slab_size():
    return COMPS * FULL + len(DEEP_5) + len(DEEP_6)


def row_tile(c, x, tile, u, in_a, in_b, even_x):
    rows_x = u.shape[1]
    span = slice(tile * SUBL, (tile + 1) * SUBL)
    if 0 <= x < rows_x:
        return u[c, x, span, :]
    k = slab_index(c, -x if x < 0 else x - rows_x + 1, x < 0)
    if k is None:
        return None
    low, high = (in_b, in_a) if x < 0 else (in_a, in_b)
    return jnp.where(even_x, low[k, span, :], high[k, span, :])


def conduct(v):
    return jnp.where(v == 0, POWDER_COND, jnp.where(v == 1, SOLID_COND, LIQUID_COND)).astype(F32)


def surface_tops(t, m):
    rows, cols = t.shape[0], t.shape[1]
    per = LANES // cols
    out = []
    for ref in (t, m):
        for j in range(rows // per):
            block = ref[j * per : (j + 1) * per].reshape(LANES, LANES)
            out.append(jnp.transpose(block)[:TOP])
    return out


def pack_kernel(
    reach, meta, u_in, t_in, m_in, lev_in, to_a, to_b, to_z, to_d, to_h, to_part,
    u, m, lev, out_z, out_d, out_h, part, sems,
):
    rows_x, own_y = u.shape[1], u.shape[2]
    rows, cols = m.shape[0], m.shape[1]
    t, k = part.at[0:rows], part.at[rows : 2 * rows]
    pairs_in = ((u_in, u), (t_in, t), (m_in, m), (lev_in, lev))
    fetches = [pltpu.make_async_copy(src, dst, sems.at[i]) for i, (src, dst) in enumerate(pairs_in)]
    for copy in fetches:
        copy.start()
    even = lax.rem(meta[0], 2) == 0
    low_z = meta[2] == 0
    tiles = own_y // SUBL
    copies = []

    def send(src, dst):
        copy = pltpu.make_async_copy(src, dst, sems.at[len(fetches) + len(copies)])
        copy.start()
        copies.append(copy)

    fetches[0].wait()
    for out, high in ((to_a, even), (to_b, jnp.logical_not(even))):
        first = jnp.where(high, rows_x - FULL, 0)
        for c in range(COMPS):
            send(u.at[c, pl.ds(first, FULL)], out.at[pl.ds(c * FULL, FULL)])
        base = COMPS * FULL
        row = jnp.where(high, rows_x - FULL - 1, FULL)
        send(u.at[pl.ds(DEEP_5[0], len(DEEP_5)), row], out.at[pl.ds(base, len(DEEP_5))])
        row = jnp.where(high, rows_x - reach, reach - 1)
        for j, c in enumerate(DEEP_6):
            send(u.at[c, row], out.at[base + len(DEEP_5) + j])
    for copy in fetches[1:]:
        copy.wait()
    k[...] = conduct(m[...])
    tops = surface_tops(t, k)
    for j, value in enumerate(tops):
        part[2 * rows, j * SUBL : (j + 1) * SUBL, :] = value
    for out in (to_a, to_b):
        for j in range(cols // own_y):
            send(part.at[2 * rows, pl.ds(j * own_y, own_y)], out.at[slab_size() + j])
    send(part, to_part)
    col_tiles = cols // SUBL
    n = 0
    for ref in (t, k):
        for r in range(SKIN):
            for y in range(col_tiles):
                lo = ref[r, y * SUBL : (y + 1) * SUBL, :]
                hi = ref[rows - SKIN + r, y * SUBL : (y + 1) * SUBL, :]
                out_z[n] = jnp.where(low_z, hi, lo)
                out_d[n] = jnp.where(low_z, lo, hi)
                n += 1
    for j, value in enumerate(tops):
        out_z[n + j] = value
        out_d[n + j] = value
    n += len(tops)
    size = u.shape[2]
    lane = iota((size, LANES), 1)
    eye = iota((size, size), 0) == iota((size, size), 1)
    levels = lev[...].astype(F32)
    acc = jnp.zeros((size, LANES), F32)
    for x in range(rows_x):
        acc = pack_heights([u[c, x] for c in range(COMPS)], x * GROUP, lane, low_z, acc)
        level = jnp.sum(jnp.where(eye, levels[x : x + 1, :], 0.0), axis=1, keepdims=True)
        acc = jnp.where((lane & -2) == x * GROUP + LEVEL, level, acc)
    for y in range(tiles):
        part = acc[y * SUBL : (y + 1) * SUBL]
        out_h[y] = part
        out_z[n + y] = part
        out_d[n + y] = part
    for src, dst in ((out_z, to_z), (out_d, to_d), (out_h, to_h)):
        send(src, dst)
    for copy in copies:
        copy.wait()


def hold_kernel(meta, u_in, part_in, u, part):
    u[...] = u_in[...]
    part[...] = part_in[...]


def part_row(r, tile, ref, at, rows, in_z, in_d, low_z, col_tiles, low_part):
    if 0 <= r < rows:
        return ref[r, tile * SUBL : (tile + 1) * SUBL, :]
    k = (at * SKIN + (r + SKIN if r < 0 else r - rows)) * col_tiles + tile
    low, high = (in_d[k], in_z[k]) if r < 0 else (in_z[k], in_d[k])
    return jnp.where(low_z, low, high)


def relay_kernel(cells, meta, u, part, in_a, in_b, in_z, in_d, in_h, out_a, out_b, part_a, part_b):
    rows = part.shape[0] // 2
    t, m = part.at[0:rows], part.at[rows : 2 * rows]
    rows_x, reach = cells
    gx, gy, gz = meta[0], meta[1], meta[2]
    even_x = lax.rem(gx, 2) == 0
    even_y = lax.rem(gy, 2) == 0
    low_z = gz == 0
    tiles = u.shape[2] // SUBL
    rows, cols = t.shape[0], t.shape[1]
    col_tiles = cols // SUBL
    half = SUBL // 2
    sub = iota((SUBL, LANES), 0)
    lane = iota((SUBL, LANES), 1)
    zero = jnp.zeros((SUBL, LANES), F32)

    def put(n, hi, lo):
        out_a[n] = jnp.where(even_y, hi, lo)
        out_b[n] = jnp.where(even_y, lo, hi)

    def both(c, x):
        pair = [row_tile(c, x, y, u, in_a, in_b, even_x) for y in (tiles - 1, 0)]
        return [zero if v is None else v for v in pair]

    n = 0
    for x in range(-NEAR, rows_x + NEAR):
        for c in range(0, COMPS, 2):
            (hi0, lo0), (hi1, lo1) = both(c, x), both(c + 1, x)
            put(n, jnp.where(sub < half, turn(hi1, half, 0), hi0), jnp.where(sub < half, lo0, turn(lo1, half, 0)))
            n += 1
    for x, skip in quarter_rows(rows_x, reach):
        hi = lo = zero
        for q, c in enumerate(QUARTERS):
            a, b = both(c, x)
            hi = jnp.where((sub & -2) == 2 * q, turn(a, 2 * q - (SUBL - 2 - skip), 0), hi)
            lo = jnp.where((sub & -2) == 2 * q, turn(b, 2 * q - skip, 0), lo)
        put(n, hi, lo)
        n += 1
    base = in_z.shape[0] - tiles
    hi_y, lo_y = tiles - 1, 0
    put(
        n,
        jnp.where(low_z, in_d[base + hi_y], in_h[hi_y]),
        jnp.where(low_z, in_d[base + lo_y], in_h[lo_y]),
    )
    put(n + 1, in_z[base + hi_y], in_z[base + lo_y])
    put(
        n + 2,
        jnp.where(low_z, in_h[hi_y], in_d[base + hi_y]),
        jnp.where(low_z, in_h[lo_y], in_d[base + lo_y]),
    )
    n += 3
    for r in range(-SKIN, rows + SKIN):
        hi_t, lo_t = [part_row(r, y, t, 0, rows, in_z, in_d, low_z, col_tiles, None) for y in (col_tiles - 1, 0)]
        hi_k, lo_k = [part_row(r, y, m, 1, rows, in_z, in_d, low_z, col_tiles, None) for y in (col_tiles - 1, 0)]
        hi = jnp.where(sub < half, turn(hi_k, half, 0), hi_t)
        lo = jnp.where(sub < half, lo_t, turn(lo_k, half, 0))
        part_a[r + SKIN] = jnp.where(even_y, hi, lo)
        part_b[r + SKIN] = jnp.where(even_y, lo, hi)
    sources = surface_sources(part, in_a, in_b, in_z, in_d, even_x, tiles)
    per = LANES // cols
    slot = lax.rem(lane, cols) // SUBL
    for v in range(len(sources) // per):
        hi = lo = zero
        for i in range(per):
            src = sources[v * per + i]
            hi = jnp.where(slot == i, turn(src, SUBL * i - (cols - SUBL), 1), hi)
            lo = jnp.where(slot == i, turn(src, SUBL * i, 1), lo)
        put(n + v, hi, lo)


def surface_sources(part, in_a, in_b, in_z, in_d, even_x, tiles):
    count = part.shape[1] // SUBL
    at = in_z.shape[0] - tiles - count

    def high(j):
        k, span = slab_size() + j // tiles, slice(j % tiles * SUBL, (j % tiles + 1) * SUBL)
        return jnp.where(even_x, in_a[k, span, :], in_b[k, span, :])

    out = []
    for a in range(2):
        span = range(a * count // 2, (a + 1) * count // 2)
        out += [part[part.shape[0] - 1, j * SUBL : (j + 1) * SUBL, :] for j in span]
        out += [in_z[at + j] for j in span]
        out += [high(j) for j in span]
        out += [in_d[at + j] for j in span]
    return out


def heat_source(row, col, beam, step):
    a = beam[step, 0].astype(F32)
    b = beam[step, 1].astype(F32)
    along_x = jnp.exp(-(((row - a) / SPOT_RADIUS) ** 2))
    along_y = jnp.exp(-(((col - b) / SPOT_RADIUS) ** 2))
    return LASER_POWER * along_x * along_y


def bulk_kernel(meta, beam, part, in_z, in_d, gy_a, gy_b, out, temp, other, cond, kx, ky, kz, above):
    rows = part.shape[0] // 2
    t, m = part.at[0:rows], part.at[rows : 2 * rows]
    gx, gy, gz = meta[0], meta[1], meta[2]
    even_y = lax.rem(gy, 2) == 0
    low_z = gz == 0
    rows, cols, depth = t.shape
    col_tiles = cols // SUBL
    half = SUBL // 2
    size = cols + SUBL
    n = rows + 2 * SKIN
    sub = iota((SUBL, LANES), 0)
    for i in range(n):
        for y in range(col_tiles):
            span = slice(y * SUBL, (y + 1) * SUBL)
            temp[i, span, :] = part_row(i - SKIN, y, t, 0, rows, in_z, in_d, low_z, col_tiles, None)
            cond[i, span, :] = part_row(i - SKIN, y, m, 1, rows, in_z, in_d, low_z, col_tiles, None)
        up = jnp.where(even_y, gy_a[i], gy_b[i])
        low = jnp.where(even_y, gy_b[i], gy_a[i])
        temp[i, cols:size, :] = jnp.where(sub < half, up, low)
        cond[i, cols:size, :] = turn(jnp.where(sub < half, low, up), half, 0)

    lane = iota((size, LANES), 1)
    for i in range(n):
        k = cond[i]
        if i + 1 < n:
            kx[i] = 0.5 * (k + cond[i + 1])
        ky[i] = 0.5 * (k + turn(k, -1, 0))
        kz[i] = 0.5 * (k + jnp.where(lane == depth - 1, 0.0, turn(k, -1, 1)))
        above[i] = 0.5 * (k + jnp.where(lane == 0, 0.0, turn(k, 1, 1)))

    col_g = gy * cols + wrapped(iota((size, LANES), 0), cols, size)
    inside_y = jnp.where((col_g >= 0) & (col_g < meta[4] * cols), 1.0, 0.0)
    col_f = col_g.astype(F32)
    fall = jnp.exp(-lane.astype(F32) / ABSORB_DEPTH)
    first_row = (gx * meta[5] + gz) * rows - SKIN

    for s in range(STEPS * SUBSTEPS):
        src, dst = (temp, other) if s % 2 == 0 else (other, temp)
        last = s == STEPS * SUBSTEPS - 1
        a = beam[s, 0].astype(F32)
        b = beam[s, 1].astype(F32)
        spot = LASER_POWER * fall * jnp.exp(-(((col_f - b) / SPOT_RADIUS) ** 2))
        lo, hi = s + 1, n - 1 - s
        fx0 = kx[lo - 1] * (src[lo] - src[lo - 1])
        for i in range(lo, hi):
            v = src[i]
            fx = kx[i] * (src[i + 1] - v)
            fy = ky[i] * (turn(v, -1, 0) - v)
            down = kz[i] * (jnp.where(lane == depth - 1, 0.0, turn(v, -1, 1)) - v)
            up = above[i] * (jnp.where(lane == 0, 0.0, turn(v, 1, 1)) - v)
            row = first_row + i
            along_x = jnp.exp(-((jnp.full((1, LANES), row.astype(F32) - a) / SPOT_RADIUS) ** 2))
            change = (fx - fx0) + (fy - turn(fy, 1, 0)) + (down + up) + spot * along_x
            new = v + HEAT_STEP * change
            if last:
                out[i - SKIN] = new[:cols]
            else:
                ok = (row >= 0) & (row < meta[3] * meta[5] * rows)
                dst[i] = new * (inside_y * jnp.where(ok, 1.0, 0.0))
            fx0 = fx


def seal_kernel(meta, bulk, mine, given, out):
    rows, cols, depth = bulk.shape
    per = LANES // cols
    lane = iota((LANES, LANES), 1)
    for j in range(mine.shape[0]):
        skin = jnp.where(meta[2] == 0, mine[j], given[j])
        skin = jnp.concatenate([skin, jnp.zeros((LANES - SUBL, LANES), F32)], axis=0)
        block = jnp.where(lane < SKIN, jnp.transpose(skin), bulk[j * per : (j + 1) * per].reshape(LANES, LANES))
        out[j * per : (j + 1) * per] = block.reshape(per, cols, LANES)


def pack_skin(t, rows, cols, scratch, out):
    per = LANES // cols
    lane = iota((SUBL, LANES), 1)
    for j in range(SUBL // per):
        acc = jnp.zeros((SUBL, LANES), F32)
        for q in range(per):
            acc = jnp.where(lane // cols == q, turn(scratch[rows + j * per + q], cols * q, 1), acc)
        out[j] = acc


def split(value):
    high = value.astype(jnp.bfloat16)
    rest = (value - high.astype(F32)).astype(jnp.bfloat16)
    return jnp.concatenate([high, rest], axis=1)


def height_matrix():
    shape = (2 * LANES, 2 * LANES)
    k = iota(shape, 0) & (LANES - 1)
    j = iota(shape, 1)
    above = jnp.where(k == (j & (LANES - 1)) + 1, 1.0, 0.0)
    below = jnp.where(k == (j & (LANES - 1)) - 1, 1.0, 0.0)
    return (above + jnp.where(j < LANES, -below, below)).astype(jnp.bfloat16)


def height_terms(ref, first, last, matrix, diff, total, start=0, comps=tuple(range(COMPS))):
    size = diff.shape[2]
    for c in comps:
        rows = ref[c, first:last, start : start + size].reshape((last - first) * size, LANES)
        both = jnp.dot(split(rows), matrix, preferred_element_type=F32)
        diff[c, first:last] = both[:, :LANES].reshape(last - first, size, LANES)
        total[c, first:last] = both[:, LANES:].reshape(last - first, size, LANES)


def cut_weights(low_z, scale):
    lane = iota((1, LANES), 1)
    up = (lane == LANES - 1) & low_z
    down = (lane == 0) & jnp.logical_not(low_z)
    weight = {}
    for v in sorted(set(VISCOSITY)):
        side = scale * GAS_STEP * v
        drift = 0.5 * DRIFT_SPEED * scale * GAS_STEP
        weight[v] = jnp.where(up, side - drift, jnp.where(down, side + drift, 0.0))
    return jnp.where(up, 1.0, jnp.where(down, -1.0, 0.0)), weight


def stepped(comps, ref, i, diff, total, h, cut, scale, start, size, skip=0):
    sign, weight = cut
    half = 0.5 * scale * GAS_STEP
    span = pl.ds(start, size)
    terms = pl.ds(start - skip, size)

    def dx(c):
        return ref[c, i + 1, span, :] - ref[c, i - 1, span, :]

    def dy(c):
        return ref[c, i, pl.ds(start + 1, size), :] - ref[c, i, pl.ds(start - 1, size), :]

    def dz(c):
        return diff[c, i, terms, :] + sign * h[i, span, 2 * c : 2 * c + 1]

    spread = half * (dx(2) + dy(3) + dz(4))
    out = {}
    for c in comps:
        v = VISCOSITY[c]
        side = scale * GAS_STEP * v
        drift = 0.5 * DRIFT_SPEED * scale * GAS_STEP
        sides = (ref[c, i + 1, span, :] + ref[c, i - 1, span, :]) + (
            ref[c, i, pl.ds(start + 1, size), :] + ref[c, i, pl.ds(start - 1, size), :]
        )
        across = h[i, span, 2 * c : 2 * c + 1]
        new = (
            scale * (1.0 - 6.0 * GAS_STEP * v) * ref[c, i, span, :]
            + side * (sides + total[c, i, terms, :])
            - drift * diff[c, i, terms, :]
            + weight[v] * across
        )
        if c == 2:
            new = new - half * dx(5)
        elif c == 3:
            new = new - half * dy(5)
        elif c == 4:
            new = new - half * dz(5)
        else:
            new = new - {0: VAPOR_LOAD, 1: AMBIENT_LOAD, 5: STIFFNESS}[c] * spread
        out[c] = new
    return out


def by_comp(lane, values):
    out = jnp.full(lane.shape, values[-1], F32)
    for c, v in enumerate(values[:-1]):
        out = jnp.where(lane == 2 * c, v, out)
    return out


def couple_matrix():
    shape = (6 * LANES, LANES)
    k = iota(shape, 0)
    j = iota(shape, 1)
    axis = k // (2 * LANES)
    lane = k & (LANES - 1)
    spread = (lane == 4 + 2 * axis) & ((j == 0) | (j == 2) | (j == 10))
    slope = (lane == 10) & (j == 4 + 2 * axis)
    return jnp.where(spread | slope, 1.0, 0.0).astype(jnp.bfloat16)


def halo_stepped(h0, h1, g, low_z, mask_of, start, size, out, at):
    n = h0.shape[0]
    span = slice(start, start + size)
    rows = (n - 2) * size
    lane = iota((1, LANES), 1)
    more = jnp.where(low_z, 1, 0)
    flat_lane = iota((rows, LANES), 1)
    touch = jnp.zeros((rows, LANES), F32)
    for c in range(COMPS):
        own = g[c, 1 : n - 1, span].reshape(rows, LANES)
        touch = jnp.where(flat_lane == 2 * c, turn(own, 2 * c + more, 1), touch)
    mid = h0[1 : n - 1, span].reshape(rows, LANES)
    east = h0[2:n, span].reshape(rows, LANES)
    west = h0[0 : n - 2, span].reshape(rows, LANES)
    if start:
        north = h0[1 : n - 1, start + 1 : start + size + 1].reshape(rows, LANES)
        south = h0[1 : n - 1, start - 1 : start + size - 1].reshape(rows, LANES)
    else:
        north, south = turn(mid, -1, 0), turn(mid, 1, 0)
    behind = h1[1 : n - 1, span].reshape(rows, LANES)
    slopes = [east - west, north - south, jnp.where(low_z, 1.0, -1.0) * (behind - touch)]
    coupled = jnp.dot(
        jnp.concatenate([split(v) for v in slopes], axis=1), couple_matrix(), preferred_element_type=F32
    )
    up = by_comp(lane, [GAS_STEP * (v - 0.5 * DRIFT_SPEED) for v in VISCOSITY])
    down = by_comp(lane, [GAS_STEP * (v + 0.5 * DRIFT_SPEED) for v in VISCOSITY])
    half = 0.5 * GAS_STEP
    pull = by_comp(lane, [-half * VAPOR_LOAD, -half * AMBIENT_LOAD, -half, -half, -half, -half * STIFFNESS])
    new = (
        by_comp(lane, [1.0 - 6.0 * GAS_STEP * v for v in VISCOSITY]) * mid
        + by_comp(lane, [GAS_STEP * v for v in VISCOSITY]) * ((east + west) + (north + south))
        + jnp.where(low_z, up, down) * behind
        + jnp.where(low_z, down, up) * touch
        + pull * coupled
    )
    for i in range(1, n - 1):
        row = new[(i - 1) * size : i * size] * mask_of(i, start, size)
        if at < 0:
            row, at_row = turn(row, at, 0), 0
        else:
            at_row = at
        out[i - 1, at_row : at_row + size] = row


def grid_masks(meta, n, size, own_x, own_y):
    before, before_y = (n - own_x) // 2, (size - own_y) // 2

    def mask_of(i, start, count):
        x_g = meta[0] * own_x + i - before
        ok = (x_g >= 0) & (x_g < meta[3] * own_x)
        y_g = meta[1] * own_y + iota((count, LANES), 0) + start - before_y
        return jnp.where((y_g >= 0) & (y_g < meta[4] * own_y), 1.0, 0.0) * jnp.where(ok, 1.0, 0.0)

    return mask_of


def first_stage(meta, g, h0, windows, f, mask_of, unroll, comps=tuple(range(COMPS)), edge=(2, 5)):
    n = g.shape[1]
    cut = cut_weights(meta[2] == 0, 1.0)

    def one(comps):
        def body(i, carry):
            for start, size, diff, total, skip, at in windows:
                new = stepped(comps, g, i, diff, total, h0, cut, 1.0, start, size, skip)
                m = mask_of(i, start, size)
                for c in comps:
                    f[c, i - 1, at : at + size, :] = new[c] * m
            return carry

        return body

    lax.fori_loop(2, n - 2, one(comps), 0, unroll=unroll)
    for i in (1, n - 2) if edge else ():
        one(edge)(i, 0)


def second_stage(meta, g, f, fh, diff, total, skip, reach, own_y, mask_of, store):
    start = (g.shape[2] - own_y) // 2 - reach
    count = own_y + 2 * reach
    cut = cut_weights(meta[2] == 0, 0.5)

    def two(comps):
        def body(i, carry):
            new = stepped(comps, f, i - 1, diff, total, fh, cut, 0.5, start - skip, count)
            m = mask_of(i, start, count)
            for c in comps:
                new[c] = (0.5 * g[c, i, pl.ds(start, count), :] + new[c]) * m
            store(i, new)
            return carry

        return body

    return two


class Joined:
    def __init__(self, low, high):
        self.low, self.high = low, high

    def __getitem__(self, key):
        return (self.low if key[0] < self.low.shape[0] else self.high)[key]


def lane_sums(value):
    high = value.astype(jnp.bfloat16)
    rest = value - high.astype(F32)
    middle = rest.astype(jnp.bfloat16)
    low = (rest - middle.astype(F32)).astype(jnp.bfloat16)
    parts = jnp.concatenate([high, middle, low], axis=1)
    ones = jnp.ones((3 * LANES, LANES), jnp.bfloat16)
    return jnp.dot(parts, ones, preferred_element_type=F32)


def fine_pressure(meta, p, h0, own_x, own_y, part_rows):
    n, count = p.shape[0], p.shape[1]
    skip = (h0.shape[1] - count) // 2
    skip_x = (h0.shape[0] - n) // 2
    before = (n - own_x) // 2
    y_l = iota((count, LANES), 0) - (count - own_y) // 2
    col_y = lax.div(wrapped(iota((count, LANES), 1), 2 * own_y, LANES) + LANES, 2) - LANES // 2
    pick = col_y == y_l
    row_x = lax.div(wrapped(iota((part_rows, LANES), 0), 2 * own_x, part_rows) + LANES, 2) - LANES // 2
    height = (iota((count, LANES), 1) + meta[2] * LANES).astype(F32)
    fine = jnp.zeros((part_rows, LANES), F32)
    full = -(-count // SUBL) * SUBL
    pad = [jnp.zeros((full - count, LANES), F32)] if full > count else []
    found = []
    for i in range(n):
        level = h0[i + skip_x, skip : skip + count, LEVEL : LEVEL + 1]
        found += [jnp.where(height == level, p[i], 0.0)] + pad
    at = lane_sums(jnp.concatenate(found, axis=0))
    for i in range(n):
        line = jnp.sum(jnp.where(pick, at[i * full : i * full + count], 0.0), axis=0, keepdims=True)
        fine = jnp.where(row_x == i - before, line, fine)
    return fine


def top_heat(meta, beam, first, t, k, fine, own_rows, cols):
    gx, gy = meta[0], meta[1]
    shape = fine.shape
    row = gx * own_rows + wrapped(iota(shape, 0), own_rows, shape[0])
    col = gy * cols + wrapped(iota(shape, 1), cols, shape[1])
    row, col = row.astype(F32), col.astype(F32)
    deep = TOP - 1 - first
    kx = [0.5 * (v + turn(v, -1, 0)) for v in k[:deep]]
    ky = [0.5 * (v + turn(v, -1, 1)) for v in k[:deep]]
    ky_low = [0.5 * (v + turn(v, 1, 1)) for v in k[:deep]]
    kz = [0.5 * (k[d] + k[d + 1]) for d in range(deep)]
    for s in range(SUBSTEPS):
        beam_xy = heat_source(row, col, beam, first + s)
        before = 0.5 * k[0] * t[0]
        new = []
        for d in range(TOP - 1 - first - s):
            fx = kx[d] * (turn(t[d], -1, 0) - t[d])
            fy = ky[d] * (turn(t[d], -1, 1) - t[d]) + ky_low[d] * (turn(t[d], 1, 1) - t[d])
            fz = kz[d] * (t[d + 1] - t[d])
            factor = jnp.exp(jnp.full(shape, -d / ABSORB_DEPTH, F32))
            change = (fx - turn(fx, 1, 0)) + fy + (fz - before) + beam_xy * factor
            if d == 0:
                change = change - LATENT_HEAT * softplus(t[0] - BOIL_LEVEL - BACK_PRESSURE * fine)
            new.append(jnp.where(k[d] > 0, t[d] + HEAT_STEP * change, 0.0))
            before = fz
        t = new
    return t


def vapor_mass(t0, fine):
    four = t0 + turn(t0, -1, 1)
    four = four + turn(four, -1, 0)
    return softplus(0.25 * four - BOIL_LEVEL - BACK_PRESSURE * fine)


def mass_rows(meta, h, mass, first, rows, count, own_y):
    skip = (h.shape[1] - count) // 2
    skip_x = (h.shape[0] - rows) // 2
    y_l = iota((count, LANES), 0) - (count - own_y) // 2
    col = wrapped(iota((count, LANES), 1), 2 * own_y, LANES)
    pick = col == 2 * y_l
    height = (iota((count, LANES), 1) + meta[2] * LANES).astype(F32)
    found = []
    for i in range(rows):
        r = (2 * (i + first)) % mass.shape[0]
        found.append(jnp.where(pick, mass[r : r + 1, :], 0.0))
    at = lane_sums(jnp.concatenate(found, axis=0))
    out = []
    for i in range(rows):
        level = h[i + skip_x, skip : skip + count, LEVEL : LEVEL + 1]
        out.append(jnp.where(height == level, at[i * count : (i + 1) * count], 0.0))
    return out


def inner_kernel(cells, meta, u, in_a, in_b, in_z, in_d, in_h, g, f, h0, h1, fh, diff, total):
    rows_x, reach = cells
    even_x = lax.rem(meta[0], 2) == 0
    low_z = meta[2] == 0
    own_y = u.shape[2]
    tiles = own_y // SUBL
    size = g.shape[2]
    n = g.shape[1]
    zero = jnp.zeros((SUBL, LANES), F32)
    for x in range(-reach, rows_x + reach):
        for c in range(COMPS):
            for y in range(tiles):
                value = row_tile(c, x, y, u, in_a, in_b, even_x)
                g[c, x + reach, (y + 1) * SUBL : (y + 2) * SUBL, :] = zero if value is None else value
    base = in_z.shape[0] - tiles
    for b in range(3):
        parts = []
        for y in range(tiles):
            if b == 0:
                parts.append(jnp.where(low_z, in_d[base + y], in_h[y]))
            elif b == 1:
                parts.append(in_z[base + y])
            else:
                parts.append(jnp.where(low_z, in_h[y], in_d[base + y]))
        unpack_group(jnp.concatenate(parts, axis=0), b, rows_x, reach, low_z, h0, h1, SUBL, own_y)
    mask_of = grid_masks(meta, n, size, rows_x, own_y)
    halo_stepped(h0, h1, g, low_z, mask_of, SUBL, own_y, fh, 0)
    height_terms(g, 1, n - 1, height_matrix(), diff, total, SUBL)
    first_stage(meta, g, h0, [(SUBL, own_y, diff, total, SUBL, 0)], f, mask_of, True)


def unpack_group(packed, b, rows_x, reach, low_z, h0, h1, start, size):
    for x in range(-reach, rows_x + reach):
        if (x + rows_x) // rows_x == b:
            base = GROUP * ((x + rows_x) % rows_x)
            here, other = turn(packed, -base, 1), turn(packed, -base - 1, 1)
            h0[x + reach, start : start + size] = jnp.where(low_z, here, other)
            h1[x + reach, start : start + size] = jnp.where(low_z, other, here)


def first_kernel(
    cells, meta, beam, part, in_a, in_b, in_z, in_d, gy_a, gy_b, g_in, f_in, h0_in, h1_in, fh_in,
    out_g, out_m, out_t, out_k, g, h, h1, f, fh, diff_lo, total_lo, diff_hi, total_hi, diff, total, p, mass, skin,
):
    rows_x, reach = cells
    gx, gy, gz = meta[0], meta[1], meta[2]
    even_x = lax.rem(gx, 2) == 0
    even_y = lax.rem(gy, 2) == 0
    low_z = gz == 0
    n, size = g.shape[1], g.shape[2]
    own_y = size - 2 * SUBL
    tiles = own_y // SUBL
    half = SUBL // 2
    sub = iota((SUBL, LANES), 0)
    zero = jnp.zeros((SUBL, LANES), F32)
    inner = slice(SUBL, SUBL + own_y)

    def side(k):
        upper = jnp.where(even_y, gy_a[k], gy_b[k])
        lower = jnp.where(even_y, gy_b[k], gy_a[k])
        return upper, lower

    quarter = (rows_x + 2 * NEAR) * COMPS // 2
    places_of = {}
    for k, (x, skip) in enumerate(quarter_rows(rows_x, reach)):
        places_of[x, skip] = quarter + k
    for x in range(-reach, rows_x + reach):
        i = x + reach
        for c in range(COMPS):
            g[c, i, inner, :] = g_in[c, i, inner, :]
            upper = lower = zero
            if -NEAR <= x < rows_x + NEAR:
                near_up, near_low = side((x + NEAR) * COMPS // 2 + c // 2)
                if c % 2:
                    near_up, near_low = turn(near_up, half, 0), turn(near_low, half, 0)
                upper = jnp.where(sub < half, near_up, 0.0)
                lower = jnp.where(sub >= half, near_low, 0.0)
            for skip in (0, FULL):
                if (x, skip) in places_of and c in QUARTERS:
                    q = 2 * QUARTERS.index(c)
                    up, low = side(places_of[x, skip])
                    upper = jnp.where((sub & -2) == skip, turn(up, skip - q, 0), upper)
                    lower = jnp.where((sub & -2) == SUBL - 2 - skip, turn(low, SUBL - 2 - skip - q, 0), lower)
            g[c, i, own_y + SUBL : size, :] = upper
            g[c, i, :SUBL, :] = lower
    h[:, inner, :] = h0_in[:, inner, :]
    h1[:, inner, :] = h1_in[:, inner, :]
    for b in range(3):
        upper, lower = side(quarter + len(places_of) + b)
        unpack_group(lower, b, rows_x, reach, low_z, h, h1, 0, SUBL)
        unpack_group(upper, b, rows_x, reach, low_z, h, h1, own_y + SUBL, SUBL)

    def store(i, new):
        p[i - 2] = new[COMPS - 1]
        if len(new) > 1:
            for c in range(COMPS):
                out_g[c, i - 3] = new[c] if c in new else jnp.zeros_like(new[COMPS - 1])

    mask_of = grid_masks(meta, n, size, rows_x, own_y)
    f[:, :, inner, :] = f_in[...]
    fh[:, inner, :] = fh_in[...]
    upper_at = size - SUBL - 1
    windows = []
    for start, d, t in ((1, diff_lo, total_lo), (upper_at, diff_hi, total_hi)):
        halo_stepped(h, h1, g, low_z, mask_of, start, SUBL, fh, start)
        height_terms(g, 1, n - 1, height_matrix(), d, t, start)
        windows.append((start, SUBL, d, t, start, start))
    first_stage(meta, g, h, windows, f, mask_of, True)
    height_terms(f, 1, n - 3, height_matrix(), diff, total)
    two = second_stage(meta, g, f, fh, diff, total, 0, reach - 2, own_y, mask_of, store)
    lax.fori_loop(4, n - 4, two(tuple(range(COMPS))), 0, unroll=True)
    for i in (2, n - 3):
        two((5,))(i, 0)
    for i in (3, n - 4):
        two((2, 5))(i, 0)
    fine = fine_pressure(meta, p, h, rows_x, own_y, mass.shape[0])

    cols = LANES // 4
    per = LANES // cols
    lane = iota((SUBL, LANES), 1)
    sources = surface_sources(part, in_a, in_b, in_z, in_d, even_x, tiles)
    count = len(sources) // 2
    top_at = gy_a.shape[0] - len(sources) // per
    layers = []
    for a in range(2):
        for s in range(count):
            src = sources[a * count + s]
            upper, lower = side(top_at + (a * count + s) // per)
            i = s % per
            for q in range(per):
                at = cols * q + SUBL * i
                skin[s * per + q] = jnp.where(
                    lane < cols,
                    turn(src, -cols * q, 1),
                    jnp.where(
                        lane < cols + SUBL,
                        turn(upper, cols - at, 1),
                        jnp.where(lane >= LANES - SUBL, turn(lower, LANES - SUBL - at, 1), 0.0),
                    ),
                )
        for d in range(TOP):
            layers.append(skin[:, d, :])
    t, k = layers[:TOP], layers[TOP:]
    t = top_heat(meta, beam, 0, t, k, fine, 2 * rows_x, cols)
    for d in range(TOP - SUBSTEPS):
        out_t[d] = t[d]
        out_k[d] = k[d]
    mass[...] = vapor_mass(t[0], fine)

    count, small = out_g.shape[1], out_g.shape[2]
    masses = mass_rows(meta, h, mass, -REACH_LAST, count, small, own_y)
    lane_s = iota((small, LANES), 1)
    y_g = gy * own_y + iota((small, LANES), 0) - (small - own_y) // 2
    inside_y = jnp.where((y_g >= 0) & (y_g < meta[4] * own_y), 1.0, 0.0)
    skip = (size - small) // 2
    per = LANES // GROUP
    acc = jnp.zeros((small, LANES), F32)
    for i in range(count):
        x = i - REACH_LAST
        x_g = gx * rows_x + x
        ok = jnp.where((x_g >= 0) & (x_g < meta[3] * rows_x), 1.0, 0.0)
        add = masses[i] * (inside_y * ok)
        rows = [out_g[c, i] for c in range(COMPS)]
        for c, load in ((0, VAPOR_SOURCE), (4, RECOIL_PUSH), (5, RECOIL_PRESSURE)):
            rows[c] = rows[c] + load * add
            out_g[c, i] = rows[c]
        j, q = divmod(i, per)
        acc = pack_heights(rows, GROUP * q, lane_s, low_z, acc)
        level = h[x + reach, skip : skip + small, LEVEL : LEVEL + 1]
        acc = jnp.where((lane_s & -2) == GROUP * q + LEVEL, level, acc)
        if q == per - 1 or i == count - 1:
            out_m[j] = acc
            acc = jnp.zeros((small, LANES), F32)


def last_kernel(
    cells, meta, beam, g, g_diff, g_total, in_m, in_t, in_k, bulk, out_t, out_f, mass, p, h, f, fh, h1, diff, total, skin
):
    rows_x, own_y = cells
    n, size = g.shape[1], g.shape[2]
    for i in range(n):
        j, q = divmod(i, LANES // GROUP)
        unpack_heights(in_m[j], GROUP * q, meta[2] == 0, h, h1, i)
    mask_of = grid_masks(meta, n, size, rows_x, own_y)
    matrix = height_matrix()
    halo_stepped(h, h1, g, meta[2] == 0, mask_of, 0, size, fh, -1)
    flow = tuple(range(2, COMPS))
    first_stage(meta, g, h, [(1, size - 2, g_diff, g_total, 0, 0)], f, mask_of, True, flow)
    height_terms(f, 1, n - 3, matrix, diff, total, 0, (4, 5))

    def store(i, new):
        p[i - 2] = new[COMPS - 1]

    two = second_stage(meta, g, f, fh, diff, total, 1, REACH_LAST - 2, own_y, mask_of, store)
    lax.fori_loop(2, n - 2, two((COMPS - 1,)), 0, unroll=True)
    fine = fine_pressure(meta, p, h, rows_x, own_y, mass.shape[0])
    cols = LANES // 4
    t = [in_t[d] for d in range(TOP - SUBSTEPS)]
    k = [in_k[d] for d in range(TOP - SUBSTEPS)]
    t = top_heat(meta, beam, SUBSTEPS, t, k, fine, 2 * rows_x, cols)
    skin[...] = jnp.zeros_like(skin)
    for d in range(SKIN):
        skin[:, d, :] = t[d]
    pack_skin(t, 0, cols, skin, out_t)
    pack_skin(t, SUBL, cols, skin, out_f)
    mass[...] = vapor_mass(t[0], fine)


def terms_kernel(meta, g, diff, total):
    height_terms(g, 1, g.shape[1] - 1, height_matrix(), diff, total)


def gas_kernel(meta, g, g_diff, g_total, mass, p, h, flow, fh, out_g, f, diff, total):
    rows_x, own_y = out_g.shape[1], out_g.shape[2]
    n, size = g.shape[1], g.shape[2]
    matrix = height_matrix()
    mask_of = grid_masks(meta, n, size, rows_x, own_y)
    first_stage(meta, g, h, [(1, size - 2, g_diff, g_total, 0, 0)], f, mask_of, True, (0, 1), ())
    both = Joined(f, flow)
    height_terms(both, 2, n - 4, matrix, diff, total, 0, tuple(range(COMPS)))
    masses = mass_rows(meta, h, mass, 0, rows_x, own_y, own_y)
    loads = {0: VAPOR_SOURCE, 4: RECOIL_PUSH, 5: RECOIL_PRESSURE}

    def store(i, new):
        x = i - (n - rows_x) // 2
        for c in new:
            out_g[c, x] = new[c] + loads[c] * masses[x] if c in loads else new[c]

    two = second_stage(meta, g, both, fh, diff, total, 1, 0, own_y, lambda i, start, count: 1.0, store)
    for i in range(REACH_LAST, n - REACH_LAST):
        two(tuple(range(COMPS - 1)))(i, 0)
        x = i - (n - rows_x) // 2
        out_g[COMPS - 1, x] = p[i - 2, 1 : own_y + 1] + RECOIL_PRESSURE * masses[x]


def places():
    axes = ("gx", "gy", "gz")
    return [lax.axis_index(a) for a in axes] + [lax.axis_size(a) for a in axes]


def call(body, outs, scratch=(), scalars=0, count=0):
    def kernel(*refs):
        body(places(), *refs)

    vmem = pl.BlockSpec(memory_space=pltpu.VMEM)
    smem = pl.BlockSpec(memory_space=pltpu.SMEM)
    return pl.pallas_call(
        kernel,
        out_shape=[jax.ShapeDtypeStruct(s, F32) for s in outs],
        in_specs=[smem] * scalars + [vmem] * count,
        out_specs=[vmem] * len(outs),
        scratch_shapes=[pltpu.VMEM(s, F32) for s in scratch],
        compiler_params=pltpu.CompilerParams(vmem_limit_bytes=VMEM_LIMIT),
    )


def pairs(count, odd):
    out = []
    for i in range(odd, count - 1, 2):
        out += [(i, i + 1), (i + 1, i)]
    return out


def cross(nx, nz, upper):
    out = []
    for i in range(nx - 1):
        a, b = i * nz + (nz - 1 if upper else 0), (i + 1) * nz + (0 if upper else nz - 1)
        out += [(a, b), (b, a)]
    return out


def shards(u, t, m, lev, beam):
    nx, ny, nz = (lax.axis_size(a) for a in ("gx", "gy", "gz"))
    _, rows_x, own_y, _ = u.shape
    t, m = jnp.transpose(t, (1, 2, 0)), jnp.transpose(m, (1, 2, 0))
    rows, cols, depth = t.shape
    tiles = own_y // SUBL
    block = (SUBL, LANES)
    n_top = 2 * rows * cols // LANES
    top = (n_top // tiles, own_y, LANES)
    n_x = slab_size() + top[0]
    n_z = 2 * SKIN * cols // SUBL + n_top + tiles
    vmem = pl.BlockSpec(memory_space=pltpu.VMEM)
    hbm = pl.BlockSpec(memory_space=pltpu.HBM)

    def pack(*refs):
        pack_kernel(REACH, places(), *refs)

    whole = (2 * rows + 1, cols, depth)
    copies = 4 + 2 * (COMPS + 1 + len(DEEP_6) + top[0]) + 4
    shapes = [(n_x, own_y, LANES)] * 2 + [(n_z, *block)] * 2 + [(tiles, *block), whole]
    msg_a, msg_b, msg_z, msg_d, msg_h, part = pl.pallas_call(
        pack,
        out_shape=[jax.ShapeDtypeStruct(v, F32) for v in shapes],
        in_specs=[hbm] * 4,
        out_specs=[hbm] * 6,
        scratch_shapes=[pltpu.VMEM(u.shape, F32), pltpu.VMEM(m.shape, jnp.int32), pltpu.VMEM(lev.shape, jnp.int32)]
        + [pltpu.VMEM(v, F32) for v in shapes[2:]]
        + [pltpu.SemaphoreType.DMA((copies,))],
        compiler_params=pltpu.CompilerParams(vmem_limit_bytes=60 * 1024 * 1024),
    )(u, t, m, lev)
    u, part = call(hold_kernel, [u.shape, whole], count=2)(u, part)
    in_a = lax.ppermute(msg_a, "gx", pairs(nx, 0))
    in_b = lax.ppermute(msg_b, "gx", pairs(nx, 1))
    in_z = lax.ppermute(msg_z, "gz", pairs(nz, 0))
    in_d = lax.ppermute(msg_d, ("gx", "gz"), cross(nx, nz, True))
    in_h = lax.ppermute(msg_h, ("gx", "gz"), cross(nx, nz, False))
    n_y = (rows_x + 2 * NEAR) * COMPS // 2 + len(quarter_rows(rows_x, REACH)) + 3 + n_top
    n_part = rows + 2 * SKIN
    msg_a, msg_b, part_a, part_b = call(
        functools.partial(relay_kernel, (rows_x, REACH)), [(n_y, *block)] * 2 + [(n_part, *block)] * 2, count=7
    )(u, part, in_a, in_b, in_z, in_d, in_h)
    gy_b = lax.ppermute(msg_b, "gy", pairs(ny, 1))
    gy_a = lax.ppermute(msg_a, "gy", pairs(ny, 0))
    part_b = lax.ppermute(part_b, "gy", pairs(ny, 1))
    part_a = lax.ppermute(part_a, "gy", pairs(ny, 0))

    size = own_y + 2 * SUBL
    n = rows_x + 2 * REACH
    n2 = rows_x + 2 * REACH_LAST
    small = own_y + SUBL
    part_rows = 4 * SUBL
    n_m = -(-n2 // (LANES // GROUP))
    row = (size, LANES)
    own_row = (own_y, LANES)
    g1, f1, h0, h1, fh1 = call(
        functools.partial(inner_kernel, (rows_x, REACH)),
        [(COMPS, n, *row), (COMPS, n - 2, *own_row), (n, *row), (n, *row), (n - 2, *own_row)],
        scratch=[(COMPS, n - 1, *own_row)] * 2,
        count=6,
    )(u, in_a, in_b, in_z, in_d, in_h)
    g2, msg_m, top_t, top_k = call(
        functools.partial(first_kernel, (rows_x, REACH)),
        [
            (COMPS, n2, small, LANES),
            (n_m, small, LANES),
            (TOP - SUBSTEPS, part_rows, LANES),
            (TOP - SUBSTEPS, part_rows, LANES),
        ],
        scratch=[(COMPS, n, *row), (n, *row), (n, *row), (COMPS, n - 2, *row), (n - 2, *row)]
        + [(COMPS, n - 1, *block)] * 4
        + [(COMPS, n - 3, *row)] * 2
        + [(n - 4, own_y + 2 * (REACH - 2), LANES), (part_rows, LANES), (part_rows, *block)],
        scalars=1,
        count=12,
    )(beam, part, in_a, in_b, in_z, in_d, gy_a, gy_b, g1, f1, h0, h1, fh1)
    in_m = lax.ppermute(msg_m, "gz", pairs(nz, 0))
    field = (rows + 2 * SKIN, cols + SUBL, depth)
    (bulk,) = call(
        bulk_kernel, [t.shape], scratch=[field] * 7, scalars=1, count=5
    )(beam, part, in_z, in_d, part_a, part_b)
    low_row = (small, LANES)
    g_diff, g_total = call(terms_kernel, [(COMPS, n2 - 1, *low_row)] * 2, count=1)(g2)
    mine, other, mass, p, h, f, fh = call(
        functools.partial(last_kernel, (rows_x, own_y)),
        [
            (n_top // 2, *block),
            (n_top // 2, *block),
            (part_rows, LANES),
            (n2 - 4, own_y + 2 * (REACH_LAST - 2), LANES),
            (n2, *low_row),
            (COMPS, n2 - 2, *low_row),
            (n2 - 2, *low_row),
        ],
        scratch=[(n2, *low_row)] + [(COMPS, n2 - 1, *low_row)] * 2 + [(part_rows, *block)],
        scalars=1,
        count=7,
    )(beam, g2, g_diff, g_total, in_m, top_t, top_k, bulk)
    (gas,) = call(
        gas_kernel,
        [u.shape],
        scratch=[(2, n2 - 2, *low_row)] + [(COMPS, n2 - 1, *low_row)] * 2,
        count=8,
    )(g2, g_diff, g_total, mass, p, h, f, fh)
    given = lax.ppermute(other, "gz", pairs(nz, 0))
    (out,) = call(seal_kernel, [t.shape], count=3)(bulk, mine, given)
    return gas, jnp.transpose(out, (2, 0, 1))


def solution(mesh):
    return jax.shard_map(
        shards,
        mesh=mesh,
        in_specs=(
            P(None, "gx", "gy", "gz"),
            P(None, ("gx", "gz"), "gy"),
            P(None, ("gx", "gz"), "gy"),
            P("gx", "gy"),
            P(),
        ),
        out_specs=(P(None, "gx", "gy", "gz"), P(None, ("gx", "gz"), "gy")),
        check_vma=False,
    )
```

```python
import functools

import jax
import jax.numpy as jnp
from jax import lax
from jax.experimental import pallas as pl
from jax.experimental.pallas import tpu as pltpu
from jax.sharding import PartitionSpec as P

STEPS = 2
SUBSTEPS = 2
GAS_STEP = 0.3
DRIFT_SPEED = 0.5
VAPOR_LOAD = 0.3
AMBIENT_LOAD = 0.7
STIFFNESS = 1.0
VISCOSITY = (0.2, 0.1, 0.15, 0.15, 0.15, 0.2)
HEAT_STEP = 1.0
POWDER_COND = 0.04
SOLID_COND = 0.15
LIQUID_COND = 0.09
LASER_POWER = 3.0
SPOT_RADIUS = 6.0
ABSORB_DEPTH = 4.0
BOIL_LEVEL = 1.0
BACK_PRESSURE = 0.5
LATENT_HEAT = 0.3
VAPOR_SOURCE = 0.5
RECOIL_PUSH = 0.4
RECOIL_PRESSURE = 0.6

COMPS = 6
LANES = 128
VMEM_LIMIT = 32 * 1024 * 1024
SUBL = 8
F32 = jnp.float32
REACH = 6
REACH_LAST = 3
SKIN = 4
TOP = 8
GROUP = 16
LEVEL = 2 * COMPS


def iota(shape, axis):
    return lax.broadcasted_iota(jnp.int32, shape, axis)


def wrapped(index, own, size):
    return jnp.where(index < own + (size - own) // 2, index, index - size)


def turn(value, amount, axis):
    size = value.shape[axis]
    if isinstance(amount, int):
        amount = amount % size
        if amount == 0:
            return value
    return pltpu.roll(value, amount, axis)


def softplus(x):
    return jnp.maximum(x, 0.0) + jnp.log1p(jnp.exp(-jnp.abs(x)))


def pack_heights(rows, base, lane, low_z, acc):
    more = jnp.where(low_z, 2, 0)
    for c, row in enumerate(rows):
        acc = jnp.where((lane & -2) == base + 2 * c, turn(row, base + 2 * c + more, 1), acc)
    return acc


def unpack_heights(packed, base, low_z, h0, h1, i):
    here = turn(packed, -base, 1)
    other = turn(packed, -base - 1, 1)
    h0[i] = jnp.where(low_z, here, other)
    h1[i] = jnp.where(low_z, other, here)


DEEP_5 = (2, 3, 4, 5)
DEEP_6 = (2, 5)
FULL = 4
QUARTERS = (5, 3, 2, 4)
NEAR = 3


def quarter_rows(rows_x, reach):
    far = [x for d in range(NEAR + 1, reach) for x in (-d, rows_x + d - 1)]
    return [(x, 0) for x in far] + [(x, FULL) for x in range(-1, rows_x + 1)]


def slab_index(c, layer, below):
    if layer <= FULL:
        return c * FULL + (FULL - layer if below else layer - 1)
    base = COMPS * FULL
    if layer == FULL + 1:
        return base + DEEP_5.index(c) if c in DEEP_5 else None
    return base + len(DEEP_5) + DEEP_6.index(c) if c in DEEP_6 else None


def slab_size():
    return COMPS * FULL + len(DEEP_5) + len(DEEP_6)


def row_tile(c, x, tile, u, in_a, in_b, even_x):
    rows_x = u.shape[1]
    span = slice(tile * SUBL, (tile + 1) * SUBL)
    if 0 <= x < rows_x:
        return u[c, x, span, :]
    k = slab_index(c, -x if x < 0 else x - rows_x + 1, x < 0)
    if k is None:
        return None
    low, high = (in_b, in_a) if x < 0 else (in_a, in_b)
    return jnp.where(even_x, low[k, span, :], high[k, span, :])


def conduct(v):
    return jnp.where(v == 0, POWDER_COND, jnp.where(v == 1, SOLID_COND, LIQUID_COND)).astype(F32)


def surface_tops(t, m):
    rows, cols = t.shape[0], t.shape[1]
    per = LANES // cols
    out = []
    for ref in (t, m):
        for j in range(rows // per):
            block = ref[j * per : (j + 1) * per].reshape(LANES, LANES)
            out.append(jnp.transpose(block)[:TOP])
    return out


def pack_kernel(
    reach, meta, u_in, t_in, m_in, lev_in, to_a, to_b, to_z, to_d, to_h, to_part,
    u, m, lev, out_z, out_d, out_h, part, sems,
):
    rows_x, own_y = u.shape[1], u.shape[2]
    rows, cols = m.shape[0], m.shape[1]
    t, k = part.at[0:rows], part.at[rows : 2 * rows]
    pairs_in = ((u_in, u), (t_in, t), (m_in, m), (lev_in, lev))
    fetches = [pltpu.make_async_copy(src, dst, sems.at[i]) for i, (src, dst) in enumerate(pairs_in)]
    for copy in fetches:
        copy.start()
    even = lax.rem(meta[0], 2) == 0
    low_z = meta[2] == 0
    tiles = own_y // SUBL
    copies = []

    def send(src, dst):
        copy = pltpu.make_async_copy(src, dst, sems.at[len(fetches) + len(copies)])
        copy.start()
        copies.append(copy)

    fetches[0].wait()
    for out, high in ((to_a, even), (to_b, jnp.logical_not(even))):
        first = jnp.where(high, rows_x - FULL, 0)
        for c in range(COMPS):
            send(u.at[c, pl.ds(first, FULL)], out.at[pl.ds(c * FULL, FULL)])
        base = COMPS * FULL
        row = jnp.where(high, rows_x - FULL - 1, FULL)
        send(u.at[pl.ds(DEEP_5[0], len(DEEP_5)), row], out.at[pl.ds(base, len(DEEP_5))])
        row = jnp.where(high, rows_x - reach, reach - 1)
        for j, c in enumerate(DEEP_6):
            send(u.at[c, row], out.at[base + len(DEEP_5) + j])
    for copy in fetches[1:]:
        copy.wait()
    k[...] = conduct(m[...])
    tops = surface_tops(t, k)
    for j, value in enumerate(tops):
        part[2 * rows, j * SUBL : (j + 1) * SUBL, :] = value
    for out in (to_a, to_b):
        for j in range(cols // own_y):
            send(part.at[2 * rows, pl.ds(j * own_y, own_y)], out.at[slab_size() + j])
    send(part, to_part)
    col_tiles = cols // SUBL
    n = 0
    for ref in (t, k):
        for r in range(SKIN):
            for y in range(col_tiles):
                lo = ref[r, y * SUBL : (y + 1) * SUBL, :]
                hi = ref[rows - SKIN + r, y * SUBL : (y + 1) * SUBL, :]
                out_z[n] = jnp.where(low_z, hi, lo)
                out_d[n] = jnp.where(low_z, lo, hi)
                n += 1
    for j, value in enumerate(tops):
        out_z[n + j] = value
        out_d[n + j] = value
    n += len(tops)
    size = u.shape[2]
    lane = iota((size, LANES), 1)
    eye = iota((size, size), 0) == iota((size, size), 1)
    levels = lev[...].astype(F32)
    acc = jnp.zeros((size, LANES), F32)
    for x in range(rows_x):
        acc = pack_heights([u[c, x] for c in range(COMPS)], x * GROUP, lane, low_z, acc)
        level = jnp.sum(jnp.where(eye, levels[x : x + 1, :], 0.0), axis=1, keepdims=True)
        acc = jnp.where((lane & -2) == x * GROUP + LEVEL, level, acc)
    for y in range(tiles):
        part = acc[y * SUBL : (y + 1) * SUBL]
        out_h[y] = part
        out_z[n + y] = part
        out_d[n + y] = part
    for src, dst in ((out_z, to_z), (out_d, to_d), (out_h, to_h)):
        send(src, dst)
    for copy in copies:
        copy.wait()


def hold_kernel(meta, u_in, part_in, u, part):
    u[...] = u_in[...]
    part[...] = part_in[...]


def part_row(r, tile, ref, at, rows, in_z, in_d, low_z, col_tiles, low_part):
    if 0 <= r < rows:
        return ref[r, tile * SUBL : (tile + 1) * SUBL, :]
    k = (at * SKIN + (r + SKIN if r < 0 else r - rows)) * col_tiles + tile
    low, high = (in_d[k], in_z[k]) if r < 0 else (in_z[k], in_d[k])
    return jnp.where(low_z, low, high)


def relay_kernel(cells, meta, u, part, in_a, in_b, in_z, in_d, in_h, out_a, out_b, part_a, part_b):
    rows = part.shape[0] // 2
    t, m = part.at[0:rows], part.at[rows : 2 * rows]
    rows_x, reach = cells
    gx, gy, gz = meta[0], meta[1], meta[2]
    even_x = lax.rem(gx, 2) == 0
    even_y = lax.rem(gy, 2) == 0
    low_z = gz == 0
    tiles = u.shape[2] // SUBL
    rows, cols = t.shape[0], t.shape[1]
    col_tiles = cols // SUBL
    half = SUBL // 2
    sub = iota((SUBL, LANES), 0)
    lane = iota((SUBL, LANES), 1)
    zero = jnp.zeros((SUBL, LANES), F32)

    def put(n, hi, lo):
        out_a[n] = jnp.where(even_y, hi, lo)
        out_b[n] = jnp.where(even_y, lo, hi)

    def both(c, x):
        pair = [row_tile(c, x, y, u, in_a, in_b, even_x) for y in (tiles - 1, 0)]
        return [zero if v is None else v for v in pair]

    n = 0
    for x in range(-NEAR, rows_x + NEAR):
        for c in range(0, COMPS, 2):
            (hi0, lo0), (hi1, lo1) = both(c, x), both(c + 1, x)
            put(n, jnp.where(sub < half, turn(hi1, half, 0), hi0), jnp.where(sub < half, lo0, turn(lo1, half, 0)))
            n += 1
    for x, skip in quarter_rows(rows_x, reach):
        hi = lo = zero
        for q, c in enumerate(QUARTERS):
            a, b = both(c, x)
            hi = jnp.where((sub & -2) == 2 * q, turn(a, 2 * q - (SUBL - 2 - skip), 0), hi)
            lo = jnp.where((sub & -2) == 2 * q, turn(b, 2 * q - skip, 0), lo)
        put(n, hi, lo)
        n += 1
    base = in_z.shape[0] - tiles
    hi_y, lo_y = tiles - 1, 0
    put(
        n,
        jnp.where(low_z, in_d[base + hi_y], in_h[hi_y]),
        jnp.where(low_z, in_d[base + lo_y], in_h[lo_y]),
    )
    put(n + 1, in_z[base + hi_y], in_z[base + lo_y])
    put(
        n + 2,
        jnp.where(low_z, in_h[hi_y], in_d[base + hi_y]),
        jnp.where(low_z, in_h[lo_y], in_d[base + lo_y]),
    )
    n += 3
    for r in range(-SKIN, rows + SKIN):
        hi_t, lo_t = [part_row(r, y, t, 0, rows, in_z, in_d, low_z, col_tiles, None) for y in (col_tiles - 1, 0)]
        hi_k, lo_k = [part_row(r, y, m, 1, rows, in_z, in_d, low_z, col_tiles, None) for y in (col_tiles - 1, 0)]
        hi = jnp.where(sub < half, turn(hi_k, half, 0), hi_t)
        lo = jnp.where(sub < half, lo_t, turn(lo_k, half, 0))
        part_a[r + SKIN] = jnp.where(even_y, hi, lo)
        part_b[r + SKIN] = jnp.where(even_y, lo, hi)
    sources = surface_sources(part, in_a, in_b, in_z, in_d, even_x, tiles)
    per = LANES // cols
    slot = lax.rem(lane, cols) // SUBL
    for v in range(len(sources) // per):
        hi = lo = zero
        for i in range(per):
            src = sources[v * per + i]
            hi = jnp.where(slot == i, turn(src, SUBL * i - (cols - SUBL), 1), hi)
            lo = jnp.where(slot == i, turn(src, SUBL * i, 1), lo)
        put(n + v, hi, lo)


def surface_sources(part, in_a, in_b, in_z, in_d, even_x, tiles):
    count = part.shape[1] // SUBL
    at = in_z.shape[0] - tiles - count

    def high(j):
        k, span = slab_size() + j // tiles, slice(j % tiles * SUBL, (j % tiles + 1) * SUBL)
        return jnp.where(even_x, in_a[k, span, :], in_b[k, span, :])

    out = []
    for a in range(2):
        span = range(a * count // 2, (a + 1) * count // 2)
        out += [part[part.shape[0] - 1, j * SUBL : (j + 1) * SUBL, :] for j in span]
        out += [in_z[at + j] for j in span]
        out += [high(j) for j in span]
        out += [in_d[at + j] for j in span]
    return out


def heat_source(row, col, beam, step):
    a = beam[step, 0].astype(F32)
    b = beam[step, 1].astype(F32)
    along_x = jnp.exp(-(((row - a) / SPOT_RADIUS) ** 2))
    along_y = jnp.exp(-(((col - b) / SPOT_RADIUS) ** 2))
    return LASER_POWER * along_x * along_y


def bulk_kernel(meta, beam, part, in_z, in_d, gy_a, gy_b, out, temp, other, cond, kx, ky, kz, above):
    rows = part.shape[0] // 2
    t, m = part.at[0:rows], part.at[rows : 2 * rows]
    gx, gy, gz = meta[0], meta[1], meta[2]
    even_y = lax.rem(gy, 2) == 0
    low_z = gz == 0
    rows, cols, depth = t.shape
    col_tiles = cols // SUBL
    half = SUBL // 2
    size = cols + SUBL
    n = rows + 2 * SKIN
    sub = iota((SUBL, LANES), 0)
    for i in range(n):
        for y in range(col_tiles):
            span = slice(y * SUBL, (y + 1) * SUBL)
            temp[i, span, :] = part_row(i - SKIN, y, t, 0, rows, in_z, in_d, low_z, col_tiles, None)
            cond[i, span, :] = part_row(i - SKIN, y, m, 1, rows, in_z, in_d, low_z, col_tiles, None)
        up = jnp.where(even_y, gy_a[i], gy_b[i])
        low = jnp.where(even_y, gy_b[i], gy_a[i])
        temp[i, cols:size, :] = jnp.where(sub < half, up, low)
        cond[i, cols:size, :] = turn(jnp.where(sub < half, low, up), half, 0)

    lane = iota((size, LANES), 1)
    for i in range(n):
        k = cond[i]
        if i + 1 < n:
            kx[i] = 0.5 * (k + cond[i + 1])
        ky[i] = 0.5 * (k + turn(k, -1, 0))
        kz[i] = 0.5 * (k + jnp.where(lane == depth - 1, 0.0, turn(k, -1, 1)))
        above[i] = 0.5 * (k + jnp.where(lane == 0, 0.0, turn(k, 1, 1)))

    col_g = gy * cols + wrapped(iota((size, LANES), 0), cols, size)
    inside_y = jnp.where((col_g >= 0) & (col_g < meta[4] * cols), 1.0, 0.0)
    col_f = col_g.astype(F32)
    fall = jnp.exp(-lane.astype(F32) / ABSORB_DEPTH)
    first_row = (gx * meta[5] + gz) * rows - SKIN

    for s in range(STEPS * SUBSTEPS):
        src, dst = (temp, other) if s % 2 == 0 else (other, temp)
        last = s == STEPS * SUBSTEPS - 1
        a = beam[s, 0].astype(F32)
        b = beam[s, 1].astype(F32)
        spot = LASER_POWER * fall * jnp.exp(-(((col_f - b) / SPOT_RADIUS) ** 2))
        lo, hi = s + 1, n - 1 - s
        fx0 = kx[lo - 1] * (src[lo] - src[lo - 1])
        for i in range(lo, hi):
            v = src[i]
            fx = kx[i] * (src[i + 1] - v)
            fy = ky[i] * (turn(v, -1, 0) - v)
            down = kz[i] * (jnp.where(lane == depth - 1, 0.0, turn(v, -1, 1)) - v)
            up = above[i] * (jnp.where(lane == 0, 0.0, turn(v, 1, 1)) - v)
            row = first_row + i
            along_x = jnp.exp(-((jnp.full((1, LANES), row.astype(F32) - a) / SPOT_RADIUS) ** 2))
            change = (fx - fx0) + (fy - turn(fy, 1, 0)) + (down + up) + spot * along_x
            new = v + HEAT_STEP * change
            if last:
                out[i - SKIN] = new[:cols]
            else:
                ok = (row >= 0) & (row < meta[3] * meta[5] * rows)
                dst[i] = new * (inside_y * jnp.where(ok, 1.0, 0.0))
            fx0 = fx


def seal_kernel(meta, bulk, mine, given, out):
    rows, cols, depth = bulk.shape
    per = LANES // cols
    lane = iota((LANES, LANES), 1)
    for j in range(mine.shape[0]):
        skin = jnp.where(meta[2] == 0, mine[j], given[j])
        skin = jnp.concatenate([skin, jnp.zeros((LANES - SUBL, LANES), F32)], axis=0)
        block = jnp.where(lane < SKIN, jnp.transpose(skin), bulk[j * per : (j + 1) * per].reshape(LANES, LANES))
        out[j * per : (j + 1) * per] = block.reshape(per, cols, LANES)


def pack_skin(t, rows, cols, scratch, out):
    per = LANES // cols
    lane = iota((SUBL, LANES), 1)
    for j in range(SUBL // per):
        acc = jnp.zeros((SUBL, LANES), F32)
        for q in range(per):
            acc = jnp.where(lane // cols == q, turn(scratch[rows + j * per + q], cols * q, 1), acc)
        out[j] = acc


def split(value):
    high = value.astype(jnp.bfloat16)
    rest = (value - high.astype(F32)).astype(jnp.bfloat16)
    return jnp.concatenate([high, rest], axis=1)


def height_matrix():
    shape = (2 * LANES, 2 * LANES)
    k = iota(shape, 0) & (LANES - 1)
    j = iota(shape, 1)
    above = jnp.where(k == (j & (LANES - 1)) + 1, 1.0, 0.0)
    below = jnp.where(k == (j & (LANES - 1)) - 1, 1.0, 0.0)
    return (above + jnp.where(j < LANES, -below, below)).astype(jnp.bfloat16)


def height_terms(ref, first, last, matrix, diff, total, start=0, comps=tuple(range(COMPS))):
    size = diff.shape[2]
    for c in comps:
        rows = ref[c, first:last, start : start + size].reshape((last - first) * size, LANES)
        both = jnp.dot(split(rows), matrix, preferred_element_type=F32)
        diff[c, first:last] = both[:, :LANES].reshape(last - first, size, LANES)
        total[c, first:last] = both[:, LANES:].reshape(last - first, size, LANES)


def cut_weights(low_z, scale):
    lane = iota((1, LANES), 1)
    up = (lane == LANES - 1) & low_z
    down = (lane == 0) & jnp.logical_not(low_z)
    weight = {}
    for v in sorted(set(VISCOSITY)):
        side = scale * GAS_STEP * v
        drift = 0.5 * DRIFT_SPEED * scale * GAS_STEP
        weight[v] = jnp.where(up, side - drift, jnp.where(down, side + drift, 0.0))
    return jnp.where(up, 1.0, jnp.where(down, -1.0, 0.0)), weight


def stepped(comps, ref, i, diff, total, h, cut, scale, start, size, skip=0):
    sign, weight = cut
    half = 0.5 * scale * GAS_STEP
    span = pl.ds(start, size)
    terms = pl.ds(start - skip, size)

    def dx(c):
        return ref[c, i + 1, span, :] - ref[c, i - 1, span, :]

    def dy(c):
        return ref[c, i, pl.ds(start + 1, size), :] - ref[c, i, pl.ds(start - 1, size), :]

    def dz(c):
        return diff[c, i, terms, :] + sign * h[i, span, 2 * c : 2 * c + 1]

    spread = half * (dx(2) + dy(3) + dz(4))
    out = {}
    for c in comps:
        v = VISCOSITY[c]
        side = scale * GAS_STEP * v
        drift = 0.5 * DRIFT_SPEED * scale * GAS_STEP
        sides = (ref[c, i + 1, span, :] + ref[c, i - 1, span, :]) + (
            ref[c, i, pl.ds(start + 1, size), :] + ref[c, i, pl.ds(start - 1, size), :]
        )
        across = h[i, span, 2 * c : 2 * c + 1]
        new = (
            scale * (1.0 - 6.0 * GAS_STEP * v) * ref[c, i, span, :]
            + side * (sides + total[c, i, terms, :])
            - drift * diff[c, i, terms, :]
            + weight[v] * across
        )
        if c == 2:
            new = new - half * dx(5)
        elif c == 3:
            new = new - half * dy(5)
        elif c == 4:
            new = new - half * dz(5)
        else:
            new = new - {0: VAPOR_LOAD, 1: AMBIENT_LOAD, 5: STIFFNESS}[c] * spread
        out[c] = new
    return out


def by_comp(lane, values):
    out = jnp.full(lane.shape, values[-1], F32)
    for c, v in enumerate(values[:-1]):
        out = jnp.where(lane == 2 * c, v, out)
    return out


def couple_matrix():
    shape = (6 * LANES, LANES)
    k = iota(shape, 0)
    j = iota(shape, 1)
    axis = k // (2 * LANES)
    lane = k & (LANES - 1)
    spread = (lane == 4 + 2 * axis) & ((j == 0) | (j == 2) | (j == 10))
    slope = (lane == 10) & (j == 4 + 2 * axis)
    return jnp.where(spread | slope, 1.0, 0.0).astype(jnp.bfloat16)


def halo_stepped(h0, h1, g, low_z, mask_of, start, size, out, at):
    n = h0.shape[0]
    span = slice(start, start + size)
    rows = (n - 2) * size
    lane = iota((1, LANES), 1)
    more = jnp.where(low_z, 1, 0)
    flat_lane = iota((rows, LANES), 1)
    touch = jnp.zeros((rows, LANES), F32)
    for c in range(COMPS):
        own = g[c, 1 : n - 1, span].reshape(rows, LANES)
        touch = jnp.where(flat_lane == 2 * c, turn(own, 2 * c + more, 1), touch)
    mid = h0[1 : n - 1, span].reshape(rows, LANES)
    east = h0[2:n, span].reshape(rows, LANES)
    west = h0[0 : n - 2, span].reshape(rows, LANES)
    if start:
        north = h0[1 : n - 1, start + 1 : start + size + 1].reshape(rows, LANES)
        south = h0[1 : n - 1, start - 1 : start + size - 1].reshape(rows, LANES)
    else:
        north, south = turn(mid, -1, 0), turn(mid, 1, 0)
    behind = h1[1 : n - 1, span].reshape(rows, LANES)
    slopes = [east - west, north - south, jnp.where(low_z, 1.0, -1.0) * (behind - touch)]
    coupled = jnp.dot(
        jnp.concatenate([split(v) for v in slopes], axis=1), couple_matrix(), preferred_element_type=F32
    )
    up = by_comp(lane, [GAS_STEP * (v - 0.5 * DRIFT_SPEED) for v in VISCOSITY])
    down = by_comp(lane, [GAS_STEP * (v + 0.5 * DRIFT_SPEED) for v in VISCOSITY])
    half = 0.5 * GAS_STEP
    pull = by_comp(lane, [-half * VAPOR_LOAD, -half * AMBIENT_LOAD, -half, -half, -half, -half * STIFFNESS])
    new = (
        by_comp(lane, [1.0 - 6.0 * GAS_STEP * v for v in VISCOSITY]) * mid
        + by_comp(lane, [GAS_STEP * v for v in VISCOSITY]) * ((east + west) + (north + south))
        + jnp.where(low_z, up, down) * behind
        + jnp.where(low_z, down, up) * touch
        + pull * coupled
    )
    for i in range(1, n - 1):
        row = new[(i - 1) * size : i * size] * mask_of(i, start, size)
        if at < 0:
            row, at_row = turn(row, at, 0), 0
        else:
            at_row = at
        out[i - 1, at_row : at_row + size] = row


def grid_masks(meta, n, size, own_x, own_y):
    before, before_y = (n - own_x) // 2, (size - own_y) // 2

    def mask_of(i, start, count):
        x_g = meta[0] * own_x + i - before
        ok = (x_g >= 0) & (x_g < meta[3] * own_x)
        y_g = meta[1] * own_y + iota((count, LANES), 0) + start - before_y
        return jnp.where((y_g >= 0) & (y_g < meta[4] * own_y), 1.0, 0.0) * jnp.where(ok, 1.0, 0.0)

    return mask_of


def first_stage(meta, g, h0, windows, f, mask_of, unroll, comps=tuple(range(COMPS)), edge=(2, 5)):
    n = g.shape[1]
    cut = cut_weights(meta[2] == 0, 1.0)

    def one(comps):
        def body(i, carry):
            for start, size, diff, total, skip, at in windows:
                new = stepped(comps, g, i, diff, total, h0, cut, 1.0, start, size, skip)
                m = mask_of(i, start, size)
                for c in comps:
                    f[c, i - 1, at : at + size, :] = new[c] * m
            return carry

        return body

    lax.fori_loop(2, n - 2, one(comps), 0, unroll=unroll)
    for i in (1, n - 2) if edge else ():
        one(edge)(i, 0)


def second_stage(meta, g, f, fh, diff, total, skip, reach, own_y, mask_of, store):
    start = (g.shape[2] - own_y) // 2 - reach
    count = own_y + 2 * reach
    cut = cut_weights(meta[2] == 0, 0.5)

    def two(comps):
        def body(i, carry):
            new = stepped(comps, f, i - 1, diff, total, fh, cut, 0.5, start - skip, count)
            m = mask_of(i, start, count)
            for c in comps:
                new[c] = (0.5 * g[c, i, pl.ds(start, count), :] + new[c]) * m
            store(i, new)
            return carry

        return body

    return two


class Joined:
    def __init__(self, low, high):
        self.low, self.high = low, high

    def __getitem__(self, key):
        return (self.low if key[0] < self.low.shape[0] else self.high)[key]


def lane_sums(value):
    high = value.astype(jnp.bfloat16)
    rest = value - high.astype(F32)
    middle = rest.astype(jnp.bfloat16)
    low = (rest - middle.astype(F32)).astype(jnp.bfloat16)
    parts = jnp.concatenate([high, middle, low], axis=1)
    ones = jnp.ones((3 * LANES, LANES), jnp.bfloat16)
    return jnp.dot(parts, ones, preferred_element_type=F32)


def fine_pressure(meta, p, h0, own_x, own_y, part_rows):
    n, count = p.shape[0], p.shape[1]
    skip = (h0.shape[1] - count) // 2
    skip_x = (h0.shape[0] - n) // 2
    before = (n - own_x) // 2
    y_l = iota((count, LANES), 0) - (count - own_y) // 2
    col_y = lax.div(wrapped(iota((count, LANES), 1), 2 * own_y, LANES) + LANES, 2) - LANES // 2
    pick = col_y == y_l
    row_x = lax.div(wrapped(iota((part_rows, LANES), 0), 2 * own_x, part_rows) + LANES, 2) - LANES // 2
    height = (iota((count, LANES), 1) + meta[2] * LANES).astype(F32)
    fine = jnp.zeros((part_rows, LANES), F32)
    full = -(-count // SUBL) * SUBL
    pad = [jnp.zeros((full - count, LANES), F32)] if full > count else []
    found = []
    for i in range(n):
        level = h0[i + skip_x, skip : skip + count, LEVEL : LEVEL + 1]
        found += [jnp.where(height == level, p[i], 0.0)] + pad
    at = lane_sums(jnp.concatenate(found, axis=0))
    for i in range(n):
        line = jnp.sum(jnp.where(pick, at[i * full : i * full + count], 0.0), axis=0, keepdims=True)
        fine = jnp.where(row_x == i - before, line, fine)
    return fine


def top_heat(meta, beam, first, t, k, fine, own_rows, cols):
    gx, gy = meta[0], meta[1]
    shape = fine.shape
    row = gx * own_rows + wrapped(iota(shape, 0), own_rows, shape[0])
    col = gy * cols + wrapped(iota(shape, 1), cols, shape[1])
    row, col = row.astype(F32), col.astype(F32)
    deep = TOP - 1 - first
    kx = [0.5 * (v + turn(v, -1, 0)) for v in k[:deep]]
    ky = [0.5 * (v + turn(v, -1, 1)) for v in k[:deep]]
    ky_low = [0.5 * (v + turn(v, 1, 1)) for v in k[:deep]]
    kz = [0.5 * (k[d] + k[d + 1]) for d in range(deep)]
    for s in range(SUBSTEPS):
        beam_xy = heat_source(row, col, beam, first + s)
        before = 0.5 * k[0] * t[0]
        new = []
        for d in range(TOP - 1 - first - s):
            fx = kx[d] * (turn(t[d], -1, 0) - t[d])
            fy = ky[d] * (turn(t[d], -1, 1) - t[d]) + ky_low[d] * (turn(t[d], 1, 1) - t[d])
            fz = kz[d] * (t[d + 1] - t[d])
            factor = jnp.exp(jnp.full(shape, -d / ABSORB_DEPTH, F32))
            change = (fx - turn(fx, 1, 0)) + fy + (fz - before) + beam_xy * factor
            if d == 0:
                change = change - LATENT_HEAT * softplus(t[0] - BOIL_LEVEL - BACK_PRESSURE * fine)
            new.append(jnp.where(k[d] > 0, t[d] + HEAT_STEP * change, 0.0))
            before = fz
        t = new
    return t


def vapor_mass(t0, fine):
    four = t0 + turn(t0, -1, 1)
    four = four + turn(four, -1, 0)
    return softplus(0.25 * four - BOIL_LEVEL - BACK_PRESSURE * fine)


def mass_rows(meta, h, mass, first, rows, count, own_y):
    skip = (h.shape[1] - count) // 2
    skip_x = (h.shape[0] - rows) // 2
    y_l = iota((count, LANES), 0) - (count - own_y) // 2
    col = wrapped(iota((count, LANES), 1), 2 * own_y, LANES)
    pick = col == 2 * y_l
    height = (iota((count, LANES), 1) + meta[2] * LANES).astype(F32)
    found = []
    for i in range(rows):
        r = (2 * (i + first)) % mass.shape[0]
        found.append(jnp.where(pick, mass[r : r + 1, :], 0.0))
    at = lane_sums(jnp.concatenate(found, axis=0))
    out = []
    for i in range(rows):
        level = h[i + skip_x, skip : skip + count, LEVEL : LEVEL + 1]
        out.append(jnp.where(height == level, at[i * count : (i + 1) * count], 0.0))
    return out


def inner_kernel(cells, meta, u, in_a, in_b, in_z, in_d, in_h, g, f, h0, h1, fh, diff, total):
    rows_x, reach = cells
    even_x = lax.rem(meta[0], 2) == 0
    low_z = meta[2] == 0
    own_y = u.shape[2]
    tiles = own_y // SUBL
    size = g.shape[2]
    n = g.shape[1]
    zero = jnp.zeros((SUBL, LANES), F32)
    for x in range(-reach, rows_x + reach):
        for c in range(COMPS):
            for y in range(tiles):
                value = row_tile(c, x, y, u, in_a, in_b, even_x)
                g[c, x + reach, (y + 1) * SUBL : (y + 2) * SUBL, :] = zero if value is None else value
    base = in_z.shape[0] - tiles
    for b in range(3):
        parts = []
        for y in range(tiles):
            if b == 0:
                parts.append(jnp.where(low_z, in_d[base + y], in_h[y]))
            elif b == 1:
                parts.append(in_z[base + y])
            else:
                parts.append(jnp.where(low_z, in_h[y], in_d[base + y]))
        unpack_group(jnp.concatenate(parts, axis=0), b, rows_x, reach, low_z, h0, h1, SUBL, own_y)
    mask_of = grid_masks(meta, n, size, rows_x, own_y)
    halo_stepped(h0, h1, g, low_z, mask_of, SUBL, own_y, fh, 0)
    height_terms(g, 1, n - 1, height_matrix(), diff, total, SUBL)
    first_stage(meta, g, h0, [(SUBL, own_y, diff, total, SUBL, 0)], f, mask_of, True)


def unpack_group(packed, b, rows_x, reach, low_z, h0, h1, start, size):
    for x in range(-reach, rows_x + reach):
        if (x + rows_x) // rows_x == b:
            base = GROUP * ((x + rows_x) % rows_x)
            here, other = turn(packed, -base, 1), turn(packed, -base - 1, 1)
            h0[x + reach, start : start + size] = jnp.where(low_z, here, other)
            h1[x + reach, start : start + size] = jnp.where(low_z, other, here)


def first_kernel(
    cells, meta, beam, part, in_a, in_b, in_z, in_d, gy_a, gy_b, g_in, f_in, h0_in, h1_in, fh_in,
    out_g, out_m, out_t, out_k, g, h, h1, f, fh, diff_lo, total_lo, diff_hi, total_hi, diff, total, p, mass, skin,
):
    rows_x, reach = cells
    gx, gy, gz = meta[0], meta[1], meta[2]
    even_x = lax.rem(gx, 2) == 0
    even_y = lax.rem(gy, 2) == 0
    low_z = gz == 0
    n, size = g.shape[1], g.shape[2]
    own_y = size - 2 * SUBL
    tiles = own_y // SUBL
    half = SUBL // 2
    sub = iota((SUBL, LANES), 0)
    zero = jnp.zeros((SUBL, LANES), F32)
    inner = slice(SUBL, SUBL + own_y)

    def side(k):
        upper = jnp.where(even_y, gy_a[k], gy_b[k])
        lower = jnp.where(even_y, gy_b[k], gy_a[k])
        return upper, lower

    quarter = (rows_x + 2 * NEAR) * COMPS // 2
    places_of = {}
    for k, (x, skip) in enumerate(quarter_rows(rows_x, reach)):
        places_of[x, skip] = quarter + k
    for x in range(-reach, rows_x + reach):
        i = x + reach
        for c in range(COMPS):
            g[c, i, inner, :] = g_in[c, i, inner, :]
            upper = lower = zero
            if -NEAR <= x < rows_x + NEAR:
                near_up, near_low = side((x + NEAR) * COMPS // 2 + c // 2)
                if c % 2:
                    near_up, near_low = turn(near_up, half, 0), turn(near_low, half, 0)
                upper = jnp.where(sub < half, near_up, 0.0)
                lower = jnp.where(sub >= half, near_low, 0.0)
            for skip in (0, FULL):
                if (x, skip) in places_of and c in QUARTERS:
                    q = 2 * QUARTERS.index(c)
                    up, low = side(places_of[x, skip])
                    upper = jnp.where((sub & -2) == skip, turn(up, skip - q, 0), upper)
                    lower = jnp.where((sub & -2) == SUBL - 2 - skip, turn(low, SUBL - 2 - skip - q, 0), lower)
            g[c, i, own_y + SUBL : size, :] = upper
            g[c, i, :SUBL, :] = lower
    h[:, inner, :] = h0_in[:, inner, :]
    h1[:, inner, :] = h1_in[:, inner, :]
    for b in range(3):
        upper, lower = side(quarter + len(places_of) + b)
        unpack_group(lower, b, rows_x, reach, low_z, h, h1, 0, SUBL)
        unpack_group(upper, b, rows_x, reach, low_z, h, h1, own_y + SUBL, SUBL)

    def store(i, new):
        p[i - 2] = new[COMPS - 1]
        if len(new) > 1:
            for c in range(COMPS):
                out_g[c, i - 3] = new[c] if c in new else jnp.zeros_like(new[COMPS - 1])

    mask_of = grid_masks(meta, n, size, rows_x, own_y)
    f[:, :, inner, :] = f_in[...]
    fh[:, inner, :] = fh_in[...]
    upper_at = size - SUBL - 1
    windows = []
    for start, d, t in ((1, diff_lo, total_lo), (upper_at, diff_hi, total_hi)):
        halo_stepped(h, h1, g, low_z, mask_of, start, SUBL, fh, start)
        height_terms(g, 1, n - 1, height_matrix(), d, t, start)
        windows.append((start, SUBL, d, t, start, start))
    first_stage(meta, g, h, windows, f, mask_of, True)
    height_terms(f, 1, n - 3, height_matrix(), diff, total)
    two = second_stage(meta, g, f, fh, diff, total, 0, reach - 2, own_y, mask_of, store)
    lax.fori_loop(4, n - 4, two(tuple(range(COMPS))), 0, unroll=True)
    for i in (2, n - 3):
        two((5,))(i, 0)
    for i in (3, n - 4):
        two((2, 5))(i, 0)
    fine = fine_pressure(meta, p, h, rows_x, own_y, mass.shape[0])

    cols = LANES // 4
    per = LANES // cols
    lane = iota((SUBL, LANES), 1)
    sources = surface_sources(part, in_a, in_b, in_z, in_d, even_x, tiles)
    count = len(sources) // 2
    top_at = gy_a.shape[0] - len(sources) // per
    layers = []
    for a in range(2):
        for s in range(count):
            src = sources[a * count + s]
            upper, lower = side(top_at + (a * count + s) // per)
            i = s % per
            for q in range(per):
                at = cols * q + SUBL * i
                skin[s * per + q] = jnp.where(
                    lane < cols,
                    turn(src, -cols * q, 1),
                    jnp.where(
                        lane < cols + SUBL,
                        turn(upper, cols - at, 1),
                        jnp.where(lane >= LANES - SUBL, turn(lower, LANES - SUBL - at, 1), 0.0),
                    ),
                )
        for d in range(TOP):
            layers.append(skin[:, d, :])
    t, k = layers[:TOP], layers[TOP:]
    t = top_heat(meta, beam, 0, t, k, fine, 2 * rows_x, cols)
    for d in range(TOP - SUBSTEPS):
        out_t[d] = t[d]
        out_k[d] = k[d]
    mass[...] = vapor_mass(t[0], fine)

    count, small = out_g.shape[1], out_g.shape[2]
    masses = mass_rows(meta, h, mass, -REACH_LAST, count, small, own_y)
    lane_s = iota((small, LANES), 1)
    y_g = gy * own_y + iota((small, LANES), 0) - (small - own_y) // 2
    inside_y = jnp.where((y_g >= 0) & (y_g < meta[4] * own_y), 1.0, 0.0)
    skip = (size - small) // 2
    per = LANES // GROUP
    acc = jnp.zeros((small, LANES), F32)
    for i in range(count):
        x = i - REACH_LAST
        x_g = gx * rows_x + x
        ok = jnp.where((x_g >= 0) & (x_g < meta[3] * rows_x), 1.0, 0.0)
        add = masses[i] * (inside_y * ok)
        rows = [out_g[c, i] for c in range(COMPS)]
        for c, load in ((0, VAPOR_SOURCE), (4, RECOIL_PUSH), (5, RECOIL_PRESSURE)):
            rows[c] = rows[c] + load * add
            out_g[c, i] = rows[c]
        j, q = divmod(i, per)
        acc = pack_heights(rows, GROUP * q, lane_s, low_z, acc)
        level = h[x + reach, skip : skip + small, LEVEL : LEVEL + 1]
        acc = jnp.where((lane_s & -2) == GROUP * q + LEVEL, level, acc)
        if q == per - 1 or i == count - 1:
            out_m[j] = acc
            acc = jnp.zeros((small, LANES), F32)


def last_kernel(
    cells, meta, beam, g, g_diff, g_total, in_m, in_t, in_k, bulk, out_t, out_f, mass, p, h, f, fh, h1, diff, total, skin
):
    rows_x, own_y = cells
    n, size = g.shape[1], g.shape[2]
    for i in range(n):
        j, q = divmod(i, LANES // GROUP)
        unpack_heights(in_m[j], GROUP * q, meta[2] == 0, h, h1, i)
    mask_of = grid_masks(meta, n, size, rows_x, own_y)
    matrix = height_matrix()
    halo_stepped(h, h1, g, meta[2] == 0, mask_of, 0, size, fh, -1)
    flow = tuple(range(2, COMPS))
    first_stage(meta, g, h, [(1, size - 2, g_diff, g_total, 0, 0)], f, mask_of, True, flow)
    height_terms(f, 1, n - 3, matrix, diff, total, 0, (4, 5))

    def store(i, new):
        p[i - 2] = new[COMPS - 1]

    two = second_stage(meta, g, f, fh, diff, total, 1, REACH_LAST - 2, own_y, mask_of, store)
    lax.fori_loop(2, n - 2, two((COMPS - 1,)), 0, unroll=True)
    fine = fine_pressure(meta, p, h, rows_x, own_y, mass.shape[0])
    cols = LANES // 4
    t = [in_t[d] for d in range(TOP - SUBSTEPS)]
    k = [in_k[d] for d in range(TOP - SUBSTEPS)]
    t = top_heat(meta, beam, SUBSTEPS, t, k, fine, 2 * rows_x, cols)
    skin[...] = jnp.zeros_like(skin)
    for d in range(SKIN):
        skin[:, d, :] = t[d]
    pack_skin(t, 0, cols, skin, out_t)
    pack_skin(t, SUBL, cols, skin, out_f)
    mass[...] = vapor_mass(t[0], fine)


def terms_kernel(meta, g, diff, total):
    height_terms(g, 1, g.shape[1] - 1, height_matrix(), diff, total)


def gas_kernel(meta, g, g_diff, g_total, mass, p, h, flow, fh, out_g, f, diff, total):
    rows_x, own_y = out_g.shape[1], out_g.shape[2]
    n, size = g.shape[1], g.shape[2]
    matrix = height_matrix()
    mask_of = grid_masks(meta, n, size, rows_x, own_y)
    first_stage(meta, g, h, [(1, size - 2, g_diff, g_total, 0, 0)], f, mask_of, True, (0, 1), ())
    both = Joined(f, flow)
    height_terms(both, 2, n - 4, matrix, diff, total, 0, tuple(range(COMPS)))
    masses = mass_rows(meta, h, mass, 0, rows_x, own_y, own_y)
    loads = {0: VAPOR_SOURCE, 4: RECOIL_PUSH, 5: RECOIL_PRESSURE}

    def store(i, new):
        x = i - (n - rows_x) // 2
        for c in new:
            out_g[c, x] = new[c] + loads[c] * masses[x] if c in loads else new[c]

    two = second_stage(meta, g, both, fh, diff, total, 1, 0, own_y, lambda i, start, count: 1.0, store)
    for i in range(REACH_LAST, n - REACH_LAST):
        two(tuple(range(COMPS - 1)))(i, 0)
        x = i - (n - rows_x) // 2
        out_g[COMPS - 1, x] = p[i - 2, 1 : own_y + 1] + RECOIL_PRESSURE * masses[x]


def places():
    axes = ("gx", "gy", "gz")
    return [lax.axis_index(a) for a in axes] + [lax.axis_size(a) for a in axes]


def call(body, outs, scratch=(), scalars=0, count=0):
    def kernel(*refs):
        body(places(), *refs)

    vmem = pl.BlockSpec(memory_space=pltpu.VMEM)
    smem = pl.BlockSpec(memory_space=pltpu.SMEM)
    return pl.pallas_call(
        kernel,
        out_shape=[jax.ShapeDtypeStruct(s, F32) for s in outs],
        in_specs=[smem] * scalars + [vmem] * count,
        out_specs=[vmem] * len(outs),
        scratch_shapes=[pltpu.VMEM(s, F32) for s in scratch],
        compiler_params=pltpu.CompilerParams(vmem_limit_bytes=VMEM_LIMIT),
    )


def pairs(count, odd):
    out = []
    for i in range(odd, count - 1, 2):
        out += [(i, i + 1), (i + 1, i)]
    return out


def cross(nx, nz, upper):
    out = []
    for i in range(nx - 1):
        a, b = i * nz + (nz - 1 if upper else 0), (i + 1) * nz + (0 if upper else nz - 1)
        out += [(a, b), (b, a)]
    return out


def shards(u, t, m, lev, beam):
    nx, ny, nz = (lax.axis_size(a) for a in ("gx", "gy", "gz"))
    _, rows_x, own_y, _ = u.shape
    t, m = jnp.transpose(t, (1, 2, 0)), jnp.transpose(m, (1, 2, 0))
    rows, cols, depth = t.shape
    tiles = own_y // SUBL
    block = (SUBL, LANES)
    n_top = 2 * rows * cols // LANES
    top = (n_top // tiles, own_y, LANES)
    n_x = slab_size() + top[0]
    n_z = 2 * SKIN * cols // SUBL + n_top + tiles
    vmem = pl.BlockSpec(memory_space=pltpu.VMEM)
    hbm = pl.BlockSpec(memory_space=pltpu.HBM)

    def pack(*refs):
        pack_kernel(REACH, places(), *refs)

    whole = (2 * rows + 1, cols, depth)
    copies = 4 + 2 * (COMPS + 1 + len(DEEP_6) + top[0]) + 4
    shapes = [(n_x, own_y, LANES)] * 2 + [(n_z, *block)] * 2 + [(tiles, *block), whole]
    msg_a, msg_b, msg_z, msg_d, msg_h, part = pl.pallas_call(
        pack,
        out_shape=[jax.ShapeDtypeStruct(v, F32) for v in shapes],
        in_specs=[hbm] * 4,
        out_specs=[hbm] * 6,
        scratch_shapes=[pltpu.VMEM(u.shape, F32), pltpu.VMEM(m.shape, jnp.int32), pltpu.VMEM(lev.shape, jnp.int32)]
        + [pltpu.VMEM(v, F32) for v in shapes[2:]]
        + [pltpu.SemaphoreType.DMA((copies,))],
        compiler_params=pltpu.CompilerParams(vmem_limit_bytes=60 * 1024 * 1024),
    )(u, t, m, lev)
    u, part = call(hold_kernel, [u.shape, whole], count=2)(u, part)
    in_a = lax.ppermute(msg_a, "gx", pairs(nx, 0))
    in_b = lax.ppermute(msg_b, "gx", pairs(nx, 1))
    in_z = lax.ppermute(msg_z, "gz", pairs(nz, 0))
    in_d = lax.ppermute(msg_d, ("gx", "gz"), cross(nx, nz, True))
    in_h = lax.ppermute(msg_h, ("gx", "gz"), cross(nx, nz, False))
    n_y = (rows_x + 2 * NEAR) * COMPS // 2 + len(quarter_rows(rows_x, REACH)) + 3 + n_top
    n_part = rows + 2 * SKIN
    msg_a, msg_b, part_a, part_b = call(
        functools.partial(relay_kernel, (rows_x, REACH)), [(n_y, *block)] * 2 + [(n_part, *block)] * 2, count=7
    )(u, part, in_a, in_b, in_z, in_d, in_h)
    gy_b = lax.ppermute(msg_b, "gy", pairs(ny, 1))
    gy_a = lax.ppermute(msg_a, "gy", pairs(ny, 0))
    part_b = lax.ppermute(part_b, "gy", pairs(ny, 1))
    part_a = lax.ppermute(part_a, "gy", pairs(ny, 0))

    size = own_y + 2 * SUBL
    n = rows_x + 2 * REACH
    n2 = rows_x + 2 * REACH_LAST
    small = own_y + SUBL
    part_rows = 4 * SUBL
    n_m = -(-n2 // (LANES // GROUP))
    row = (size, LANES)
    own_row = (own_y, LANES)
    g1, f1, h0, h1, fh1 = call(
        functools.partial(inner_kernel, (rows_x, REACH)),
        [(COMPS, n, *row), (COMPS, n - 2, *own_row), (n, *row), (n, *row), (n - 2, *own_row)],
        scratch=[(COMPS, n - 1, *own_row)] * 2,
        count=6,
    )(u, in_a, in_b, in_z, in_d, in_h)
    g2, msg_m, top_t, top_k = call(
        functools.partial(first_kernel, (rows_x, REACH)),
        [
            (COMPS + 1, n2, small, LANES),
            (n_m, small, LANES),
            (TOP - SUBSTEPS, part_rows, LANES),
            (TOP - SUBSTEPS, part_rows, LANES),
        ],
        scratch=[(COMPS, n, *row), (n, *row), (n, *row), (COMPS, n - 2, *row), (n - 2, *row)]
        + [(COMPS, n - 1, *block)] * 4
        + [(COMPS, n - 3, *row)] * 2
        + [(n - 4, own_y + 2 * (REACH - 2), LANES), (part_rows, LANES), (part_rows, *block)],
        scalars=1,
        count=12,
    )(beam, part, in_a, in_b, in_z, in_d, gy_a, gy_b, g1, f1, h0, h1, fh1)
    in_m = lax.ppermute(msg_m, "gz", pairs(nz, 0))
    field = (rows + 2 * SKIN, cols + SUBL, depth)
    (bulk,) = call(
        bulk_kernel, [t.shape], scratch=[field] * 7, scalars=1, count=5
    )(beam, part, in_z, in_d, part_a, part_b)
    low_row = (small, LANES)
    g_diff, g_total = call(terms_kernel, [(COMPS + 1, n2 - 1, *low_row)] * 2, count=1)(g2)
    mine, other, mass, p, h, f, fh = call(
        functools.partial(last_kernel, (rows_x, own_y)),
        [
            (n_top // 2, *block),
            (n_top // 2, *block),
            (part_rows, LANES),
            (n2 - 4, own_y + 2 * (REACH_LAST - 2), LANES),
            (n2, *low_row),
            (COMPS + 1, n2 - 2, *low_row),
            (n2 - 2, *low_row),
        ],
        scratch=[(n2, *low_row)] + [(COMPS + 1, n2 - 1, *low_row)] * 2 + [(part_rows, *block)],
        scalars=1,
        count=7,
    )(beam, g2, g_diff, g_total, in_m, top_t, top_k, bulk)
    (gas,) = call(
        gas_kernel,
        [u.shape],
        scratch=[(2, n2 - 2, *low_row)] + [(COMPS, n2 - 1, *low_row)] * 2,
        count=8,
    )(g2, g_diff, g_total, mass, p, h, f, fh)
    given = lax.ppermute(other, "gz", pairs(nz, 0))
    (out,) = call(seal_kernel, [t.shape], count=3)(bulk, mine, given)
    return gas, jnp.transpose(out, (2, 0, 1))


def solution(mesh):
    return jax.shard_map(
        shards,
        mesh=mesh,
        in_specs=(
            P(None, "gx", "gy", "gz"),
            P(None, ("gx", "gz"), "gy"),
            P(None, ("gx", "gz"), "gy"),
            P("gx", "gy"),
            P(),
        ),
        out_specs=(P(None, "gx", "gy", "gz"), P(None, ("gx", "gz"), "gy")),
        check_vma=False,
    )
```

```python
import functools

import jax
import jax.numpy as jnp
from jax import lax
from jax.experimental import pallas as pl
from jax.experimental.pallas import tpu as pltpu
from jax.sharding import PartitionSpec as P

STEPS = 2
SUBSTEPS = 2
GAS_STEP = 0.3
DRIFT_SPEED = 0.5
VAPOR_LOAD = 0.3
AMBIENT_LOAD = 0.7
STIFFNESS = 1.0
VISCOSITY = (0.2, 0.1, 0.15, 0.15, 0.15, 0.2)
HEAT_STEP = 1.0
POWDER_COND = 0.04
SOLID_COND = 0.15
LIQUID_COND = 0.09
LASER_POWER = 3.0
SPOT_RADIUS = 6.0
ABSORB_DEPTH = 4.0
BOIL_LEVEL = 1.0
BACK_PRESSURE = 0.5
LATENT_HEAT = 0.3
VAPOR_SOURCE = 0.5
RECOIL_PUSH = 0.4
RECOIL_PRESSURE = 0.6

COMPS = 6
LANES = 128
VMEM_LIMIT = 32 * 1024 * 1024
SUBL = 8
F32 = jnp.float32
REACH = 6
REACH_LAST = 3
SKIN = 4
TOP = 8
GROUP = 16
LEVEL = 2 * COMPS


def iota(shape, axis):
    return lax.broadcasted_iota(jnp.int32, shape, axis)


def wrapped(index, own, size):
    return jnp.where(index < own + (size - own) // 2, index, index - size)


def turn(value, amount, axis):
    size = value.shape[axis]
    if isinstance(amount, int):
        amount = amount % size
        if amount == 0:
            return value
    return pltpu.roll(value, amount, axis)


def softplus(x):
    return jnp.maximum(x, 0.0) + jnp.log1p(jnp.exp(-jnp.abs(x)))


def pack_heights(rows, base, lane, low_z, acc):
    more = jnp.where(low_z, 2, 0)
    for c, row in enumerate(rows):
        acc = jnp.where((lane & -2) == base + 2 * c, turn(row, base + 2 * c + more, 1), acc)
    return acc


def unpack_heights(packed, base, low_z, h0, h1, i):
    here = turn(packed, -base, 1)
    other = turn(packed, -base - 1, 1)
    h0[i] = jnp.where(low_z, here, other)
    h1[i] = jnp.where(low_z, other, here)


DEEP_5 = (2, 3, 4, 5)
DEEP_6 = (2, 5)
FULL = 4
QUARTERS = (5, 3, 2, 4)
NEAR = 3


def quarter_rows(rows_x, reach):
    far = [x for d in range(NEAR + 1, reach) for x in (-d, rows_x + d - 1)]
    return [(x, 0) for x in far] + [(x, FULL) for x in range(-1, rows_x + 1)]


def slab_index(c, layer, below):
    if layer <= FULL:
        return c * FULL + (FULL - layer if below else layer - 1)
    base = COMPS * FULL
    if layer == FULL + 1:
        return base + DEEP_5.index(c) if c in DEEP_5 else None
    return base + len(DEEP_5) + DEEP_6.index(c) if c in DEEP_6 else None


def slab_size():
    return COMPS * FULL + len(DEEP_5) + len(DEEP_6)


def row_tile(c, x, tile, u, in_a, in_b, even_x):
    rows_x = u.shape[1]
    span = slice(tile * SUBL, (tile + 1) * SUBL)
    if 0 <= x < rows_x:
        return u[c, x, span, :]
    k = slab_index(c, -x if x < 0 else x - rows_x + 1, x < 0)
    if k is None:
        return None
    low, high = (in_b, in_a) if x < 0 else (in_a, in_b)
    return jnp.where(even_x, low[k, span, :], high[k, span, :])


def conduct(v):
    return jnp.where(v == 0, POWDER_COND, jnp.where(v == 1, SOLID_COND, LIQUID_COND)).astype(F32)


def surface_tops(t, m):
    rows, cols = t.shape[0], t.shape[1]
    per = LANES // cols
    out = []
    for ref in (t, m):
        for j in range(rows // per):
            block = ref[j * per : (j + 1) * per].reshape(LANES, LANES)
            out.append(jnp.transpose(block)[:TOP])
    return out


def pack_kernel(
    reach, meta, u_in, t_in, m_in, lev_in, to_a, to_b, to_z, to_d, to_h, to_part,
    u, m, lev, out_z, out_d, out_h, part, sems,
):
    rows_x, own_y = u.shape[1], u.shape[2]
    rows, cols = m.shape[0], m.shape[1]
    t, k = part.at[0:rows], part.at[rows : 2 * rows]
    pairs_in = ((u_in, u), (t_in, t), (m_in, m), (lev_in, lev))
    fetches = [pltpu.make_async_copy(src, dst, sems.at[i]) for i, (src, dst) in enumerate(pairs_in)]
    for copy in fetches:
        copy.start()
    even = lax.rem(meta[0], 2) == 0
    low_z = meta[2] == 0
    tiles = own_y // SUBL
    copies = []

    def send(src, dst):
        copy = pltpu.make_async_copy(src, dst, sems.at[len(fetches) + len(copies)])
        copy.start()
        copies.append(copy)

    fetches[0].wait()
    for out, high in ((to_a, even), (to_b, jnp.logical_not(even))):
        first = jnp.where(high, rows_x - FULL, 0)
        for c in range(COMPS):
            send(u.at[c, pl.ds(first, FULL)], out.at[pl.ds(c * FULL, FULL)])
        base = COMPS * FULL
        row = jnp.where(high, rows_x - FULL - 1, FULL)
        send(u.at[pl.ds(DEEP_5[0], len(DEEP_5)), row], out.at[pl.ds(base, len(DEEP_5))])
        row = jnp.where(high, rows_x - reach, reach - 1)
        for j, c in enumerate(DEEP_6):
            send(u.at[c, row], out.at[base + len(DEEP_5) + j])
    for copy in fetches[1:]:
        copy.wait()
    k[...] = conduct(m[...])
    tops = surface_tops(t, k)
    for j, value in enumerate(tops):
        part[2 * rows, j * SUBL : (j + 1) * SUBL, :] = value
    for out in (to_a, to_b):
        for j in range(cols // own_y):
            send(part.at[2 * rows, pl.ds(j * own_y, own_y)], out.at[slab_size() + j])
    send(part, to_part)
    col_tiles = cols // SUBL
    n = 0
    for ref in (t, k):
        for r in range(SKIN):
            for y in range(col_tiles):
                lo = ref[r, y * SUBL : (y + 1) * SUBL, :]
                hi = ref[rows - SKIN + r, y * SUBL : (y + 1) * SUBL, :]
                out_z[n] = jnp.where(low_z, hi, lo)
                out_d[n] = jnp.where(low_z, lo, hi)
                n += 1
    for j, value in enumerate(tops):
        out_z[n + j] = value
        out_d[n + j] = value
    n += len(tops)
    size = u.shape[2]
    lane = iota((size, LANES), 1)
    eye = iota((size, size), 0) == iota((size, size), 1)
    levels = lev[...].astype(F32)
    acc = jnp.zeros((size, LANES), F32)
    for x in range(rows_x):
        acc = pack_heights([u[c, x] for c in range(COMPS)], x * GROUP, lane, low_z, acc)
        level = jnp.sum(jnp.where(eye, levels[x : x + 1, :], 0.0), axis=1, keepdims=True)
        acc = jnp.where((lane & -2) == x * GROUP + LEVEL, level, acc)
    for y in range(tiles):
        part = acc[y * SUBL : (y + 1) * SUBL]
        out_h[y] = part
        out_z[n + y] = part
        out_d[n + y] = part
    for src, dst in ((out_z, to_z), (out_d, to_d), (out_h, to_h)):
        send(src, dst)
    for copy in copies:
        copy.wait()


def hold_kernel(meta, u_in, part_in, u, part):
    u[...] = u_in[...]
    part[...] = part_in[...]


def part_row(r, tile, ref, at, rows, in_z, in_d, low_z, col_tiles, low_part):
    if 0 <= r < rows:
        return ref[r, tile * SUBL : (tile + 1) * SUBL, :]
    k = (at * SKIN + (r + SKIN if r < 0 else r - rows)) * col_tiles + tile
    low, high = (in_d[k], in_z[k]) if r < 0 else (in_z[k], in_d[k])
    return jnp.where(low_z, low, high)


def relay_kernel(cells, meta, u, part, in_a, in_b, in_z, in_d, in_h, out_a, out_b, part_a, part_b):
    rows = part.shape[0] // 2
    t, m = part.at[0:rows], part.at[rows : 2 * rows]
    rows_x, reach = cells
    gx, gy, gz = meta[0], meta[1], meta[2]
    even_x = lax.rem(gx, 2) == 0
    even_y = lax.rem(gy, 2) == 0
    low_z = gz == 0
    tiles = u.shape[2] // SUBL
    rows, cols = t.shape[0], t.shape[1]
    col_tiles = cols // SUBL
    half = SUBL // 2
    sub = iota((SUBL, LANES), 0)
    lane = iota((SUBL, LANES), 1)
    zero = jnp.zeros((SUBL, LANES), F32)

    def put(n, hi, lo):
        out_a[n] = jnp.where(even_y, hi, lo)
        out_b[n] = jnp.where(even_y, lo, hi)

    def both(c, x):
        pair = [row_tile(c, x, y, u, in_a, in_b, even_x) for y in (tiles - 1, 0)]
        return [zero if v is None else v for v in pair]

    n = 0
    for x in range(-NEAR, rows_x + NEAR):
        for c in range(0, COMPS, 2):
            (hi0, lo0), (hi1, lo1) = both(c, x), both(c + 1, x)
            put(n, jnp.where(sub < half, turn(hi1, half, 0), hi0), jnp.where(sub < half, lo0, turn(lo1, half, 0)))
            n += 1
    for x, skip in quarter_rows(rows_x, reach):
        hi = lo = zero
        for q, c in enumerate(QUARTERS):
            a, b = both(c, x)
            hi = jnp.where((sub & -2) == 2 * q, turn(a, 2 * q - (SUBL - 2 - skip), 0), hi)
            lo = jnp.where((sub & -2) == 2 * q, turn(b, 2 * q - skip, 0), lo)
        put(n, hi, lo)
        n += 1
    base = in_z.shape[0] - tiles
    hi_y, lo_y = tiles - 1, 0
    put(
        n,
        jnp.where(low_z, in_d[base + hi_y], in_h[hi_y]),
        jnp.where(low_z, in_d[base + lo_y], in_h[lo_y]),
    )
    put(n + 1, in_z[base + hi_y], in_z[base + lo_y])
    put(
        n + 2,
        jnp.where(low_z, in_h[hi_y], in_d[base + hi_y]),
        jnp.where(low_z, in_h[lo_y], in_d[base + lo_y]),
    )
    n += 3
    for r in range(-SKIN, rows + SKIN):
        hi_t, lo_t = [part_row(r, y, t, 0, rows, in_z, in_d, low_z, col_tiles, None) for y in (col_tiles - 1, 0)]
        hi_k, lo_k = [part_row(r, y, m, 1, rows, in_z, in_d, low_z, col_tiles, None) for y in (col_tiles - 1, 0)]
        hi = jnp.where(sub < half, turn(hi_k, half, 0), hi_t)
        lo = jnp.where(sub < half, lo_t, turn(lo_k, half, 0))
        part_a[r + SKIN] = jnp.where(even_y, hi, lo)
        part_b[r + SKIN] = jnp.where(even_y, lo, hi)
    sources = surface_sources(part, in_a, in_b, in_z, in_d, even_x, tiles)
    per = LANES // cols
    slot = lax.rem(lane, cols) // SUBL
    for v in range(len(sources) // per):
        hi = lo = zero
        for i in range(per):
            src = sources[v * per + i]
            hi = jnp.where(slot == i, turn(src, SUBL * i - (cols - SUBL), 1), hi)
            lo = jnp.where(slot == i, turn(src, SUBL * i, 1), lo)
        put(n + v, hi, lo)


def surface_sources(part, in_a, in_b, in_z, in_d, even_x, tiles):
    count = part.shape[1] // SUBL
    at = in_z.shape[0] - tiles - count

    def high(j):
        k, span = slab_size() + j // tiles, slice(j % tiles * SUBL, (j % tiles + 1) * SUBL)
        return jnp.where(even_x, in_a[k, span, :], in_b[k, span, :])

    out = []
    for a in range(2):
        span = range(a * count // 2, (a + 1) * count // 2)
        out += [part[part.shape[0] - 1, j * SUBL : (j + 1) * SUBL, :] for j in span]
        out += [in_z[at + j] for j in span]
        out += [high(j) for j in span]
        out += [in_d[at + j] for j in span]
    return out


def heat_source(row, col, beam, step):
    a = beam[step, 0].astype(F32)
    b = beam[step, 1].astype(F32)
    along_x = jnp.exp(-(((row - a) / SPOT_RADIUS) ** 2))
    along_y = jnp.exp(-(((col - b) / SPOT_RADIUS) ** 2))
    return LASER_POWER * along_x * along_y


def bulk_kernel(meta, beam, part, in_z, in_d, gy_a, gy_b, out, temp, other, cond, kx, ky, kz, above):
    rows = part.shape[0] // 2
    t, m = part.at[0:rows], part.at[rows : 2 * rows]
    gx, gy, gz = meta[0], meta[1], meta[2]
    even_y = lax.rem(gy, 2) == 0
    low_z = gz == 0
    rows, cols, depth = t.shape
    col_tiles = cols // SUBL
    half = SUBL // 2
    size = cols + SUBL
    n = rows + 2 * SKIN
    sub = iota((SUBL, LANES), 0)
    for i in range(n):
        for y in range(col_tiles):
            span = slice(y * SUBL, (y + 1) * SUBL)
            temp[i, span, :] = part_row(i - SKIN, y, t, 0, rows, in_z, in_d, low_z, col_tiles, None)
            cond[i, span, :] = part_row(i - SKIN, y, m, 1, rows, in_z, in_d, low_z, col_tiles, None)
        up = jnp.where(even_y, gy_a[i], gy_b[i])
        low = jnp.where(even_y, gy_b[i], gy_a[i])
        temp[i, cols:size, :] = jnp.where(sub < half, up, low)
        cond[i, cols:size, :] = turn(jnp.where(sub < half, low, up), half, 0)

    lane = iota((size, LANES), 1)
    for i in range(n):
        k = cond[i]
        if i + 1 < n:
            kx[i] = 0.5 * (k + cond[i + 1])
        ky[i] = 0.5 * (k + turn(k, -1, 0))
        kz[i] = 0.5 * (k + jnp.where(lane == depth - 1, 0.0, turn(k, -1, 1)))
        above[i] = 0.5 * (k + jnp.where(lane == 0, 0.0, turn(k, 1, 1)))

    col_g = gy * cols + wrapped(iota((size, LANES), 0), cols, size)
    inside_y = jnp.where((col_g >= 0) & (col_g < meta[4] * cols), 1.0, 0.0)
    col_f = col_g.astype(F32)
    fall = jnp.exp(-lane.astype(F32) / ABSORB_DEPTH)
    first_row = (gx * meta[5] + gz) * rows - SKIN

    for s in range(STEPS * SUBSTEPS):
        src, dst = (temp, other) if s % 2 == 0 else (other, temp)
        last = s == STEPS * SUBSTEPS - 1
        a = beam[s, 0].astype(F32)
        b = beam[s, 1].astype(F32)
        spot = LASER_POWER * fall * jnp.exp(-(((col_f - b) / SPOT_RADIUS) ** 2))
        lo, hi = s + 1, n - 1 - s
        fx0 = kx[lo - 1] * (src[lo] - src[lo - 1])
        for i in range(lo, hi):
            v = src[i]
            fx = kx[i] * (src[i + 1] - v)
            fy = ky[i] * (turn(v, -1, 0) - v)
            down = kz[i] * (jnp.where(lane == depth - 1, 0.0, turn(v, -1, 1)) - v)
            up = above[i] * (jnp.where(lane == 0, 0.0, turn(v, 1, 1)) - v)
            row = first_row + i
            along_x = jnp.exp(-((jnp.full((1, LANES), row.astype(F32) - a) / SPOT_RADIUS) ** 2))
            change = (fx - fx0) + (fy - turn(fy, 1, 0)) + (down + up) + spot * along_x
            new = v + HEAT_STEP * change
            if last:
                out[i - SKIN] = new[:cols]
            else:
                ok = (row >= 0) & (row < meta[3] * meta[5] * rows)
                dst[i] = new * (inside_y * jnp.where(ok, 1.0, 0.0))
            fx0 = fx


def seal_kernel(meta, bulk, mine, given, out):
    rows, cols, depth = bulk.shape
    per = LANES // cols
    lane = iota((LANES, LANES), 1)
    for j in range(mine.shape[0]):
        skin = jnp.where(meta[2] == 0, mine[j], given[j])
        skin = jnp.concatenate([skin, jnp.zeros((LANES - SUBL, LANES), F32)], axis=0)
        block = jnp.where(lane < SKIN, jnp.transpose(skin), bulk[j * per : (j + 1) * per].reshape(LANES, LANES))
        out[j * per : (j + 1) * per] = block.reshape(per, cols, LANES)


def pack_skin(t, rows, cols, scratch, out):
    per = LANES // cols
    lane = iota((SUBL, LANES), 1)
    for j in range(SUBL // per):
        acc = jnp.zeros((SUBL, LANES), F32)
        for q in range(per):
            acc = jnp.where(lane // cols == q, turn(scratch[rows + j * per + q], cols * q, 1), acc)
        out[j] = acc


def split(value):
    high = value.astype(jnp.bfloat16)
    rest = (value - high.astype(F32)).astype(jnp.bfloat16)
    return jnp.concatenate([high, rest], axis=1)


def height_matrix():
    shape = (2 * LANES, 2 * LANES)
    k = iota(shape, 0) & (LANES - 1)
    j = iota(shape, 1)
    above = jnp.where(k == (j & (LANES - 1)) + 1, 1.0, 0.0)
    below = jnp.where(k == (j & (LANES - 1)) - 1, 1.0, 0.0)
    return (above + jnp.where(j < LANES, -below, below)).astype(jnp.bfloat16)


def height_terms(ref, first, last, matrix, diff, total, start=0, comps=tuple(range(COMPS))):
    size = diff.shape[2]
    for c in comps:
        rows = ref[c, first:last, start : start + size].reshape((last - first) * size, LANES)
        both = jnp.dot(split(rows), matrix, preferred_element_type=F32)
        diff[c, first:last] = both[:, :LANES].reshape(last - first, size, LANES)
        total[c, first:last] = both[:, LANES:].reshape(last - first, size, LANES)


def cut_weights(low_z, scale):
    lane = iota((1, LANES), 1)
    up = (lane == LANES - 1) & low_z
    down = (lane == 0) & jnp.logical_not(low_z)
    weight = {}
    for v in sorted(set(VISCOSITY)):
        side = scale * GAS_STEP * v
        drift = 0.5 * DRIFT_SPEED * scale * GAS_STEP
        weight[v] = jnp.where(up, side - drift, jnp.where(down, side + drift, 0.0))
    return jnp.where(up, 1.0, jnp.where(down, -1.0, 0.0)), weight


def stepped(comps, ref, i, diff, total, h, cut, scale, start, size, skip=0):
    sign, weight = cut
    half = 0.5 * scale * GAS_STEP
    span = pl.ds(start, size)
    terms = pl.ds(start - skip, size)

    def dx(c):
        return ref[c, i + 1, span, :] - ref[c, i - 1, span, :]

    def dy(c):
        return ref[c, i, pl.ds(start + 1, size), :] - ref[c, i, pl.ds(start - 1, size), :]

    def dz(c):
        return diff[c, i, terms, :] + sign * h[i, span, 2 * c : 2 * c + 1]

    spread = half * (dx(2) + dy(3) + dz(4))
    out = {}
    for c in comps:
        v = VISCOSITY[c]
        side = scale * GAS_STEP * v
        drift = 0.5 * DRIFT_SPEED * scale * GAS_STEP
        sides = (ref[c, i + 1, span, :] + ref[c, i - 1, span, :]) + (
            ref[c, i, pl.ds(start + 1, size), :] + ref[c, i, pl.ds(start - 1, size), :]
        )
        across = h[i, span, 2 * c : 2 * c + 1]
        new = (
            scale * (1.0 - 6.0 * GAS_STEP * v) * ref[c, i, span, :]
            + side * (sides + total[c, i, terms, :])
            - drift * diff[c, i, terms, :]
            + weight[v] * across
        )
        if c == 2:
            new = new - half * dx(5)
        elif c == 3:
            new = new - half * dy(5)
        elif c == 4:
            new = new - half * dz(5)
        else:
            new = new - {0: VAPOR_LOAD, 1: AMBIENT_LOAD, 5: STIFFNESS}[c] * spread
        out[c] = new
    return out


def by_comp(lane, values):
    out = jnp.full(lane.shape, values[-1], F32)
    for c, v in enumerate(values[:-1]):
        out = jnp.where(lane == 2 * c, v, out)
    return out


def couple_matrix():
    shape = (6 * LANES, LANES)
    k = iota(shape, 0)
    j = iota(shape, 1)
    axis = lax.shift_right_logical(k, (2 * LANES).bit_length() - 1)
    lane = k & (LANES - 1)
    spread = (lane == 4 + 2 * axis) & ((j == 0) | (j == 2) | (j == 10))
    slope = (lane == 10) & (j == 4 + 2 * axis)
    return jnp.where(spread | slope, 1.0, 0.0).astype(jnp.bfloat16)


def halo_stepped(h0, h1, g, low_z, mask_of, start, size, out, at, couple):
    n = h0.shape[0]
    span = slice(start, start + size)
    rows = (n - 2) * size
    lane = iota((1, LANES), 1)
    more = jnp.where(low_z, 1, 0)
    flat_lane = iota((rows, LANES), 1)
    touch = jnp.zeros((rows, LANES), F32)
    for c in range(COMPS):
        own = g[c, 1 : n - 1, span].reshape(rows, LANES)
        touch = jnp.where(flat_lane == 2 * c, turn(own, 2 * c + more, 1), touch)
    mid = h0[1 : n - 1, span].reshape(rows, LANES)
    east = h0[2:n, span].reshape(rows, LANES)
    west = h0[0 : n - 2, span].reshape(rows, LANES)
    if start:
        north = h0[1 : n - 1, start + 1 : start + size + 1].reshape(rows, LANES)
        south = h0[1 : n - 1, start - 1 : start + size - 1].reshape(rows, LANES)
    else:
        north, south = turn(mid, -1, 0), turn(mid, 1, 0)
    behind = h1[1 : n - 1, span].reshape(rows, LANES)
    slopes = [east - west, north - south, jnp.where(low_z, 1.0, -1.0) * (behind - touch)]
    coupled = jnp.dot(
        jnp.concatenate([split(v) for v in slopes], axis=1), couple, preferred_element_type=F32
    )
    up = by_comp(lane, [GAS_STEP * (v - 0.5 * DRIFT_SPEED) for v in VISCOSITY])
    down = by_comp(lane, [GAS_STEP * (v + 0.5 * DRIFT_SPEED) for v in VISCOSITY])
    half = 0.5 * GAS_STEP
    pull = by_comp(lane, [-half * VAPOR_LOAD, -half * AMBIENT_LOAD, -half, -half, -half, -half * STIFFNESS])
    new = (
        by_comp(lane, [1.0 - 6.0 * GAS_STEP * v for v in VISCOSITY]) * mid
        + by_comp(lane, [GAS_STEP * v for v in VISCOSITY]) * ((east + west) + (north + south))
        + jnp.where(low_z, up, down) * behind
        + jnp.where(low_z, down, up) * touch
        + pull * coupled
    )
    for i in range(1, n - 1):
        row = new[(i - 1) * size : i * size] * mask_of(i, start, size)
        if at < 0:
            row, at_row = turn(row, at, 0), 0
        else:
            at_row = at
        out[i - 1, at_row : at_row + size] = row


def grid_masks(meta, n, size, own_x, own_y):
    before, before_y = (n - own_x) // 2, (size - own_y) // 2

    def mask_of(i, start, count):
        x_g = meta[0] * own_x + i - before
        ok = (x_g >= 0) & (x_g < meta[3] * own_x)
        y_g = meta[1] * own_y + iota((count, LANES), 0) + start - before_y
        return jnp.where((y_g >= 0) & (y_g < meta[4] * own_y), 1.0, 0.0) * jnp.where(ok, 1.0, 0.0)

    return mask_of


def first_stage(meta, g, h0, windows, f, mask_of, unroll, comps=tuple(range(COMPS)), edge=(2, 5)):
    n = g.shape[1]
    cut = cut_weights(meta[2] == 0, 1.0)

    def one(comps):
        def body(i, carry):
            for start, size, diff, total, skip, at in windows:
                new = stepped(comps, g, i, diff, total, h0, cut, 1.0, start, size, skip)
                m = mask_of(i, start, size)
                for c in comps:
                    f[c, i - 1, at : at + size, :] = new[c] * m
            return carry

        return body

    lax.fori_loop(2, n - 2, one(comps), 0, unroll=unroll)
    for i in (1, n - 2) if edge else ():
        one(edge)(i, 0)


def second_stage(meta, g, f, fh, diff, total, skip, reach, own_y, mask_of, store):
    start = (g.shape[2] - own_y) // 2 - reach
    count = own_y + 2 * reach
    cut = cut_weights(meta[2] == 0, 0.5)

    def two(comps):
        def body(i, carry):
            new = stepped(comps, f, i - 1, diff, total, fh, cut, 0.5, start - skip, count)
            m = mask_of(i, start, count)
            for c in comps:
                new[c] = (0.5 * g[c, i, pl.ds(start, count), :] + new[c]) * m
            store(i, new)
            return carry

        return body

    return two


class Joined:
    def __init__(self, low, high):
        self.low, self.high = low, high

    def __getitem__(self, key):
        return (self.low if key[0] < self.low.shape[0] else self.high)[key]


def lane_sums(value):
    high = value.astype(jnp.bfloat16)
    rest = value - high.astype(F32)
    middle = rest.astype(jnp.bfloat16)
    low = (rest - middle.astype(F32)).astype(jnp.bfloat16)
    parts = jnp.concatenate([high, middle, low], axis=1)
    ones = jnp.ones((3 * LANES, LANES), jnp.bfloat16)
    return jnp.dot(parts, ones, preferred_element_type=F32)


def fine_pressure(meta, p, h0, own_x, own_y, part_rows):
    n, count = p.shape[0], p.shape[1]
    skip = (h0.shape[1] - count) // 2
    skip_x = (h0.shape[0] - n) // 2
    before = (n - own_x) // 2
    y_l = iota((count, LANES), 0) - (count - own_y) // 2
    col_y = lax.div(wrapped(iota((count, LANES), 1), 2 * own_y, LANES) + LANES, 2) - LANES // 2
    pick = col_y == y_l
    row_x = lax.div(wrapped(iota((part_rows, LANES), 0), 2 * own_x, part_rows) + LANES, 2) - LANES // 2
    height = (iota((count, LANES), 1) + meta[2] * LANES).astype(F32)
    fine = jnp.zeros((part_rows, LANES), F32)
    full = -(-count // SUBL) * SUBL
    pad = [jnp.zeros((full - count, LANES), F32)] if full > count else []
    found = []
    for i in range(n):
        level = h0[i + skip_x, skip : skip + count, LEVEL : LEVEL + 1]
        found += [jnp.where(height == level, p[i], 0.0)] + pad
    at = lane_sums(jnp.concatenate(found, axis=0))
    for i in range(n):
        line = jnp.sum(jnp.where(pick, at[i * full : i * full + count], 0.0), axis=0, keepdims=True)
        fine = jnp.where(row_x == i - before, line, fine)
    return fine


def top_heat(meta, beam, first, t, k, fine, own_rows, cols):
    gx, gy = meta[0], meta[1]
    shape = fine.shape
    row = gx * own_rows + wrapped(iota(shape, 0), own_rows, shape[0])
    col = gy * cols + wrapped(iota(shape, 1), cols, shape[1])
    row, col = row.astype(F32), col.astype(F32)
    deep = TOP - 1 - first
    kx = [0.5 * (v + turn(v, -1, 0)) for v in k[:deep]]
    ky = [0.5 * (v + turn(v, -1, 1)) for v in k[:deep]]
    ky_low = [0.5 * (v + turn(v, 1, 1)) for v in k[:deep]]
    kz = [0.5 * (k[d] + k[d + 1]) for d in range(deep)]
    for s in range(SUBSTEPS):
        beam_xy = heat_source(row, col, beam, first + s)
        before = 0.5 * k[0] * t[0]
        new = []
        for d in range(TOP - 1 - first - s):
            fx = kx[d] * (turn(t[d], -1, 0) - t[d])
            fy = ky[d] * (turn(t[d], -1, 1) - t[d]) + ky_low[d] * (turn(t[d], 1, 1) - t[d])
            fz = kz[d] * (t[d + 1] - t[d])
            factor = jnp.exp(jnp.full(shape, -d / ABSORB_DEPTH, F32))
            change = (fx - turn(fx, 1, 0)) + fy + (fz - before) + beam_xy * factor
            if d == 0:
                change = change - LATENT_HEAT * softplus(t[0] - BOIL_LEVEL - BACK_PRESSURE * fine)
            new.append(jnp.where(k[d] > 0, t[d] + HEAT_STEP * change, 0.0))
            before = fz
        t = new
    return t


def vapor_mass(t0, fine):
    four = t0 + turn(t0, -1, 1)
    four = four + turn(four, -1, 0)
    return softplus(0.25 * four - BOIL_LEVEL - BACK_PRESSURE * fine)


def mass_rows(meta, h, mass, first, rows, count, own_y):
    skip = (h.shape[1] - count) // 2
    skip_x = (h.shape[0] - rows) // 2
    y_l = iota((count, LANES), 0) - (count - own_y) // 2
    col = wrapped(iota((count, LANES), 1), 2 * own_y, LANES)
    pick = col == 2 * y_l
    height = (iota((count, LANES), 1) + meta[2] * LANES).astype(F32)
    found = []
    for i in range(rows):
        r = (2 * (i + first)) % mass.shape[0]
        found.append(jnp.where(pick, mass[r : r + 1, :], 0.0))
    at = lane_sums(jnp.concatenate(found, axis=0))
    out = []
    for i in range(rows):
        level = h[i + skip_x, skip : skip + count, LEVEL : LEVEL + 1]
        out.append(jnp.where(height == level, at[i * count : (i + 1) * count], 0.0))
    return out


def inner_kernel(cells, meta, u, in_a, in_b, in_z, in_d, in_h, g, f, h0, h1, fh, diff, total):
    rows_x, reach = cells
    even_x = lax.rem(meta[0], 2) == 0
    low_z = meta[2] == 0
    own_y = u.shape[2]
    tiles = own_y // SUBL
    size = g.shape[2]
    n = g.shape[1]
    zero = jnp.zeros((SUBL, LANES), F32)
    for x in range(-reach, rows_x + reach):
        for c in range(COMPS):
            for y in range(tiles):
                value = row_tile(c, x, y, u, in_a, in_b, even_x)
                g[c, x + reach, (y + 1) * SUBL : (y + 2) * SUBL, :] = zero if value is None else value
    base = in_z.shape[0] - tiles
    for b in range(3):
        parts = []
        for y in range(tiles):
            if b == 0:
                parts.append(jnp.where(low_z, in_d[base + y], in_h[y]))
            elif b == 1:
                parts.append(in_z[base + y])
            else:
                parts.append(jnp.where(low_z, in_h[y], in_d[base + y]))
        unpack_group(jnp.concatenate(parts, axis=0), b, rows_x, reach, low_z, h0, h1, SUBL, own_y)
    mask_of = grid_masks(meta, n, size, rows_x, own_y)
    halo_stepped(h0, h1, g, low_z, mask_of, SUBL, own_y, fh, 0, couple_matrix())
    height_terms(g, 1, n - 1, height_matrix(), diff, total, SUBL)
    first_stage(meta, g, h0, [(SUBL, own_y, diff, total, SUBL, 0)], f, mask_of, True)


def unpack_group(packed, b, rows_x, reach, low_z, h0, h1, start, size):
    for x in range(-reach, rows_x + reach):
        if (x + rows_x) // rows_x == b:
            base = GROUP * ((x + rows_x) % rows_x)
            here, other = turn(packed, -base, 1), turn(packed, -base - 1, 1)
            h0[x + reach, start : start + size] = jnp.where(low_z, here, other)
            h1[x + reach, start : start + size] = jnp.where(low_z, other, here)


def first_kernel(
    cells, meta, beam, part, in_a, in_b, in_z, in_d, gy_a, gy_b, g_in, f_in, h0_in, h1_in, fh_in,
    out_g, out_m, out_t, out_k, g, h, h1, f, fh, diff_lo, total_lo, diff_hi, total_hi, diff, total, p, mass, skin,
):
    rows_x, reach = cells
    gx, gy, gz = meta[0], meta[1], meta[2]
    even_x = lax.rem(gx, 2) == 0
    even_y = lax.rem(gy, 2) == 0
    low_z = gz == 0
    n, size = g.shape[1], g.shape[2]
    own_y = size - 2 * SUBL
    tiles = own_y // SUBL
    half = SUBL // 2
    sub = iota((SUBL, LANES), 0)
    zero = jnp.zeros((SUBL, LANES), F32)
    inner = slice(SUBL, SUBL + own_y)

    def side(k):
        upper = jnp.where(even_y, gy_a[k], gy_b[k])
        lower = jnp.where(even_y, gy_b[k], gy_a[k])
        return upper, lower

    quarter = (rows_x + 2 * NEAR) * COMPS // 2
    places_of = {}
    for k, (x, skip) in enumerate(quarter_rows(rows_x, reach)):
        places_of[x, skip] = quarter + k
    for x in range(-reach, rows_x + reach):
        i = x + reach
        for c in range(COMPS):
            g[c, i, inner, :] = g_in[c, i, inner, :]
            upper = lower = zero
            if -NEAR <= x < rows_x + NEAR:
                near_up, near_low = side((x + NEAR) * COMPS // 2 + c // 2)
                if c % 2:
                    near_up, near_low = turn(near_up, half, 0), turn(near_low, half, 0)
                upper = jnp.where(sub < half, near_up, 0.0)
                lower = jnp.where(sub >= half, near_low, 0.0)
            for skip in (0, FULL):
                if (x, skip) in places_of and c in QUARTERS:
                    q = 2 * QUARTERS.index(c)
                    up, low = side(places_of[x, skip])
                    upper = jnp.where((sub & -2) == skip, turn(up, skip - q, 0), upper)
                    lower = jnp.where((sub & -2) == SUBL - 2 - skip, turn(low, SUBL - 2 - skip - q, 0), lower)
            g[c, i, own_y + SUBL : size, :] = upper
            g[c, i, :SUBL, :] = lower
    h[:, inner, :] = h0_in[:, inner, :]
    h1[:, inner, :] = h1_in[:, inner, :]
    for b in range(3):
        upper, lower = side(quarter + len(places_of) + b)
        unpack_group(lower, b, rows_x, reach, low_z, h, h1, 0, SUBL)
        unpack_group(upper, b, rows_x, reach, low_z, h, h1, own_y + SUBL, SUBL)

    def store(i, new):
        p[i - 2] = new[COMPS - 1]
        if len(new) > 1:
            for c in range(COMPS):
                out_g[c, i - 3] = new[c] if c in new else jnp.zeros_like(new[COMPS - 1])

    mask_of = grid_masks(meta, n, size, rows_x, own_y)
    f[:, :, inner, :] = f_in[...]
    fh[:, inner, :] = fh_in[...]
    upper_at = size - SUBL - 1
    windows = []
    matrix, couple = height_matrix(), couple_matrix()
    for start, d, t in ((1, diff_lo, total_lo), (upper_at, diff_hi, total_hi)):
        halo_stepped(h, h1, g, low_z, mask_of, start, SUBL, fh, start, couple)
        height_terms(g, 1, n - 1, matrix, d, t, start)
        windows.append((start, SUBL, d, t, start, start))
    first_stage(meta, g, h, windows, f, mask_of, True)
    height_terms(f, 1, n - 3, matrix, diff, total)
    two = second_stage(meta, g, f, fh, diff, total, 0, reach - 2, own_y, mask_of, store)
    lax.fori_loop(4, n - 4, two(tuple(range(COMPS))), 0, unroll=True)
    for i in (2, n - 3):
        two((5,))(i, 0)
    for i in (3, n - 4):
        two((2, 5))(i, 0)
    fine = fine_pressure(meta, p, h, rows_x, own_y, mass.shape[0])

    cols = LANES // 4
    per = LANES // cols
    lane = iota((SUBL, LANES), 1)
    sources = surface_sources(part, in_a, in_b, in_z, in_d, even_x, tiles)
    count = len(sources) // 2
    top_at = gy_a.shape[0] - len(sources) // per
    layers = []
    for a in range(2):
        for s in range(count):
            src = sources[a * count + s]
            upper, lower = side(top_at + (a * count + s) // per)
            i = s % per
            for q in range(per):
                at = cols * q + SUBL * i
                skin[s * per + q] = jnp.where(
                    lane < cols,
                    turn(src, -cols * q, 1),
                    jnp.where(
                        lane < cols + SUBL,
                        turn(upper, cols - at, 1),
                        jnp.where(lane >= LANES - SUBL, turn(lower, LANES - SUBL - at, 1), 0.0),
                    ),
                )
        for d in range(TOP):
            layers.append(skin[:, d, :])
    t, k = layers[:TOP], layers[TOP:]
    t = top_heat(meta, beam, 0, t, k, fine, 2 * rows_x, cols)
    for d in range(TOP - SUBSTEPS):
        out_t[d] = t[d]
        out_k[d] = k[d]
    mass[...] = vapor_mass(t[0], fine)

    count, small = out_g.shape[1], out_g.shape[2]
    masses = mass_rows(meta, h, mass, -REACH_LAST, count, small, own_y)
    lane_s = iota((small, LANES), 1)
    y_g = gy * own_y + iota((small, LANES), 0) - (small - own_y) // 2
    inside_y = jnp.where((y_g >= 0) & (y_g < meta[4] * own_y), 1.0, 0.0)
    skip = (size - small) // 2
    per = LANES // GROUP
    acc = jnp.zeros((small, LANES), F32)
    for i in range(count):
        x = i - REACH_LAST
        x_g = gx * rows_x + x
        ok = jnp.where((x_g >= 0) & (x_g < meta[3] * rows_x), 1.0, 0.0)
        add = masses[i] * (inside_y * ok)
        rows = [out_g[c, i] for c in range(COMPS)]
        for c, load in ((0, VAPOR_SOURCE), (4, RECOIL_PUSH), (5, RECOIL_PRESSURE)):
            rows[c] = rows[c] + load * add
            out_g[c, i] = rows[c]
        j, q = divmod(i, per)
        acc = pack_heights(rows, GROUP * q, lane_s, low_z, acc)
        level = h[x + reach, skip : skip + small, LEVEL : LEVEL + 1]
        acc = jnp.where((lane_s & -2) == GROUP * q + LEVEL, level, acc)
        if q == per - 1 or i == count - 1:
            out_m[j] = acc
            acc = jnp.zeros((small, LANES), F32)


def last_kernel(
    cells, meta, beam, g, g_diff, g_total, in_m, in_t, in_k, bulk, out_t, out_f, mass, p, h, f, fh, h1, diff, total, skin
):
    rows_x, own_y = cells
    n, size = g.shape[1], g.shape[2]
    for i in range(n):
        j, q = divmod(i, LANES // GROUP)
        unpack_heights(in_m[j], GROUP * q, meta[2] == 0, h, h1, i)
    mask_of = grid_masks(meta, n, size, rows_x, own_y)
    matrix = height_matrix()
    halo_stepped(h, h1, g, meta[2] == 0, mask_of, 0, size, fh, -1, couple_matrix())
    flow = tuple(range(2, COMPS))
    first_stage(meta, g, h, [(1, size - 2, g_diff, g_total, 0, 0)], f, mask_of, True, flow)
    height_terms(f, 1, n - 3, matrix, diff, total, 0, (4, 5))

    def store(i, new):
        p[i - 2] = new[COMPS - 1]

    two = second_stage(meta, g, f, fh, diff, total, 1, REACH_LAST - 2, own_y, mask_of, store)
    lax.fori_loop(2, n - 2, two((COMPS - 1,)), 0, unroll=True)
    fine = fine_pressure(meta, p, h, rows_x, own_y, mass.shape[0])
    cols = LANES // 4
    t = [in_t[d] for d in range(TOP - SUBSTEPS)]
    k = [in_k[d] for d in range(TOP - SUBSTEPS)]
    t = top_heat(meta, beam, SUBSTEPS, t, k, fine, 2 * rows_x, cols)
    skin[...] = jnp.zeros_like(skin)
    for d in range(SKIN):
        skin[:, d, :] = t[d]
    pack_skin(t, 0, cols, skin, out_t)
    pack_skin(t, SUBL, cols, skin, out_f)
    mass[...] = vapor_mass(t[0], fine)


def terms_kernel(meta, g, diff, total):
    height_terms(g, 1, g.shape[1] - 1, height_matrix(), diff, total)


def gas_kernel(meta, g, g_diff, g_total, mass, p, h, flow, fh, out_g, f, diff, total):
    rows_x, own_y = out_g.shape[1], out_g.shape[2]
    n, size = g.shape[1], g.shape[2]
    matrix = height_matrix()
    mask_of = grid_masks(meta, n, size, rows_x, own_y)
    first_stage(meta, g, h, [(1, size - 2, g_diff, g_total, 0, 0)], f, mask_of, True, (0, 1), ())
    both = Joined(f, flow)
    height_terms(both, 2, n - 4, matrix, diff, total, 0, tuple(range(COMPS)))
    masses = mass_rows(meta, h, mass, 0, rows_x, own_y, own_y)
    loads = {0: VAPOR_SOURCE, 4: RECOIL_PUSH, 5: RECOIL_PRESSURE}

    def store(i, new):
        x = i - (n - rows_x) // 2
        for c in new:
            out_g[c, x] = new[c] + loads[c] * masses[x] if c in loads else new[c]

    two = second_stage(meta, g, both, fh, diff, total, 1, 0, own_y, lambda i, start, count: 1.0, store)
    for i in range(REACH_LAST, n - REACH_LAST):
        two(tuple(range(COMPS - 1)))(i, 0)
        x = i - (n - rows_x) // 2
        out_g[COMPS - 1, x] = p[i - 2, 1 : own_y + 1] + RECOIL_PRESSURE * masses[x]


def places():
    axes = ("gx", "gy", "gz")
    return [lax.axis_index(a) for a in axes] + [lax.axis_size(a) for a in axes]


def call(body, outs, scratch=(), scalars=0, count=0):
    def kernel(*refs):
        body(places(), *refs)

    vmem = pl.BlockSpec(memory_space=pltpu.VMEM)
    smem = pl.BlockSpec(memory_space=pltpu.SMEM)
    return pl.pallas_call(
        kernel,
        out_shape=[jax.ShapeDtypeStruct(s, F32) for s in outs],
        in_specs=[smem] * scalars + [vmem] * count,
        out_specs=[vmem] * len(outs),
        scratch_shapes=[pltpu.VMEM(s, F32) for s in scratch],
        compiler_params=pltpu.CompilerParams(vmem_limit_bytes=VMEM_LIMIT),
    )


def pairs(count, odd):
    out = []
    for i in range(odd, count - 1, 2):
        out += [(i, i + 1), (i + 1, i)]
    return out


def cross(nx, nz, upper):
    out = []
    for i in range(nx - 1):
        a, b = i * nz + (nz - 1 if upper else 0), (i + 1) * nz + (0 if upper else nz - 1)
        out += [(a, b), (b, a)]
    return out


def shards(u, t, m, lev, beam):
    nx, ny, nz = (lax.axis_size(a) for a in ("gx", "gy", "gz"))
    _, rows_x, own_y, _ = u.shape
    t, m = jnp.transpose(t, (1, 2, 0)), jnp.transpose(m, (1, 2, 0))
    rows, cols, depth = t.shape
    tiles = own_y // SUBL
    block = (SUBL, LANES)
    n_top = 2 * rows * cols // LANES
    top = (n_top // tiles, own_y, LANES)
    n_x = slab_size() + top[0]
    n_z = 2 * SKIN * cols // SUBL + n_top + tiles
    vmem = pl.BlockSpec(memory_space=pltpu.VMEM)
    hbm = pl.BlockSpec(memory_space=pltpu.HBM)

    def pack(*refs):
        pack_kernel(REACH, places(), *refs)

    whole = (2 * rows + 1, cols, depth)
    copies = 4 + 2 * (COMPS + 1 + len(DEEP_6) + top[0]) + 4
    shapes = [(n_x, own_y, LANES)] * 2 + [(n_z, *block)] * 2 + [(tiles, *block), whole]
    msg_a, msg_b, msg_z, msg_d, msg_h, part = pl.pallas_call(
        pack,
        out_shape=[jax.ShapeDtypeStruct(v, F32) for v in shapes],
        in_specs=[hbm] * 4,
        out_specs=[hbm] * 6,
        scratch_shapes=[pltpu.VMEM(u.shape, F32), pltpu.VMEM(m.shape, jnp.int32), pltpu.VMEM(lev.shape, jnp.int32)]
        + [pltpu.VMEM(v, F32) for v in shapes[2:]]
        + [pltpu.SemaphoreType.DMA((copies,))],
        compiler_params=pltpu.CompilerParams(vmem_limit_bytes=60 * 1024 * 1024),
    )(u, t, m, lev)
    u, part = call(hold_kernel, [u.shape, whole], count=2)(u, part)
    in_a = lax.ppermute(msg_a, "gx", pairs(nx, 0))
    in_b = lax.ppermute(msg_b, "gx", pairs(nx, 1))
    in_z = lax.ppermute(msg_z, "gz", pairs(nz, 0))
    in_d = lax.ppermute(msg_d, ("gx", "gz"), cross(nx, nz, True))
    in_h = lax.ppermute(msg_h, ("gx", "gz"), cross(nx, nz, False))
    n_y = (rows_x + 2 * NEAR) * COMPS // 2 + len(quarter_rows(rows_x, REACH)) + 3 + n_top
    n_part = rows + 2 * SKIN
    msg_a, msg_b, part_a, part_b = call(
        functools.partial(relay_kernel, (rows_x, REACH)), [(n_y, *block)] * 2 + [(n_part, *block)] * 2, count=7
    )(u, part, in_a, in_b, in_z, in_d, in_h)
    gy_b = lax.ppermute(msg_b, "gy", pairs(ny, 1))
    gy_a = lax.ppermute(msg_a, "gy", pairs(ny, 0))
    part_b = lax.ppermute(part_b, "gy", pairs(ny, 1))
    part_a = lax.ppermute(part_a, "gy", pairs(ny, 0))

    size = own_y + 2 * SUBL
    n = rows_x + 2 * REACH
    n2 = rows_x + 2 * REACH_LAST
    small = own_y + SUBL
    part_rows = 4 * SUBL
    n_m = -(-n2 // (LANES // GROUP))
    row = (size, LANES)
    own_row = (own_y, LANES)
    g1, f1, h0, h1, fh1 = call(
        functools.partial(inner_kernel, (rows_x, REACH)),
        [(COMPS, n, *row), (COMPS, n - 2, *own_row), (n, *row), (n, *row), (n - 2, *own_row)],
        scratch=[(COMPS, n - 1, *own_row)] * 2,
        count=6,
    )(u, in_a, in_b, in_z, in_d, in_h)
    g2, msg_m, top_t, top_k = call(
        functools.partial(first_kernel, (rows_x, REACH)),
        [
            (COMPS + 1, n2, small, LANES),
            (n_m, small, LANES),
            (TOP - SUBSTEPS, part_rows, LANES),
            (TOP - SUBSTEPS, part_rows, LANES),
        ],
        scratch=[(COMPS, n, *row), (n, *row), (n, *row), (COMPS, n - 2, *row), (n - 2, *row)]
        + [(COMPS, n - 1, *block)] * 4
        + [(COMPS, n - 3, *row)] * 2
        + [(n - 4, own_y + 2 * (REACH - 2), LANES), (part_rows, LANES), (part_rows, *block)],
        scalars=1,
        count=12,
    )(beam, part, in_a, in_b, in_z, in_d, gy_a, gy_b, g1, f1, h0, h1, fh1)
    in_m = lax.ppermute(msg_m, "gz", pairs(nz, 0))
    field = (rows + 2 * SKIN, cols + SUBL, depth)
    (bulk,) = call(
        bulk_kernel, [t.shape], scratch=[field] * 7, scalars=1, count=5
    )(beam, part, in_z, in_d, part_a, part_b)
    low_row = (small, LANES)
    g_diff, g_total = call(terms_kernel, [(COMPS + 1, n2 - 1, *low_row)] * 2, count=1)(g2)
    mine, other, mass, p, h, f, fh = call(
        functools.partial(last_kernel, (rows_x, own_y)),
        [
            (n_top // 2, *block),
            (n_top // 2, *block),
            (part_rows, LANES),
            (n2 - 4, own_y + 2 * (REACH_LAST - 2), LANES),
            (n2, *low_row),
            (COMPS + 1, n2 - 2, *low_row),
            (n2 - 2, *low_row),
        ],
        scratch=[(n2, *low_row)] + [(COMPS + 1, n2 - 1, *low_row)] * 2 + [(part_rows, *block)],
        scalars=1,
        count=7,
    )(beam, g2, g_diff, g_total, in_m, top_t, top_k, bulk)
    (gas,) = call(
        gas_kernel,
        [u.shape],
        scratch=[(2, n2 - 2, *low_row)] + [(COMPS, n2 - 1, *low_row)] * 2,
        count=8,
    )(g2, g_diff, g_total, mass, p, h, f, fh)
    given = lax.ppermute(other, "gz", pairs(nz, 0))
    (out,) = call(seal_kernel, [t.shape], count=3)(bulk, mine, given)
    return gas, jnp.transpose(out, (2, 0, 1))


def solution(mesh):
    return jax.shard_map(
        shards,
        mesh=mesh,
        in_specs=(
            P(None, "gx", "gy", "gz"),
            P(None, ("gx", "gz"), "gy"),
            P(None, ("gx", "gz"), "gy"),
            P("gx", "gy"),
            P(),
        ),
        out_specs=(P(None, "gx", "gy", "gz"), P(None, ("gx", "gz"), "gy")),
        check_vma=False,
    )
```

```python
import functools

import jax
import jax.numpy as jnp
from jax import lax
from jax.experimental import pallas as pl
from jax.experimental.pallas import tpu as pltpu
from jax.sharding import PartitionSpec as P

STEPS = 2
SUBSTEPS = 2
GAS_STEP = 0.3
DRIFT_SPEED = 0.5
VAPOR_LOAD = 0.3
AMBIENT_LOAD = 0.7
STIFFNESS = 1.0
VISCOSITY = (0.2, 0.1, 0.15, 0.15, 0.15, 0.2)
HEAT_STEP = 1.0
POWDER_COND = 0.04
SOLID_COND = 0.15
LIQUID_COND = 0.09
LASER_POWER = 3.0
SPOT_RADIUS = 6.0
ABSORB_DEPTH = 4.0
BOIL_LEVEL = 1.0
BACK_PRESSURE = 0.5
LATENT_HEAT = 0.3
VAPOR_SOURCE = 0.5
RECOIL_PUSH = 0.4
RECOIL_PRESSURE = 0.6

COMPS = 6
LANES = 128
VMEM_LIMIT = 32 * 1024 * 1024
SUBL = 8
F32 = jnp.float32
REACH = 6
REACH_LAST = 3
SKIN = 4
TOP = 8
GROUP = 16
LEVEL = 2 * COMPS


def iota(shape, axis):
    return lax.broadcasted_iota(jnp.int32, shape, axis)


def wrapped(index, own, size):
    return jnp.where(index < own + (size - own) // 2, index, index - size)


def turn(value, amount, axis):
    size = value.shape[axis]
    if isinstance(amount, int):
        amount = amount % size
        if amount == 0:
            return value
    return pltpu.roll(value, amount, axis)


def softplus(x):
    return jnp.maximum(x, 0.0) + jnp.log1p(jnp.exp(-jnp.abs(x)))


def pack_heights(rows, base, lane, low_z, acc):
    more = jnp.where(low_z, 2, 0)
    for c, row in enumerate(rows):
        acc = jnp.where((lane & -2) == base + 2 * c, turn(row, base + 2 * c + more, 1), acc)
    return acc


def unpack_heights(packed, base, low_z, h0, h1, i):
    here = turn(packed, -base, 1)
    other = turn(packed, -base - 1, 1)
    h0[i] = jnp.where(low_z, here, other)
    h1[i] = jnp.where(low_z, other, here)


DEEP_5 = (2, 3, 4, 5)
DEEP_6 = (2, 5)
FULL = 4
QUARTERS = (5, 3, 2, 4)
NEAR = 3


def quarter_rows(rows_x, reach):
    far = [x for d in range(NEAR + 1, reach) for x in (-d, rows_x + d - 1)]
    return [(x, 0) for x in far] + [(x, FULL) for x in range(-1, rows_x + 1)]


def slab_index(c, layer, below):
    if layer <= FULL:
        return c * FULL + (FULL - layer if below else layer - 1)
    base = COMPS * FULL
    if layer == FULL + 1:
        return base + DEEP_5.index(c) if c in DEEP_5 else None
    return base + len(DEEP_5) + DEEP_6.index(c) if c in DEEP_6 else None


def slab_size():
    return COMPS * FULL + len(DEEP_5) + len(DEEP_6)


def row_tile(c, x, tile, u, in_a, in_b, even_x):
    rows_x = u.shape[1]
    span = slice(tile * SUBL, (tile + 1) * SUBL)
    if 0 <= x < rows_x:
        return u[c, x, span, :]
    k = slab_index(c, -x if x < 0 else x - rows_x + 1, x < 0)
    if k is None:
        return None
    low, high = (in_b, in_a) if x < 0 else (in_a, in_b)
    return jnp.where(even_x, low[k, span, :], high[k, span, :])


def conduct(v):
    return jnp.where(v == 0, POWDER_COND, jnp.where(v == 1, SOLID_COND, LIQUID_COND)).astype(F32)


def surface_tops(t, m):
    rows, cols = t.shape[0], t.shape[1]
    per = LANES // cols
    out = []
    for ref in (t, m):
        for j in range(rows // per):
            block = ref[j * per : (j + 1) * per].reshape(LANES, LANES)
            out.append(jnp.transpose(block)[:TOP])
    return out


def pack_kernel(
    reach, meta, u_in, t_in, m_in, lev_in, to_a, to_b, to_z, to_d, to_h, to_part,
    u, m, lev, out_z, out_d, out_h, part, sems,
):
    rows_x, own_y = u.shape[1], u.shape[2]
    rows, cols = m.shape[0], m.shape[1]
    t, k = part.at[0:rows], part.at[rows : 2 * rows]
    pairs_in = ((u_in, u), (t_in, t), (m_in, m), (lev_in, lev))
    fetches = [pltpu.make_async_copy(src, dst, sems.at[i]) for i, (src, dst) in enumerate(pairs_in)]
    for copy in fetches:
        copy.start()
    even = lax.rem(meta[0], 2) == 0
    low_z = meta[2] == 0
    tiles = own_y // SUBL
    copies = []

    def send(src, dst):
        copy = pltpu.make_async_copy(src, dst, sems.at[len(fetches) + len(copies)])
        copy.start()
        copies.append(copy)

    fetches[0].wait()
    for out, high in ((to_a, even), (to_b, jnp.logical_not(even))):
        first = jnp.where(high, rows_x - FULL, 0)
        for c in range(COMPS):
            send(u.at[c, pl.ds(first, FULL)], out.at[pl.ds(c * FULL, FULL)])
        base = COMPS * FULL
        row = jnp.where(high, rows_x - FULL - 1, FULL)
        send(u.at[pl.ds(DEEP_5[0], len(DEEP_5)), row], out.at[pl.ds(base, len(DEEP_5))])
        row = jnp.where(high, rows_x - reach, reach - 1)
        for j, c in enumerate(DEEP_6):
            send(u.at[c, row], out.at[base + len(DEEP_5) + j])
    for copy in fetches[1:]:
        copy.wait()
    k[...] = conduct(m[...])
    tops = surface_tops(t, k)
    for j, value in enumerate(tops):
        part[2 * rows, j * SUBL : (j + 1) * SUBL, :] = value
    for out in (to_a, to_b):
        for j in range(cols // own_y):
            send(part.at[2 * rows, pl.ds(j * own_y, own_y)], out.at[slab_size() + j])
    send(part, to_part)
    col_tiles = cols // SUBL
    n = 0
    for ref in (t, k):
        for r in range(SKIN):
            for y in range(col_tiles):
                lo = ref[r, y * SUBL : (y + 1) * SUBL, :]
                hi = ref[rows - SKIN + r, y * SUBL : (y + 1) * SUBL, :]
                out_z[n] = jnp.where(low_z, hi, lo)
                out_d[n] = jnp.where(low_z, lo, hi)
                n += 1
    for j, value in enumerate(tops):
        out_z[n + j] = value
        out_d[n + j] = value
    n += len(tops)
    size = u.shape[2]
    lane = iota((size, LANES), 1)
    eye = iota((size, size), 0) == iota((size, size), 1)
    levels = lev[...].astype(F32)
    acc = jnp.zeros((size, LANES), F32)
    for x in range(rows_x):
        acc = pack_heights([u[c, x] for c in range(COMPS)], x * GROUP, lane, low_z, acc)
        level = jnp.sum(jnp.where(eye, levels[x : x + 1, :], 0.0), axis=1, keepdims=True)
        acc = jnp.where((lane & -2) == x * GROUP + LEVEL, level, acc)
    for y in range(tiles):
        part = acc[y * SUBL : (y + 1) * SUBL]
        out_h[y] = part
        out_z[n + y] = part
        out_d[n + y] = part
    for src, dst in ((out_z, to_z), (out_d, to_d), (out_h, to_h)):
        send(src, dst)
    for copy in copies:
        copy.wait()


def hold_kernel(meta, u_in, part_in, u, part):
    u[...] = u_in[...]
    part[...] = part_in[...]


def part_row(r, tile, ref, at, rows, in_z, in_d, low_z, col_tiles, low_part):
    if 0 <= r < rows:
        return ref[r, tile * SUBL : (tile + 1) * SUBL, :]
    k = (at * SKIN + (r + SKIN if r < 0 else r - rows)) * col_tiles + tile
    low, high = (in_d[k], in_z[k]) if r < 0 else (in_z[k], in_d[k])
    return jnp.where(low_z, low, high)


def relay_kernel(cells, meta, u, part, in_a, in_b, in_z, in_d, in_h, out_a, out_b, part_a, part_b):
    rows = part.shape[0] // 2
    t, m = part.at[0:rows], part.at[rows : 2 * rows]
    rows_x, reach = cells
    gx, gy, gz = meta[0], meta[1], meta[2]
    even_x = lax.rem(gx, 2) == 0
    even_y = lax.rem(gy, 2) == 0
    low_z = gz == 0
    tiles = u.shape[2] // SUBL
    rows, cols = t.shape[0], t.shape[1]
    col_tiles = cols // SUBL
    half = SUBL // 2
    sub = iota((SUBL, LANES), 0)
    lane = iota((SUBL, LANES), 1)
    zero = jnp.zeros((SUBL, LANES), F32)

    def put(n, hi, lo):
        out_a[n] = jnp.where(even_y, hi, lo)
        out_b[n] = jnp.where(even_y, lo, hi)

    def both(c, x):
        pair = [row_tile(c, x, y, u, in_a, in_b, even_x) for y in (tiles - 1, 0)]
        return [zero if v is None else v for v in pair]

    n = 0
    for x in range(-NEAR, rows_x + NEAR):
        for c in range(0, COMPS, 2):
            (hi0, lo0), (hi1, lo1) = both(c, x), both(c + 1, x)
            put(n, jnp.where(sub < half, turn(hi1, half, 0), hi0), jnp.where(sub < half, lo0, turn(lo1, half, 0)))
            n += 1
    for x, skip in quarter_rows(rows_x, reach):
        hi = lo = zero
        for q, c in enumerate(QUARTERS):
            a, b = both(c, x)
            hi = jnp.where((sub & -2) == 2 * q, turn(a, 2 * q - (SUBL - 2 - skip), 0), hi)
            lo = jnp.where((sub & -2) == 2 * q, turn(b, 2 * q - skip, 0), lo)
        put(n, hi, lo)
        n += 1
    base = in_z.shape[0] - tiles
    hi_y, lo_y = tiles - 1, 0
    put(
        n,
        jnp.where(low_z, in_d[base + hi_y], in_h[hi_y]),
        jnp.where(low_z, in_d[base + lo_y], in_h[lo_y]),
    )
    put(n + 1, in_z[base + hi_y], in_z[base + lo_y])
    put(
        n + 2,
        jnp.where(low_z, in_h[hi_y], in_d[base + hi_y]),
        jnp.where(low_z, in_h[lo_y], in_d[base + lo_y]),
    )
    n += 3
    for r in range(-SKIN, rows + SKIN):
        hi_t, lo_t = [part_row(r, y, t, 0, rows, in_z, in_d, low_z, col_tiles, None) for y in (col_tiles - 1, 0)]
        hi_k, lo_k = [part_row(r, y, m, 1, rows, in_z, in_d, low_z, col_tiles, None) for y in (col_tiles - 1, 0)]
        hi = jnp.where(sub < half, turn(hi_k, half, 0), hi_t)
        lo = jnp.where(sub < half, lo_t, turn(lo_k, half, 0))
        part_a[r + SKIN] = jnp.where(even_y, hi, lo)
        part_b[r + SKIN] = jnp.where(even_y, lo, hi)
    sources = surface_sources(part, in_a, in_b, in_z, in_d, even_x, tiles)
    per = LANES // cols
    slot = lax.rem(lane, cols) // SUBL
    for v in range(len(sources) // per):
        hi = lo = zero
        for i in range(per):
            src = sources[v * per + i]
            hi = jnp.where(slot == i, turn(src, SUBL * i - (cols - SUBL), 1), hi)
            lo = jnp.where(slot == i, turn(src, SUBL * i, 1), lo)
        put(n + v, hi, lo)


def surface_sources(part, in_a, in_b, in_z, in_d, even_x, tiles):
    count = part.shape[1] // SUBL
    at = in_z.shape[0] - tiles - count

    def high(j):
        k, span = slab_size() + j // tiles, slice(j % tiles * SUBL, (j % tiles + 1) * SUBL)
        return jnp.where(even_x, in_a[k, span, :], in_b[k, span, :])

    out = []
    for a in range(2):
        span = range(a * count // 2, (a + 1) * count // 2)
        out += [part[part.shape[0] - 1, j * SUBL : (j + 1) * SUBL, :] for j in span]
        out += [in_z[at + j] for j in span]
        out += [high(j) for j in span]
        out += [in_d[at + j] for j in span]
    return out


def heat_source(row, col, beam, step):
    a = beam[step, 0].astype(F32)
    b = beam[step, 1].astype(F32)
    along_x = jnp.exp(-(((row - a) / SPOT_RADIUS) ** 2))
    along_y = jnp.exp(-(((col - b) / SPOT_RADIUS) ** 2))
    return LASER_POWER * along_x * along_y


def bulk_kernel(meta, beam, part, in_z, in_d, gy_a, gy_b, out, temp, other, cond, kx, ky, kz, above):
    rows = part.shape[0] // 2
    t, m = part.at[0:rows], part.at[rows : 2 * rows]
    gx, gy, gz = meta[0], meta[1], meta[2]
    even_y = lax.rem(gy, 2) == 0
    low_z = gz == 0
    rows, cols, depth = t.shape
    col_tiles = cols // SUBL
    half = SUBL // 2
    size = cols + SUBL
    n = rows + 2 * SKIN
    sub = iota((SUBL, LANES), 0)
    for i in range(n):
        for y in range(col_tiles):
            span = slice(y * SUBL, (y + 1) * SUBL)
            temp[i, span, :] = part_row(i - SKIN, y, t, 0, rows, in_z, in_d, low_z, col_tiles, None)
            cond[i, span, :] = part_row(i - SKIN, y, m, 1, rows, in_z, in_d, low_z, col_tiles, None)
        up = jnp.where(even_y, gy_a[i], gy_b[i])
        low = jnp.where(even_y, gy_b[i], gy_a[i])
        temp[i, cols:size, :] = jnp.where(sub < half, up, low)
        cond[i, cols:size, :] = turn(jnp.where(sub < half, low, up), half, 0)

    lane = iota((size, LANES), 1)
    for i in range(n):
        k = cond[i]
        if i + 1 < n:
            kx[i] = 0.5 * (k + cond[i + 1])
        ky[i] = 0.5 * (k + turn(k, -1, 0))
        kz[i] = 0.5 * (k + jnp.where(lane == depth - 1, 0.0, turn(k, -1, 1)))
        above[i] = 0.5 * (k + jnp.where(lane == 0, 0.0, turn(k, 1, 1)))

    col_g = gy * cols + wrapped(iota((size, LANES), 0), cols, size)
    inside_y = jnp.where((col_g >= 0) & (col_g < meta[4] * cols), 1.0, 0.0)
    col_f = col_g.astype(F32)
    fall = jnp.exp(-lane.astype(F32) / ABSORB_DEPTH)
    first_row = (gx * meta[5] + gz) * rows - SKIN

    for s in range(STEPS * SUBSTEPS):
        src, dst = (temp, other) if s % 2 == 0 else (other, temp)
        last = s == STEPS * SUBSTEPS - 1
        a = beam[s, 0].astype(F32)
        b = beam[s, 1].astype(F32)
        spot = LASER_POWER * fall * jnp.exp(-(((col_f - b) / SPOT_RADIUS) ** 2))
        lo, hi = s + 1, n - 1 - s
        fx0 = kx[lo - 1] * (src[lo] - src[lo - 1])
        for i in range(lo, hi):
            v = src[i]
            fx = kx[i] * (src[i + 1] - v)
            fy = ky[i] * (turn(v, -1, 0) - v)
            down = kz[i] * (jnp.where(lane == depth - 1, 0.0, turn(v, -1, 1)) - v)
            up = above[i] * (jnp.where(lane == 0, 0.0, turn(v, 1, 1)) - v)
            row = first_row + i
            along_x = jnp.exp(-((jnp.full((1, LANES), row.astype(F32) - a) / SPOT_RADIUS) ** 2))
            change = (fx - fx0) + (fy - turn(fy, 1, 0)) + (down + up) + spot * along_x
            new = v + HEAT_STEP * change
            if last:
                out[i - SKIN] = new[:cols]
            else:
                ok = (row >= 0) & (row < meta[3] * meta[5] * rows)
                dst[i] = new * (inside_y * jnp.where(ok, 1.0, 0.0))
            fx0 = fx


def seal_kernel(meta, bulk, mine, given, out):
    rows, cols, depth = bulk.shape
    per = LANES // cols
    lane = iota((LANES, LANES), 1)
    for j in range(mine.shape[0]):
        skin = jnp.where(meta[2] == 0, mine[j], given[j])
        skin = jnp.concatenate([skin, jnp.zeros((LANES - SUBL, LANES), F32)], axis=0)
        block = jnp.where(lane < SKIN, jnp.transpose(skin), bulk[j * per : (j + 1) * per].reshape(LANES, LANES))
        out[j * per : (j + 1) * per] = block.reshape(per, cols, LANES)


def pack_skin(t, rows, cols, scratch, out):
    per = LANES // cols
    lane = iota((SUBL, LANES), 1)
    for j in range(SUBL // per):
        acc = jnp.zeros((SUBL, LANES), F32)
        for q in range(per):
            acc = jnp.where(lane // cols == q, turn(scratch[rows + j * per + q], cols * q, 1), acc)
        out[j] = acc


def split(value):
    high = value.astype(jnp.bfloat16)
    rest = (value - high.astype(F32)).astype(jnp.bfloat16)
    return jnp.concatenate([high, rest], axis=1)


def height_matrix():
    shape = (2 * LANES, 2 * LANES)
    k = iota(shape, 0) & (LANES - 1)
    j = iota(shape, 1)
    above = jnp.where(k == (j & (LANES - 1)) + 1, 1.0, 0.0)
    below = jnp.where(k == (j & (LANES - 1)) - 1, 1.0, 0.0)
    return (above + jnp.where(j < LANES, -below, below)).astype(jnp.bfloat16)


def height_terms(ref, first, last, matrix, diff, total, start=0, comps=tuple(range(COMPS))):
    size = diff.shape[2]
    for c in comps:
        rows = ref[c, first:last, start : start + size].reshape((last - first) * size, LANES)
        both = jnp.dot(split(rows), matrix, preferred_element_type=F32)
        diff[c, first:last] = both[:, :LANES].reshape(last - first, size, LANES)
        total[c, first:last] = both[:, LANES:].reshape(last - first, size, LANES)


def cut_weights(low_z, scale):
    lane = iota((1, LANES), 1)
    up = (lane == LANES - 1) & low_z
    down = (lane == 0) & jnp.logical_not(low_z)
    weight = {}
    for v in sorted(set(VISCOSITY)):
        side = scale * GAS_STEP * v
        drift = 0.5 * DRIFT_SPEED * scale * GAS_STEP
        weight[v] = jnp.where(up, side - drift, jnp.where(down, side + drift, 0.0))
    return jnp.where(up, 1.0, jnp.where(down, -1.0, 0.0)), weight


def stepped(comps, ref, i, diff, total, h, cut, scale, start, size, skip=0):
    sign, weight = cut
    half = 0.5 * scale * GAS_STEP
    span = pl.ds(start, size)
    terms = pl.ds(start - skip, size)

    def dx(c):
        return ref[c, i + 1, span, :] - ref[c, i - 1, span, :]

    def dy(c):
        return ref[c, i, pl.ds(start + 1, size), :] - ref[c, i, pl.ds(start - 1, size), :]

    def dz(c):
        return diff[c, i, terms, :] + sign * h[i, span, 2 * c : 2 * c + 1]

    spread = half * (dx(2) + dy(3) + dz(4))
    out = {}
    for c in comps:
        v = VISCOSITY[c]
        side = scale * GAS_STEP * v
        drift = 0.5 * DRIFT_SPEED * scale * GAS_STEP
        sides = (ref[c, i + 1, span, :] + ref[c, i - 1, span, :]) + (
            ref[c, i, pl.ds(start + 1, size), :] + ref[c, i, pl.ds(start - 1, size), :]
        )
        across = h[i, span, 2 * c : 2 * c + 1]
        new = (
            scale * (1.0 - 6.0 * GAS_STEP * v) * ref[c, i, span, :]
            + side * (sides + total[c, i, terms, :])
            - drift * diff[c, i, terms, :]
            + weight[v] * across
        )
        if c == 2:
            new = new - half * dx(5)
        elif c == 3:
            new = new - half * dy(5)
        elif c == 4:
            new = new - half * dz(5)
        else:
            new = new - {0: VAPOR_LOAD, 1: AMBIENT_LOAD, 5: STIFFNESS}[c] * spread
        out[c] = new
    return out


def by_comp(lane, values):
    out = jnp.full(lane.shape, values[-1], F32)
    for c, v in enumerate(values[:-1]):
        out = jnp.where(lane == 2 * c, v, out)
    return out


def couple_matrix():
    shape = (6 * LANES, LANES)
    k = iota(shape, 0)
    j = iota(shape, 1)
    axis = k // (2 * LANES)
    lane = k & (LANES - 1)
    spread = (lane == 4 + 2 * axis) & ((j == 0) | (j == 2) | (j == 10))
    slope = (lane == 10) & (j == 4 + 2 * axis)
    return jnp.where(spread | slope, 1.0, 0.0).astype(jnp.bfloat16)


def halo_stepped(h0, h1, g, low_z, mask_of, start, size, out, at):
    n = h0.shape[0]
    span = slice(start, start + size)
    rows = (n - 2) * size
    lane = iota((1, LANES), 1)
    more = jnp.where(low_z, 1, 0)
    flat_lane = iota((rows, LANES), 1)
    touch = jnp.zeros((rows, LANES), F32)
    for c in range(COMPS):
        own = g[c, 1 : n - 1, span].reshape(rows, LANES)
        touch = jnp.where(flat_lane == 2 * c, turn(own, 2 * c + more, 1), touch)
    mid = h0[1 : n - 1, span].reshape(rows, LANES)
    east = h0[2:n, span].reshape(rows, LANES)
    west = h0[0 : n - 2, span].reshape(rows, LANES)
    if start:
        north = h0[1 : n - 1, start + 1 : start + size + 1].reshape(rows, LANES)
        south = h0[1 : n - 1, start - 1 : start + size - 1].reshape(rows, LANES)
    else:
        north, south = turn(mid, -1, 0), turn(mid, 1, 0)
    behind = h1[1 : n - 1, span].reshape(rows, LANES)
    slopes = [east - west, north - south, jnp.where(low_z, 1.0, -1.0) * (behind - touch)]
    coupled = jnp.dot(
        jnp.concatenate([split(v) for v in slopes], axis=1), couple_matrix(), preferred_element_type=F32
    )
    up = by_comp(lane, [GAS_STEP * (v - 0.5 * DRIFT_SPEED) for v in VISCOSITY])
    down = by_comp(lane, [GAS_STEP * (v + 0.5 * DRIFT_SPEED) for v in VISCOSITY])
    half = 0.5 * GAS_STEP
    pull = by_comp(lane, [-half * VAPOR_LOAD, -half * AMBIENT_LOAD, -half, -half, -half, -half * STIFFNESS])
    new = (
        by_comp(lane, [1.0 - 6.0 * GAS_STEP * v for v in VISCOSITY]) * mid
        + by_comp(lane, [GAS_STEP * v for v in VISCOSITY]) * ((east + west) + (north + south))
        + jnp.where(low_z, up, down) * behind
        + jnp.where(low_z, down, up) * touch
        + pull * coupled
    )
    for i in range(1, n - 1):
        row = new[(i - 1) * size : i * size] * mask_of(i, start, size)
        if at < 0:
            row, at_row = turn(row, at, 0), 0
        else:
            at_row = at
        out[i - 1, at_row : at_row + size] = row


def grid_masks(meta, n, size, own_x, own_y):
    before, before_y = (n - own_x) // 2, (size - own_y) // 2

    def mask_of(i, start, count):
        x_g = meta[0] * own_x + i - before
        ok = (x_g >= 0) & (x_g < meta[3] * own_x)
        y_g = meta[1] * own_y + iota((count, LANES), 0) + start - before_y
        return jnp.where((y_g >= 0) & (y_g < meta[4] * own_y), 1.0, 0.0) * jnp.where(ok, 1.0, 0.0)

    return mask_of


def first_stage(meta, g, h0, windows, f, mask_of, unroll, comps=tuple(range(COMPS)), edge=(2, 5)):
    n = g.shape[1]
    cut = cut_weights(meta[2] == 0, 1.0)

    def one(comps):
        def body(i, carry):
            for start, size, diff, total, skip, at in windows:
                new = stepped(comps, g, i, diff, total, h0, cut, 1.0, start, size, skip)
                m = mask_of(i, start, size)
                for c in comps:
                    f[c, i - 1, at : at + size, :] = new[c] * m
            return carry

        return body

    lax.fori_loop(2, n - 2, one(comps), 0, unroll=unroll)
    for i in (1, n - 2) if edge else ():
        one(edge)(i, 0)


def second_stage(meta, g, f, fh, diff, total, skip, reach, own_y, mask_of, store):
    start = (g.shape[2] - own_y) // 2 - reach
    count = own_y + 2 * reach
    cut = cut_weights(meta[2] == 0, 0.5)

    def two(comps):
        def body(i, carry):
            new = stepped(comps, f, i - 1, diff, total, fh, cut, 0.5, start - skip, count)
            m = mask_of(i, start, count)
            for c in comps:
                new[c] = (0.5 * g[c, i, pl.ds(start, count), :] + new[c]) * m
            store(i, new)
            return carry

        return body

    return two


class Joined:
    def __init__(self, low, high):
        self.low, self.high = low, high

    def __getitem__(self, key):
        return (self.low if key[0] < self.low.shape[0] else self.high)[key]


def lane_sums(value):
    high = value.astype(jnp.bfloat16)
    rest = value - high.astype(F32)
    middle = rest.astype(jnp.bfloat16)
    low = (rest - middle.astype(F32)).astype(jnp.bfloat16)
    parts = jnp.concatenate([high, middle, low], axis=1)
    ones = jnp.ones((3 * LANES, LANES), jnp.bfloat16)
    return jnp.dot(parts, ones, preferred_element_type=F32)


def fine_pressure(meta, p, h0, own_x, own_y, part_rows):
    n, count = p.shape[0], p.shape[1]
    skip = (h0.shape[1] - count) // 2
    skip_x = (h0.shape[0] - n) // 2
    before = (n - own_x) // 2
    y_l = iota((count, LANES), 0) - (count - own_y) // 2
    col_y = lax.div(wrapped(iota((count, LANES), 1), 2 * own_y, LANES) + LANES, 2) - LANES // 2
    pick = col_y == y_l
    row_x = lax.div(wrapped(iota((part_rows, LANES), 0), 2 * own_x, part_rows) + LANES, 2) - LANES // 2
    height = (iota((count, LANES), 1) + meta[2] * LANES).astype(F32)
    fine = jnp.zeros((part_rows, LANES), F32)
    full = -(-count // SUBL) * SUBL
    pad = [jnp.zeros((full - count, LANES), F32)] if full > count else []
    found = []
    for i in range(n):
        level = h0[i + skip_x, skip : skip + count, LEVEL : LEVEL + 1]
        found += [jnp.where(height == level, p[i], 0.0)] + pad
    at = lane_sums(jnp.concatenate(found, axis=0))
    for i in range(n):
        line = jnp.sum(jnp.where(pick, at[i * full : i * full + count], 0.0), axis=0, keepdims=True)
        fine = jnp.where(row_x == i - before, line, fine)
    return fine


def top_heat(meta, beam, first, t, k, fine, own_rows, cols):
    gx, gy = meta[0], meta[1]
    shape = fine.shape
    row = gx * own_rows + wrapped(iota(shape, 0), own_rows, shape[0])
    col = gy * cols + wrapped(iota(shape, 1), cols, shape[1])
    row, col = row.astype(F32), col.astype(F32)
    deep = TOP - 1 - first
    kx = [0.5 * (v + turn(v, -1, 0)) for v in k[:deep]]
    ky = [0.5 * (v + turn(v, -1, 1)) for v in k[:deep]]
    ky_low = [0.5 * (v + turn(v, 1, 1)) for v in k[:deep]]
    kz = [0.5 * (k[d] + k[d + 1]) for d in range(deep)]
    for s in range(SUBSTEPS):
        beam_xy = heat_source(row, col, beam, first + s)
        before = 0.5 * k[0] * t[0]
        new = []
        for d in range(TOP - 1 - first - s):
            fx = kx[d] * (turn(t[d], -1, 0) - t[d])
            fy = ky[d] * (turn(t[d], -1, 1) - t[d]) + ky_low[d] * (turn(t[d], 1, 1) - t[d])
            fz = kz[d] * (t[d + 1] - t[d])
            factor = jnp.exp(jnp.full(shape, -d / ABSORB_DEPTH, F32))
            change = (fx - turn(fx, 1, 0)) + fy + (fz - before) + beam_xy * factor
            if d == 0:
                change = change - LATENT_HEAT * softplus(t[0] - BOIL_LEVEL - BACK_PRESSURE * fine)
            new.append(jnp.where(k[d] > 0, t[d] + HEAT_STEP * change, 0.0))
            before = fz
        t = new
    return t


def vapor_mass(t0, fine):
    four = t0 + turn(t0, -1, 1)
    four = four + turn(four, -1, 0)
    return softplus(0.25 * four - BOIL_LEVEL - BACK_PRESSURE * fine)


def mass_rows(meta, h, mass, first, rows, count, own_y):
    skip = (h.shape[1] - count) // 2
    skip_x = (h.shape[0] - rows) // 2
    y_l = iota((count, LANES), 0) - (count - own_y) // 2
    col = wrapped(iota((count, LANES), 1), 2 * own_y, LANES)
    pick = col == 2 * y_l
    height = (iota((count, LANES), 1) + meta[2] * LANES).astype(F32)
    found = []
    for i in range(rows):
        r = (2 * (i + first)) % mass.shape[0]
        found.append(jnp.where(pick, mass[r : r + 1, :], 0.0))
    at = lane_sums(jnp.concatenate(found, axis=0))
    out = []
    for i in range(rows):
        level = h[i + skip_x, skip : skip + count, LEVEL : LEVEL + 1]
        out.append(jnp.where(height == level, at[i * count : (i + 1) * count], 0.0))
    return out


def inner_kernel(cells, meta, u, in_a, in_b, in_z, in_d, in_h, g, f, h0, h1, fh, diff, total):
    rows_x, reach = cells
    even_x = lax.rem(meta[0], 2) == 0
    low_z = meta[2] == 0
    own_y = u.shape[2]
    tiles = own_y // SUBL
    size = g.shape[2]
    n = g.shape[1]
    zero = jnp.zeros((SUBL, LANES), F32)
    for x in range(-reach, rows_x + reach):
        for c in range(COMPS):
            for y in range(tiles):
                value = row_tile(c, x, y, u, in_a, in_b, even_x)
                g[c, x + reach, (y + 1) * SUBL : (y + 2) * SUBL, :] = zero if value is None else value
    base = in_z.shape[0] - tiles
    for b in range(3):
        parts = []
        for y in range(tiles):
            if b == 0:
                parts.append(jnp.where(low_z, in_d[base + y], in_h[y]))
            elif b == 1:
                parts.append(in_z[base + y])
            else:
                parts.append(jnp.where(low_z, in_h[y], in_d[base + y]))
        unpack_group(jnp.concatenate(parts, axis=0), b, rows_x, reach, low_z, h0, h1, SUBL, own_y)
    mask_of = grid_masks(meta, n, size, rows_x, own_y)
    halo_stepped(h0, h1, g, low_z, mask_of, SUBL, own_y, fh, 0)
    height_terms(g, 1, n - 1, height_matrix(), diff, total, SUBL)
    first_stage(meta, g, h0, [(SUBL, own_y, diff, total, SUBL, 0)], f, mask_of, True)


def unpack_group(packed, b, rows_x, reach, low_z, h0, h1, start, size):
    for x in range(-reach, rows_x + reach):
        if (x + rows_x) // rows_x == b:
            base = GROUP * ((x + rows_x) % rows_x)
            here, other = turn(packed, -base, 1), turn(packed, -base - 1, 1)
            h0[x + reach, start : start + size] = jnp.where(low_z, here, other)
            h1[x + reach, start : start + size] = jnp.where(low_z, other, here)


def first_kernel(
    cells, meta, beam, part, in_a, in_b, in_z, in_d, gy_a, gy_b, g_in, f_in, h0_in, h1_in, fh_in,
    out_g, out_m, out_t, out_k, g, h, h1, f, fh, diff_lo, total_lo, diff_hi, total_hi, diff, total, p, mass, skin,
):
    rows_x, reach = cells
    gx, gy, gz = meta[0], meta[1], meta[2]
    even_x = lax.rem(gx, 2) == 0
    even_y = lax.rem(gy, 2) == 0
    low_z = gz == 0
    n, size = g.shape[1], g.shape[2]
    own_y = size - 2 * SUBL
    tiles = own_y // SUBL
    half = SUBL // 2
    sub = iota((SUBL, LANES), 0)
    zero = jnp.zeros((SUBL, LANES), F32)
    inner = slice(SUBL, SUBL + own_y)

    def side(k):
        upper = jnp.where(even_y, gy_a[k], gy_b[k])
        lower = jnp.where(even_y, gy_b[k], gy_a[k])
        return upper, lower

    quarter = (rows_x + 2 * NEAR) * COMPS // 2
    places_of = {}
    for k, (x, skip) in enumerate(quarter_rows(rows_x, reach)):
        places_of[x, skip] = quarter + k
    for x in range(-reach, rows_x + reach):
        i = x + reach
        for c in range(COMPS):
            g[c, i, inner, :] = g_in[c, i, inner, :]
            upper = lower = zero
            if -NEAR <= x < rows_x + NEAR:
                near_up, near_low = side((x + NEAR) * COMPS // 2 + c // 2)
                if c % 2:
                    near_up, near_low = turn(near_up, half, 0), turn(near_low, half, 0)
                upper = jnp.where(sub < half, near_up, 0.0)
                lower = jnp.where(sub >= half, near_low, 0.0)
            for skip in (0, FULL):
                if (x, skip) in places_of and c in QUARTERS:
                    q = 2 * QUARTERS.index(c)
                    up, low = side(places_of[x, skip])
                    upper = jnp.where((sub & -2) == skip, turn(up, skip - q, 0), upper)
                    lower = jnp.where((sub & -2) == SUBL - 2 - skip, turn(low, SUBL - 2 - skip - q, 0), lower)
            g[c, i, own_y + SUBL : size, :] = upper
            g[c, i, :SUBL, :] = lower
    h[:, inner, :] = h0_in[:, inner, :]
    h1[:, inner, :] = h1_in[:, inner, :]
    for b in range(3):
        upper, lower = side(quarter + len(places_of) + b)
        unpack_group(lower, b, rows_x, reach, low_z, h, h1, 0, SUBL)
        unpack_group(upper, b, rows_x, reach, low_z, h, h1, own_y + SUBL, SUBL)

    def store(i, new):
        p[i - 2] = new[COMPS - 1]
        if len(new) > 1:
            for c in range(COMPS):
                out_g[c, i - 3] = new[c] if c in new else jnp.zeros_like(new[COMPS - 1])

    mask_of = grid_masks(meta, n, size, rows_x, own_y)
    f[:, :, inner, :] = f_in[...]
    fh[:, inner, :] = fh_in[...]
    upper_at = size - SUBL - 1
    windows = []
    for start, d, t in ((1, diff_lo, total_lo), (upper_at, diff_hi, total_hi)):
        halo_stepped(h, h1, g, low_z, mask_of, start, SUBL, fh, start)
        height_terms(g, 1, n - 1, height_matrix(), d, t, start)
        windows.append((start, SUBL, d, t, start, start))
    first_stage(meta, g, h, windows, f, mask_of, True)
    height_terms(f, 1, n - 3, height_matrix(), diff, total)
    two = second_stage(meta, g, f, fh, diff, total, 0, reach - 2, own_y, mask_of, store)
    lax.fori_loop(4, n - 4, two(tuple(range(COMPS))), 0, unroll=True)
    for i in (2, n - 3):
        two((5,))(i, 0)
    for i in (3, n - 4):
        two((2, 5))(i, 0)
    fine = fine_pressure(meta, p, h, rows_x, own_y, mass.shape[0])

    cols = LANES // 4
    per = LANES // cols
    lane = iota((SUBL, LANES), 1)
    sources = surface_sources(part, in_a, in_b, in_z, in_d, even_x, tiles)
    count = len(sources) // 2
    top_at = gy_a.shape[0] - len(sources) // per
    layers = []
    for a in range(2):
        for s in range(count):
            src = sources[a * count + s]
            upper, lower = side(top_at + (a * count + s) // per)
            i = s % per
            for q in range(per):
                at = cols * q + SUBL * i
                skin[s * per + q] = jnp.where(
                    lane < cols,
                    turn(src, -cols * q, 1),
                    jnp.where(
                        lane < cols + SUBL,
                        turn(upper, cols - at, 1),
                        jnp.where(lane >= LANES - SUBL, turn(lower, LANES - SUBL - at, 1), 0.0),
                    ),
                )
        for d in range(TOP):
            layers.append(skin[:, d, :])
    t, k = layers[:TOP], layers[TOP:]
    t = top_heat(meta, beam, 0, t, k, fine, 2 * rows_x, cols)
    for d in range(TOP - SUBSTEPS):
        out_t[d] = t[d]
        out_k[d] = k[d]
    mass[...] = vapor_mass(t[0], fine)

    count, small = out_g.shape[1], out_g.shape[2]
    masses = mass_rows(meta, h, mass, -REACH_LAST, count, small, own_y)
    lane_s = iota((small, LANES), 1)
    y_g = gy * own_y + iota((small, LANES), 0) - (small - own_y) // 2
    inside_y = jnp.where((y_g >= 0) & (y_g < meta[4] * own_y), 1.0, 0.0)
    skip = (size - small) // 2
    per = LANES // GROUP
    acc = jnp.zeros((small, LANES), F32)
    for i in range(count):
        x = i - REACH_LAST
        x_g = gx * rows_x + x
        ok = jnp.where((x_g >= 0) & (x_g < meta[3] * rows_x), 1.0, 0.0)
        add = masses[i] * (inside_y * ok)
        rows = [out_g[c, i] for c in range(COMPS)]
        for c, load in ((0, VAPOR_SOURCE), (4, RECOIL_PUSH), (5, RECOIL_PRESSURE)):
            rows[c] = rows[c] + load * add
            out_g[c, i] = rows[c]
        j, q = divmod(i, per)
        acc = pack_heights(rows, GROUP * q, lane_s, low_z, acc)
        level = h[x + reach, skip : skip + small, LEVEL : LEVEL + 1]
        acc = jnp.where((lane_s & -2) == GROUP * q + LEVEL, level, acc)
        if q == per - 1 or i == count - 1:
            out_m[j] = acc
            acc = jnp.zeros((small, LANES), F32)


def last_kernel(
    cells, meta, beam, g, g_diff, g_total, in_m, in_t, in_k, bulk, out_t, out_f, top, fine_out, p, h, f, fh, h1, diff, total, skin
):
    rows_x, own_y = cells
    n, size = g.shape[1], g.shape[2]
    for i in range(n):
        j, q = divmod(i, LANES // GROUP)
        unpack_heights(in_m[j], GROUP * q, meta[2] == 0, h, h1, i)
    mask_of = grid_masks(meta, n, size, rows_x, own_y)
    matrix = height_matrix()
    halo_stepped(h, h1, g, meta[2] == 0, mask_of, 0, size, fh, -1)
    flow = tuple(range(2, COMPS))
    first_stage(meta, g, h, [(1, size - 2, g_diff, g_total, 0, 0)], f, mask_of, True, flow)
    height_terms(f, 1, n - 3, matrix, diff, total, 0, (4, 5))

    def store(i, new):
        p[i - 2] = new[COMPS - 1]

    two = second_stage(meta, g, f, fh, diff, total, 1, REACH_LAST - 2, own_y, mask_of, store)
    lax.fori_loop(2, n - 2, two((COMPS - 1,)), 0, unroll=True)
    fine = fine_pressure(meta, p, h, rows_x, own_y, top.shape[0])
    cols = LANES // 4
    t = [in_t[d] for d in range(TOP - SUBSTEPS)]
    k = [in_k[d] for d in range(TOP - SUBSTEPS)]
    t = top_heat(meta, beam, SUBSTEPS, t, k, fine, 2 * rows_x, cols)
    skin[...] = jnp.zeros_like(skin)
    for d in range(SKIN):
        skin[:, d, :] = t[d]
    pack_skin(t, 0, cols, skin, out_t)
    pack_skin(t, SUBL, cols, skin, out_f)
    top[...] = t[0]
    fine_out[...] = fine


def terms_kernel(meta, g, diff, total):
    height_terms(g, 1, g.shape[1] - 1, height_matrix(), diff, total)


def gas_kernel(meta, g, g_diff, g_total, top, fine, p, h, flow, fh, out_g, f, diff, total, mass):
    rows_x, own_y = out_g.shape[1], out_g.shape[2]
    n, size = g.shape[1], g.shape[2]
    matrix = height_matrix()
    mask_of = grid_masks(meta, n, size, rows_x, own_y)
    first_stage(meta, g, h, [(1, size - 2, g_diff, g_total, 0, 0)], f, mask_of, True, (0, 1), ())
    both = Joined(f, flow)
    height_terms(both, 2, n - 4, matrix, diff, total, 0, tuple(range(COMPS)))
    mass[...] = vapor_mass(top[...], fine[...])
    masses = mass_rows(meta, h, mass, 0, rows_x, own_y, own_y)
    loads = {0: VAPOR_SOURCE, 4: RECOIL_PUSH, 5: RECOIL_PRESSURE}

    def store(i, new):
        x = i - (n - rows_x) // 2
        for c in new:
            out_g[c, x] = new[c] + loads[c] * masses[x] if c in loads else new[c]

    two = second_stage(meta, g, both, fh, diff, total, 1, 0, own_y, lambda i, start, count: 1.0, store)
    for i in range(REACH_LAST, n - REACH_LAST):
        two(tuple(range(COMPS - 1)))(i, 0)
        x = i - (n - rows_x) // 2
        out_g[COMPS - 1, x] = p[i - 2, 1 : own_y + 1] + RECOIL_PRESSURE * masses[x]


def places():
    axes = ("gx", "gy", "gz")
    return [lax.axis_index(a) for a in axes] + [lax.axis_size(a) for a in axes]


def call(body, outs, scratch=(), scalars=0, count=0):
    def kernel(*refs):
        body(places(), *refs)

    vmem = pl.BlockSpec(memory_space=pltpu.VMEM)
    smem = pl.BlockSpec(memory_space=pltpu.SMEM)
    return pl.pallas_call(
        kernel,
        out_shape=[jax.ShapeDtypeStruct(s, F32) for s in outs],
        in_specs=[smem] * scalars + [vmem] * count,
        out_specs=[vmem] * len(outs),
        scratch_shapes=[pltpu.VMEM(s, F32) for s in scratch],
        compiler_params=pltpu.CompilerParams(vmem_limit_bytes=VMEM_LIMIT),
    )


def pairs(count, odd):
    out = []
    for i in range(odd, count - 1, 2):
        out += [(i, i + 1), (i + 1, i)]
    return out


def cross(nx, nz, upper):
    out = []
    for i in range(nx - 1):
        a, b = i * nz + (nz - 1 if upper else 0), (i + 1) * nz + (0 if upper else nz - 1)
        out += [(a, b), (b, a)]
    return out


def shards(u, t, m, lev, beam):
    nx, ny, nz = (lax.axis_size(a) for a in ("gx", "gy", "gz"))
    _, rows_x, own_y, _ = u.shape
    t, m = jnp.transpose(t, (1, 2, 0)), jnp.transpose(m, (1, 2, 0))
    rows, cols, depth = t.shape
    tiles = own_y // SUBL
    block = (SUBL, LANES)
    n_top = 2 * rows * cols // LANES
    top = (n_top // tiles, own_y, LANES)
    n_x = slab_size() + top[0]
    n_z = 2 * SKIN * cols // SUBL + n_top + tiles
    vmem = pl.BlockSpec(memory_space=pltpu.VMEM)
    hbm = pl.BlockSpec(memory_space=pltpu.HBM)

    def pack(*refs):
        pack_kernel(REACH, places(), *refs)

    whole = (2 * rows + 1, cols, depth)
    copies = 4 + 2 * (COMPS + 1 + len(DEEP_6) + top[0]) + 4
    shapes = [(n_x, own_y, LANES)] * 2 + [(n_z, *block)] * 2 + [(tiles, *block), whole]
    msg_a, msg_b, msg_z, msg_d, msg_h, part = pl.pallas_call(
        pack,
        out_shape=[jax.ShapeDtypeStruct(v, F32) for v in shapes],
        in_specs=[hbm] * 4,
        out_specs=[hbm] * 6,
        scratch_shapes=[pltpu.VMEM(u.shape, F32), pltpu.VMEM(m.shape, jnp.int32), pltpu.VMEM(lev.shape, jnp.int32)]
        + [pltpu.VMEM(v, F32) for v in shapes[2:]]
        + [pltpu.SemaphoreType.DMA((copies,))],
        compiler_params=pltpu.CompilerParams(vmem_limit_bytes=60 * 1024 * 1024),
    )(u, t, m, lev)
    u, part = call(hold_kernel, [u.shape, whole], count=2)(u, part)
    in_a = lax.ppermute(msg_a, "gx", pairs(nx, 0))
    in_b = lax.ppermute(msg_b, "gx", pairs(nx, 1))
    in_z = lax.ppermute(msg_z, "gz", pairs(nz, 0))
    in_d = lax.ppermute(msg_d, ("gx", "gz"), cross(nx, nz, True))
    in_h = lax.ppermute(msg_h, ("gx", "gz"), cross(nx, nz, False))
    n_y = (rows_x + 2 * NEAR) * COMPS // 2 + len(quarter_rows(rows_x, REACH)) + 3 + n_top
    n_part = rows + 2 * SKIN
    msg_a, msg_b, part_a, part_b = call(
        functools.partial(relay_kernel, (rows_x, REACH)), [(n_y, *block)] * 2 + [(n_part, *block)] * 2, count=7
    )(u, part, in_a, in_b, in_z, in_d, in_h)
    gy_b = lax.ppermute(msg_b, "gy", pairs(ny, 1))
    gy_a = lax.ppermute(msg_a, "gy", pairs(ny, 0))
    part_b = lax.ppermute(part_b, "gy", pairs(ny, 1))
    part_a = lax.ppermute(part_a, "gy", pairs(ny, 0))

    size = own_y + 2 * SUBL
    n = rows_x + 2 * REACH
    n2 = rows_x + 2 * REACH_LAST
    small = own_y + SUBL
    part_rows = 4 * SUBL
    n_m = -(-n2 // (LANES // GROUP))
    row = (size, LANES)
    own_row = (own_y, LANES)
    g1, f1, h0, h1, fh1 = call(
        functools.partial(inner_kernel, (rows_x, REACH)),
        [(COMPS, n, *row), (COMPS, n - 2, *own_row), (n, *row), (n, *row), (n - 2, *own_row)],
        scratch=[(COMPS, n - 1, *own_row)] * 2,
        count=6,
    )(u, in_a, in_b, in_z, in_d, in_h)
    g2, msg_m, top_t, top_k = call(
        functools.partial(first_kernel, (rows_x, REACH)),
        [
            (COMPS + 1, n2, small, LANES),
            (n_m, small, LANES),
            (TOP - SUBSTEPS, part_rows, LANES),
            (TOP - SUBSTEPS, part_rows, LANES),
        ],
        scratch=[(COMPS, n, *row), (n, *row), (n, *row), (COMPS, n - 2, *row), (n - 2, *row)]
        + [(COMPS, n - 1, *block)] * 4
        + [(COMPS, n - 3, *row)] * 2
        + [(n - 4, own_y + 2 * (REACH - 2), LANES), (part_rows, LANES), (part_rows, *block)],
        scalars=1,
        count=12,
    )(beam, part, in_a, in_b, in_z, in_d, gy_a, gy_b, g1, f1, h0, h1, fh1)
    in_m = lax.ppermute(msg_m, "gz", pairs(nz, 0))
    field = (rows + 2 * SKIN, cols + SUBL, depth)
    (bulk,) = call(
        bulk_kernel, [t.shape], scratch=[field] * 7, scalars=1, count=5
    )(beam, part, in_z, in_d, part_a, part_b)
    low_row = (small, LANES)
    g_diff, g_total = call(terms_kernel, [(COMPS + 1, n2 - 1, *low_row)] * 2, count=1)(g2)
    mine, other, top_last, fine, p, h, f, fh = call(
        functools.partial(last_kernel, (rows_x, own_y)),
        [
            (n_top // 2, *block),
            (n_top // 2, *block),
            (part_rows, LANES),
            (part_rows, LANES),
            (n2 - 4, own_y + 2 * (REACH_LAST - 2), LANES),
            (n2, *low_row),
            (COMPS + 1, n2 - 2, *low_row),
            (n2 - 2, *low_row),
        ],
        scratch=[(n2, *low_row)] + [(COMPS + 1, n2 - 1, *low_row)] * 2 + [(part_rows, *block)],
        scalars=1,
        count=7,
    )(beam, g2, g_diff, g_total, in_m, top_t, top_k, bulk)
    (gas,) = call(
        gas_kernel,
        [u.shape],
        scratch=[(2, n2 - 2, *low_row)] + [(COMPS, n2 - 1, *low_row)] * 2 + [(part_rows, LANES)],
        count=9,
    )(g2, g_diff, g_total, top_last, fine, p, h, f, fh)
    given = lax.ppermute(other, "gz", pairs(nz, 0))
    (out,) = call(seal_kernel, [t.shape], count=3)(bulk, mine, given)
    return gas, jnp.transpose(out, (2, 0, 1))


def solution(mesh):
    return jax.shard_map(
        shards,
        mesh=mesh,
        in_specs=(
            P(None, "gx", "gy", "gz"),
            P(None, ("gx", "gz"), "gy"),
            P(None, ("gx", "gz"), "gy"),
            P("gx", "gy"),
            P(),
        ),
        out_specs=(P(None, "gx", "gy", "gz"), P(None, ("gx", "gz"), "gy")),
        check_vma=False,
    )
```
